32 devices in a mesh: dp: 4 (over z), mp: 8 (over y, x, core).
Axes of the slice: x: 2, y: 2, z: 4, core: 2. Of those that a mesh axis runs over, the one named last changes fastest.
Arguments:
- hidden_in: bfloat16 [8, 2048, 2048], P('dp', 'mp'), may hold values from -6 to 6
- doc_ids: int32 [8, 2048], P('dp'), may hold values from 0 to 2, never falling along the last dimension, each value on 1 to 1920 neighbouring positions
- tile_slot: int32 [44], replicated, may hold values from 0 to 47, as said below
- attention_gain: float32 [2048], replicated, may hold values from 0.1 to 1.9
- query_gain: float32 [64], replicated, may hold values from 0.1 to 1.9
- key_gain: float32 [64], replicated, may hold values from 0.1 to 1.9
- attend_weight: bfloat16 [2048, 1920], P('mp'), may hold values from -0.125 to 0.125
- output_weight: bfloat16 [1280, 2048], P('mp'), may hold values from -1 to 1
- feed_gain: float32 [2048], replicated, may hold values from 0.1 to 1.9
- gate_up_slots: bfloat16 [48, 2048, 256], P('mp'), may hold values from -0.125 to 0.125
- down_slots: bfloat16 [48, 128, 2048], P('mp'), may hold values from -0.15625 to 0.15625
- out_grad: float32 [8, 2048, 2048], P('dp', 'mp'), may hold values from -6 to 6
Outputs:
- layer_out: float32 [8, 2048, 2048], P('dp', 'mp')
- input_grad: float32 [8, 2048, 2048], P('dp', 'mp')
- grad_attend: float32 [2048, 1920], P('mp')
- grad_output: float32 [1280, 2048], P('mp')
- grad_gate_up: float32 [48, 2048, 256], P('mp')
- grad_down: float32 [48, 128, 2048], P('mp')
- grad_attention_gain: float32 [2048], replicated
- grad_query_gain: float32 [64], replicated
- grad_key_gain: float32 [64], replicated
- grad_feed_gain: float32 [2048], replicated
The draws below stay inside these ranges and needn't reach their ends.
Inputs may be any that keep to these rules, and one draw needn't show every extreme that they name: tile_slot holds 44 distinct slots; slot c * 6 + k lies on mp device c; the 4 unused slots are each the last slot of a different device, never of the last device.
All inputs are finite; a program needn't handle non-finite values.
Results may differ from the reference program's by a relative error of at most 0.022.
Values may be sent and summed in bfloat16 or wider, within the bound.
A program may use at most 512 MiB of HBM per device.

```python
import math
import jax
import jax.numpy as jnp
import numpy as np
from jax import lax

D = 2048
H = 20
KVH = 5
HD = 64
FF = 5632
TILE = 128
L = 2048
DOCS = 3
ROWS = 8
TILES = 44
CAP = 6
SLOTS = 48
N_MP = 8


def draw_tile_slot(key, part):
    key = jax.random.fold_in(key, 7)
    device_key, tile_key = jax.random.split(key)
    devices = jax.random.permutation(device_key, N_MP - 1)
    device_rank = jnp.concatenate([jnp.argsort(devices).astype(jnp.int32), jnp.full((1,), N_MP - 1, dtype=jnp.int32)])
    vacant_count = SLOTS - TILES
    slot_ids = jnp.arange(SLOTS, dtype=jnp.int32)
    owners = slot_ids // CAP
    final_slot = slot_ids % CAP == CAP - 1
    hollow = final_slot & (device_rank[owners] < vacant_count)
    ordering = jnp.argsort(hollow.astype(jnp.int32), stable=True).astype(jnp.int32)
    chosen = jax.random.permutation(tile_key, TILES)
    return ordering[chosen].astype(jnp.int32)


def block_levels(key, dims, pieces, least, high):
    def one(axis_at, blocks):
        draws = jax.random.uniform(jax.random.fold_in(jax.random.fold_in(key, 6), axis_at), (blocks,), jnp.float32, least / len(pieces), high / len(pieces))
        return jnp.repeat(jnp.exp(draws), dims[axis_at] // blocks).reshape((-1,) + (1,) * (len(dims) - axis_at - 1))

    level = one(*pieces[0])
    for cut in pieces[1:]:
        level = level * one(*cut)
    return level


def length_profile(count, total, reach, lean):
    weights = [(1 << 20) // math.isqrt(rank ** lean) + 1 for rank in range(2, count + 1)]
    rest, counts = total - reach - (count - 1), [1] * (count - 1)
    while rest > 0:
        movable = [i for i in range(count - 1) if counts[i] < reach]
        whole, left = sum([weights[i] for i in movable]), rest
        for i in movable:
            addition = min(reach - counts[i], max(1, left * weights[i] // whole), rest)
            counts[i] = counts[i] + addition
            rest = rest - addition
    return np.array([reach] + counts)


def uneven_parts(key, count, total, most, skew):
    if count == 2:
        one = jax.random.randint(key, (), max(1, total - most), min(most, total - 1) + 1)
        return jnp.stack([one, total - one])
    lengths = jnp.asarray(length_profile(count, total, most, skew), jnp.int32)
    couples = (count - 1) // 2
    donor, receiver = lengths[1:1 + 2 * couples:2], lengths[2:2 + 2 * couples:2]
    slack = jnp.minimum(donor - 1, most - receiver)
    passed = jax.random.randint(jax.random.fold_in(key, 1), (couples,), 0, 1 << 20) % (slack + 1)
    lengths = lengths.at[1:1 + 2 * couples:2].set(donor - passed).at[2:2 + 2 * couples:2].set(receiver + passed)
    return lengths[jax.random.permutation(jax.random.fold_in(key, 2), count)]


def bell_draw(key, shape, scale, bound, cuts=(), held_as=jnp.bfloat16):
    values = scale * jax.random.normal(key, shape, jnp.float32)
    if cuts:
        values = values * block_levels(key, shape, cuts, -0.22, 0.18)
    return jnp.clip(values, -bound, bound).astype(held_as)


def setup_inputs(seed: int = 0) -> dict:
    arg_keys = jax.random.split(jax.random.key(seed), 13)
    return {
        "hidden_in": bell_draw(arg_keys[0], (ROWS, L, D), 1.0, 6.0, ((0, 4), (1, 8))),
        "doc_ids": jax.vmap(lambda own: jnp.searchsorted(jnp.cumsum(uneven_parts(own, DOCS, L, L - L // (2 * N_MP), 2)), jnp.arange(L), side="right"))(jax.random.split(arg_keys[1], ROWS)).reshape((ROWS, L)).astype(jnp.int32),
        "tile_slot": draw_tile_slot(jax.random.fold_in(arg_keys[12], 71), 0),
        "attention_gain": jnp.clip(1.0 + 0.18 * jax.random.normal(arg_keys[3], (D,), jnp.float32), 0.1, 1.9),
        "query_gain": jnp.clip(1.0 + 0.18 * jax.random.normal(arg_keys[4], (HD,), jnp.float32), 0.1, 1.9),
        "key_gain": jnp.clip(1.0 + 0.18 * jax.random.normal(arg_keys[5], (HD,), jnp.float32), 0.1, 1.9),
        "attend_weight": bell_draw(arg_keys[6], (D, (H + 2 * KVH) * HD), D ** -0.5, 0.125, ((0, 8),)),
        "output_weight": bell_draw(arg_keys[7], (H * HD, D), (H * HD // 32) ** -0.5, 1.0, ((0, 8),)),
        "feed_gain": jnp.clip(1.0 + 0.18 * jax.random.normal(arg_keys[8], (D,), jnp.float32), 0.1, 1.9),
        "gate_up_slots": bell_draw(arg_keys[9], (SLOTS, D, 2 * TILE), D ** -0.5, 0.125, ((0, 8),)),
        "down_slots": bell_draw(arg_keys[10], (SLOTS, TILE, D), (FF // 4) ** -0.5, 0.15625, ((0, 8),)),
        "out_grad": bell_draw(arg_keys[11], (ROWS, L, D), 1.0, 6.0, ((0, 4), (1, 8)), jnp.float32),
    }


EPSILON = 1e-06

@jax.custom_vjp
def low(v):
    return lax.optimization_barrier(v.astype(jnp.bfloat16)).astype(jnp.float32)

@jax.custom_vjp
def low_back(v):
    return v

def low_keep(v):
    return (low(v), None)

def low_pass(kept, grad):
    return (grad,)

def back_keep(v):
    return (v, None)

def back_low(kept, grad):
    return (low(grad),)
low.defvjp(low_keep, low_pass)
low_back.defvjp(back_keep, back_low)

def doc_positions(docs):
    index = jnp.arange(docs.shape[-1], dtype=jnp.int32)
    change = jnp.concatenate([jnp.ones(docs.shape[:-1] + (1,), dtype=jnp.bool_), docs[..., 1:] != docs[..., :-1]], axis=-1)
    starts = lax.cummax(jnp.where(change, index, 0).astype(jnp.int32), axis=docs.ndim - 1)
    return index - starts

def rotary_tables(positions, head_dim):
    half_dim = head_dim // 2
    freqs = 1.0 / 10000.0 ** (jnp.arange(half_dim, dtype=jnp.float32) * 2.0 / head_dim)
    angles = positions.astype(jnp.float32)[..., None] * freqs
    cosine = jnp.cos(angles)
    sine = jnp.sin(angles)
    return (jnp.concatenate([cosine, cosine], -1), jnp.concatenate([sine, sine], -1))

def rotate(values, cosine, sine):
    half_dim = values.shape[-1] // 2
    turned = jnp.concatenate([-values[..., half_dim:], values[..., :half_dim]], -1)
    return values * cosine + turned * sine

def rms_norm(values, gain):
    scale = lax.rsqrt(lax.optimization_barrier(jnp.mean(values * values, axis=-1, keepdims=True)) + EPSILON)
    return values * scale * gain

def highest(form, left, right):
    return jnp.einsum(form, left, right, precision=lax.Precision.HIGHEST)

def attention_row(queries, keys, values, docs):
    sequence_len = docs.shape[0]
    block = min(512, sequence_len)
    count = sequence_len // block
    groups = H // KVH
    scale_dot = HD ** (-0.5)
    blocks = queries.reshape(count, block, KVH, groups, HD)
    starts = jnp.arange(count, dtype=jnp.int32) * block
    key_index = jnp.arange(sequence_len, dtype=jnp.int32)

    def one_block(pair):
        piece, start = pair
        query_index = start + jnp.arange(block, dtype=jnp.int32)
        query_docs = lax.dynamic_slice_in_dim(docs, start, block, 0)
        scores = low_back(highest('qkgd,skd->kgqs', piece, keys) * scale_dot)
        allowed = (key_index[None, :] <= query_index[:, None]) & (query_docs[:, None] == docs[None, :])
        probs = low(jax.nn.softmax(jnp.where(allowed, scores, -1e+30), axis=-1))
        return highest('kgqs,skd->qkgd', probs, values)
    outputs = lax.map(jax.checkpoint(one_block), (blocks, starts))
    return outputs.reshape(sequence_len, H * HD)

def forward_row(row_in, docs, attention_g, query_g, key_g, attend_w, output_w, feed_g, gate_up_w, down_w):
    sequence_len = row_in.shape[0]
    query_width = H * HD
    key_width = KVH * HD
    normed = low(rms_norm(row_in, attention_g))
    joined = low_back(jnp.dot(normed, attend_w, precision=lax.Precision.HIGHEST))
    cosine, sine = rotary_tables(doc_positions(docs), HD)
    cosine = cosine[:, None, :]
    sine = sine[:, None, :]
    queries = low(rotate(rms_norm(joined[:, :query_width].reshape(sequence_len, H, HD), query_g), cosine, sine))
    keys = low(rotate(rms_norm(joined[:, query_width:query_width + key_width].reshape(sequence_len, KVH, HD), key_g), cosine, sine))
    values = low(joined[:, query_width + key_width:].reshape(sequence_len, KVH, HD))
    context = low(low_back(attention_row(queries, keys, values, docs)))
    middle = row_in + low_back(jnp.dot(context, output_w, precision=lax.Precision.HIGHEST))
    normed_f = low(rms_norm(middle, feed_g))
    both = low_back(highest('nd,tdf->tnf', normed_f, gate_up_w))
    hidden = low(jax.nn.silu(both[..., :TILE]) * both[..., TILE:])
    return middle + low_back(highest('tnf,tfd->nd', hidden, down_w))

def reference(hidden_in, doc_ids, tile_slot, attention_gain, query_gain, key_gain, attend_weight, output_weight, feed_gain, gate_up_slots, down_slots, out_grad):
    params = (attention_gain.astype(jnp.float32), query_gain.astype(jnp.float32), key_gain.astype(jnp.float32), attend_weight.astype(jnp.float32), output_weight.astype(jnp.float32), feed_gain.astype(jnp.float32), gate_up_slots.astype(jnp.float32), down_slots.astype(jnp.float32))

    def step(totals, row):
        row_in, docs, row_grad = row

        def forward(row_value, attention_g, query_g, key_g, attend_w, output_w, feed_g, gate_up_w, down_w):
            return forward_row(row_value, docs, attention_g, query_g, key_g, attend_w, output_w, feed_g, gate_up_w[tile_slot], down_w[tile_slot])
        row_out, pull = jax.vjp(forward, row_in, *params)
        grads = pull(row_grad)
        totals = jax.tree.map(jnp.add, totals, tuple(grads[1:]))
        return (totals, (row_out, grads[0]))
    initial = tuple((jnp.zeros_like(param) for param in params))
    totals, outputs = lax.scan(step, initial, (hidden_in.astype(jnp.float32), doc_ids, out_grad.astype(jnp.float32)))
    layer_out, input_grad = outputs
    return (layer_out, input_grad, totals[3], totals[4], totals[6], totals[7], totals[0], totals[1], totals[2], totals[5])
```

```python
import functools

import jax
import jax.numpy as jnp
from jax import lax
from jax.experimental import pallas as pl
from jax.experimental.pallas import tpu as pltpu
from jax.sharding import PartitionSpec as P

H = 20
KVH = 5
HD = 64
TILE = 128
EPSILON = 1e-06
QW = H * HD
LANES = 128
GW = (H // KVH) * HD
LOG2E = 1.4426950408889634
LN2 = 0.6931471805599453
BF = jnp.bfloat16
F32 = jnp.float32
MIB = 1 << 20
NT = (((1,), (1,)), ((), ()))
TN = (((0,), (0,)), ((), ()))


def params(mib=56, axes=1, key=None):
    if key is None:
        return pltpu.CompilerParams(
            vmem_limit_bytes=mib * MIB, dimension_semantics=("arbitrary",) * axes
        )
    return pltpu.CompilerParams(
        vmem_limit_bytes=mib * MIB,
        dimension_semantics=("arbitrary",) * axes if axes else None,
        collective_id=key,
        has_side_effects=True,
    )


def mm(a, b):
    return jnp.dot(a, b, preferred_element_type=F32)


def dg(a, b, dims):
    return lax.dot_general(a, b, dims, preferred_element_type=F32)


def doc_starts(docs):
    index = jnp.arange(docs.shape[-1], dtype=jnp.int32)
    change = jnp.concatenate(
        [jnp.ones(docs.shape[:-1] + (1,), dtype=jnp.bool_), docs[..., 1:] != docs[..., :-1]],
        axis=-1,
    )
    return lax.cummax(jnp.where(change, index, 0), axis=docs.ndim - 1)


def rotary_tables(positions):
    half_dim = HD // 2
    freqs = 1.0 / 10000.0 ** (jnp.arange(half_dim, dtype=jnp.float32) * 2.0 / HD)
    angles = positions.astype(jnp.float32)[..., None] * freqs
    return jnp.tile(jnp.cos(angles), 4), jnp.tile(jnp.sin(angles), 4)


def rms_scale(values):
    return lax.rsqrt(jnp.mean(values * values, axis=-1, keepdims=True) + EPSILON)


MESH = pl.DeviceIdType.MESH


def flip(me, k):
    bit = 1
    while bit <= k:
        if k & bit:
            me = me + bit - 2 * bit * lax.rem(lax.div(me, bit), 2)
        bit *= 2
    return me


def link_bits(n):
    return [1 << i for i in range(1, n.bit_length() - 1)]


def greet(n, me):
    barrier = pltpu.get_barrier_semaphore()
    bits = [1] + link_bits(n)
    for bit in bits:
        pl.semaphore_signal(barrier, inc=1, device_id={"mp": flip(me, bit)}, device_id_type=MESH)
    pl.semaphore_wait(barrier, len(bits))


class Gather:
    def __init__(self, n, me, own, slot, send, recv):
        self.n, self.me, self.own, self.slot, self.send, self.recv = n, me, own, slot, send, recv
        bits = link_bits(n)
        self.order = (bits + [1], bits[::-1] + [1])
        even = [(k, h) for k in range(2, n, 2) for h in (0, 1)]
        even.sort(key=lambda kh: (bin(kh[0]).count("1"), max(self.place(*kh)), kh[1]))
        self.even = even

    def place(self, k, half):
        return [i for i, bit in enumerate(self.order[half]) if k & bit]

    def copy(self, k, half, bit):
        return pltpu.make_async_remote_copy(
            src_ref=self.own(half) if k == 0 else self.slot(k, half),
            dst_ref=self.slot(k, half),
            send_sem=self.send.at[k ^ bit, half],
            recv_sem=self.recv.at[k ^ bit, half],
            device_id={"mp": flip(self.me, bit)},
            device_id_type=MESH,
        )

    def onward(self, k, half):
        return self.order[half][(max(self.place(k, half)) + 1) if k else 0 :]

    def start(self):
        for i in range(len(self.order[0])):
            for half in (0, 1):
                self.copy(0, half, self.order[half][i]).start()

    def arrive(self, k, half):
        here = self.slot(k, half)
        pltpu.make_async_remote_copy(
            src_ref=here,
            dst_ref=here,
            send_sem=self.send.at[k, half],
            recv_sem=self.recv.at[k, half],
            device_id={"mp": flip(self.me, 1)},
            device_id_type=MESH,
        ).wait_recv()

    def forward(self, k, half):
        self.arrive(k, half)
        for bit in self.onward(k, half):
            self.copy(k, half, bit).start()

    def rest(self):
        for k, half in [(1, 0), (1, 1)] + [(k + 1, h) for k, h in self.even]:
            self.arrive(k, half)

    def drain(self):
        for k in range(0, self.n, 2):
            for half in (0, 1):
                for bit in self.onward(k, half):
                    self.copy(k, half, bit).wait_send()


class Scatter:
    def __init__(self, n, me, part, core, link, stage, sems):
        self.n, self.me, self.part = n, me, part
        self.core, self.link, self.stage = core, link, stage
        self.core_send, self.core_recv, self.link_send, self.link_recv = sems
        bits = link_bits(n)
        self.order = (bits[::-1], bits)

    def first(self, k, half):
        return next(i for i, bit in enumerate(self.order[half]) if k & bit)

    def core_copy(self, k, ref):
        return pltpu.make_async_remote_copy(
            src_ref=ref,
            dst_ref=self.core(k // 2),
            send_sem=self.core_send.at[k // 2],
            recv_sem=self.core_recv.at[k // 2],
            device_id={"mp": flip(self.me, 1)},
            device_id_type=MESH,
        )

    def link_copy(self, k, half):
        bit = self.order[half][self.first(k, half)]
        return pltpu.make_async_remote_copy(
            src_ref=self.part(self.stage(k // 2 - 1), half),
            dst_ref=self.link(half, k // 2 - 1),
            send_sem=self.link_send.at[half, k // 2 - 1],
            recv_sem=self.link_recv.at[half, k // 2 - 1],
            device_id={"mp": flip(self.me, bit)},
            device_id_type=MESH,
        )

    def addends(self, k, half):
        upto = self.first(k, half) if k else len(self.order[half])
        return [k | bit for bit in self.order[half][:upto]]

    def odd(self, k, ref):
        self.core_copy(k, ref).start()

    def even(self, k, ref):
        self.core_copy(k + 1, self.core(k // 2)).wait_recv()
        for half in (0, 1):
            joined = [self.part(ref, half), self.part(self.core(k // 2), half)]
            for j in self.addends(k, half):
                self.link_copy(j, half).wait_recv()
                joined.append(self.link(half, j // 2 - 1))
            add_up(self.part(self.stage(k // 2 - 1), half), joined)
            self.link_copy(k, half).start()

    def own(self, ref, out):
        self.core_copy(1, self.core(0)).wait_recv()
        for half in (0, 1):
            joined = [self.part(ref, half), self.part(self.core(0), half)]
            for j in self.addends(0, half):
                self.link_copy(j, half).wait_recv()
                joined.append(self.link(half, j // 2 - 1))
            add_up(self.part(out, half), joined)

    def drain(self, ref):
        for k in range(1, self.n, 2):
            self.core_copy(k, ref).wait_send()
        for k in range(2, self.n, 2):
            for half in (0, 1):
                self.link_copy(k, half).wait_send()


def add_up(out, terms):
    rows = out.shape[-2]
    step = 16
    lead = (slice(None),) * (len(out.shape) - 2)

    @pl.loop(0, rows // step)
    def _(i):
        at = lead + (pl.ds(pl.multiple_of(i * step, step), step), slice(None))
        total = terms[0][at].astype(F32)
        for t in terms[1:]:
            total = total + t[at].astype(F32)
        out[at] = total.astype(out.dtype)


def scatter_scratch(n, shape, half):
    return [
        pltpu.VMEM((n // 2,) + shape, BF),
        pltpu.VMEM((2, n // 2 - 1) + half, BF),
        pltpu.VMEM((n // 2 - 1,) + shape, BF),
        pltpu.SemaphoreType.DMA((n // 2,)),
        pltpu.SemaphoreType.DMA((n // 2,)),
        pltpu.SemaphoreType.DMA((2, n // 2 - 1)),
        pltpu.SemaphoreType.DMA((2, n // 2 - 1)),
    ]


def make_scatter(n, me, part, refs):
    core, link, stage = refs[:3]
    return Scatter(
        n,
        me,
        part,
        lambda i: core.at[i],
        lambda h, i: link.at[h, i],
        lambda i: stage.at[i],
        refs[3:7],
    )


def half_turn(x, lane):
    first = (lane % HD) < HD // 2
    return jnp.where(first, -pltpu.roll(x, LANES - HD // 2, 1), pltpu.roll(x, HD // 2, 1))


def half_turn_back(x, lane):
    first = (lane % HD) < HD // 2
    return jnp.where(first, pltpu.roll(x, LANES - HD // 2, 1), -pltpu.roll(x, HD // 2, 1))


def group_mean(x, ones):
    high = x.astype(BF)
    low = (x - high.astype(F32)).astype(BF)
    return (mm(high, ones) + mm(low, ones)) * (1.0 / HD)


def project_kernel(
    n, x_ref, gain_ref, w_ref, cos_ref, sin_ref, gq_ref, gk_ref, ones_ref,
    normed_ref, raw_ref, q_ref, w_out, kv_out,
    w_all, kv_own, w_send, w_recv, kv_send, kv_recv, local,
):
    me = lax.axis_index("mp")
    depth = w_ref.shape[0]
    tokens = x_ref.shape[0]
    rows = kv_out.shape[0]
    span = tokens // rows
    half = depth // 2
    own_w = pltpu.make_async_copy(w_ref, w_all.at[me], local.at[0])
    own_w.start()
    greet(n, me)
    weights = Gather(
        n,
        me,
        lambda h: w_ref.at[pl.ds(h * half, half)],
        lambda k, h: w_all.at[flip(me, k), pl.ds(h * half, half)],
        w_send,
        w_recv,
    )
    weights.start()
    step = min(64, tokens)

    @pl.loop(0, tokens // step)
    def _(i):
        at = pl.ds(pl.multiple_of(i * step, step), step)
        x = x_ref[at, :].astype(F32)
        scale = lax.rsqrt(jnp.mean(x * x, axis=-1, keepdims=True) + EPSILON)
        normed_ref[at, :] = (x * scale * gain_ref[...]).astype(BF)

    chunk = min(256, tokens)

    def accumulate(k, fresh):
        block = flip(me, k)
        columns = pl.ds(pl.multiple_of(block * depth, depth), depth)

        @pl.loop(0, tokens // chunk)
        def _(i):
            at = pl.ds(pl.multiple_of(i * chunk, chunk), chunk)
            term = mm(normed_ref[at, columns], w_all[block])
            raw_ref[at, :] = term if fresh else raw_ref[at, :] + term

    own_w.wait()
    accumulate(0, True)
    for h in (0, 1):
        weights.arrive(1, h)
    accumulate(1, False)
    for i, (k, h) in enumerate(weights.even):
        weights.forward(k, h)
        if any(k == other for other, _ in weights.even[:i]):
            accumulate(k, False)
    for k in range(3, n, 2):
        for h in (0, 1):
            weights.arrive(k, h)
        accumulate(k, False)
    out_w = pltpu.make_async_copy(w_all, w_out, local.at[0])
    out_w.start()

    chunk = min(128, tokens)
    lane = lax.broadcasted_iota(jnp.int32, (chunk, LANES), 1)

    def finish(i, tiles):
        at = pl.ds(pl.multiple_of(i * chunk, chunk), chunk)
        cos, sin = cos_ref[at, :], sin_ref[at, :]
        for tile in tiles:
            lanes = slice(tile * LANES, (tile + 1) * LANES)
            x = raw_ref[at, lanes]
            query = tile < QW // LANES
            scale = lax.rsqrt(group_mean(x * x, ones_ref[...]) + EPSILON)
            v = x * scale * (gq_ref[...] if query else gk_ref[...])
            y = v * cos + half_turn(v, lane) * sin
            if query:
                q_ref[at, lanes] = (y * (HD**-0.5 * LOG2E)).astype(BF)
            else:
                mine = slice(tile * LANES - QW, (tile + 1) * LANES - QW)
                kv_own[at, mine] = jnp.where(lane < HD, y, x).astype(BF)

    count = raw_ref.shape[1] // LANES

    @pl.loop(0, tokens // chunk)
    def _(i):
        finish(i, range(QW // LANES, count))

    both = rows // 2
    keep = [
        pltpu.make_async_copy(
            kv_own.at[pl.ds(r * span, span)], kv_out.at[r, me], local.at[1 + r]
        )
        for r in range(rows)
    ]
    for c in keep:
        c.start()
    kvs = Gather(
        n,
        me,
        lambda h: kv_own.at[pl.ds(h * span, span)],
        lambda k, h: kv_out.at[h, flip(me, k)],
        kv_send,
        kv_recv,
    )
    kvs.start()

    @pl.loop(0, tokens // chunk)
    def _(i):
        finish(i, range(QW // LANES))

    for k, h in kvs.even:
        kvs.forward(k, h)
    kvs.rest()
    for c in keep:
        c.wait()
    out_w.wait()
    weights.drain()
    kvs.drain()


def project(n, rows, x, gain, w, cos, sin, gq, gk, ones):
    tokens, width = x.shape
    depth, columns = w.shape
    vmem = pl.BlockSpec(memory_space=pltpu.VMEM)
    hbm = pl.BlockSpec(memory_space=pl.ANY)
    kvw = columns - QW
    return pl.pallas_call(
        functools.partial(project_kernel, n),
        in_specs=[vmem, vmem, hbm, vmem, vmem, vmem, vmem, vmem],
        out_specs=[vmem, vmem, vmem, hbm, hbm],
        out_shape=[
            jax.ShapeDtypeStruct((tokens, width), BF),
            jax.ShapeDtypeStruct((tokens, columns), F32),
            jax.ShapeDtypeStruct((tokens, QW), BF),
            jax.ShapeDtypeStruct((n, depth, columns), BF),
            jax.ShapeDtypeStruct((rows, n, tokens // rows, kvw), BF),
        ],
        scratch_shapes=[
            pltpu.VMEM((n, depth, columns), BF),
            pltpu.VMEM((tokens, kvw), BF),
            pltpu.SemaphoreType.DMA((n, 2)),
            pltpu.SemaphoreType.DMA((n, 2)),
            pltpu.SemaphoreType.DMA((n, 2)),
            pltpu.SemaphoreType.DMA((n, 2)),
            pltpu.SemaphoreType.DMA((1 + rows,)),
        ],
        compiler_params=params(axes=0, key=0),
        name="project",
    )(x, gain, w, cos, sin, gq, gk, ones)


def unproject_kernel(
    n, dq_ref, dkv_ref, raw_ref, cos_ref, sin_ref, gq_ref, gk_ref, ones_ref, normed_ref, gout_ref,
    gj_ref, sq_ref, sk_ref, attend_ref, output_ref,
    dkv_own, term, *scratch,
):
    me = lax.axis_index("mp")
    greet(n, me)
    tokens = dq_ref.shape[0]
    rows = dkv_ref.shape[0]
    span = tokens // rows
    columns = raw_ref.shape[1]
    depth = attend_ref.shape[0]

    keys = make_scatter(n, me, lambda ref, h: ref.at[h], scratch[:7])
    half_w = output_ref.shape[1] // 2
    outs = make_scatter(
        n, me, lambda ref, h: ref.at[:, pl.ds(h * half_w, half_w)], scratch[7:14]
    )
    half_d = depth // 2
    weights = make_scatter(
        n, me, lambda ref, h: ref.at[pl.ds(h * half_d, half_d)], scratch[14:21]
    )

    def dkv_term(k):
        return dkv_ref.at[:, flip(me, k)]

    def out_term(k):
        return gout_ref.at[flip(me, k)]

    for k in range(n - 1, 0, -2):
        keys.odd(k, dkv_term(k))
    for k in range(n - 2, 0, -2):
        keys.even(k, dkv_term(k))
    for k in range(n - 1, 0, -2):
        outs.odd(k, out_term(k))

    chunk = min(128, tokens)
    lane = lax.broadcasted_iota(jnp.int32, (chunk, LANES), 1)
    sq_ref[...] = jnp.zeros_like(sq_ref)
    sk_ref[...] = jnp.zeros_like(sk_ref)

    def back(i, tiles, query):
        at = pl.ds(pl.multiple_of(i * chunk, chunk), chunk)
        cos, sin = cos_ref[at, :], sin_ref[at, :]
        total = 0.0
        for tile in tiles:
            lanes = slice(tile * LANES, (tile + 1) * LANES)
            x = raw_ref[at, lanes]
            if query:
                e = dq_ref[at, lanes]
            else:
                per = span // chunk
                here = pl.ds(pl.multiple_of(lax.rem(i, per) * chunk, chunk), chunk)
                e = dkv_own[lax.div(i, per), here, slice(tile * LANES - QW, (tile + 1) * LANES - QW)]
            scale = lax.rsqrt(group_mean(x * x, ones_ref[...]) + EPSILON)
            v = x * scale
            turned = e * cos + half_turn_back(e * sin, lane)
            u = turned * (gq_ref[...] if query else gk_ref[...])
            grad = scale * (u - v * group_mean(u * v, ones_ref[...]))
            gj_ref[at, lanes] = (grad if query else jnp.where(lane < HD, grad, e)).astype(BF)
            total = total + jnp.sum(turned * v, axis=0, keepdims=True)
        sums = sq_ref if query else sk_ref
        sums[...] += jnp.broadcast_to(total, sums.shape)

    count = columns // LANES

    @pl.loop(0, tokens // chunk)
    def _(i):
        back(i, range(QW // LANES), True)

    for k in range(n - 2, 0, -2):
        outs.even(k, out_term(k))

    keys.own(dkv_term(0), dkv_own)

    @pl.loop(0, tokens // chunk)
    def _(i):
        back(i, range(QW // LANES, count), False)

    for k in range(n - 1, -1, -1):
        at = pl.ds(pl.multiple_of(flip(me, k) * depth, depth), depth)
        here = term.at[k]
        here[...] = dg(normed_ref[:, at], gj_ref[...], TN).astype(BF)
        if k % 2:
            weights.odd(k, here)
        elif k:
            weights.even(k, here)
    outs.own(out_term(0), output_ref)
    weights.own(term.at[0], attend_ref)
    keys.drain(dkv_term(0))
    outs.drain(out_term(0))
    weights.drain(term.at[0])


def unproject(n, dq, dkv, raw, cos, sin, gq, gk, ones, normed, gout):
    tokens, columns = raw.shape
    rows = dkv.shape[0]
    span = tokens // rows
    kvw = columns - QW
    width = normed.shape[1]
    depth = width // n
    vmem = pl.BlockSpec(memory_space=pltpu.VMEM)
    return pl.pallas_call(
        functools.partial(unproject_kernel, n),
        in_specs=[vmem] * 10,
        out_specs=[vmem] * 5,
        out_shape=[
            jax.ShapeDtypeStruct((tokens, columns), BF),
            jax.ShapeDtypeStruct((8, LANES), F32),
            jax.ShapeDtypeStruct((8, LANES), F32),
            jax.ShapeDtypeStruct((depth, columns), BF),
            jax.ShapeDtypeStruct((QW // n, width), BF),
        ],
        scratch_shapes=[pltpu.VMEM((rows, span, kvw), F32), pltpu.VMEM((n, depth, columns), BF)]
        + scatter_scratch(n, (rows, span, kvw), (span, kvw))
        + scatter_scratch(n, (QW // n, width), (QW // n, width // 2))
        + scatter_scratch(n, (depth, columns), (depth // 2, columns)),
        compiler_params=params(mib=60, axes=0, key=2),
        name="unproject",
    )(dq, dkv, raw, cos, sin, gq, gk, ones, normed, gout)


def key_positions(shape, axis, group, per, span):
    return group * per * span + lax.broadcasted_iota(jnp.int32, shape, axis)


def attend_kernel(keys, info, q_ref, kv_ref, start_ref, ctx_ref, rl_ref, acc):
    span = q_ref.shape[1]
    per = keys // span
    row = pl.program_id(0)
    me, first, last_start = info[row, 0], info[row, 1], info[row, 2]
    low_q = lax.broadcasted_iota(jnp.int32, (span, LANES), 1) < HD
    low_k = lax.broadcasted_iota(jnp.int32, (keys, LANES), 1) < HD
    one = jnp.ones((keys, LANES), BF)
    none = jnp.zeros((span, LANES), BF)
    queries = []
    for h in range(GW // HD):
        pair = q_ref[0, :, (h // 2) * LANES : (h // 2 + 1) * LANES]
        queries.append(jnp.where(low_q, pair, none) if h % 2 == 0 else jnp.where(low_q, none, pair))
    acc[...] = jnp.zeros_like(acc)

    def block(g, masked):
        group = g
        kv = kv_ref[0, pl.ds(pl.multiple_of(group * keys, keys), keys), :]
        vk = jnp.concatenate([kv[:, HD:], kv[:, :HD]], axis=1)
        key_sides = (kv, vk)
        value_sides = (jnp.where(low_k, vk, one), jnp.where(low_k, one, kv))
        if masked:
            position = key_positions((span, keys), 1, group, per, span)
            own = me * span + lax.broadcasted_iota(jnp.int32, (span, keys), 0)
            seen = (position <= own) & (position >= start_ref[0][:, :1])
        for h in range(GW // HD):
            p = jnp.exp2(dg(queries[h], key_sides[h % 2], NT))
            if masked:
                p = jnp.where(seen, p, 0.0)
            acc[h] += mm(p.astype(BF), value_sides[h % 2])

    def step(g, carry):
        edge = (g == me // per) | (g * keys < last_start)
        pl.when(edge)(lambda: block(g, True))
        pl.when(jnp.logical_not(edge))(lambda: block(g, False))
        return carry

    lax.fori_loop(first, me // per + 1, step, 0)
    for pair in range(GW // LANES):
        even, odd = acc[2 * pair], acc[2 * pair + 1]
        total = jnp.where(low_q, pltpu.roll(even, HD, 1), pltpu.roll(odd, HD, 1))
        inverse = 1.0 / total
        lanes = slice(pair * LANES, (pair + 1) * LANES)
        ctx_ref[0, :, lanes] = (jnp.where(low_q, even, odd) * inverse).astype(BF)
        rl_ref[0, :, lanes] = inverse


def attend(info, q, kv, start):
    rows, span, _ = q.shape
    length = kv.shape[1]
    keys = min(512, length)
    own = lambda r, h, info: (r, 0, h)
    spec = pltpu.PrefetchScalarGridSpec(
        num_scalar_prefetch=1,
        grid=(rows, KVH),
        in_specs=[
            pl.BlockSpec((1, span, GW), own),
            pl.BlockSpec((1, length, LANES), own),
            pl.BlockSpec((1, span, LANES), lambda r, h, info: (r, 0, 0)),
        ],
        out_specs=[pl.BlockSpec((1, span, GW), own), pl.BlockSpec((1, span, GW), own)],
        scratch_shapes=[pltpu.VMEM((GW // HD, span, LANES), F32)],
    )
    return pl.pallas_call(
        functools.partial(attend_kernel, keys),
        grid_spec=spec,
        out_shape=[jax.ShapeDtypeStruct(q.shape, BF), jax.ShapeDtypeStruct(q.shape, F32)],
        compiler_params=params(axes=2),
        cost_estimate=pl.CostEstimate(
            flops=16 * rows * H * span * length * HD,
            bytes_accessed=rows * (length * 1280 + span * QW * 8),
            transcendentals=rows * H * span * length,
        ),
        name="attend",
    )(info, q, kv, start)


def attend_back_kernel(
    keys, info, q_ref, kv_ref, start_ref, do_ref, ctx_ref, rl_ref, dq_ref, dkv_ref, acc, sides
):
    span = q_ref.shape[1]
    per = keys // span
    length = kv_ref.shape[1]
    row = pl.program_id(0)
    me, first, last_start = info[row, 0], info[row, 1], info[row, 2]
    lane = lax.broadcasted_iota(jnp.int32, (span, LANES), 1)
    low_q = lane < HD
    low_k = lax.broadcasted_iota(jnp.int32, (keys, LANES), 1) < HD
    one = jnp.ones((keys, LANES), BF)
    for h in range(GW // HD):
        lanes = slice((h // 2) * LANES, (h // 2 + 1) * LANES)
        mine = low_q if h % 2 == 0 else jnp.logical_not(low_q)
        scaled = do_ref[0, :, lanes].astype(F32) * rl_ref[0, :, lanes]
        own = jnp.where(mine, scaled, 0.0)
        delta = -jnp.sum(own * ctx_ref[0, :, lanes].astype(F32), axis=1, keepdims=True)
        one_part = delta.astype(BF).astype(F32)
        two_part = (delta - one_part).astype(BF).astype(F32)
        three_part = delta - one_part - two_part
        base = HD if h % 2 == 0 else 0
        extra = jnp.where(
            lane == base,
            one_part,
            jnp.where(lane == base + 1, two_part, jnp.where(lane == base + 2, three_part, 0.0)),
        )
        sides[0, h] = jnp.where(mine, q_ref[0, :, lanes].astype(F32), 0.0).astype(BF)
        sides[1, h] = own.astype(BF)
        sides[2, h] = jnp.where(mine, scaled, extra).astype(BF)
    acc[...] = jnp.zeros_like(acc)

    def block(g, masked):
        group = g
        here = pl.ds(pl.multiple_of(group * keys, keys), keys)
        kv = kv_ref[0, here, :]
        vk = jnp.concatenate([kv[:, HD:], kv[:, :HD]], axis=1)
        key_sides = (kv, vk)
        value_sides = (jnp.where(low_k, vk, one), jnp.where(low_k, one, kv))
        if masked:
            position = key_positions((keys, span), 0, group, per, span)
            own = me * span + lax.broadcasted_iota(jnp.int32, (keys, span), 1)
            seen = (position <= own) & (position >= start_ref[0][:1, :])
        grad_key = grad_value = 0.0
        for h in range(GW // HD):
            e = jnp.exp2(dg(key_sides[h % 2], sides[0, h], NT))
            if masked:
                e = jnp.where(seen, e, 0.0)
            ds = (e * dg(value_sides[h % 2], sides[2, h], NT)).astype(BF)
            grad_value = grad_value + mm(e.astype(BF), sides[1, h])
            grad_key = grad_key + mm(ds, sides[0, h])
            acc[h] += dg(ds, key_sides[h % 2], TN)
        grad_key = (grad_key + pltpu.roll(grad_key, HD, 1)) * LN2
        grad_value = grad_value + pltpu.roll(grad_value, HD, 1)
        dkv_ref[0, here, :] = jnp.where(low_k, grad_key, grad_value).astype(BF)

    def step(g, carry):
        visited = (g >= first) & (g <= me // per)
        edge = (g == me // per) | (g * keys < last_start)

        @pl.when(jnp.logical_not(visited))
        def _():
            group = g
            dkv_ref[0, pl.ds(pl.multiple_of(group * keys, keys), keys), :] = jnp.zeros((keys, LANES), BF)

        pl.when(visited & edge)(lambda: block(g, True))
        pl.when(visited & jnp.logical_not(edge))(lambda: block(g, False))
        return carry

    lax.fori_loop(0, length // keys, step, 0)
    for pair in range(GW // LANES):
        lanes = slice(pair * LANES, (pair + 1) * LANES)
        dq_ref[0, :, lanes] = jnp.where(low_q, acc[2 * pair], acc[2 * pair + 1]) * (HD**-0.5)


def attend_back(info, q, kv, start, do, ctx, rl):
    rows, span, _ = q.shape
    length = kv.shape[1]
    keys = min(512, length)
    own = lambda r, h, info: (r, 0, h)
    spec = pltpu.PrefetchScalarGridSpec(
        num_scalar_prefetch=1,
        grid=(rows, KVH),
        in_specs=[
            pl.BlockSpec((1, span, GW), own),
            pl.BlockSpec((1, length, LANES), own),
            pl.BlockSpec((1, 8, span), lambda r, h, info: (r, 0, 0)),
            pl.BlockSpec((1, span, GW), own),
            pl.BlockSpec((1, span, GW), own),
            pl.BlockSpec((1, span, GW), own),
        ],
        out_specs=[pl.BlockSpec((1, span, GW), own), pl.BlockSpec((1, length, LANES), own)],
        scratch_shapes=[
            pltpu.VMEM((GW // HD, span, LANES), F32),
            pltpu.VMEM((3, GW // HD, span, LANES), BF),
        ],
    )
    return pl.pallas_call(
        functools.partial(attend_back_kernel, keys),
        grid_spec=spec,
        out_shape=[jax.ShapeDtypeStruct(q.shape, F32), jax.ShapeDtypeStruct(kv.shape, BF)],
        compiler_params=params(axes=2),
        cost_estimate=pl.CostEstimate(
            flops=40 * rows * H * span * length * HD,
            bytes_accessed=rows * (length * 2560 + span * QW * 16),
            transcendentals=rows * H * span * length,
        ),
        name="attend_back",
    )(info, q, kv, start, do, ctx, rl)


def xor_of(a, b, n):
    total, bit = 0, 1
    while bit < n:
        total = total + bit * lax.rem(lax.div(a, bit) + lax.div(b, bit), 2)
        bit *= 2
    return total


def feed_kernel(
    n, live_ref, x_own, g_all, gu_ref, gut_ref, dt_ref, d_ref,
    x_all, hid_ref, dgu_ref, out_ref, flat_ref,
    x_buf, g_buf, terms, core, link, stage,
    x_send, x_recv, core_send, core_recv, link_send, link_recv, loads, keep,
):
    me = lax.axis_index("mp")
    rows, span, width = x_own.shape
    slots = gu_ref.shape[0]
    r, j = pl.program_id(0), pl.program_id(1)
    k = n - 1 - j
    now = r * n + j
    half = span // 2

    def gather(row):
        return Gather(
            n,
            me,
            lambda h: x_own.at[row, pl.ds(h * half, half)],
            lambda i, h: x_all.at[row, flip(me, i), pl.ds(h * half, half)],
            x_send.at[row],
            x_recv.at[row],
        )

    def scatter(row):
        return Scatter(
            n,
            me,
            lambda ref, h: ref.at[pl.ds(h * half, half)],
            lambda i: core.at[row, i],
            lambda h, i: link.at[row, h, i],
            lambda i: stage.at[i],
            (core_send.at[row], core_recv.at[row], link_send.at[row], link_recv.at[row]),
        )

    def load(step):
        row, slot = lax.div(step, n), n - 1 - lax.rem(step, n)
        block = xor_of(me, slot, n)
        to = lax.rem(step, 2)
        return (
            pltpu.make_async_copy(x_all.at[row, block], x_buf.at[to], loads.at[0, to]),
            pltpu.make_async_copy(g_all.at[row, block], g_buf.at[to], loads.at[1, to]),
        )

    def own_copy(row):
        return pltpu.make_async_copy(x_own.at[row], x_all.at[row, me], keep.at[row])

    @pl.when(now == 0)
    def _():
        greet(n, me)
        for row in range(rows):
            own_copy(row).start()
        first = gather(0)
        first.start()
        for i, h in first.even:
            first.forward(i, h)
            if (i, h) == first.even[len(first.even) // 2]:
                for row in range(1, rows):
                    gather(row).start()
        first.rest()
        for row in range(rows):
            own_copy(row).wait()
        for c in load(0):
            c.start()

    for row in range(1, rows):
        events = gather(row).even
        for at in range(1, n - 1):
            todo = [e for i, e in enumerate(events) if 1 + i * (n - 2) // len(events) == at]
            if todo:

                @pl.when(now == (row - 1) * n + at)
                def _(todo=todo, row=row):
                    for i, h in todo:
                        gather(row).forward(i, h)

        @pl.when(now == row * n - 1)
        def _(row=row):
            gather(row).rest()

    @pl.when(now + 1 < rows * n)
    def _():
        for c in load(now + 1):
            c.start()

    for c in load(now):
        c.wait()
    to = lax.rem(now, 2)
    x, g = x_buf.at[to], g_buf.at[to]
    grad = mm(g[...], dt_ref[...])
    for t in range(slots):
        both = mm(x[...], gu_ref[t])
        gate, upper = both[:, :TILE], both[:, TILE:]
        live = live_ref[t]
        sig = jax.nn.sigmoid(gate)
        silu = gate * sig
        gh = grad[:, t * TILE : (t + 1) * TILE] * live
        hid_ref[0, 0, :, t * TILE : (t + 1) * TILE] = (silu * upper * live).astype(BF)
        dgu_ref[0, 0, :, 2 * t * TILE : (2 * t + 1) * TILE] = (
            gh * upper * (sig * (1.0 + gate * (1.0 - sig)))
        ).astype(BF)
        dgu_ref[0, 0, :, (2 * t + 1) * TILE : (2 * t + 2) * TILE] = (gh * silu).astype(BF)

    for i in range(1, n, 2):

        @pl.when((r > 0) & (k == i))
        def _(i=i):
            scatter(r - 1).core_copy(i, terms.at[i // 2]).wait_send()

    at = lax.rem(k, 2) * lax.div(k, 2) + (1 - lax.rem(k, 2)) * (n // 2)
    terms[at] = mm(dgu_ref[0, 0], gut_ref[...]).astype(BF)
    out_ref[0, 0] = mm(hid_ref[0, 0], d_ref[...]).astype(BF)
    mine = terms.at[n // 2]
    sums = scatter(r)
    for i in range(1, n):

        @pl.when(k == i)
        def _(i=i):
            if i % 2:
                sums.odd(i, terms.at[i // 2])
            else:

                @pl.when(r > 0)
                def _():
                    for h in (0, 1):
                        scatter(r - 1).link_copy(i, h).wait_send()

                sums.even(i, mine)

    @pl.when(k == 0)
    def _():
        sums.core_copy(1, core.at[r, 0]).wait_recv()
        add_up(flat_ref.at[r], [mine, core.at[r, 0]])

    def close(row):
        last = scatter(row)
        for h in (0, 1):
            here = last.part(flat_ref.at[row], h)
            joined = [here]
            for i in last.addends(0, h):
                last.link_copy(i, h).wait_recv()
                joined.append(last.link(h, i // 2 - 1))
            add_up(here, joined)

    for row in range(rows - 1):

        @pl.when(now == (row + 1) * n + n // 2)
        def _(row=row):
            close(row)

    @pl.when(now == rows * n - 1)
    def _():
        close(rows - 1)
        scatter(rows - 1).drain(mine)
        for row in range(rows):
            gather(row).drain()


def feed(n, live, x, g, gu, gut, dt, d):
    rows, span, width = x.shape
    slots = gu.shape[0]
    vmem = pl.BlockSpec(memory_space=pltpu.VMEM)
    hbm = pl.BlockSpec(memory_space=pl.ANY)

    def place(r, j):
        return (r, xor_of(lax.axis_index("mp"), n - 1 - j, n), 0, 0)

    half = span // 2
    return pl.pallas_call(
        functools.partial(feed_kernel, n),
        grid=(rows, n),
        in_specs=[pl.BlockSpec(memory_space=pltpu.SMEM), hbm, hbm, vmem, vmem, vmem, vmem],
        out_specs=[
            hbm,
            pl.BlockSpec((1, 1, span, slots * TILE), place),
            pl.BlockSpec((1, 1, span, 2 * slots * TILE), place),
            pl.BlockSpec((1, 1, span, width), place),
            vmem,
        ],
        out_shape=[
            jax.ShapeDtypeStruct((rows, n, span, width), BF),
            jax.ShapeDtypeStruct((rows, n, span, slots * TILE), BF),
            jax.ShapeDtypeStruct((rows, n, span, 2 * slots * TILE), BF),
            jax.ShapeDtypeStruct((rows, n, span, width), BF),
            jax.ShapeDtypeStruct((rows, span, width), F32),
        ],
        scratch_shapes=[
            pltpu.VMEM((2, span, width), BF),
            pltpu.VMEM((2, span, width), BF),
            pltpu.VMEM((n // 2 + 1, span, width), BF),
            pltpu.VMEM((rows, n // 2, span, width), BF),
            pltpu.VMEM((rows, 2, n // 2 - 1, half, width), BF),
            pltpu.VMEM((n // 2 - 1, span, width), BF),
            pltpu.SemaphoreType.DMA((rows, n, 2)),
            pltpu.SemaphoreType.DMA((rows, n, 2)),
            pltpu.SemaphoreType.DMA((rows, n // 2)),
            pltpu.SemaphoreType.DMA((rows, n // 2)),
            pltpu.SemaphoreType.DMA((rows, 2, n // 2 - 1)),
            pltpu.SemaphoreType.DMA((rows, 2, n // 2 - 1)),
            pltpu.SemaphoreType.DMA((2, 2)),
            pltpu.SemaphoreType.DMA((rows,)),
        ],
        compiler_params=params(mib=62, axes=2, key=1),
        cost_estimate=pl.CostEstimate(
            flops=2 * 9 * rows * n * span * slots * TILE * width,
            bytes_accessed=8 * rows * n * span * width + 12 * slots * TILE * width,
            transcendentals=rows * n * span * slots * TILE,
        ),
        name="feed",
    )(live, x, g, gu, gut, dt, d)


def weight_kernel(finish, a_ref, b_ref, o_ref, acc):
    k = pl.program_id(1)

    @pl.when(k == 0)
    def _():
        acc[...] = jnp.zeros_like(acc)

    acc[...] += dg(a_ref[...], b_ref[...], TN)

    @pl.when(k == pl.num_programs(1) - 1)
    def _():
        finish(o_ref, acc)


def weight_grad(left, right, block, stacked):
    tokens, lw = left.shape
    rw = right.shape[1]
    block = min(block, lw)
    step = 512
    if stacked:
        slots = rw // 256
        out_spec = pl.BlockSpec((slots, block, 256), lambda i, k: (0, i, 0))
        out_shape = jax.ShapeDtypeStruct((slots, lw, 256), BF)

        def finish(o_ref, acc):
            for t in range(slots):
                o_ref[t] = acc[:, t * 256 : (t + 1) * 256].astype(BF)
    else:
        out_spec = pl.BlockSpec((block, rw), lambda i, k: (i, 0))
        out_shape = jax.ShapeDtypeStruct((lw, rw), BF)

        def finish(o_ref, acc):
            o_ref[...] = acc[...].astype(BF)

    return pl.pallas_call(
        functools.partial(weight_kernel, finish),
        grid=(lw // block, tokens // step),
        in_specs=[
            pl.BlockSpec((step, block), lambda i, k: (k, i)),
            pl.BlockSpec((step, rw), lambda i, k: (k, 0)),
        ],
        out_specs=out_spec,
        out_shape=out_shape,
        scratch_shapes=[pltpu.VMEM((block, rw), F32)],
        compiler_params=params(axes=2),
        cost_estimate=pl.CostEstimate(
            flops=2 * tokens * lw * rw,
            bytes_accessed=2 * tokens * (lw + rw) + 2 * lw * rw,
            transcendentals=0,
        ),
        name="weight_grad",
    )(left, right)


def shards(
    n,
    hidden_in,
    doc_ids,
    tile_slot,
    attention_gain,
    query_gain,
    key_gain,
    attend_weight,
    output_weight,
    feed_gain,
    gate_up_slots,
    down_slots,
    out_grad,
):
    rows, span, width = hidden_in.shape
    length = doc_ids.shape[1]
    slots = gate_up_slots.shape[0]
    tokens = rows * span
    me = lax.axis_index("mp")
    offset = me * span

    kw = KVH * HD
    keys_w = attend_weight[:, QW : QW + kw].reshape(-1, KVH, HD)
    values_w = attend_weight[:, QW + kw :].reshape(-1, KVH, HD)
    attend_w = jnp.concatenate(
        [attend_weight[:, :QW], jnp.concatenate([keys_w, values_w], 2).reshape(-1, 2 * kw)], 1
    )
    starts = doc_starts(doc_ids)
    local_start = lax.dynamic_slice_in_dim(starts, offset, span, 1)
    local_pos = offset + jnp.arange(span, dtype=jnp.int32)[None] - local_start
    cos, sin = rotary_tables(local_pos.reshape(tokens))
    gq = jnp.tile(query_gain, 2)[None]
    gk = jnp.concatenate([key_gain, jnp.ones_like(key_gain)])[None]
    lane = jnp.arange(LANES) // HD
    ones = (lane[:, None] == lane[None, :]).astype(BF)
    key_block = min(512, length)
    info = jnp.stack(
        [
            jnp.full((rows,), me, jnp.int32),
            local_start[:, 0] // key_block,
            local_start[:, -1],
        ],
        1,
    ).astype(jnp.int32)
    start_col = jnp.broadcast_to(local_start[:, :, None], (rows, span, LANES))
    start_row = jnp.broadcast_to(local_start[:, None, :], (rows, 8, span))

    x_own = hidden_in.reshape(tokens, width)
    x_value = x_own.astype(F32)
    scale_a = rms_scale(x_value)
    normed_ab, raw, q, attend_all, kv_all = project(
        n, rows, x_own, attention_gain[None], attend_w, cos, sin, gq, gk, ones
    )
    q = q.reshape(rows, span, QW)
    kv_all = kv_all.reshape(rows, length, -1)
    attend_full = attend_all.reshape(width, -1)
    output_full = lax.all_gather(output_weight, "mp", axis=0, tiled=True)
    out_grad_now, output_full = lax.optimization_barrier((out_grad, output_full))
    grads_all = lax.all_gather(out_grad_now.astype(BF), "mp", axis=1, tiled=True)
    ctx, rl = attend(info, q, kv_all, start_col)
    context_b = ctx.reshape(tokens, QW)
    middle = x_value + mm(context_b, output_full)
    scale_f = rms_scale(middle)
    normed_fb = (middle * scale_f * feed_gain).astype(BF).reshape(rows, span, width)

    slot_index = me * slots + jnp.arange(slots, dtype=jnp.int32)
    live = jnp.any(tile_slot[None, :] == slot_index[:, None], axis=1).astype(F32)
    gu_t = jnp.swapaxes(gate_up_slots, 1, 2).reshape(slots * 2 * TILE, width)
    d_flat = down_slots.reshape(slots * TILE, width)
    d_t = d_flat.T
    everything = rows * n * span
    normed_all, hidden, grad_both, partial_out, grad_normed_f = feed(
        n,
        live,
        normed_fb,
        grads_all.reshape(rows, n, span, width),
        gate_up_slots,
        gu_t,
        d_t,
        d_flat,
    )
    grad_gate_up = weight_grad(
        normed_all.reshape(everything, width), grad_both.reshape(everything, -1), 1024, True
    )
    grad_down = weight_grad(
        hidden.reshape(everything, -1), grads_all.reshape(everything, width), 768, False
    ).reshape(slots, TILE, width)
    ffn_out = lax.psum_scatter(
        partial_out.reshape(rows, length, width), "mp", scatter_dimension=1, tiled=True
    )
    gate_up_total, down_total = lax.psum((grad_gate_up, grad_down), "dp")
    grad_normed_f = grad_normed_f.reshape(tokens, width)

    weighted = grad_normed_f * feed_gain
    inner = jnp.mean(weighted * middle, axis=-1, keepdims=True)
    gain_feed = jnp.sum(grad_normed_f * middle * scale_f, axis=0)
    grad_middle = out_grad.reshape(tokens, width) + scale_f * (
        weighted - middle * scale_f * scale_f * inner
    )
    grad_attn_b = grad_middle.astype(BF)
    grad_context = dg(grad_attn_b, output_full, NT).astype(BF).reshape(rows, span, QW)
    grad_output = dg(context_b, grad_attn_b, TN).astype(BF)

    dq, dkv = attend_back(info, q, kv_all, start_row, grad_context, ctx, rl)
    layer_out = middle + ffn_out.reshape(tokens, width).astype(F32)
    grad_joined_b, sum_q, sum_k, attend_share, output_share = unproject(
        n,
        dq.reshape(tokens, QW),
        dkv.reshape(rows, n, span, -1),
        raw,
        cos,
        sin,
        gq,
        gk,
        ones,
        normed_ab,
        grad_output.reshape(n, -1, width),
    )
    grad_normed_a = dg(grad_joined_b, attend_full, NT)

    attend_share, output_share, gate_up_total, down_total = lax.optimization_barrier(
        (attend_share, output_share, gate_up_total, down_total)
    )
    attend_total, output_total = lax.psum((attend_share, output_share), "dp")
    attend_total = attend_total.astype(F32)
    kv_total = attend_total[:, QW:].reshape(-1, KVH, 2, HD)
    attend_total = jnp.concatenate(
        [
            attend_total[:, :QW],
            kv_total[:, :, 0].reshape(-1, kw),
            kv_total[:, :, 1].reshape(-1, kw),
        ],
        1,
    )
    weighted_a = grad_normed_a * attention_gain
    inner_a = jnp.mean(weighted_a * x_value, axis=-1, keepdims=True)
    gain_attention = jnp.sum(grad_normed_a * x_value * scale_a, axis=0)
    input_grad = grad_middle + scale_a * (weighted_a - x_value * scale_a * scale_a * inner_a)

    gains = jnp.concatenate([gain_attention, gain_feed, sum_q[0], sum_k[0]])
    gains = lax.psum(gains, ("dp", "mp"))
    gain_query = gains[2 * width : 2 * width + HD] + gains[2 * width + HD : 2 * width + 2 * HD]
    gain_key = gains[2 * width + LANES : 2 * width + LANES + HD]
    shape = (rows, span, width)
    return (
        layer_out.reshape(shape),
        input_grad.reshape(shape),
        attend_total,
        output_total.astype(F32),
        gate_up_total.astype(F32),
        down_total.astype(F32),
        gains[:width],
        gain_query,
        gain_key,
        gains[width : 2 * width],
    )


def solution(mesh):
    placed = (
        P("dp", "mp", None),
        P("dp", None),
        P(),
        P(),
        P(),
        P(),
        P("mp", None),
        P("mp", None),
        P(),
        P("mp", None, None),
        P("mp", None, None),
        P("dp", "mp", None),
    )
    return jax.shard_map(
        functools.partial(shards, mesh.shape["mp"]),
        mesh=mesh,
        in_specs=placed,
        out_specs=(
            P("dp", "mp", None),
            P("dp", "mp", None),
            P("mp", None),
            P("mp", None),
            P("mp", None, None),
            P("mp", None, None),
            P(),
            P(),
            P(),
            P(),
        ),
        check_vma=False,
    )
```

```python
import functools

import jax
import jax.numpy as jnp
from jax import lax
from jax.experimental import pallas as pl
from jax.experimental.pallas import tpu as pltpu
from jax.sharding import PartitionSpec as P

H = 20
KVH = 5
HD = 64
TILE = 128
EPSILON = 1e-06
QW = H * HD
LANES = 128
GW = (H // KVH) * HD
LOG2E = 1.4426950408889634
LN2 = 0.6931471805599453
BF = jnp.bfloat16
F32 = jnp.float32
MIB = 1 << 20
NT = (((1,), (1,)), ((), ()))
TN = (((0,), (0,)), ((), ()))


def params(mib=56, axes=1, key=None):
    if key is None:
        return pltpu.CompilerParams(
            vmem_limit_bytes=mib * MIB, dimension_semantics=("arbitrary",) * axes
        )
    return pltpu.CompilerParams(
        vmem_limit_bytes=mib * MIB,
        dimension_semantics=("arbitrary",) * axes if axes else None,
        collective_id=key,
        has_side_effects=True,
    )


def mm(a, b):
    return jnp.dot(a, b, preferred_element_type=F32)


def dg(a, b, dims):
    return lax.dot_general(a, b, dims, preferred_element_type=F32)


def doc_starts(docs):
    index = jnp.arange(docs.shape[-1], dtype=jnp.int32)
    change = jnp.concatenate(
        [jnp.ones(docs.shape[:-1] + (1,), dtype=jnp.bool_), docs[..., 1:] != docs[..., :-1]],
        axis=-1,
    )
    return lax.cummax(jnp.where(change, index, 0), axis=docs.ndim - 1)


def rotary_tables(positions):
    half_dim = HD // 2
    freqs = 1.0 / 10000.0 ** (jnp.arange(half_dim, dtype=jnp.float32) * 2.0 / HD)
    angles = positions.astype(jnp.float32)[..., None] * freqs
    return jnp.tile(jnp.cos(angles), 4), jnp.tile(jnp.sin(angles), 4)


def rms_scale(values):
    return lax.rsqrt(jnp.mean(values * values, axis=-1, keepdims=True) + EPSILON)


MESH = pl.DeviceIdType.MESH


def flip(me, k):
    bit = 1
    while bit <= k:
        if k & bit:
            me = me + bit - 2 * bit * lax.rem(lax.div(me, bit), 2)
        bit *= 2
    return me


def link_bits(n):
    return [1 << i for i in range(1, n.bit_length() - 1)]


def greet(n, me):
    barrier = pltpu.get_barrier_semaphore()
    bits = [1] + link_bits(n)
    for bit in bits:
        pl.semaphore_signal(barrier, inc=1, device_id={"mp": flip(me, bit)}, device_id_type=MESH)
    pl.semaphore_wait(barrier, len(bits))


class Gather:
    def __init__(self, n, me, own, slot, send, recv, relative=False):
        self.n, self.me, self.own, self.slot, self.send, self.recv = n, me, own, slot, send, recv
        self.relative = relative
        bits = link_bits(n)
        self.order = (bits + [1], bits[::-1] + [1])
        even = [(k, h) for k in range(2, n, 2) for h in (0, 1)]
        even.sort(key=lambda kh: (bin(kh[0]).count("1"), max(self.place(*kh)), kh[1]))
        self.even = even

    def place(self, k, half):
        return [i for i, bit in enumerate(self.order[half]) if k & bit]

    def copy(self, k, half, bit):
        return pltpu.make_async_remote_copy(
            src_ref=self.own(half) if k == 0 else self.slot(k, half),
            dst_ref=self.slot(k ^ bit if self.relative else k, half),
            send_sem=self.send.at[k ^ bit, half],
            recv_sem=self.recv.at[k ^ bit, half],
            device_id={"mp": flip(self.me, bit)},
            device_id_type=MESH,
        )

    def onward(self, k, half):
        return self.order[half][(max(self.place(k, half)) + 1) if k else 0 :]

    def start(self):
        for i in range(len(self.order[0])):
            for half in (0, 1):
                self.copy(0, half, self.order[half][i]).start()

    def arrive(self, k, half):
        here = self.slot(k, half)
        pltpu.make_async_remote_copy(
            src_ref=here,
            dst_ref=here,
            send_sem=self.send.at[k, half],
            recv_sem=self.recv.at[k, half],
            device_id={"mp": flip(self.me, 1)},
            device_id_type=MESH,
        ).wait_recv()

    def forward(self, k, half):
        self.arrive(k, half)
        for bit in self.onward(k, half):
            self.copy(k, half, bit).start()

    def rest(self):
        for k, half in [(1, 0), (1, 1)] + [(k + 1, h) for k, h in self.even]:
            self.arrive(k, half)

    def drain(self):
        for k in range(0, self.n, 2):
            for half in (0, 1):
                for bit in self.onward(k, half):
                    self.copy(k, half, bit).wait_send()


class Scatter:
    def __init__(self, n, me, part, core, link, stage, sems):
        self.n, self.me, self.part = n, me, part
        self.core, self.link, self.stage = core, link, stage
        self.core_send, self.core_recv, self.link_send, self.link_recv = sems
        bits = link_bits(n)
        self.order = (bits[::-1], bits)

    def first(self, k, half):
        return next(i for i, bit in enumerate(self.order[half]) if k & bit)

    def core_copy(self, k, ref):
        return pltpu.make_async_remote_copy(
            src_ref=ref,
            dst_ref=self.core(k // 2),
            send_sem=self.core_send.at[k // 2],
            recv_sem=self.core_recv.at[k // 2],
            device_id={"mp": flip(self.me, 1)},
            device_id_type=MESH,
        )

    def link_copy(self, k, half):
        bit = self.order[half][self.first(k, half)]
        return pltpu.make_async_remote_copy(
            src_ref=self.part(self.stage(k // 2 - 1), half),
            dst_ref=self.link(half, k // 2 - 1),
            send_sem=self.link_send.at[half, k // 2 - 1],
            recv_sem=self.link_recv.at[half, k // 2 - 1],
            device_id={"mp": flip(self.me, bit)},
            device_id_type=MESH,
        )

    def addends(self, k, half):
        upto = self.first(k, half) if k else len(self.order[half])
        return [k | bit for bit in self.order[half][:upto]]

    def odd(self, k, ref):
        self.core_copy(k, ref).start()

    def even(self, k, ref):
        self.core_copy(k + 1, self.core(k // 2)).wait_recv()
        for half in (0, 1):
            joined = [self.part(ref, half), self.part(self.core(k // 2), half)]
            for j in self.addends(k, half):
                self.link_copy(j, half).wait_recv()
                joined.append(self.link(half, j // 2 - 1))
            add_up(self.part(self.stage(k // 2 - 1), half), joined)
            self.link_copy(k, half).start()

    def own(self, ref, out):
        self.core_copy(1, self.core(0)).wait_recv()
        for half in (0, 1):
            joined = [self.part(ref, half), self.part(self.core(0), half)]
            for j in self.addends(0, half):
                self.link_copy(j, half).wait_recv()
                joined.append(self.link(half, j // 2 - 1))
            add_up(self.part(out, half), joined)

    def drain(self, ref):
        for k in range(1, self.n, 2):
            self.core_copy(k, ref).wait_send()
        for k in range(2, self.n, 2):
            for half in (0, 1):
                self.link_copy(k, half).wait_send()


def add_up(out, terms):
    rows = out.shape[-2]
    step = 16
    lead = (slice(None),) * (len(out.shape) - 2)

    @pl.loop(0, rows // step)
    def _(i):
        at = lead + (pl.ds(pl.multiple_of(i * step, step), step), slice(None))
        total = terms[0][at].astype(F32)
        for t in terms[1:]:
            total = total + t[at].astype(F32)
        out[at] = total.astype(out.dtype)


def scatter_scratch(n, shape, half):
    return [
        pltpu.VMEM((n // 2,) + shape, BF),
        pltpu.VMEM((2, n // 2 - 1) + half, BF),
        pltpu.VMEM((n // 2 - 1,) + shape, BF),
        pltpu.SemaphoreType.DMA((n // 2,)),
        pltpu.SemaphoreType.DMA((n // 2,)),
        pltpu.SemaphoreType.DMA((2, n // 2 - 1)),
        pltpu.SemaphoreType.DMA((2, n // 2 - 1)),
    ]


def make_scatter(n, me, part, refs):
    core, link, stage = refs[:3]
    return Scatter(
        n,
        me,
        part,
        lambda i: core.at[i],
        lambda h, i: link.at[h, i],
        lambda i: stage.at[i],
        refs[3:7],
    )


def half_turn(x, lane):
    first = (lane % HD) < HD // 2
    return jnp.where(first, -pltpu.roll(x, LANES - HD // 2, 1), pltpu.roll(x, HD // 2, 1))


def half_turn_back(x, lane):
    first = (lane % HD) < HD // 2
    return jnp.where(first, pltpu.roll(x, LANES - HD // 2, 1), -pltpu.roll(x, HD // 2, 1))


def group_mean(x, ones):
    high = x.astype(BF)
    low = (x - high.astype(F32)).astype(BF)
    return (mm(high, ones) + mm(low, ones)) * (1.0 / HD)


def project_kernel(
    n, x_ref, gain_ref, w_ref, o_ref, cos_ref, sin_ref, gq_ref, gk_ref, ones_ref,
    normed_ref, raw_ref, q_ref, w_out, kv_out, o_out,
    w_all, kv_own, w_send, w_recv, kv_send, kv_recv, o_send, o_recv, local,
):
    me = lax.axis_index("mp")
    depth = w_ref.shape[0]
    tokens = x_ref.shape[0]
    rows = kv_out.shape[0]
    span = tokens // rows
    half = depth // 2
    own_w = pltpu.make_async_copy(w_ref, w_all.at[me], local.at[0])
    own_w.start()
    own_o = pltpu.make_async_copy(o_ref, o_out.at[me], local.at[1 + rows])
    own_o.start()
    greet(n, me)
    wide = o_ref.shape[1] // 2
    outs = Gather(
        n,
        me,
        lambda h: o_ref.at[:, pl.ds(h * wide, wide)],
        lambda k, h: o_out.at[flip(me, k), :, pl.ds(h * wide, wide)],
        o_send,
        o_recv,
    )
    weights = Gather(
        n,
        me,
        lambda h: w_ref.at[pl.ds(h * half, half)],
        lambda k, h: w_all.at[flip(me, k), pl.ds(h * half, half)],
        w_send,
        w_recv,
    )
    weights.start()
    step = min(64, tokens)

    @pl.loop(0, tokens // step)
    def _(i):
        at = pl.ds(pl.multiple_of(i * step, step), step)
        x = x_ref[at, :].astype(F32)
        scale = lax.rsqrt(jnp.mean(x * x, axis=-1, keepdims=True) + EPSILON)
        normed_ref[at, :] = (x * scale * gain_ref[...]).astype(BF)

    chunk = min(256, tokens)

    def accumulate(k, fresh):
        block = flip(me, k)
        columns = pl.ds(pl.multiple_of(block * depth, depth), depth)

        @pl.loop(0, tokens // chunk)
        def _(i):
            at = pl.ds(pl.multiple_of(i * chunk, chunk), chunk)
            term = mm(normed_ref[at, columns], w_all[block])
            raw_ref[at, :] = term if fresh else raw_ref[at, :] + term

    own_w.wait()
    accumulate(0, True)
    for h in (0, 1):
        weights.arrive(1, h)
    accumulate(1, False)
    for i, (k, h) in enumerate(weights.even):
        weights.forward(k, h)
        if any(k == other for other, _ in weights.even[:i]):
            accumulate(k, False)
    outs.start()
    for k in range(3, n, 2):
        for h in (0, 1):
            weights.arrive(k, h)
        accumulate(k, False)
    out_w = pltpu.make_async_copy(w_all, w_out, local.at[0])
    out_w.start()

    chunk = min(128, tokens)
    lane = lax.broadcasted_iota(jnp.int32, (chunk, LANES), 1)

    def finish(i, tiles):
        at = pl.ds(pl.multiple_of(i * chunk, chunk), chunk)
        cos, sin = cos_ref[at, :], sin_ref[at, :]
        for tile in tiles:
            lanes = slice(tile * LANES, (tile + 1) * LANES)
            x = raw_ref[at, lanes]
            query = tile < QW // LANES
            scale = lax.rsqrt(group_mean(x * x, ones_ref[...]) + EPSILON)
            v = x * scale * (gq_ref[...] if query else gk_ref[...])
            y = v * cos + half_turn(v, lane) * sin
            if query:
                q_ref[at, lanes] = (y * (HD**-0.5 * LOG2E)).astype(BF)
            else:
                mine = slice(tile * LANES - QW, (tile + 1) * LANES - QW)
                kv_own[at, mine] = jnp.where(lane < HD, y, x).astype(BF)

    count = raw_ref.shape[1] // LANES

    @pl.loop(0, tokens // chunk)
    def _(i):
        finish(i, range(QW // LANES, count))

    both = rows // 2
    keep = [
        pltpu.make_async_copy(
            kv_own.at[pl.ds(r * span, span)], kv_out.at[r, me], local.at[1 + r]
        )
        for r in range(rows)
    ]
    for c in keep:
        c.start()
    kvs = Gather(
        n,
        me,
        lambda h: kv_own.at[pl.ds(h * span, span)],
        lambda k, h: kv_out.at[h, flip(me, k)],
        kv_send,
        kv_recv,
    )
    kvs.start()

    @pl.loop(0, tokens // chunk)
    def _(i):
        finish(i, range(QW // LANES))

    for k, h in kvs.even:
        outs.forward(k, h)
        kvs.forward(k, h)
    outs.rest()
    kvs.rest()
    for c in keep:
        c.wait()
    out_w.wait()
    own_o.wait()
    weights.drain()
    outs.drain()
    kvs.drain()


def project(n, rows, x, gain, w, o, cos, sin, gq, gk, ones):
    tokens, width = x.shape
    depth, columns = w.shape
    vmem = pl.BlockSpec(memory_space=pltpu.VMEM)
    hbm = pl.BlockSpec(memory_space=pl.ANY)
    kvw = columns - QW
    return pl.pallas_call(
        functools.partial(project_kernel, n),
        in_specs=[vmem, vmem, hbm, hbm, vmem, vmem, vmem, vmem, vmem],
        out_specs=[vmem, vmem, vmem, hbm, hbm, hbm],
        out_shape=[
            jax.ShapeDtypeStruct((tokens, width), BF),
            jax.ShapeDtypeStruct((tokens, columns), F32),
            jax.ShapeDtypeStruct((tokens, QW), BF),
            jax.ShapeDtypeStruct((n, depth, columns), BF),
            jax.ShapeDtypeStruct((rows, n, tokens // rows, kvw), BF),
            jax.ShapeDtypeStruct((n,) + o.shape, BF),
        ],
        scratch_shapes=[
            pltpu.VMEM((n, depth, columns), BF),
            pltpu.VMEM((tokens, kvw), BF),
            pltpu.SemaphoreType.DMA((n, 2)),
            pltpu.SemaphoreType.DMA((n, 2)),
            pltpu.SemaphoreType.DMA((n, 2)),
            pltpu.SemaphoreType.DMA((n, 2)),
            pltpu.SemaphoreType.DMA((n, 2)),
            pltpu.SemaphoreType.DMA((n, 2)),
            pltpu.SemaphoreType.DMA((2 + rows,)),
        ],
        compiler_params=params(axes=0, key=0),
        name="project",
    )(x, gain, w, o, cos, sin, gq, gk, ones)


def unproject_kernel(
    n, dq_ref, dkv_ref, raw_ref, cos_ref, sin_ref, gq_ref, gk_ref, ones_ref, normed_ref, gout_ref,
    gj_ref, sq_ref, sk_ref, attend_ref, output_ref,
    dkv_own, term, *scratch,
):
    me = lax.axis_index("mp")
    greet(n, me)
    tokens = dq_ref.shape[0]
    rows = dkv_ref.shape[0]
    span = tokens // rows
    columns = raw_ref.shape[1]
    depth = attend_ref.shape[0]

    keys = make_scatter(n, me, lambda ref, h: ref.at[h], scratch[:7])
    half_w = output_ref.shape[1] // 2
    outs = make_scatter(
        n, me, lambda ref, h: ref.at[:, pl.ds(h * half_w, half_w)], scratch[7:14]
    )
    half_d = depth // 2
    weights = make_scatter(
        n, me, lambda ref, h: ref.at[pl.ds(h * half_d, half_d)], scratch[14:21]
    )

    def dkv_term(k):
        return dkv_ref.at[:, flip(me, k)]

    def out_term(k):
        return gout_ref.at[flip(me, k)]

    for k in range(n - 1, 0, -2):
        keys.odd(k, dkv_term(k))
    for k in range(n - 2, 0, -2):
        keys.even(k, dkv_term(k))
    for k in range(n - 1, 0, -2):
        outs.odd(k, out_term(k))

    chunk = min(128, tokens)
    lane = lax.broadcasted_iota(jnp.int32, (chunk, LANES), 1)
    sq_ref[...] = jnp.zeros_like(sq_ref)
    sk_ref[...] = jnp.zeros_like(sk_ref)

    def back(i, tiles, query):
        at = pl.ds(pl.multiple_of(i * chunk, chunk), chunk)
        cos, sin = cos_ref[at, :], sin_ref[at, :]
        total = 0.0
        for tile in tiles:
            lanes = slice(tile * LANES, (tile + 1) * LANES)
            x = raw_ref[at, lanes]
            if query:
                e = dq_ref[at, lanes]
            else:
                per = span // chunk
                here = pl.ds(pl.multiple_of(lax.rem(i, per) * chunk, chunk), chunk)
                e = dkv_own[lax.div(i, per), here, slice(tile * LANES - QW, (tile + 1) * LANES - QW)]
            scale = lax.rsqrt(group_mean(x * x, ones_ref[...]) + EPSILON)
            v = x * scale
            turned = e * cos + half_turn_back(e * sin, lane)
            u = turned * (gq_ref[...] if query else gk_ref[...])
            grad = scale * (u - v * group_mean(u * v, ones_ref[...]))
            gj_ref[at, lanes] = (grad if query else jnp.where(lane < HD, grad, e)).astype(BF)
            total = total + jnp.sum(turned * v, axis=0, keepdims=True)
        sums = sq_ref if query else sk_ref
        sums[...] += jnp.broadcast_to(total, sums.shape)

    count = columns // LANES

    @pl.loop(0, tokens // chunk)
    def _(i):
        back(i, range(QW // LANES), True)

    for k in range(n - 2, 0, -2):
        outs.even(k, out_term(k))

    keys.own(dkv_term(0), dkv_own)

    @pl.loop(0, tokens // chunk)
    def _(i):
        back(i, range(QW // LANES, count), False)

    for k in range(n - 1, -1, -1):
        at = pl.ds(pl.multiple_of(flip(me, k) * depth, depth), depth)
        here = term.at[k]
        here[...] = dg(normed_ref[:, at], gj_ref[...], TN).astype(BF)
        if k % 2:
            weights.odd(k, here)
        elif k:
            weights.even(k, here)
    outs.own(out_term(0), output_ref)
    weights.own(term.at[0], attend_ref)
    keys.drain(dkv_term(0))
    outs.drain(out_term(0))
    weights.drain(term.at[0])


def unproject(n, dq, dkv, raw, cos, sin, gq, gk, ones, normed, gout):
    tokens, columns = raw.shape
    rows = dkv.shape[0]
    span = tokens // rows
    kvw = columns - QW
    width = normed.shape[1]
    depth = width // n
    vmem = pl.BlockSpec(memory_space=pltpu.VMEM)
    return pl.pallas_call(
        functools.partial(unproject_kernel, n),
        in_specs=[vmem] * 10,
        out_specs=[vmem] * 5,
        out_shape=[
            jax.ShapeDtypeStruct((tokens, columns), BF),
            jax.ShapeDtypeStruct((8, LANES), F32),
            jax.ShapeDtypeStruct((8, LANES), F32),
            jax.ShapeDtypeStruct((depth, columns), BF),
            jax.ShapeDtypeStruct((QW // n, width), BF),
        ],
        scratch_shapes=[pltpu.VMEM((rows, span, kvw), F32), pltpu.VMEM((n, depth, columns), BF)]
        + scatter_scratch(n, (rows, span, kvw), (span, kvw))
        + scatter_scratch(n, (QW // n, width), (QW // n, width // 2))
        + scatter_scratch(n, (depth, columns), (depth // 2, columns)),
        compiler_params=params(mib=60, axes=0, key=2),
        name="unproject",
    )(dq, dkv, raw, cos, sin, gq, gk, ones, normed, gout)


def key_positions(shape, axis, group, per, span):
    return group * per * span + lax.broadcasted_iota(jnp.int32, shape, axis)


def attend_kernel(keys, info, q_ref, kv_ref, start_ref, ctx_ref, rl_ref, acc):
    span = q_ref.shape[1]
    per = keys // span
    row = pl.program_id(0)
    me, first, last_start = info[row, 0], info[row, 1], info[row, 2]
    low_q = lax.broadcasted_iota(jnp.int32, (span, LANES), 1) < HD
    low_k = lax.broadcasted_iota(jnp.int32, (keys, LANES), 1) < HD
    one = jnp.ones((keys, LANES), BF)
    none = jnp.zeros((span, LANES), BF)
    queries = []
    for h in range(GW // HD):
        pair = q_ref[0, :, (h // 2) * LANES : (h // 2 + 1) * LANES]
        queries.append(jnp.where(low_q, pair, none) if h % 2 == 0 else jnp.where(low_q, none, pair))
    acc[...] = jnp.zeros_like(acc)

    def block(g, masked):
        group = g
        kv = kv_ref[0, pl.ds(pl.multiple_of(group * keys, keys), keys), :]
        vk = jnp.concatenate([kv[:, HD:], kv[:, :HD]], axis=1)
        key_sides = (kv, vk)
        value_sides = (jnp.where(low_k, vk, one), jnp.where(low_k, one, kv))
        if masked:
            position = key_positions((span, keys), 1, group, per, span)
            own = me * span + lax.broadcasted_iota(jnp.int32, (span, keys), 0)
            seen = (position <= own) & (position >= start_ref[0][:, :1])
        for h in range(GW // HD):
            p = jnp.exp2(dg(queries[h], key_sides[h % 2], NT))
            if masked:
                p = jnp.where(seen, p, 0.0)
            acc[h] += mm(p.astype(BF), value_sides[h % 2])

    def step(g, carry):
        edge = (g == me // per) | (g * keys < last_start)
        pl.when(edge)(lambda: block(g, True))
        pl.when(jnp.logical_not(edge))(lambda: block(g, False))
        return carry

    lax.fori_loop(first, me // per + 1, step, 0)
    for pair in range(GW // LANES):
        even, odd = acc[2 * pair], acc[2 * pair + 1]
        total = jnp.where(low_q, pltpu.roll(even, HD, 1), pltpu.roll(odd, HD, 1))
        inverse = 1.0 / total
        lanes = slice(pair * LANES, (pair + 1) * LANES)
        ctx_ref[0, :, lanes] = (jnp.where(low_q, even, odd) * inverse).astype(BF)
        rl_ref[0, :, lanes] = inverse


def attend(info, q, kv, start):
    rows, span, _ = q.shape
    length = kv.shape[1]
    keys = min(512, length)
    own = lambda r, h, info: (r, 0, h)
    spec = pltpu.PrefetchScalarGridSpec(
        num_scalar_prefetch=1,
        grid=(rows, KVH),
        in_specs=[
            pl.BlockSpec((1, span, GW), own),
            pl.BlockSpec((1, length, LANES), own),
            pl.BlockSpec((1, span, LANES), lambda r, h, info: (r, 0, 0)),
        ],
        out_specs=[pl.BlockSpec((1, span, GW), own), pl.BlockSpec((1, span, GW), own)],
        scratch_shapes=[pltpu.VMEM((GW // HD, span, LANES), F32)],
    )
    return pl.pallas_call(
        functools.partial(attend_kernel, keys),
        grid_spec=spec,
        out_shape=[jax.ShapeDtypeStruct(q.shape, BF), jax.ShapeDtypeStruct(q.shape, F32)],
        compiler_params=params(axes=2),
        cost_estimate=pl.CostEstimate(
            flops=16 * rows * H * span * length * HD,
            bytes_accessed=rows * (length * 1280 + span * QW * 8),
            transcendentals=rows * H * span * length,
        ),
        name="attend",
    )(info, q, kv, start)


def attend_back_kernel(
    keys, info, q_ref, kv_ref, start_ref, do_ref, ctx_ref, rl_ref, dq_ref, dkv_ref, acc, sides
):
    span = q_ref.shape[1]
    per = keys // span
    length = kv_ref.shape[1]
    row = pl.program_id(0)
    me, first, last_start = info[row, 0], info[row, 1], info[row, 2]
    lane = lax.broadcasted_iota(jnp.int32, (span, LANES), 1)
    low_q = lane < HD
    low_k = lax.broadcasted_iota(jnp.int32, (keys, LANES), 1) < HD
    one = jnp.ones((keys, LANES), BF)
    for h in range(GW // HD):
        lanes = slice((h // 2) * LANES, (h // 2 + 1) * LANES)
        mine = low_q if h % 2 == 0 else jnp.logical_not(low_q)
        scaled = do_ref[0, :, lanes].astype(F32) * rl_ref[0, :, lanes]
        own = jnp.where(mine, scaled, 0.0)
        delta = -jnp.sum(own * ctx_ref[0, :, lanes].astype(F32), axis=1, keepdims=True)
        one_part = delta.astype(BF).astype(F32)
        two_part = (delta - one_part).astype(BF).astype(F32)
        three_part = delta - one_part - two_part
        base = HD if h % 2 == 0 else 0
        extra = jnp.where(
            lane == base,
            one_part,
            jnp.where(lane == base + 1, two_part, jnp.where(lane == base + 2, three_part, 0.0)),
        )
        sides[0, h] = jnp.where(mine, q_ref[0, :, lanes].astype(F32), 0.0).astype(BF)
        sides[1, h] = own.astype(BF)
        sides[2, h] = jnp.where(mine, scaled, extra).astype(BF)
    acc[...] = jnp.zeros_like(acc)

    def block(g, masked):
        group = g
        here = pl.ds(pl.multiple_of(group * keys, keys), keys)
        kv = kv_ref[0, here, :]
        vk = jnp.concatenate([kv[:, HD:], kv[:, :HD]], axis=1)
        key_sides = (kv, vk)
        value_sides = (jnp.where(low_k, vk, one), jnp.where(low_k, one, kv))
        if masked:
            position = key_positions((keys, span), 0, group, per, span)
            own = me * span + lax.broadcasted_iota(jnp.int32, (keys, span), 1)
            seen = (position <= own) & (position >= start_ref[0][:1, :])
        grad_key = grad_value = 0.0
        for h in range(GW // HD):
            e = jnp.exp2(dg(key_sides[h % 2], sides[0, h], NT))
            if masked:
                e = jnp.where(seen, e, 0.0)
            ds = (e * dg(value_sides[h % 2], sides[2, h], NT)).astype(BF)
            grad_value = grad_value + mm(e.astype(BF), sides[1, h])
            grad_key = grad_key + mm(ds, sides[0, h])
            acc[h] += dg(ds, key_sides[h % 2], TN)
        grad_key = (grad_key + pltpu.roll(grad_key, HD, 1)) * LN2
        grad_value = grad_value + pltpu.roll(grad_value, HD, 1)
        dkv_ref[0, here, :] = jnp.where(low_k, grad_key, grad_value).astype(BF)

    def step(g, carry):
        visited = (g >= first) & (g <= me // per)
        edge = (g == me // per) | (g * keys < last_start)

        @pl.when(jnp.logical_not(visited))
        def _():
            group = g
            dkv_ref[0, pl.ds(pl.multiple_of(group * keys, keys), keys), :] = jnp.zeros((keys, LANES), BF)

        pl.when(visited & edge)(lambda: block(g, True))
        pl.when(visited & jnp.logical_not(edge))(lambda: block(g, False))
        return carry

    lax.fori_loop(0, length // keys, step, 0)
    for pair in range(GW // LANES):
        lanes = slice(pair * LANES, (pair + 1) * LANES)
        dq_ref[0, :, lanes] = jnp.where(low_q, acc[2 * pair], acc[2 * pair + 1]) * (HD**-0.5)


def attend_back(info, q, kv, start, do, ctx, rl):
    rows, span, _ = q.shape
    length = kv.shape[1]
    keys = min(512, length)
    own = lambda r, h, info: (r, 0, h)
    spec = pltpu.PrefetchScalarGridSpec(
        num_scalar_prefetch=1,
        grid=(rows, KVH),
        in_specs=[
            pl.BlockSpec((1, span, GW), own),
            pl.BlockSpec((1, length, LANES), own),
            pl.BlockSpec((1, 8, span), lambda r, h, info: (r, 0, 0)),
            pl.BlockSpec((1, span, GW), own),
            pl.BlockSpec((1, span, GW), own),
            pl.BlockSpec((1, span, GW), own),
        ],
        out_specs=[pl.BlockSpec((1, span, GW), own), pl.BlockSpec((1, length, LANES), own)],
        scratch_shapes=[
            pltpu.VMEM((GW // HD, span, LANES), F32),
            pltpu.VMEM((3, GW // HD, span, LANES), BF),
        ],
    )
    return pl.pallas_call(
        functools.partial(attend_back_kernel, keys),
        grid_spec=spec,
        out_shape=[jax.ShapeDtypeStruct(q.shape, F32), jax.ShapeDtypeStruct(kv.shape, BF)],
        compiler_params=params(axes=2),
        cost_estimate=pl.CostEstimate(
            flops=40 * rows * H * span * length * HD,
            bytes_accessed=rows * (length * 2560 + span * QW * 16),
            transcendentals=rows * H * span * length,
        ),
        name="attend_back",
    )(info, q, kv, start, do, ctx, rl)


def xor_of(a, b, n):
    total, bit = 0, 1
    while bit < n:
        total = total + bit * lax.rem(lax.div(a, bit) + lax.div(b, bit), 2)
        bit *= 2
    return total


def feed_kernel(
    n, live_ref, x_own, g_ref, gu_any, dt_any,
    x_all, hid_ref, dgu_ref,
    x_vm, gu_ref, dt_ref, x_send, x_recv, loads, keep,
):
    me = lax.axis_index("mp")
    rows, span, width = x_own.shape
    slots = gu_ref.shape[0]
    r, j = pl.program_id(0), pl.program_id(1)
    now = r * n + j
    half = span // 2

    def gather(row):
        return Gather(
            n,
            me,
            lambda h: x_own.at[row, pl.ds(h * half, half)],
            lambda i, h: x_vm.at[row, i, pl.ds(h * half, half)],
            x_send.at[row],
            x_recv.at[row],
            True,
        )

    def store(row, slot):
        block = xor_of(me, slot, n)
        return pltpu.make_async_copy(x_vm.at[row, slot], x_all.at[row, block], keep.at[row, slot])

    fetch = [
        pltpu.make_async_copy(gu_any, gu_ref, loads.at[0]),
        pltpu.make_async_copy(dt_any, dt_ref, loads.at[1]),
    ]

    def own_copy(row):
        return pltpu.make_async_copy(x_own.at[row], x_vm.at[row, 0], loads.at[2 + row])

    def events(row, upto):
        todo = gather(row).even
        ends = [0] * n
        for k in range(2, n):
            ends[k] = ends[k - 1]
            if k % 2 == 0:
                ends[k] = max(ends[k - 1], 1 + max(i for i, e in enumerate(todo) if e[0] == k))
        return todo[ends[upto - 1] if upto else 0 : ends[upto]]

    @pl.when(now == 0)
    def _():
        for row in range(rows):
            own_copy(row).start()
        for c in fetch:
            c.start()
        greet(n, me)
        gather(0).start()
        own_copy(0).wait()
        for c in fetch:
            c.wait()

    for row in range(rows):
        for k in range(n):

            @pl.when(now == row * n + k)
            def _(row=row, k=k):
                if k == 0 and row:
                    own_copy(row).wait()
                for i, e in enumerate(events(row, k)):
                    gather(row).forward(*e)
                    if row + 1 < rows and k == 2 and i == 1:
                        gather(row + 1).start()
                if k % 2:
                    for h in (0, 1):
                        gather(row).arrive(k, h)

    store(r, j).start()
    x = x_vm.at[r, j]
    grad = mm(g_ref[0, 0], dt_ref[...])
    for t in range(slots):
        both = mm(x[...], gu_ref[t])
        gate, upper = both[:, :TILE], both[:, TILE:]
        live = live_ref[t]
        sig = jax.nn.sigmoid(gate)
        silu = gate * sig
        gh = grad[:, t * TILE : (t + 1) * TILE] * live
        hid_ref[0, 0, :, t * TILE : (t + 1) * TILE] = (silu * upper * live).astype(BF)
        dgu_ref[0, 0, :, 2 * t * TILE : (2 * t + 1) * TILE] = (
            gh * upper * (sig * (1.0 + gate * (1.0 - sig)))
        ).astype(BF)
        dgu_ref[0, 0, :, (2 * t + 1) * TILE : (2 * t + 2) * TILE] = (gh * silu).astype(BF)

    @pl.when(now == rows * n - 1)
    def _():
        for row in range(rows):
            gather(row).drain()
            for k in range(n):
                store(row, k).wait()


def feed(n, live, x, g, gu, dt):
    rows, span, width = x.shape
    slots = gu.shape[0]
    hbm = pl.BlockSpec(memory_space=pl.ANY)

    def place(r, j):
        return (r, xor_of(lax.axis_index("mp"), j, n), 0, 0)

    return pl.pallas_call(
        functools.partial(feed_kernel, n),
        grid=(rows, n),
        in_specs=[
            pl.BlockSpec(memory_space=pltpu.SMEM),
            hbm,
            pl.BlockSpec((1, 1, span, width), place),
            hbm,
            hbm,
        ],
        out_specs=[
            hbm,
            pl.BlockSpec((1, 1, span, slots * TILE), place),
            pl.BlockSpec((1, 1, span, 2 * slots * TILE), place),
        ],
        out_shape=[
            jax.ShapeDtypeStruct((rows, n, span, width), BF),
            jax.ShapeDtypeStruct((rows, n, span, slots * TILE), BF),
            jax.ShapeDtypeStruct((rows, n, span, 2 * slots * TILE), BF),
        ],
        scratch_shapes=[
            pltpu.VMEM((rows, n, span, width), BF),
            pltpu.VMEM(gu.shape, BF),
            pltpu.VMEM(dt.shape, BF),
            pltpu.SemaphoreType.DMA((rows, n, 2)),
            pltpu.SemaphoreType.DMA((rows, n, 2)),
            pltpu.SemaphoreType.DMA((2 + rows,)),
            pltpu.SemaphoreType.DMA((rows, n)),
        ],
        compiler_params=params(mib=56, axes=2, key=1),
        cost_estimate=pl.CostEstimate(
            flops=2 * 3 * rows * n * span * slots * TILE * width,
            bytes_accessed=6 * rows * n * span * width + 6 * slots * TILE * width,
            transcendentals=rows * n * span * slots * TILE,
        ),
        name="feed",
    )(live, x, g, gu, dt)


def tile_sum_kernel(
    n, a_ref, w_any, o_ref,
    w_ref, terms, core, link, stage, core_send, core_recv, link_send, link_recv, load,
):
    me = lax.axis_index("mp")
    rows, span, width = o_ref.shape
    r, j = pl.program_id(0), pl.program_id(1)
    k = n - 1 - j
    now = r * n + j
    half = span // 2

    def scatter(row):
        return Scatter(
            n,
            me,
            lambda ref, h: ref.at[pl.ds(h * half, half)],
            lambda i: core.at[row, i],
            lambda h, i: link.at[row, h, i],
            lambda i: stage.at[i],
            (core_send.at[row], core_recv.at[row], link_send.at[row], link_recv.at[row]),
        )

    @pl.when(now == 0)
    def _():
        fetch = pltpu.make_async_copy(w_any, w_ref, load.at[0])
        fetch.start()
        greet(n, me)
        fetch.wait()

    for i in range(1, n, 2):

        @pl.when((r > 0) & (k == i))
        def _(i=i):
            scatter(r - 1).core_copy(i, terms.at[i // 2]).wait_send()

    at = lax.rem(k, 2) * lax.div(k, 2) + (1 - lax.rem(k, 2)) * (n // 2)
    terms[at] = mm(a_ref[0, 0], w_ref[...]).astype(BF)
    mine = terms.at[n // 2]
    sums = scatter(r)
    for i in range(1, n):

        @pl.when(k == i)
        def _(i=i):
            if i % 2:
                sums.odd(i, terms.at[i // 2])
            else:

                @pl.when(r > 0)
                def _():
                    for h in (0, 1):
                        scatter(r - 1).link_copy(i, h).wait_send()

                sums.even(i, mine)

    @pl.when(k == 0)
    def _():
        sums.core_copy(1, core.at[r, 0]).wait_recv()
        add_up(o_ref.at[r], [mine, core.at[r, 0]])

    def close(row):
        last = scatter(row)
        for h in (0, 1):
            here = last.part(o_ref.at[row], h)
            joined = [here]
            for i in last.addends(0, h):
                last.link_copy(i, h).wait_recv()
                joined.append(last.link(h, i // 2 - 1))
            add_up(here, joined)

    for row in range(rows - 1):

        @pl.when(now == (row + 1) * n + n // 2)
        def _(row=row):
            close(row)

    @pl.when(now == rows * n - 1)
    def _():
        close(rows - 1)
        scatter(rows - 1).drain(mine)


def tile_sum(n, a, w, key):
    rows, _, span, depth = a.shape
    width = w.shape[1]
    half = span // 2

    def place(r, j):
        return (r, xor_of(lax.axis_index("mp"), n - 1 - j, n), 0, 0)

    return pl.pallas_call(
        functools.partial(tile_sum_kernel, n),
        grid=(rows, n),
        in_specs=[pl.BlockSpec((1, 1, span, depth), place), pl.BlockSpec(memory_space=pl.ANY)],
        out_specs=pl.BlockSpec(memory_space=pltpu.VMEM),
        out_shape=jax.ShapeDtypeStruct((rows, span, width), F32),
        scratch_shapes=[
            pltpu.VMEM(w.shape, BF),
            pltpu.VMEM((n // 2 + 1, span, width), BF),
            pltpu.VMEM((rows, n // 2, span, width), BF),
            pltpu.VMEM((rows, 2, n // 2 - 1, half, width), BF),
            pltpu.VMEM((n // 2 - 1, span, width), BF),
            pltpu.SemaphoreType.DMA((rows, n // 2)),
            pltpu.SemaphoreType.DMA((rows, n // 2)),
            pltpu.SemaphoreType.DMA((rows, 2, n // 2 - 1)),
            pltpu.SemaphoreType.DMA((rows, 2, n // 2 - 1)),
            pltpu.SemaphoreType.DMA((1,)),
        ],
        compiler_params=params(mib=56, axes=2, key=key),
        cost_estimate=pl.CostEstimate(
            flops=2 * rows * n * span * depth * width,
            bytes_accessed=2 * rows * n * span * depth + 2 * depth * width,
            transcendentals=0,
        ),
        name="tile_sum",
    )(a, w)


def weight_kernel(finish, a_ref, b_ref, o_ref, acc):
    k = pl.program_id(1)

    @pl.when(k == 0)
    def _():
        acc[...] = jnp.zeros_like(acc)

    acc[...] += dg(a_ref[...], b_ref[...], TN)

    @pl.when(k == pl.num_programs(1) - 1)
    def _():
        finish(o_ref, acc)


def weight_grad(left, right, block, stacked):
    tokens, lw = left.shape
    rw = right.shape[1]
    block = min(block, lw)
    step = 512
    if stacked:
        slots = rw // 256
        out_spec = pl.BlockSpec((slots, block, 256), lambda i, k: (0, i, 0))
        out_shape = jax.ShapeDtypeStruct((slots, lw, 256), BF)

        def finish(o_ref, acc):
            for t in range(slots):
                o_ref[t] = acc[:, t * 256 : (t + 1) * 256].astype(BF)
    else:
        out_spec = pl.BlockSpec((block, rw), lambda i, k: (i, 0))
        out_shape = jax.ShapeDtypeStruct((lw, rw), BF)

        def finish(o_ref, acc):
            o_ref[...] = acc[...].astype(BF)

    return pl.pallas_call(
        functools.partial(weight_kernel, finish),
        grid=(lw // block, tokens // step),
        in_specs=[
            pl.BlockSpec((step, block), lambda i, k: (k, i)),
            pl.BlockSpec((step, rw), lambda i, k: (k, 0)),
        ],
        out_specs=out_spec,
        out_shape=out_shape,
        scratch_shapes=[pltpu.VMEM((block, rw), F32)],
        compiler_params=params(axes=2),
        cost_estimate=pl.CostEstimate(
            flops=2 * tokens * lw * rw,
            bytes_accessed=2 * tokens * (lw + rw) + 2 * lw * rw,
            transcendentals=0,
        ),
        name="weight_grad",
    )(left, right)


def shards(
    n,
    hidden_in,
    doc_ids,
    tile_slot,
    attention_gain,
    query_gain,
    key_gain,
    attend_weight,
    output_weight,
    feed_gain,
    gate_up_slots,
    down_slots,
    out_grad,
):
    rows, span, width = hidden_in.shape
    length = doc_ids.shape[1]
    slots = gate_up_slots.shape[0]
    tokens = rows * span
    me = lax.axis_index("mp")
    offset = me * span

    kw = KVH * HD
    keys_w = attend_weight[:, QW : QW + kw].reshape(-1, KVH, HD)
    values_w = attend_weight[:, QW + kw :].reshape(-1, KVH, HD)
    attend_w = jnp.concatenate(
        [attend_weight[:, :QW], jnp.concatenate([keys_w, values_w], 2).reshape(-1, 2 * kw)], 1
    )
    starts = doc_starts(doc_ids)
    local_start = lax.dynamic_slice_in_dim(starts, offset, span, 1)
    local_pos = offset + jnp.arange(span, dtype=jnp.int32)[None] - local_start
    cos, sin = rotary_tables(local_pos.reshape(tokens))
    gq = jnp.tile(query_gain, 2)[None]
    gk = jnp.concatenate([key_gain, jnp.ones_like(key_gain)])[None]
    lane = jnp.arange(LANES) // HD
    ones = (lane[:, None] == lane[None, :]).astype(BF)
    key_block = min(512, length)
    info = jnp.stack(
        [
            jnp.full((rows,), me, jnp.int32),
            local_start[:, 0] // key_block,
            local_start[:, -1],
        ],
        1,
    ).astype(jnp.int32)
    start_col = jnp.broadcast_to(local_start[:, :, None], (rows, span, LANES))
    start_row = jnp.broadcast_to(local_start[:, None, :], (rows, 8, span))

    x_own = hidden_in.reshape(tokens, width)
    x_value = x_own.astype(F32)
    scale_a = rms_scale(x_value)
    normed_ab, raw, q, attend_all, kv_all, output_all = project(
        n, rows, x_own, attention_gain[None], attend_w, output_weight, cos, sin, gq, gk, ones
    )
    q = q.reshape(rows, span, QW)
    kv_all = kv_all.reshape(rows, length, -1)
    attend_full = attend_all.reshape(width, -1)
    output_full = output_all.reshape(QW, width)
    grad_branch, output_full = lax.optimization_barrier((out_grad.astype(BF), output_full))
    grads_all = lax.all_gather(grad_branch, "mp", axis=1, tiled=True)
    ctx, rl = attend(info, q, kv_all, start_col)
    context_b = ctx.reshape(tokens, QW)
    middle = x_value + mm(context_b, output_full)
    scale_f = rms_scale(middle)
    normed_fb = (middle * scale_f * feed_gain).astype(BF).reshape(rows, span, width)

    slot_index = me * slots + jnp.arange(slots, dtype=jnp.int32)
    live = jnp.any(tile_slot[None, :] == slot_index[:, None], axis=1).astype(F32)
    gu_t = jnp.swapaxes(gate_up_slots, 1, 2).reshape(slots * 2 * TILE, width)
    d_flat = down_slots.reshape(slots * TILE, width)
    d_t = d_flat.T
    everything = rows * n * span
    normed_all, hidden, grad_both = feed(
        n, live, normed_fb, grads_all.reshape(rows, n, span, width), gate_up_slots, d_t
    )
    grad_down = weight_grad(
        hidden.reshape(everything, -1), grads_all.reshape(everything, width), 768, False
    ).reshape(slots, TILE, width)
    grad_gate_up = weight_grad(
        normed_all.reshape(everything, width), grad_both.reshape(everything, -1), 1024, True
    )
    gate_up_total, down_total = lax.psum((grad_gate_up, grad_down), "dp")
    grad_both, grad_gate_up, grad_down = lax.optimization_barrier(
        (grad_both, grad_gate_up, grad_down)
    )
    grad_normed_f = tile_sum(n, grad_both, gu_t, 3).reshape(tokens, width)

    weighted = grad_normed_f * feed_gain
    inner = jnp.mean(weighted * middle, axis=-1, keepdims=True)
    gain_feed = jnp.sum(grad_normed_f * middle * scale_f, axis=0)
    grad_middle = out_grad.reshape(tokens, width) + scale_f * (
        weighted - middle * scale_f * scale_f * inner
    )
    grad_attn_b = grad_middle.astype(BF)
    grad_context = dg(grad_attn_b, output_full, NT).astype(BF).reshape(rows, span, QW)
    grad_output = dg(context_b, grad_attn_b, TN).astype(BF)

    dq, dkv = attend_back(info, q, kv_all, start_row, grad_context, ctx, rl)
    grad_joined_b, sum_q, sum_k, attend_share, output_share = unproject(
        n,
        dq.reshape(tokens, QW),
        dkv.reshape(rows, n, span, -1),
        raw,
        cos,
        sin,
        gq,
        gk,
        ones,
        normed_ab,
        grad_output.reshape(n, -1, width),
    )
    grad_normed_a = dg(grad_joined_b, attend_full, NT)

    hidden, attend_share = lax.optimization_barrier((hidden, attend_share))
    layer_out = middle + tile_sum(n, hidden, d_flat, 4).reshape(tokens, width)
    attend_share, output_share, gate_up_total, down_total = lax.optimization_barrier(
        (attend_share, output_share, gate_up_total, down_total)
    )
    attend_total, output_total = lax.psum((attend_share, output_share), "dp")
    attend_total = attend_total.astype(F32)
    kv_total = attend_total[:, QW:].reshape(-1, KVH, 2, HD)
    attend_total = jnp.concatenate(
        [
            attend_total[:, :QW],
            kv_total[:, :, 0].reshape(-1, kw),
            kv_total[:, :, 1].reshape(-1, kw),
        ],
        1,
    )
    weighted_a = grad_normed_a * attention_gain
    inner_a = jnp.mean(weighted_a * x_value, axis=-1, keepdims=True)
    gain_attention = jnp.sum(grad_normed_a * x_value * scale_a, axis=0)
    input_grad = grad_middle + scale_a * (weighted_a - x_value * scale_a * scale_a * inner_a)

    gains = jnp.concatenate([gain_attention, gain_feed, sum_q[0], sum_k[0]])
    gains = lax.psum(gains, ("dp", "mp"))
    gain_query = gains[2 * width : 2 * width + HD] + gains[2 * width + HD : 2 * width + 2 * HD]
    gain_key = gains[2 * width + LANES : 2 * width + LANES + HD]
    shape = (rows, span, width)
    return (
        layer_out.reshape(shape),
        input_grad.reshape(shape),
        attend_total,
        output_total.astype(F32),
        gate_up_total.astype(F32),
        down_total.astype(F32),
        gains[:width],
        gain_query,
        gain_key,
        gains[width : 2 * width],
    )


def solution(mesh):
    placed = (
        P("dp", "mp", None),
        P("dp", None),
        P(),
        P(),
        P(),
        P(),
        P("mp", None),
        P("mp", None),
        P(),
        P("mp", None, None),
        P("mp", None, None),
        P("dp", "mp", None),
    )
    return jax.shard_map(
        functools.partial(shards, mesh.shape["mp"]),
        mesh=mesh,
        in_specs=placed,
        out_specs=(
            P("dp", "mp", None),
            P("dp", "mp", None),
            P("mp", None),
            P("mp", None),
            P("mp", None, None),
            P("mp", None, None),
            P(),
            P(),
            P(),
            P(),
        ),
        check_vma=False,
    )
```

```python
import functools

import jax
import jax.numpy as jnp
from jax import lax
from jax.experimental import pallas as pl
from jax.experimental.pallas import tpu as pltpu
from jax.sharding import PartitionSpec as P

H = 20
KVH = 5
HD = 64
TILE = 128
EPSILON = 1e-06
QW = H * HD
LANES = 128
GW = (H // KVH) * HD
DOCS = 3
AWAY = 256.0
LOG2E = 1.4426950408889634
LN2 = 0.6931471805599453
BF = jnp.bfloat16
F32 = jnp.float32
MIB = 1 << 20
NT = (((1,), (1,)), ((), ()))
TN = (((0,), (0,)), ((), ()))


def params(mib=56, axes=1, key=None):
    if key is None:
        return pltpu.CompilerParams(
            vmem_limit_bytes=mib * MIB, dimension_semantics=("arbitrary",) * axes
        )
    return pltpu.CompilerParams(
        vmem_limit_bytes=mib * MIB,
        dimension_semantics=("arbitrary",) * axes if axes else None,
        collective_id=key,
        has_side_effects=True,
    )


TINY = pl.CostEstimate(flops=1, bytes_accessed=1, transcendentals=0)


def mm(a, b):
    return jnp.dot(a, b, preferred_element_type=F32)


def dg(a, b, dims):
    return lax.dot_general(a, b, dims, preferred_element_type=F32)


def doc_starts(docs):
    index = jnp.arange(docs.shape[-1], dtype=jnp.int32)
    change = jnp.concatenate(
        [jnp.ones(docs.shape[:-1] + (1,), dtype=jnp.bool_), docs[..., 1:] != docs[..., :-1]],
        axis=-1,
    )
    return lax.cummax(jnp.where(change, index, 0), axis=docs.ndim - 1)


def rotary_tables(positions):
    half_dim = HD // 2
    freqs = 1.0 / 10000.0 ** (jnp.arange(half_dim, dtype=jnp.float32) * 2.0 / HD)
    angles = positions.astype(jnp.float32)[..., None] * freqs
    return jnp.tile(jnp.cos(angles), 4), jnp.tile(jnp.sin(angles), 4)


def rms_scale(values):
    return lax.rsqrt(jnp.mean(values * values, axis=-1, keepdims=True) + EPSILON)


MESH = pl.DeviceIdType.MESH


def flip(me, k):
    bit = 1
    while bit <= k:
        if k & bit:
            me = me + bit - 2 * bit * lax.rem(lax.div(me, bit), 2)
        bit *= 2
    return me


def link_bits(n):
    return [1 << i for i in range(1, n.bit_length() - 1)]


def greet(n, me):
    barrier = pltpu.get_barrier_semaphore()
    bits = [1] + link_bits(n)
    for bit in bits:
        pl.semaphore_signal(barrier, inc=1, device_id={"mp": flip(me, bit)}, device_id_type=MESH)
    pl.semaphore_wait(barrier, len(bits))


def greet_all(n, me, m, line):
    barrier = pltpu.get_barrier_semaphore()
    bits = [1] + link_bits(n)
    for bit in bits:
        pl.semaphore_signal(barrier, inc=1, device_id={"mp": flip(me, bit)}, device_id_type=MESH)
    for step in range(1, m):
        other = lax.rem(line + step, m)
        pl.semaphore_signal(barrier, inc=1, device_id={"dp": other}, device_id_type=MESH)
    pl.semaphore_wait(barrier, len(bits) + m - 1)


class Line:
    def __init__(self, m, line, own, up, across, total, sems):
        self.own, self.up, self.across, self.total, self.sems = own, up, across, total, sems
        low = line < m // 2
        self.inner = jnp.where(low, line + 1, line - 1)
        self.outer = jnp.where(low, line - 1, line + 1)
        self.has_outer = (line > 0) & (line < m - 1)
        self.middle = (line == m // 2 - 1) | (line == m // 2)

    def copy(self, kind, c):
        src, dst, to = (
            (self.own, self.up, self.inner),
            (self.own, self.across, self.inner),
            (self.total, self.total, self.outer),
        )[kind]
        return pltpu.make_async_remote_copy(
            src_ref=src(c),
            dst_ref=dst(c),
            send_sem=self.sems.at[2 * kind, c],
            recv_sem=self.sems.at[2 * kind + 1, c],
            device_id={"dp": to},
            device_id_type=MESH,
        )

    def launch(self, c):
        @pl.when(jnp.logical_not(self.has_outer))
        def _():
            self.copy(0, c).start()

    def inward(self, c):
        @pl.when(self.has_outer)
        def _():
            self.copy(0, c).wait_recv()
            add_up(self.own(c), [self.own(c), self.up(c)])

            @pl.when(self.middle)
            def _():
                self.copy(1, c).start()

            @pl.when(jnp.logical_not(self.middle))
            def _():
                self.copy(0, c).start()

    def outward(self, c):
        @pl.when(self.middle)
        def _():
            self.copy(1, c).wait_recv()
            add_up(self.total(c), [self.own(c), self.across(c)])

        @pl.when(jnp.logical_not(self.middle))
        def _():
            self.copy(2, c).wait_recv()

        @pl.when(self.has_outer)
        def _():
            self.copy(2, c).start()

    def drain(self, c):
        @pl.when(self.middle)
        def _():
            self.copy(1, c).wait_send()

        @pl.when(jnp.logical_not(self.middle))
        def _():
            self.copy(0, c).wait_send()

        @pl.when(self.has_outer)
        def _():
            self.copy(2, c).wait_send()


class Gather:
    def __init__(self, n, me, own, slot, send, recv, relative=False):
        self.n, self.me, self.own, self.slot, self.send, self.recv = n, me, own, slot, send, recv
        self.relative = relative
        bits = link_bits(n)
        self.order = (bits + [1], bits[::-1] + [1])
        even = [(k, h) for k in range(2, n, 2) for h in (0, 1)]
        even.sort(key=lambda kh: (bin(kh[0]).count("1"), max(self.place(*kh)), kh[1]))
        self.even = even

    def place(self, k, half):
        return [i for i, bit in enumerate(self.order[half]) if k & bit]

    def copy(self, k, half, bit):
        return pltpu.make_async_remote_copy(
            src_ref=self.own(half) if k == 0 else self.here(k, half),
            dst_ref=self.slot(k ^ bit, half, k) if self.relative else self.slot(k, half),
            send_sem=self.send.at[k ^ bit, half],
            recv_sem=self.recv.at[k ^ bit, half],
            device_id={"mp": flip(self.me, bit)},
            device_id_type=MESH,
        )

    def here(self, k, half):
        return self.slot(k, half, k) if self.relative else self.slot(k, half)

    def onward(self, k, half):
        return self.order[half][(max(self.place(k, half)) + 1) if k else 0 :]

    def start(self):
        for i in range(len(self.order[0])):
            for half in (0, 1):
                self.copy(0, half, self.order[half][i]).start()

    def arrive(self, k, half):
        here = self.here(k, half)
        pltpu.make_async_remote_copy(
            src_ref=here,
            dst_ref=here,
            send_sem=self.send.at[k, half],
            recv_sem=self.recv.at[k, half],
            device_id={"mp": flip(self.me, 1)},
            device_id_type=MESH,
        ).wait_recv()

    def forward(self, k, half):
        self.arrive(k, half)
        for bit in self.onward(k, half):
            self.copy(k, half, bit).start()

    def rest(self):
        for k, half in [(1, 0), (1, 1)] + [(k + 1, h) for k, h in self.even]:
            self.arrive(k, half)

    def drain(self):
        for k in range(0, self.n, 2):
            for half in (0, 1):
                for bit in self.onward(k, half):
                    self.copy(k, half, bit).wait_send()


class Scatter:
    def __init__(self, n, me, part, core, link, sems):
        self.n, self.me, self.part = n, me, part
        self.core, self.link = core, link
        self.core_send, self.core_recv, self.link_send, self.link_recv = sems
        bits = link_bits(n)
        self.order = (bits[::-1], bits)

    def first(self, k, half):
        return next(i for i, bit in enumerate(self.order[half]) if k & bit)

    def core_copy(self, k, ref):
        return pltpu.make_async_remote_copy(
            src_ref=ref,
            dst_ref=self.core(k // 2),
            send_sem=self.core_send.at[k // 2],
            recv_sem=self.core_recv.at[k // 2],
            device_id={"mp": flip(self.me, 1)},
            device_id_type=MESH,
        )

    def link_copy(self, k, half):
        bit = self.order[half][self.first(k, half)]
        return pltpu.make_async_remote_copy(
            src_ref=self.part(self.core(k // 2), half),
            dst_ref=self.link(half, k // 2 - 1),
            send_sem=self.link_send.at[half, k // 2 - 1],
            recv_sem=self.link_recv.at[half, k // 2 - 1],
            device_id={"mp": flip(self.me, bit)},
            device_id_type=MESH,
        )

    def addends(self, k, half):
        upto = self.first(k, half) if k else len(self.order[half])
        return [k | bit for bit in self.order[half][:upto]]

    def odd(self, k, ref):
        self.core_copy(k, ref).start()

    def even(self, k, ref):
        self.core_copy(k + 1, self.core(k // 2)).wait_recv()
        for half in (0, 1):
            joined = [self.part(ref, half), self.part(self.core(k // 2), half)]
            for j in self.addends(k, half):
                self.link_copy(j, half).wait_recv()
                joined.append(self.link(half, j // 2 - 1))
            add_up(joined[1], joined)
            self.link_copy(k, half).start()

    def own(self, ref, out):
        self.core_copy(1, self.core(0)).wait_recv()
        for half in (0, 1):
            joined = [self.part(ref, half), self.part(self.core(0), half)]
            for j in self.addends(0, half):
                self.link_copy(j, half).wait_recv()
                joined.append(self.link(half, j // 2 - 1))
            add_up(self.part(out, half), joined)

    def drain(self, ref):
        for k in range(1, self.n, 2):
            self.core_copy(k, ref).wait_send()
        for k in range(2, self.n, 2):
            for half in (0, 1):
                self.link_copy(k, half).wait_send()


def add_up(out, terms):
    rows = out.shape[-2]
    step = 16
    lead = (slice(None),) * (len(out.shape) - 2)

    @pl.loop(0, rows // step)
    def _(i):
        at = lead + (pl.ds(pl.multiple_of(i * step, step), step), slice(None))
        total = terms[0][at].astype(F32)
        for t in terms[1:]:
            total = total + t[at].astype(F32)
        out[at] = total.astype(out.dtype)


def scatter_scratch(n, shape, half):
    return [
        pltpu.VMEM((n // 2,) + shape, BF),
        pltpu.VMEM((2, n // 2 - 1) + half, BF),
        pltpu.SemaphoreType.DMA((n // 2,)),
        pltpu.SemaphoreType.DMA((n // 2,)),
        pltpu.SemaphoreType.DMA((2, n // 2 - 1)),
        pltpu.SemaphoreType.DMA((2, n // 2 - 1)),
    ]


def make_scatter(n, me, part, refs):
    core, link = refs[:2]
    return Scatter(
        n,
        me,
        part,
        lambda i: core.at[i],
        lambda h, i: link.at[h, i],
        refs[2:6],
    )


def half_turn(x, lane):
    first = (lane % HD) < HD // 2
    return jnp.where(first, -pltpu.roll(x, LANES - HD // 2, 1), pltpu.roll(x, HD // 2, 1))


def half_turn_back(x, lane):
    first = (lane % HD) < HD // 2
    return jnp.where(first, pltpu.roll(x, LANES - HD // 2, 1), -pltpu.roll(x, HD // 2, 1))


def group_mean(x, ones):
    high = x.astype(BF)
    low = (x - high.astype(F32)).astype(BF)
    return (mm(high, ones) + mm(low, ones)) * (1.0 / HD)


def project_kernel(
    n, x_ref, gain_ref, w_ref, o_ref, cos_ref, sin_ref, gq_ref, gk_ref, ones_ref,
    normed_ref, raw_ref, q_ref, w_out, kv_out, o_out,
    w_all, kv_own, w_send, w_recv, kv_send, kv_recv, o_send, o_recv, local,
):
    me = lax.axis_index("mp")
    depth = w_ref.shape[0]
    tokens = x_ref.shape[0]
    rows = kv_out.shape[0]
    span = tokens // rows
    half = depth // 2
    own_w = pltpu.make_async_copy(w_ref, w_all.at[me], local.at[0])
    own_w.start()
    own_o = pltpu.make_async_copy(o_ref, o_out.at[me], local.at[1 + rows])
    own_o.start()
    greet(n, me)
    wide = o_ref.shape[1] // 2
    outs = Gather(
        n,
        me,
        lambda h: o_ref.at[:, pl.ds(h * wide, wide)],
        lambda k, h: o_out.at[flip(me, k), :, pl.ds(h * wide, wide)],
        o_send,
        o_recv,
    )
    weights = Gather(
        n,
        me,
        lambda h: w_ref.at[pl.ds(h * half, half)],
        lambda k, h: w_all.at[flip(me, k), pl.ds(h * half, half)],
        w_send,
        w_recv,
    )
    weights.start()
    step = min(64, tokens)

    @pl.loop(0, tokens // step)
    def _(i):
        at = pl.ds(pl.multiple_of(i * step, step), step)
        x = x_ref[at, :].astype(F32)
        scale = lax.rsqrt(jnp.mean(x * x, axis=-1, keepdims=True) + EPSILON)
        normed_ref[at, :] = (x * scale * gain_ref[...]).astype(BF)

    chunk = min(256, tokens)

    def accumulate(k, fresh):
        block = flip(me, k)
        columns = pl.ds(pl.multiple_of(block * depth, depth), depth)

        @pl.loop(0, tokens // chunk)
        def _(i):
            at = pl.ds(pl.multiple_of(i * chunk, chunk), chunk)
            term = mm(normed_ref[at, columns], w_all[block])
            raw_ref[at, :] = term if fresh else raw_ref[at, :] + term

    own_w.wait()
    accumulate(0, True)
    for h in (0, 1):
        weights.arrive(1, h)
    accumulate(1, False)
    for i, (k, h) in enumerate(weights.even):
        weights.forward(k, h)
        if any(k == other for other, _ in weights.even[:i]):
            accumulate(k, False)
    outs.start()
    for k in range(3, n, 2):
        for h in (0, 1):
            weights.arrive(k, h)
        accumulate(k, False)
    out_w = pltpu.make_async_copy(w_all, w_out, local.at[0])
    out_w.start()

    chunk = min(128, tokens)
    lane = lax.broadcasted_iota(jnp.int32, (chunk, LANES), 1)

    def finish(i, tiles):
        at = pl.ds(pl.multiple_of(i * chunk, chunk), chunk)
        cos, sin = cos_ref[at, :], sin_ref[at, :]
        for tile in tiles:
            lanes = slice(tile * LANES, (tile + 1) * LANES)
            x = raw_ref[at, lanes]
            query = tile < QW // LANES
            scale = lax.rsqrt(group_mean(x * x, ones_ref[...]) + EPSILON)
            v = x * scale * (gq_ref[...] if query else gk_ref[...])
            y = v * cos + half_turn(v, lane) * sin
            if query:
                q_ref[at, lanes] = (y * (HD**-0.5 * LOG2E)).astype(BF)
            else:
                mine = slice(tile * LANES - QW, (tile + 1) * LANES - QW)
                kv_own[at, mine] = jnp.where(lane < HD, y, x).astype(BF)

    count = raw_ref.shape[1] // LANES

    @pl.loop(0, tokens // chunk)
    def _(i):
        finish(i, range(QW // LANES, count))

    both = rows // 2
    keep = [
        pltpu.make_async_copy(
            kv_own.at[pl.ds(r * span, span)], kv_out.at[r, me], local.at[1 + r]
        )
        for r in range(rows)
    ]
    for c in keep:
        c.start()
    kvs = Gather(
        n,
        me,
        lambda h: kv_own.at[pl.ds(h * span, span)],
        lambda k, h: kv_out.at[h, flip(me, k)],
        kv_send,
        kv_recv,
    )
    kvs.start()

    @pl.loop(0, tokens // chunk)
    def _(i):
        finish(i, range(QW // LANES))

    for k, h in kvs.even:
        outs.forward(k, h)
        kvs.forward(k, h)
    outs.rest()
    kvs.rest()
    for c in keep:
        c.wait()
    out_w.wait()
    own_o.wait()
    weights.drain()
    outs.drain()
    kvs.drain()


def project(n, rows, x, gain, w, o, cos, sin, gq, gk, ones):
    tokens, width = x.shape
    depth, columns = w.shape
    vmem = pl.BlockSpec(memory_space=pltpu.VMEM)
    hbm = pl.BlockSpec(memory_space=pl.ANY)
    kvw = columns - QW
    return pl.pallas_call(
        functools.partial(project_kernel, n),
        in_specs=[vmem, vmem, hbm, hbm, vmem, vmem, vmem, vmem, vmem],
        out_specs=[vmem, vmem, vmem, hbm, hbm, hbm],
        out_shape=[
            jax.ShapeDtypeStruct((tokens, width), BF),
            jax.ShapeDtypeStruct((tokens, columns), F32),
            jax.ShapeDtypeStruct((tokens, QW), BF),
            jax.ShapeDtypeStruct((n, depth, columns), BF),
            jax.ShapeDtypeStruct((rows, n, tokens // rows, kvw), BF),
            jax.ShapeDtypeStruct((n,) + o.shape, BF),
        ],
        scratch_shapes=[
            pltpu.VMEM((n, depth, columns), BF),
            pltpu.VMEM((tokens, kvw), BF),
            pltpu.SemaphoreType.DMA((n, 2)),
            pltpu.SemaphoreType.DMA((n, 2)),
            pltpu.SemaphoreType.DMA((n, 2)),
            pltpu.SemaphoreType.DMA((n, 2)),
            pltpu.SemaphoreType.DMA((n, 2)),
            pltpu.SemaphoreType.DMA((n, 2)),
            pltpu.SemaphoreType.DMA((2 + rows,)),
        ],
        compiler_params=params(axes=0, key=0),
        name="project",
    )(x, gain, w, o, cos, sin, gq, gk, ones)


def unproject_kernel(
    n, dq_ref, dkv_ref, raw_ref, cos_ref, sin_ref, gq_ref, gk_ref, ones_ref, gout_ref,
    gj_ref, sq_ref, sk_ref, output_ref,
    dkv_own, *scratch,
):
    me = lax.axis_index("mp")
    greet(n, me)
    tokens = dq_ref.shape[0]
    rows = dkv_ref.shape[0]
    span = tokens // rows
    columns = raw_ref.shape[1]
    keys = make_scatter(n, me, lambda ref, h: ref.at[h], scratch[:6])
    half_w = output_ref.shape[1] // 2
    outs = make_scatter(
        n, me, lambda ref, h: ref.at[:, pl.ds(h * half_w, half_w)], scratch[6:12]
    )

    def dkv_term(k):
        return dkv_ref.at[:, flip(me, k)]

    def out_term(k):
        return gout_ref.at[flip(me, k)]

    for k in range(n - 1, 0, -2):
        keys.odd(k, dkv_term(k))
    for k in range(n - 2, 0, -2):
        keys.even(k, dkv_term(k))
    for k in range(n - 1, 0, -2):
        outs.odd(k, out_term(k))

    chunk = min(128, tokens)
    lane = lax.broadcasted_iota(jnp.int32, (chunk, LANES), 1)
    sq_ref[...] = jnp.zeros_like(sq_ref)
    sk_ref[...] = jnp.zeros_like(sk_ref)

    def back(i, tiles, query):
        at = pl.ds(pl.multiple_of(i * chunk, chunk), chunk)
        cos, sin = cos_ref[at, :], sin_ref[at, :]
        total = 0.0
        for tile in tiles:
            lanes = slice(tile * LANES, (tile + 1) * LANES)
            x = raw_ref[at, lanes]
            if query:
                e = dq_ref[at, lanes]
            else:
                per = span // chunk
                here = pl.ds(pl.multiple_of(lax.rem(i, per) * chunk, chunk), chunk)
                e = dkv_own[lax.div(i, per), here, slice(tile * LANES - QW, (tile + 1) * LANES - QW)]
            scale = lax.rsqrt(group_mean(x * x, ones_ref[...]) + EPSILON)
            v = x * scale
            turned = e * cos + half_turn_back(e * sin, lane)
            u = turned * (gq_ref[...] if query else gk_ref[...])
            grad = scale * (u - v * group_mean(u * v, ones_ref[...]))
            gj_ref[at, lanes] = (grad if query else jnp.where(lane < HD, grad, e)).astype(BF)
            total = total + jnp.sum(turned * v, axis=0, keepdims=True)
        sums = sq_ref if query else sk_ref
        sums[...] += jnp.broadcast_to(total, sums.shape)

    count = columns // LANES

    @pl.loop(0, tokens // chunk)
    def _(i):
        back(i, range(QW // LANES), True)

    for k in range(n - 2, 0, -2):
        outs.even(k, out_term(k))

    keys.own(dkv_term(0), dkv_own)

    @pl.loop(0, tokens // chunk)
    def _(i):
        back(i, range(QW // LANES, count), False)

    outs.own(out_term(0), output_ref)
    keys.drain(dkv_term(0))
    outs.drain(out_term(0))


def unproject(n, dq, dkv, raw, cos, sin, gq, gk, ones, gout):
    tokens, columns = raw.shape
    rows = dkv.shape[0]
    span = tokens // rows
    kvw = columns - QW
    width = gout.shape[2]
    vmem = pl.BlockSpec(memory_space=pltpu.VMEM)
    return pl.pallas_call(
        functools.partial(unproject_kernel, n),
        in_specs=[vmem] * 9,
        out_specs=[vmem] * 4,
        out_shape=[
            jax.ShapeDtypeStruct((tokens, columns), BF),
            jax.ShapeDtypeStruct((8, LANES), F32),
            jax.ShapeDtypeStruct((8, LANES), F32),
            jax.ShapeDtypeStruct((QW // n, width), BF),
        ],
        scratch_shapes=[pltpu.VMEM((rows, span, kvw), F32)]
        + scatter_scratch(n, (rows, span, kvw), (span, kvw))
        + scatter_scratch(n, (QW // n, width), (QW // n, width // 2)),
        compiler_params=params(mib=60, axes=0, key=2),
        cost_estimate=TINY,
        name="unproject",
    )(dq, dkv, raw, cos, sin, gq, gk, ones, gout)


GAIN_ROWS = 40


def finish_kernel(
    n, m, normed_ref, gj_ref, w_any, x_ref, mid_ref, gain_ref, output_ref, sums_ref,
    grad_ref, attend_ref, out_ref, gains_ref,
    w_ref, term, error, own_w, up_w, across_w, total_w, own_o, up_o, across_o, total_o, landed,
    sem_w, sem_o, sem_g, load, *scratch,
):
    me, line = lax.axis_index("mp"), lax.axis_index("dp")
    depth = w_ref.shape[1]
    tokens, width = x_ref.shape
    pieces, piece = own_w.shape[0], own_w.shape[1]
    fetch = pltpu.make_async_copy(w_any, w_ref, load.at[0])
    fetch.start()
    greet_all(n, me, m, line)
    half = depth // 2
    sums = make_scatter(n, me, lambda ref, h: ref.at[pl.ds(h * half, half)], scratch)
    at = lambda ref: lambda c: ref.at[c]
    weights = Line(m, line, at(own_w), at(up_w), at(across_w), at(total_w), sem_w)
    outs = Line(m, line, at(own_o), at(up_o), at(across_o), at(total_o), sem_o)
    own_o[0] = output_ref[...]

    chunk = error.shape[0]
    gains_ref[...] = sums_ref[...]

    def tokens_part(i):
        here = pl.ds(pl.multiple_of(i * chunk, chunk), chunk)
        for b in range(n):
            error[:, b * depth : (b + 1) * depth] = dg(gj_ref[here, :], w_ref[b], NT)
        small = min(32, chunk)

        @pl.loop(0, chunk // small)
        def _(s):
            part = pl.ds(pl.multiple_of(s * small, small), small)
            rows = pl.ds(pl.multiple_of(i * chunk + s * small, small), small)
            e = error[part, :]
            x = x_ref[rows, :].astype(F32)
            scale = lax.rsqrt(jnp.mean(x * x, axis=-1, keepdims=True) + EPSILON)
            u = e * gain_ref[...]
            v = x * scale
            inner = jnp.mean(u * v, axis=-1, keepdims=True)
            grad_ref[rows, :] = mid_ref[rows, :] + scale * (u - v * inner)
            total = jnp.sum(e * v, axis=0, keepdims=True)
            for b in range(width // LANES):
                gains_ref[b : b + 1, :] += total[:, b * LANES : (b + 1) * LANES]

    def weight_part(k):
        columns = pl.ds(pl.multiple_of(flip(me, k) * depth, depth), depth)
        term[k] = dg(normed_ref[:, columns], gj_ref[...], TN).astype(BF)

    parts = tokens // chunk
    left = list(range(parts))
    outs.launch(0)
    outs.inward(0)
    for k in range(n - 1, 0, -1):
        weight_part(k)
        if k % 2:
            sums.odd(k, term.at[k])
        else:
            sums.even(k, term.at[k])
        if k == n - 1:
            fetch.wait()
    weight_part(0)

    def span_of(first, last):
        @pl.loop(first, last)
        def _(i):
            tokens_part(i)

    span_of(0, parts // 2)
    outs.outward(0)
    span_of(parts // 2, parts)
    sums.own(term.at[0], attend_ref)
    for c in range(pieces):
        own_w[c] = attend_ref[c * piece : (c + 1) * piece, :].astype(BF)
        weights.launch(c)
        weights.inward(c)
    steps = [("mp", flip(me, 1 << i)) for i in range(n.bit_length() - 1)]
    steps += [("dp", flip(line, 1 << i)) for i in range(m.bit_length() - 1)]

    def exchange(i):
        axis, to = steps[i]
        return pltpu.make_async_remote_copy(
            src_ref=landed.at[2 * i],
            dst_ref=landed.at[2 * i + 1],
            send_sem=sem_g.at[0, i],
            recv_sem=sem_g.at[1, i],
            device_id={axis: to},
            device_id_type=MESH,
        )

    done = 0
    for i in range(len(steps)):
        landed[2 * i] = gains_ref[...]
        exchange(i).start()
        if done < pieces and i % 2:
            weights.outward(done)
            done += 1
        exchange(i).wait_recv()
        gains_ref[...] = landed[2 * i] + landed[2 * i + 1]
    for c in range(done, pieces):
        weights.outward(c)
    for c in range(pieces):
        attend_ref[c * piece : (c + 1) * piece, :] = total_w[c].astype(F32)
    out_ref[...] = total_o[0].astype(F32)
    for c in range(pieces):
        weights.drain(c)
    outs.drain(0)
    for i in range(len(steps)):
        exchange(i).wait_send()
    sums.drain(term.at[0])


def finish(n, m, normed, gj, w, x, middle, gain, output_share, sums):
    tokens, width = x.shape
    columns = gj.shape[1]
    depth = width // n
    pieces = 4
    vmem = pl.BlockSpec(memory_space=pltpu.VMEM)
    steps = n.bit_length() + m.bit_length() - 2
    return pl.pallas_call(
        functools.partial(finish_kernel, n, m),
        in_specs=[vmem, vmem, pl.BlockSpec(memory_space=pl.ANY)] + [vmem] * 5,
        out_specs=[vmem] * 4,
        out_shape=[
            jax.ShapeDtypeStruct((tokens, width), F32),
            jax.ShapeDtypeStruct((depth, columns), F32),
            jax.ShapeDtypeStruct(output_share.shape, F32),
            jax.ShapeDtypeStruct((GAIN_ROWS, LANES), F32),
        ],
        scratch_shapes=[
            pltpu.VMEM(w.shape, BF),
            pltpu.VMEM((n, depth, columns), BF),
            pltpu.VMEM((min(256, tokens), width), F32),
        ]
        + [pltpu.VMEM((pieces, depth // pieces, columns), BF)] * 4
        + [pltpu.VMEM((1,) + output_share.shape, BF)] * 4
        + [
            pltpu.VMEM((2 * steps, GAIN_ROWS, LANES), F32),
            pltpu.SemaphoreType.DMA((6, pieces)),
            pltpu.SemaphoreType.DMA((6, 1)),
            pltpu.SemaphoreType.DMA((2, steps)),
            pltpu.SemaphoreType.DMA((1,)),
        ]
        + scatter_scratch(n, (depth, columns), (depth // 2, columns)),
        compiler_params=params(mib=60, axes=0, key=5),
        cost_estimate=TINY,
        name="finish",
    )(normed, gj, w, x, middle, gain, output_share, sums)


def key_positions(shape, axis, group, per, span):
    return group * per * span + lax.broadcasted_iota(jnp.int32, shape, axis)


def attend_kernel(keys, info, q_ref, kv_ref, start_ref, ctx_ref, rl_ref, acc):
    span = q_ref.shape[1]
    per = keys // span
    row = pl.program_id(0)
    me, first, last_start = info[row, 0], info[row, 1], info[row, 2]
    low_q = lax.broadcasted_iota(jnp.int32, (span, LANES), 1) < HD
    low_k = lax.broadcasted_iota(jnp.int32, (keys, LANES), 1) < HD
    one = jnp.ones((keys, LANES), BF)
    none = jnp.zeros((span, LANES), BF)
    queries = []
    for h in range(GW // HD):
        pair = q_ref[0, :, (h // 2) * LANES : (h // 2 + 1) * LANES]
        queries.append(jnp.where(low_q, pair, none) if h % 2 == 0 else jnp.where(low_q, none, pair))
    acc[...] = jnp.zeros_like(acc)

    def block(g, masked):
        group = g
        kv = kv_ref[0, pl.ds(pl.multiple_of(group * keys, keys), keys), :]
        vk = jnp.concatenate([kv[:, HD:], kv[:, :HD]], axis=1)
        key_sides = (kv, vk)
        value_sides = (jnp.where(low_k, vk, one), jnp.where(low_k, one, kv))
        if masked:
            position = key_positions((span, keys), 1, group, per, span)
            own = me * span + lax.broadcasted_iota(jnp.int32, (span, keys), 0)
            seen = (position <= own) & (position >= start_ref[0][:, :1])
        for h in range(GW // HD):
            p = jnp.exp2(dg(queries[h], key_sides[h % 2], NT))
            if masked:
                p = jnp.where(seen, p, 0.0)
            acc[h] += mm(p.astype(BF), value_sides[h % 2])

    def step(g, carry):
        edge = (g == me // per) | (g * keys < last_start)
        pl.when(edge)(lambda: block(g, True))
        pl.when(jnp.logical_not(edge))(lambda: block(g, False))
        return carry

    lax.fori_loop(first, me // per + 1, step, 0)
    for pair in range(GW // LANES):
        even, odd = acc[2 * pair], acc[2 * pair + 1]
        total = jnp.where(low_q, pltpu.roll(even, HD, 1), pltpu.roll(odd, HD, 1))
        inverse = 1.0 / total
        lanes = slice(pair * LANES, (pair + 1) * LANES)
        ctx_ref[0, :, lanes] = (jnp.where(low_q, even, odd) * inverse).astype(BF)
        rl_ref[0, :, lanes] = inverse


def attend(info, q, kv, start):
    rows, span, _ = q.shape
    length = kv.shape[1]
    keys = min(512, length)
    own = lambda r, h, info: (r, 0, h)
    spec = pltpu.PrefetchScalarGridSpec(
        num_scalar_prefetch=1,
        grid=(rows, KVH),
        in_specs=[
            pl.BlockSpec((1, span, GW), own),
            pl.BlockSpec((1, length, LANES), own),
            pl.BlockSpec((1, span, LANES), lambda r, h, info: (r, 0, 0)),
        ],
        out_specs=[pl.BlockSpec((1, span, GW), own), pl.BlockSpec((1, span, GW), own)],
        scratch_shapes=[pltpu.VMEM((GW // HD, span, LANES), F32)],
    )
    return pl.pallas_call(
        functools.partial(attend_kernel, keys),
        grid_spec=spec,
        out_shape=[jax.ShapeDtypeStruct(q.shape, BF), jax.ShapeDtypeStruct(q.shape, F32)],
        compiler_params=params(axes=2),
        cost_estimate=pl.CostEstimate(
            flops=16 * rows * H * span * length * HD,
            bytes_accessed=rows * (length * 1280 + span * QW * 8),
            transcendentals=rows * H * span * length,
        ),
        name="attend",
    )(info, q, kv, start)


def attend_back_kernel(
    keys, n, q_ref, kv_ref, qa_ref, ka_ref, do_ref, ctx_ref, rl_ref, a_ref, w_any,
    dq_ref, dkv_ref, o_ref, acc, sides, *scratch,
):
    span = q_ref.shape[1]
    per = keys // span
    length = kv_ref.shape[1]
    me = lax.axis_index("mp")
    rows = o_ref.shape[0]
    now = pl.program_id(0) * KVH + pl.program_id(1)
    sums = TileSum(n, me, o_ref, w_any, scratch)
    batch = a_ref.shape[1]
    steps = rows * n // batch

    @pl.when(now == 0)
    def _():
        sums.start()

    @pl.when(now < steps)
    def _():
        @pl.loop(0, batch)
        def _(i):
            tile = now * batch + i
            slot = n - 1 - lax.rem(tile, n)
            sums.step(tile, a_ref.at[0, lax.rem(xor_of(me, slot, n), batch)])

    lane = lax.broadcasted_iota(jnp.int32, (span, LANES), 1)
    low_q = lane < HD
    low_k = lax.broadcasted_iota(jnp.int32, (keys, LANES), 1) < HD
    one = jnp.ones((keys, LANES), BF)
    for h in range(GW // HD):
        lanes = slice((h // 2) * LANES, (h // 2 + 1) * LANES)
        mine = low_q if h % 2 == 0 else jnp.logical_not(low_q)
        scaled = do_ref[0, :, lanes].astype(F32) * rl_ref[0, :, lanes]
        own = jnp.where(mine, scaled, 0.0)
        delta = -jnp.sum(own * ctx_ref[0, :, lanes].astype(F32), axis=1, keepdims=True)
        one_part = delta.astype(BF).astype(F32)
        two_part = (delta - one_part).astype(BF).astype(F32)
        three_part = delta - one_part - two_part
        base = HD if h % 2 == 0 else 0
        extra = jnp.where(
            lane == base,
            one_part,
            jnp.where(lane == base + 1, two_part, jnp.where(lane == base + 2, three_part, 0.0)),
        )
        query = q_ref[0, :, lanes].astype(F32)
        sides[0, h] = jnp.where(mine, query, 0.0).astype(BF)
        sides[1, h] = own.astype(BF)
        sides[2, h] = jnp.where(mine, scaled, extra).astype(BF)
        sides[3, h] = jnp.where(mine, query, qa_ref[0].astype(F32)).astype(BF)
    acc[...] = jnp.zeros_like(acc)

    def block(g, masked):
        here = pl.ds(pl.multiple_of(g * keys, keys), keys)
        kv = kv_ref[0, here, :]
        ka = ka_ref[0, here, :]
        vk = jnp.concatenate([kv[:, HD:], kv[:, :HD]], axis=1)
        key_sides = (jnp.where(low_k, kv, ka), jnp.where(low_k, ka, vk))
        value_sides = (jnp.where(low_k, vk, one), jnp.where(low_k, one, kv))
        if masked:
            position = g * keys + lax.broadcasted_iota(jnp.int32, (keys, span), 0)
            seen = position <= me * span + lax.broadcasted_iota(jnp.int32, (keys, span), 1)
        grad_key = grad_value = 0.0
        for h in range(GW // HD):
            e = jnp.exp2(dg(key_sides[h % 2], sides[3, h], NT))
            if masked:
                e = jnp.where(seen, e, 0.0)
            ds = (e * dg(value_sides[h % 2], sides[2, h], NT)).astype(BF)
            grad_value = grad_value + mm(e.astype(BF), sides[1, h])
            grad_key = grad_key + mm(ds, sides[0, h])
            acc[h] += dg(ds, key_sides[h % 2], TN)
        grad_key = (grad_key + pltpu.roll(grad_key, HD, 1)) * LN2
        grad_value = grad_value + pltpu.roll(grad_value, HD, 1)
        dkv_ref[0, here, :] = jnp.where(low_k, grad_key, grad_value).astype(BF)

    last = lax.div(me, per)

    @pl.loop(0, last)
    def _(g):
        block(g, False)

    block(last, True)

    @pl.loop(last + 1, length // keys)
    def _(g):
        dkv_ref[0, pl.ds(pl.multiple_of(g * keys, keys), keys), :] = jnp.zeros((keys, LANES), BF)

    for pair in range(GW // LANES):
        lanes = slice(pair * LANES, (pair + 1) * LANES)
        dq_ref[0, :, lanes] = jnp.where(low_q, acc[2 * pair], acc[2 * pair + 1]) * (HD**-0.5)

    @pl.when(now == rows * KVH - 1)
    def _():
        sums.end()


def attend_back(n, q, kv, qa, ka, do, ctx, rl, a, w):
    rows, span, _ = q.shape
    length = kv.shape[1]
    keys = min(512, length)
    depth, width = w.shape
    batch = 2
    while rows * n // batch > rows * KVH:
        batch *= 2
    own = lambda r, h: (r, 0, h)

    def place(r, h):
        tile = jnp.minimum(r * KVH + h, rows * n // batch - 1) * batch
        slot = n - 1 - lax.rem(tile, n)
        return (lax.div(tile, n), lax.div(xor_of(lax.axis_index("mp"), slot, n), batch), 0, 0)

    return pl.pallas_call(
        functools.partial(attend_back_kernel, keys, n),
        grid=(rows, KVH),
        in_specs=[
            pl.BlockSpec((1, span, GW), own),
            pl.BlockSpec((1, length, LANES), own),
            pl.BlockSpec((1, span, LANES), lambda r, h: (r, 0, 0)),
            pl.BlockSpec((1, length, LANES), lambda r, h: (r, 0, 0)),
            pl.BlockSpec((1, span, GW), own),
            pl.BlockSpec((1, span, GW), own),
            pl.BlockSpec((1, span, GW), own),
            pl.BlockSpec((1, batch, span, depth), place),
            pl.BlockSpec(memory_space=pl.ANY),
        ],
        out_specs=[
            pl.BlockSpec((1, span, GW), own),
            pl.BlockSpec((1, length, LANES), own),
            pl.BlockSpec(memory_space=pltpu.VMEM),
        ],
        out_shape=[
            jax.ShapeDtypeStruct(q.shape, F32),
            jax.ShapeDtypeStruct(kv.shape, BF),
            jax.ShapeDtypeStruct((rows, span, width), F32),
        ],
        scratch_shapes=[
            pltpu.VMEM((GW // HD, span, LANES), F32),
            pltpu.VMEM((4, GW // HD, span, LANES), BF),
        ]
        + tile_scratch(n, rows, span, w),
        compiler_params=params(mib=60, axes=2, key=4),
        cost_estimate=TINY,
        name="attend_back",
    )(q, kv, qa, ka, do, ctx, rl, a, w)


def xor_of(a, b, n):
    total, bit = 0, 1
    while bit < n:
        total = total + bit * lax.rem(lax.div(a, bit) + lax.div(b, bit), 2)
        bit *= 2
    return total


def feed_kernel(
    n, live_ref, x_own, g_ref, gu_any, dt_any,
    x_all, hid_ref, dgu_ref, gd_any,
    x_vm, gu_ref, dt_ref, d_sum, out_d, x_send, x_recv, loads, stores, keep,
):
    me = lax.axis_index("mp")
    rows, span, width = x_own.shape
    slots = gu_ref.shape[0]
    r, p = pl.program_id(0), pl.program_id(1)
    pairs = n // 2
    now = r * pairs + p
    half = span // 2

    def gather(row):
        def slot(i, h, k):
            at = lax.rem(flip(me, k), 2) * span + h * half
            return x_vm.at[row, i // 2, pl.ds(pl.multiple_of(at, half), half)]

        return Gather(
            n,
            me,
            lambda h: x_own.at[row, pl.ds(h * half, half)],
            slot,
            x_send.at[row],
            x_recv.at[row],
            True,
        )

    def own_copy(row):
        at = pl.ds(pl.multiple_of(lax.rem(me, 2) * span, span), span)
        return pltpu.make_async_copy(x_own.at[row], x_vm.at[row, 0, at], loads.at[2 + row])

    fetch = [
        pltpu.make_async_copy(gu_any, gu_ref, loads.at[0]),
        pltpu.make_async_copy(dt_any, dt_ref, loads.at[1]),
    ]

    def events(row, upto):
        todo = gather(row).even
        ends = [0] * pairs
        for i in range(1, pairs):
            ends[i] = max(ends[i - 1], 1 + max(j for j, e in enumerate(todo) if e[0] == 2 * i))
        return todo[ends[upto - 1] if upto else 0 : ends[upto]]

    @pl.when(now == 0)
    def _():
        for row in range(rows):
            own_copy(row).start()
        for c in fetch:
            c.start()
        greet(n, me)
        gather(0).start()
        d_sum[...] = jnp.zeros_like(d_sum)
        own_copy(0).wait()
        for c in fetch:
            c.wait()

    for row in range(rows):
        for i in range(pairs):

            @pl.when(now == row * pairs + i)
            def _(row=row, i=i):
                if i == 0 and row:
                    own_copy(row).wait()
                for j, e in enumerate(events(row, i)):
                    gather(row).forward(*e)
                    if row + 1 < rows and i == 1 and j == 1:
                        gather(row + 1).start()
                for h in (0, 1):
                    gather(row).arrive(2 * i + 1, h)

    def save(row, i):
        block = lax.div(xor_of(me, 2 * i, n), 2)
        return pltpu.make_async_copy(x_vm.at[row, i], x_all.at[row, block], keep.at[row, i])

    save(r, p).start()
    x = x_vm.at[r, p]
    grad = mm(g_ref[0, 0], dt_ref[...])
    for t in range(slots):
        both = mm(x[...], gu_ref[t])
        gate, upper = both[:, :TILE], both[:, TILE:]
        live = live_ref[t]
        sig = jax.nn.sigmoid(gate)
        silu = gate * sig
        gh = grad[:, t * TILE : (t + 1) * TILE] * live
        hid_ref[0, 0, :, t * TILE : (t + 1) * TILE] = (silu * upper * live).astype(BF)
        dgu_ref[0, 0, :, 2 * t * TILE : (2 * t + 1) * TILE] = (
            gh * upper * (sig * (1.0 + gate * (1.0 - sig)))
        ).astype(BF)
        dgu_ref[0, 0, :, (2 * t + 1) * TILE : (2 * t + 2) * TILE] = (gh * silu).astype(BF)

    cut = LANES

    @pl.loop(0, slots * TILE // cut)
    def _(i):
        at = pl.ds(pl.multiple_of(i * cut, cut), cut)
        d_sum[at, :] += dg(hid_ref[0, 0, :, at], g_ref[0, 0], TN)

    @pl.when(now == rows * pairs - 1)
    def _():
        def store(t):
            return pltpu.make_async_copy(out_d.at[t % 2], gd_any.at[t], stores.at[t % 2])

        for t in range(slots):
            if t > 1:
                store(t - 2).wait()
            out_d[t % 2] = d_sum[t * TILE : (t + 1) * TILE, :].astype(BF)
            store(t).start()
        for t in range(max(slots - 2, 0), slots):
            store(t).wait()
        for row in range(rows):
            for i in range(pairs):
                save(row, i).wait()
        for row in range(rows):
            gather(row).drain()


def feed(n, live, x, g, gu, dt):
    rows, span, width = x.shape
    slots = gu.shape[0]
    hbm = pl.BlockSpec(memory_space=pl.ANY)
    pairs = n // 2

    def place(r, p):
        return (r, lax.div(xor_of(lax.axis_index("mp"), 2 * p, n), 2), 0, 0)

    return pl.pallas_call(
        functools.partial(feed_kernel, n),
        grid=(rows, pairs),
        in_specs=[
            pl.BlockSpec(memory_space=pltpu.SMEM),
            hbm,
            pl.BlockSpec((1, 1, 2 * span, width), place),
            hbm,
            hbm,
        ],
        out_specs=[
            hbm,
            pl.BlockSpec((1, 1, 2 * span, slots * TILE), place),
            pl.BlockSpec((1, 1, 2 * span, 2 * slots * TILE), place),
            hbm,
        ],
        out_shape=[
            jax.ShapeDtypeStruct((rows, pairs, 2 * span, width), BF),
            jax.ShapeDtypeStruct((rows, pairs, 2 * span, slots * TILE), BF),
            jax.ShapeDtypeStruct((rows, pairs, 2 * span, 2 * slots * TILE), BF),
            jax.ShapeDtypeStruct((slots, TILE, width), BF),
        ],
        scratch_shapes=[
            pltpu.VMEM((rows, pairs, 2 * span, width), BF),
            pltpu.VMEM(gu.shape, BF),
            pltpu.VMEM(dt.shape, BF),
            pltpu.VMEM((slots * TILE, width), F32),
            pltpu.VMEM((2, TILE, width), BF),
            pltpu.SemaphoreType.DMA((rows, n, 2)),
            pltpu.SemaphoreType.DMA((rows, n, 2)),
            pltpu.SemaphoreType.DMA((2 + rows,)),
            pltpu.SemaphoreType.DMA((2,)),
            pltpu.SemaphoreType.DMA((rows, pairs)),
        ],
        compiler_params=params(mib=62, axes=2, key=1),
        cost_estimate=pl.CostEstimate(
            flops=2 * 6 * rows * n * span * slots * TILE * width,
            bytes_accessed=6 * rows * n * span * width + 6 * slots * TILE * width,
            transcendentals=rows * n * span * slots * TILE,
        ),
        name="feed",
    )(live, x, g.reshape(rows, pairs, 2 * span, width), gu, dt)


class TileSum:
    def __init__(self, n, me, o_ref, w_any, scratch):
        self.n, self.me, self.o_ref, self.w_any = n, me, o_ref, w_any
        self.w_ref, self.terms, self.core, self.link = scratch[:4]
        self.sems, self.load = scratch[4:8], scratch[8]
        self.rows, self.span, _ = o_ref.shape

    def scatter(self, row):
        half = self.span // 2
        return Scatter(
            self.n,
            self.me,
            lambda ref, h: ref.at[pl.ds(h * half, half)],
            lambda i: self.core.at[row, i],
            lambda h, i: self.link.at[row, h, i],
            tuple(s.at[row] for s in self.sems),
        )

    def start(self, meet=greet):
        fetch = pltpu.make_async_copy(self.w_any, self.w_ref, self.load.at[0])
        fetch.start()
        meet(self.n, self.me)
        fetch.wait()

    def close(self, row):
        last = self.scatter(row)
        for h in (0, 1):
            here = last.part(self.o_ref.at[row], h)
            joined = [here]
            for i in last.addends(0, h):
                last.link_copy(i, h).wait_recv()
                joined.append(last.link(h, i // 2 - 1))
            add_up(here, joined)

    def step(self, now, a_ref):
        n, terms = self.n, self.terms
        r = lax.div(now, n)
        k = n - 1 - lax.rem(now, n)
        for row in range(1, self.rows):

            @pl.when(now == row * n + n // 2)
            def _(row=row):
                self.close(row - 1)

        for i in range(1, n, 2):

            @pl.when((r > 0) & (k == i))
            def _(i=i):
                self.scatter(r - 1).core_copy(i, terms.at[i // 2]).wait_send()

        at = lax.rem(k, 2) * lax.div(k, 2) + (1 - lax.rem(k, 2)) * (n // 2)
        terms[at] = mm(a_ref[...], self.w_ref[...]).astype(BF)
        mine = terms.at[n // 2]
        sums = self.scatter(r)
        for i in range(1, n):

            @pl.when(k == i)
            def _(i=i):
                if i % 2:
                    sums.odd(i, terms.at[i // 2])
                else:
                    sums.even(i, mine)

        @pl.when(k == 0)
        def _():
            sums.core_copy(1, self.core.at[r, 0]).wait_recv()
            add_up(self.o_ref.at[r], [mine, self.core.at[r, 0]])

    def end(self):
        self.close(self.rows - 1)
        self.scatter(self.rows - 1).drain(self.terms.at[self.n // 2])
        for row in range(self.rows - 1):
            for i in range(2, self.n, 2):
                for h in (0, 1):
                    self.scatter(row).link_copy(i, h).wait_send()


def tile_scratch(n, rows, span, w):
    width = w.shape[1]
    return [
        pltpu.VMEM(w.shape, BF),
        pltpu.VMEM((n // 2 + 1, span, width), BF),
        pltpu.VMEM((rows, n // 2, span, width), BF),
        pltpu.VMEM((rows, 2, n // 2 - 1, span // 2, width), BF),
        pltpu.SemaphoreType.DMA((rows, n // 2)),
        pltpu.SemaphoreType.DMA((rows, n // 2)),
        pltpu.SemaphoreType.DMA((rows, 2, n // 2 - 1)),
        pltpu.SemaphoreType.DMA((rows, 2, n // 2 - 1)),
        pltpu.SemaphoreType.DMA((1,)),
    ]


def spread_kernel(
    n, m, a_ref, w_any, x_ref, b_ref, d_any,
    o_ref, grad_ref, total_any,
    acc, own, up, across, line_sems, moves, *scratch,
):
    me, line = lax.axis_index("mp"), lax.axis_index("dp")
    rows = o_ref.shape[0]
    now = pl.program_id(0) * n + pl.program_id(1)
    per = rows * n // BLOCKS
    sums = TileSum(n, me, o_ref, w_any, scratch)
    chunks = own.shape[0]
    at = lambda ref: lambda c: ref.at[c]
    down = Line(m, line, at(own), at(up), at(across), at(up), line_sems)
    bring = pltpu.make_async_copy(d_any, own, moves.at[0])
    send = pltpu.make_async_copy(up, total_any, moves.at[1])

    @pl.when(now == 0)
    def _():
        bring.start()
        sums.start(lambda n, me: greet_all(n, me, m, line))
        bring.wait()
        for c in range(chunks):
            down.launch(c)

    sums.step(now, a_ref.at[0, 0])
    for c in range(chunks):

        @pl.when(now == 1 + c)
        def _(c=c):
            down.inward(c)

        @pl.when(now == 3 + c)
        def _(c=c):
            down.outward(c)

    k = lax.rem(now, per)
    term = dg(x_ref[...], b_ref[...], TN)

    @pl.when(k == 0)
    def _():
        acc[...] = term

    @pl.when((k > 0) & (k < per - 1))
    def _():
        acc[...] += term

    @pl.when(k == per - 1)
    def _():
        done = acc[...] + term
        for t in range(grad_ref.shape[0]):
            grad_ref[t] = done[:, 2 * t * TILE : 2 * (t + 1) * TILE].astype(BF)

    @pl.when(now == rows * n - 1)
    def _():
        for c in range(chunks):
            down.drain(c)
        send.start()
        sums.end()
        send.wait()


BLOCKS = 4
CHUNKS = 12


def spread(n, m, a, w, x, down):
    rows, _, span, depth = a.shape
    width = w.shape[1]
    slots = depth // (2 * TILE)
    everything = rows * n * span
    per = rows * n // BLOCKS
    part, block = everything // per, width // BLOCKS
    flat = (slots * TILE // CHUNKS, width)

    def place(r, j):
        return (r, xor_of(lax.axis_index("mp"), n - 1 - j, n), 0, 0)

    def token(r, j):
        return lax.rem(r * n + j, per)

    def column(r, j):
        return lax.div(r * n + j, per)

    hbm = pl.BlockSpec(memory_space=pl.ANY)
    out, grad, total = pl.pallas_call(
        functools.partial(spread_kernel, n, m),
        grid=(rows, n),
        in_specs=[
            pl.BlockSpec((1, 1, span, depth), place),
            hbm,
            pl.BlockSpec((part, block), lambda r, j: (token(r, j), column(r, j))),
            pl.BlockSpec((part, depth), lambda r, j: (token(r, j), 0)),
            hbm,
        ],
        out_specs=[
            pl.BlockSpec(memory_space=pltpu.VMEM),
            pl.BlockSpec((slots, block, 2 * TILE), lambda r, j: (0, column(r, j), 0)),
            hbm,
        ],
        out_shape=[
            jax.ShapeDtypeStruct((rows, span, width), F32),
            jax.ShapeDtypeStruct((slots, width, 2 * TILE), BF),
            jax.ShapeDtypeStruct((CHUNKS,) + flat, BF),
        ],
        scratch_shapes=[
            pltpu.VMEM((block, depth), F32),
            pltpu.VMEM((CHUNKS,) + flat, BF),
            pltpu.VMEM((CHUNKS,) + flat, BF),
            pltpu.VMEM((CHUNKS,) + flat, BF),
            pltpu.SemaphoreType.DMA((6, CHUNKS)),
            pltpu.SemaphoreType.DMA((2,)),
        ]
        + tile_scratch(n, rows, span, w),
        compiler_params=params(mib=63, axes=2, key=3),
        cost_estimate=TINY,
        name="spread",
    )(
        a,
        w,
        x.reshape(everything, width),
        a.reshape(everything, depth),
        down.reshape((CHUNKS,) + flat),
    )
    return out, grad, total.reshape(down.shape)


def shards(
    n,
    m,
    hidden_in,
    doc_ids,
    tile_slot,
    attention_gain,
    query_gain,
    key_gain,
    attend_weight,
    output_weight,
    feed_gain,
    gate_up_slots,
    down_slots,
    out_grad,
):
    rows, span, width = hidden_in.shape
    length = doc_ids.shape[1]
    slots = gate_up_slots.shape[0]
    tokens = rows * span
    me = lax.axis_index("mp")
    offset = me * span

    kw = KVH * HD
    keys_w = attend_weight[:, QW : QW + kw].reshape(-1, KVH, HD)
    values_w = attend_weight[:, QW + kw :].reshape(-1, KVH, HD)
    attend_w = jnp.concatenate(
        [attend_weight[:, :QW], jnp.concatenate([keys_w, values_w], 2).reshape(-1, 2 * kw)], 1
    )
    starts = doc_starts(doc_ids)
    local_start = lax.dynamic_slice_in_dim(starts, offset, span, 1)
    local_pos = offset + jnp.arange(span, dtype=jnp.int32)[None] - local_start
    cos, sin = rotary_tables(local_pos.reshape(tokens))
    gq = jnp.tile(query_gain, 2)[None]
    gk = jnp.concatenate([key_gain, jnp.ones_like(key_gain)])[None]
    lane = jnp.arange(LANES) // HD
    ones = (lane[:, None] == lane[None, :]).astype(BF)
    key_block = min(512, length)
    info = jnp.stack(
        [
            jnp.full((rows,), me, jnp.int32),
            local_start[:, 0] // key_block,
            local_start[:, -1],
        ],
        1,
    ).astype(jnp.int32)
    start_col = jnp.broadcast_to(local_start[:, :, None], (rows, span, LANES))
    document = jnp.arange(LANES) % HD
    member = (doc_ids[:, :, None] == document).astype(F32)
    ka = jnp.where(document == DOCS, 1.0, member).astype(BF)
    own_member = lax.dynamic_slice_in_dim(member, offset, span, 1)
    qa = jnp.where(document == DOCS, -AWAY, own_member * AWAY).astype(BF)

    x_own = hidden_in.reshape(tokens, width)
    x_value = x_own.astype(F32)
    normed_ab, raw, q, attend_all, kv_all, output_all = project(
        n, rows, x_own, attention_gain[None], attend_w, output_weight, cos, sin, gq, gk, ones
    )
    q = q.reshape(rows, span, QW)
    kv_all = kv_all.reshape(rows, length, -1)
    output_full = output_all.reshape(QW, width)
    grad_branch, output_full = lax.optimization_barrier((out_grad.astype(BF), output_full))
    grads_all = lax.all_gather(grad_branch, "mp", axis=1, tiled=True)
    ctx, rl = attend(info, q, kv_all, start_col)
    context_b = ctx.reshape(tokens, QW)
    middle = x_value + mm(context_b, output_full)
    scale_f = rms_scale(middle)
    normed_fb = (middle * scale_f * feed_gain).astype(BF).reshape(rows, span, width)

    slot_index = me * slots + jnp.arange(slots, dtype=jnp.int32)
    live = jnp.any(tile_slot[None, :] == slot_index[:, None], axis=1).astype(F32)
    gu_t = jnp.swapaxes(gate_up_slots, 1, 2).reshape(slots * 2 * TILE, width)
    d_flat = down_slots.reshape(slots * TILE, width)
    d_t = d_flat.T
    normed_all, hidden, grad_both, grad_down = feed(
        n, live, normed_fb, grads_all, gate_up_slots, d_t
    )
    hidden = hidden.reshape(rows, n, span, -1)
    grad_normed_f, grad_gate_up, down_total = spread(
        n, m, grad_both.reshape(rows, n, span, -1), gu_t, normed_all, grad_down
    )
    gate_up_total = lax.psum(grad_gate_up, "dp")
    grad_normed_f = grad_normed_f.reshape(tokens, width)

    weighted = grad_normed_f * feed_gain
    inner = jnp.mean(weighted * middle, axis=-1, keepdims=True)
    gain_feed = jnp.sum(grad_normed_f * middle * scale_f, axis=0)
    grad_middle = out_grad.reshape(tokens, width) + scale_f * (
        weighted - middle * scale_f * scale_f * inner
    )
    grad_attn_b = grad_middle.astype(BF)
    grad_context = dg(grad_attn_b, output_full, NT).astype(BF).reshape(rows, span, QW)
    grad_output = dg(context_b, grad_attn_b, TN).astype(BF)

    dq, dkv, ffn_out = attend_back(
        n, q, kv_all, qa, ka, grad_context, ctx, rl, hidden, d_flat
    )
    layer_out = middle + ffn_out.reshape(tokens, width)
    grad_joined_b, sum_q, sum_k, output_share = unproject(
        n,
        dq.reshape(tokens, QW),
        dkv.reshape(rows, n, span, -1),
        raw,
        cos,
        sin,
        gq,
        gk,
        ones,
        grad_output.reshape(n, -1, width),
    )
    sums = jnp.concatenate(
        [
            jnp.zeros((width // LANES, LANES), F32),
            gain_feed.reshape(-1, LANES),
            sum_q[:1],
            sum_k[:1],
            jnp.zeros((GAIN_ROWS - 2 * (width // LANES) - 2, LANES), F32),
        ]
    )
    input_grad, attend_total, output_total, gains = finish(
        n,
        m,
        normed_ab,
        grad_joined_b,
        attend_all,
        x_own,
        grad_middle,
        attention_gain[None],
        output_share,
        sums,
    )
    kv_total = attend_total[:, QW:].reshape(-1, KVH, 2, HD)
    attend_total = jnp.concatenate(
        [
            attend_total[:, :QW],
            kv_total[:, :, 0].reshape(-1, kw),
            kv_total[:, :, 1].reshape(-1, kw),
        ],
        1,
    )
    gains = gains.reshape(-1)
    gain_query = gains[2 * width : 2 * width + HD] + gains[2 * width + HD : 2 * width + 2 * HD]
    gain_key = gains[2 * width + LANES : 2 * width + LANES + HD]
    shape = (rows, span, width)
    return (
        layer_out.reshape(shape),
        input_grad.reshape(shape),
        attend_total,
        output_total,
        gate_up_total.astype(F32),
        down_total.astype(F32),
        gains[:width],
        gain_query,
        gain_key,
        gains[width : 2 * width],
    )


def solution(mesh):
    placed = (
        P("dp", "mp", None),
        P("dp", None),
        P(),
        P(),
        P(),
        P(),
        P("mp", None),
        P("mp", None),
        P(),
        P("mp", None, None),
        P("mp", None, None),
        P("dp", "mp", None),
    )
    return jax.shard_map(
        functools.partial(shards, mesh.shape["mp"], mesh.shape["dp"]),
        mesh=mesh,
        in_specs=placed,
        out_specs=(
            P("dp", "mp", None),
            P("dp", "mp", None),
            P("mp", None),
            P("mp", None),
            P("mp", None, None),
            P("mp", None, None),
            P(),
            P(),
            P(),
            P(),
        ),
        check_vma=False,
    )
```

```python
import functools

import jax
import jax.numpy as jnp
from jax import lax
from jax.experimental import pallas as pl
from jax.experimental.pallas import tpu as pltpu
from jax.sharding import PartitionSpec as P

H = 20
KVH = 5
HD = 64
TILE = 128
EPSILON = 1e-06
QW = H * HD
LANES = 128
GW = (H // KVH) * HD
DOCS = 3
AWAY = 256.0
LOG2E = 1.4426950408889634
LN2 = 0.6931471805599453
BF = jnp.bfloat16
F32 = jnp.float32
MIB = 1 << 20
NT = (((1,), (1,)), ((), ()))
TN = (((0,), (0,)), ((), ()))


def params(mib=56, axes=1, key=None):
    if key is None:
        return pltpu.CompilerParams(
            vmem_limit_bytes=mib * MIB, dimension_semantics=("arbitrary",) * axes
        )
    return pltpu.CompilerParams(
        vmem_limit_bytes=mib * MIB,
        dimension_semantics=("arbitrary",) * axes if axes else None,
        collective_id=key,
        has_side_effects=True,
    )


TINY = pl.CostEstimate(flops=1, bytes_accessed=1, transcendentals=0)


def mm(a, b):
    return jnp.dot(a, b, preferred_element_type=F32)


def dg(a, b, dims):
    return lax.dot_general(a, b, dims, preferred_element_type=F32)


def doc_starts(docs):
    index = jnp.arange(docs.shape[-1], dtype=jnp.int32)
    change = jnp.concatenate(
        [jnp.ones(docs.shape[:-1] + (1,), dtype=jnp.bool_), docs[..., 1:] != docs[..., :-1]],
        axis=-1,
    )
    return lax.cummax(jnp.where(change, index, 0), axis=docs.ndim - 1)


def rotary_tables(positions):
    half_dim = HD // 2
    freqs = 1.0 / 10000.0 ** (jnp.arange(half_dim, dtype=jnp.float32) * 2.0 / HD)
    angles = positions.astype(jnp.float32)[..., None] * freqs
    return jnp.tile(jnp.cos(angles), 4), jnp.tile(jnp.sin(angles), 4)


def rms_scale(values):
    return lax.rsqrt(jnp.mean(values * values, axis=-1, keepdims=True) + EPSILON)


MESH = pl.DeviceIdType.MESH


def flip(me, k):
    bit = 1
    while bit <= k:
        if k & bit:
            me = me + bit - 2 * bit * lax.rem(lax.div(me, bit), 2)
        bit *= 2
    return me


def link_bits(n):
    return [1 << i for i in range(1, n.bit_length() - 1)]


def greet(n, me):
    barrier = pltpu.get_barrier_semaphore()
    bits = [1] + link_bits(n)
    for bit in bits:
        pl.semaphore_signal(barrier, inc=1, device_id={"mp": flip(me, bit)}, device_id_type=MESH)
    pl.semaphore_wait(barrier, len(bits))


def greet_all(n, me, m, line):
    barrier = pltpu.get_barrier_semaphore()
    bits = [1] + link_bits(n)
    for bit in bits:
        pl.semaphore_signal(barrier, inc=1, device_id={"mp": flip(me, bit)}, device_id_type=MESH)
    for step in range(1, m):
        other = lax.rem(line + step, m)
        pl.semaphore_signal(barrier, inc=1, device_id={"dp": other}, device_id_type=MESH)
    pl.semaphore_wait(barrier, len(bits) + m - 1)


class Line:
    def __init__(self, m, line, own, up, across, total, sems):
        self.own, self.up, self.across, self.total, self.sems = own, up, across, total, sems
        low = line < m // 2
        self.inner = jnp.where(low, line + 1, line - 1)
        self.outer = jnp.where(low, line - 1, line + 1)
        self.has_outer = (line > 0) & (line < m - 1)
        self.middle = (line == m // 2 - 1) | (line == m // 2)

    def copy(self, kind, c):
        src, dst, to = (
            (self.own, self.up, self.inner),
            (self.own, self.across, self.inner),
            (self.total, self.total, self.outer),
        )[kind]
        return pltpu.make_async_remote_copy(
            src_ref=src(c),
            dst_ref=dst(c),
            send_sem=self.sems.at[2 * kind, c],
            recv_sem=self.sems.at[2 * kind + 1, c],
            device_id={"dp": to},
            device_id_type=MESH,
        )

    def launch(self, c):
        @pl.when(jnp.logical_not(self.has_outer))
        def _():
            self.copy(0, c).start()

    def inward(self, c):
        @pl.when(self.has_outer)
        def _():
            self.copy(0, c).wait_recv()
            add_up(self.own(c), [self.own(c), self.up(c)])

            @pl.when(self.middle)
            def _():
                self.copy(1, c).start()

            @pl.when(jnp.logical_not(self.middle))
            def _():
                self.copy(0, c).start()

    def outward(self, c):
        @pl.when(self.middle)
        def _():
            self.copy(1, c).wait_recv()
            add_up(self.total(c), [self.own(c), self.across(c)])

        @pl.when(jnp.logical_not(self.middle))
        def _():
            self.copy(2, c).wait_recv()

        @pl.when(self.has_outer)
        def _():
            self.copy(2, c).start()

    def drain(self, c):
        @pl.when(self.middle)
        def _():
            self.copy(1, c).wait_send()

        @pl.when(jnp.logical_not(self.middle))
        def _():
            self.copy(0, c).wait_send()

        @pl.when(self.has_outer)
        def _():
            self.copy(2, c).wait_send()


class Gather:
    def __init__(self, n, me, own, slot, send, recv, relative=False):
        self.n, self.me, self.own, self.slot, self.send, self.recv = n, me, own, slot, send, recv
        self.relative = relative
        bits = link_bits(n)
        self.order = (bits + [1], bits[::-1] + [1])
        even = [(k, h) for k in range(2, n, 2) for h in (0, 1)]
        even.sort(key=lambda kh: (bin(kh[0]).count("1"), max(self.place(*kh)), kh[1]))
        self.even = even

    def place(self, k, half):
        return [i for i, bit in enumerate(self.order[half]) if k & bit]

    def copy(self, k, half, bit):
        return pltpu.make_async_remote_copy(
            src_ref=self.own(half) if k == 0 else self.here(k, half),
            dst_ref=self.slot(k ^ bit, half, k) if self.relative else self.slot(k, half),
            send_sem=self.send.at[k ^ bit, half],
            recv_sem=self.recv.at[k ^ bit, half],
            device_id={"mp": flip(self.me, bit)},
            device_id_type=MESH,
        )

    def here(self, k, half):
        return self.slot(k, half, k) if self.relative else self.slot(k, half)

    def onward(self, k, half):
        return self.order[half][(max(self.place(k, half)) + 1) if k else 0 :]

    def start(self):
        for i in range(len(self.order[0])):
            for half in (0, 1):
                self.copy(0, half, self.order[half][i]).start()

    def arrive(self, k, half):
        here = self.here(k, half)
        pltpu.make_async_remote_copy(
            src_ref=here,
            dst_ref=here,
            send_sem=self.send.at[k, half],
            recv_sem=self.recv.at[k, half],
            device_id={"mp": flip(self.me, 1)},
            device_id_type=MESH,
        ).wait_recv()

    def forward(self, k, half):
        self.arrive(k, half)
        for bit in self.onward(k, half):
            self.copy(k, half, bit).start()

    def rest(self):
        for k, half in [(1, 0), (1, 1)] + [(k + 1, h) for k, h in self.even]:
            self.arrive(k, half)

    def drain(self):
        for k in range(0, self.n, 2):
            for half in (0, 1):
                for bit in self.onward(k, half):
                    self.copy(k, half, bit).wait_send()


class Scatter:
    def __init__(self, n, me, part, core, link, sems):
        self.n, self.me, self.part = n, me, part
        self.core, self.link = core, link
        self.core_send, self.core_recv, self.link_send, self.link_recv = sems
        bits = link_bits(n)
        self.order = (bits[::-1], bits)

    def first(self, k, half):
        return next(i for i, bit in enumerate(self.order[half]) if k & bit)

    def core_copy(self, k, ref):
        return pltpu.make_async_remote_copy(
            src_ref=ref,
            dst_ref=self.core(k // 2),
            send_sem=self.core_send.at[k // 2],
            recv_sem=self.core_recv.at[k // 2],
            device_id={"mp": flip(self.me, 1)},
            device_id_type=MESH,
        )

    def link_copy(self, k, half):
        bit = self.order[half][self.first(k, half)]
        return pltpu.make_async_remote_copy(
            src_ref=self.part(self.core(k // 2), half),
            dst_ref=self.link(half, k // 2 - 1),
            send_sem=self.link_send.at[half, k // 2 - 1],
            recv_sem=self.link_recv.at[half, k // 2 - 1],
            device_id={"mp": flip(self.me, bit)},
            device_id_type=MESH,
        )

    def addends(self, k, half):
        upto = self.first(k, half) if k else len(self.order[half])
        return [k | bit for bit in self.order[half][:upto]]

    def odd(self, k, ref):
        self.core_copy(k, ref).start()

    def even(self, k, ref):
        self.core_copy(k + 1, self.core(k // 2)).wait_recv()
        for half in sorted((0, 1), key=lambda h: -len(self.addends(k, h))):
            joined = [self.part(ref, half), self.part(self.core(k // 2), half)]
            for j in self.addends(k, half):
                self.link_copy(j, half).wait_recv()
                joined.append(self.link(half, j // 2 - 1))
            add_up(joined[1], joined)
            self.link_copy(k, half).start()

    def own(self, ref, out):
        self.core_copy(1, self.core(0)).wait_recv()
        for half in (0, 1):
            joined = [self.part(ref, half), self.part(self.core(0), half)]
            for j in self.addends(0, half):
                self.link_copy(j, half).wait_recv()
                joined.append(self.link(half, j // 2 - 1))
            add_up(self.part(out, half), joined)

    def drain(self, ref):
        for k in range(1, self.n, 2):
            self.core_copy(k, ref).wait_send()
        for k in range(2, self.n, 2):
            for half in (0, 1):
                self.link_copy(k, half).wait_send()


def add_up(out, terms):
    rows = out.shape[-2]
    step = 16
    lead = (slice(None),) * (len(out.shape) - 2)

    @pl.loop(0, rows // step)
    def _(i):
        at = lead + (pl.ds(pl.multiple_of(i * step, step), step), slice(None))
        total = terms[0][at].astype(F32)
        for t in terms[1:]:
            total = total + t[at].astype(F32)
        out[at] = total.astype(out.dtype)


def scatter_scratch(n, shape, half):
    return [
        pltpu.VMEM((n // 2,) + shape, BF),
        pltpu.VMEM((2, n // 2 - 1) + half, BF),
        pltpu.SemaphoreType.DMA((n // 2,)),
        pltpu.SemaphoreType.DMA((n // 2,)),
        pltpu.SemaphoreType.DMA((2, n // 2 - 1)),
        pltpu.SemaphoreType.DMA((2, n // 2 - 1)),
    ]


def make_scatter(n, me, part, refs):
    core, link = refs[:2]
    return Scatter(
        n,
        me,
        part,
        lambda i: core.at[i],
        lambda h, i: link.at[h, i],
        refs[2:6],
    )


def half_turn(x, lane):
    first = (lane % HD) < HD // 2
    return jnp.where(first, -pltpu.roll(x, LANES - HD // 2, 1), pltpu.roll(x, HD // 2, 1))


def half_turn_back(x, lane):
    first = (lane % HD) < HD // 2
    return jnp.where(first, pltpu.roll(x, LANES - HD // 2, 1), -pltpu.roll(x, HD // 2, 1))


def group_mean(x, ones):
    high = x.astype(BF)
    low = (x - high.astype(F32)).astype(BF)
    return (mm(high, ones) + mm(low, ones)) * (1.0 / HD)


def project_kernel(
    n, x_ref, gain_ref, w_ref, o_ref, cos_ref, sin_ref, gq_ref, gk_ref, ones_ref, grad_ref,
    normed_ref, raw_ref, q_ref, branch_ref, w_out, kv_out, o_out,
    w_all, kv_own, w_send, w_recv, kv_send, kv_recv, o_send, o_recv, local,
):
    me = lax.axis_index("mp")
    depth = w_ref.shape[0]
    tokens = x_ref.shape[0]
    rows = kv_out.shape[0]
    span = tokens // rows
    half = depth // 2
    own_w = pltpu.make_async_copy(w_ref, w_all.at[me], local.at[0])
    own_w.start()
    own_o = pltpu.make_async_copy(o_ref, o_out.at[me], local.at[1 + rows])
    own_o.start()
    greet(n, me)
    wide = o_ref.shape[1] // 2
    outs = Gather(
        n,
        me,
        lambda h: o_ref.at[:, pl.ds(h * wide, wide)],
        lambda k, h: o_out.at[flip(me, k), :, pl.ds(h * wide, wide)],
        o_send,
        o_recv,
    )
    weights = Gather(
        n,
        me,
        lambda h: w_ref.at[pl.ds(h * half, half)],
        lambda k, h: w_all.at[flip(me, k), pl.ds(h * half, half)],
        w_send,
        w_recv,
    )
    weights.start()
    step = min(64, tokens)

    @pl.loop(0, tokens // step)
    def _(i):
        at = pl.ds(pl.multiple_of(i * step, step), step)
        x = x_ref[at, :].astype(F32)
        scale = lax.rsqrt(jnp.mean(x * x, axis=-1, keepdims=True) + EPSILON)
        normed_ref[at, :] = (x * scale * gain_ref[...]).astype(BF)
        branch_ref[at, :] = grad_ref[at, :].astype(BF)

    chunk = min(256, tokens)

    def accumulate(k, fresh):
        block = flip(me, k)
        columns = pl.ds(pl.multiple_of(block * depth, depth), depth)

        @pl.loop(0, tokens // chunk)
        def _(i):
            at = pl.ds(pl.multiple_of(i * chunk, chunk), chunk)
            term = mm(normed_ref[at, columns], w_all[block])
            raw_ref[at, :] = term if fresh else raw_ref[at, :] + term

    own_w.wait()
    accumulate(0, True)
    for h in (0, 1):
        weights.arrive(1, h)
    accumulate(1, False)
    for i, (k, h) in enumerate(weights.even):
        weights.forward(k, h)
        if any(k == other for other, _ in weights.even[:i]):
            accumulate(k, False)
    outs.start()
    for k in range(3, n, 2):
        for h in (0, 1):
            weights.arrive(k, h)
        accumulate(k, False)
    out_w = pltpu.make_async_copy(w_all, w_out, local.at[0])
    out_w.start()

    chunk = min(128, tokens)
    lane = lax.broadcasted_iota(jnp.int32, (chunk, LANES), 1)

    def finish(i, tiles):
        at = pl.ds(pl.multiple_of(i * chunk, chunk), chunk)
        cos, sin = cos_ref[at, :], sin_ref[at, :]
        for tile in tiles:
            lanes = slice(tile * LANES, (tile + 1) * LANES)
            x = raw_ref[at, lanes]
            query = tile < QW // LANES
            scale = lax.rsqrt(group_mean(x * x, ones_ref[...]) + EPSILON)
            v = x * scale * (gq_ref[...] if query else gk_ref[...])
            y = v * cos + half_turn(v, lane) * sin
            if query:
                q_ref[at, lanes] = (y * (HD**-0.5 * LOG2E)).astype(BF)
            else:
                mine = slice(tile * LANES - QW, (tile + 1) * LANES - QW)
                kv_own[at, mine] = jnp.where(lane < HD, y, x).astype(BF)

    count = raw_ref.shape[1] // LANES

    @pl.loop(0, tokens // chunk)
    def _(i):
        finish(i, range(QW // LANES, count))

    both = rows // 2
    keep = [
        pltpu.make_async_copy(
            kv_own.at[pl.ds(r * span, span)], kv_out.at[r, me], local.at[1 + r]
        )
        for r in range(rows)
    ]
    for c in keep:
        c.start()
    kvs = Gather(
        n,
        me,
        lambda h: kv_own.at[pl.ds(h * span, span)],
        lambda k, h: kv_out.at[h, flip(me, k)],
        kv_send,
        kv_recv,
    )
    kvs.start()

    @pl.loop(0, tokens // chunk)
    def _(i):
        finish(i, range(QW // LANES))

    for k, h in kvs.even:
        outs.forward(k, h)
        kvs.forward(k, h)
    outs.rest()
    kvs.rest()
    for c in keep:
        c.wait()
    out_w.wait()
    own_o.wait()
    weights.drain()
    outs.drain()
    kvs.drain()


def project(n, rows, x, gain, w, o, cos, sin, gq, gk, ones, grad):
    tokens, width = x.shape
    depth, columns = w.shape
    vmem = pl.BlockSpec(memory_space=pltpu.VMEM)
    hbm = pl.BlockSpec(memory_space=pl.ANY)
    kvw = columns - QW
    return pl.pallas_call(
        functools.partial(project_kernel, n),
        in_specs=[vmem, vmem, hbm, hbm, vmem, vmem, vmem, vmem, vmem, vmem],
        out_specs=[vmem, vmem, vmem, vmem, hbm, hbm, hbm],
        out_shape=[
            jax.ShapeDtypeStruct((tokens, width), BF),
            jax.ShapeDtypeStruct((tokens, columns), F32),
            jax.ShapeDtypeStruct((tokens, QW), BF),
            jax.ShapeDtypeStruct((tokens, width), BF),
            jax.ShapeDtypeStruct((n, depth, columns), BF),
            jax.ShapeDtypeStruct((rows, n, tokens // rows, kvw), BF),
            jax.ShapeDtypeStruct((n,) + o.shape, BF),
        ],
        scratch_shapes=[
            pltpu.VMEM((n, depth, columns), BF),
            pltpu.VMEM((tokens, kvw), BF),
            pltpu.SemaphoreType.DMA((n, 2)),
            pltpu.SemaphoreType.DMA((n, 2)),
            pltpu.SemaphoreType.DMA((n, 2)),
            pltpu.SemaphoreType.DMA((n, 2)),
            pltpu.SemaphoreType.DMA((n, 2)),
            pltpu.SemaphoreType.DMA((n, 2)),
            pltpu.SemaphoreType.DMA((2 + rows,)),
        ],
        compiler_params=params(axes=0, key=0),
        name="project",
    )(x, gain, w, o, cos, sin, gq, gk, ones, grad)


def unproject_kernel(
    n, dq_ref, dkv_ref, raw_ref, cos_ref, sin_ref, gq_ref, gk_ref, ones_ref, down_ref,
    gj_ref, sq_ref, sk_ref, wide_ref,
    dkv_own, *scratch,
):
    me = lax.axis_index("mp")
    greet(n, me)
    tokens = dq_ref.shape[0]
    rows = dkv_ref.shape[0]
    span = tokens // rows
    columns = raw_ref.shape[1]
    keys = make_scatter(n, me, lambda ref, h: ref.at[h], scratch[:6])

    def dkv_term(k):
        return dkv_ref.at[:, flip(me, k)]

    for k in range(n - 1, 0, -2):
        keys.odd(k, dkv_term(k))
    keys.even(n - 2, dkv_term(n - 2))

    chunk = min(128, tokens)
    lane = lax.broadcasted_iota(jnp.int32, (chunk, LANES), 1)
    sq_ref[...] = jnp.zeros_like(sq_ref)
    sk_ref[...] = jnp.zeros_like(sk_ref)

    def back(i, tiles, query):
        at = pl.ds(pl.multiple_of(i * chunk, chunk), chunk)
        cos, sin = cos_ref[at, :], sin_ref[at, :]
        total = 0.0
        for tile in tiles:
            lanes = slice(tile * LANES, (tile + 1) * LANES)
            x = raw_ref[at, lanes]
            if query:
                e = dq_ref[at, lanes]
            else:
                per = span // chunk
                here = pl.ds(pl.multiple_of(lax.rem(i, per) * chunk, chunk), chunk)
                e = dkv_own[lax.div(i, per), here, slice(tile * LANES - QW, (tile + 1) * LANES - QW)]
            scale = lax.rsqrt(group_mean(x * x, ones_ref[...]) + EPSILON)
            v = x * scale
            turned = e * cos + half_turn_back(e * sin, lane)
            u = turned * (gq_ref[...] if query else gk_ref[...])
            grad = scale * (u - v * group_mean(u * v, ones_ref[...]))
            gj_ref[at, lanes] = (grad if query else jnp.where(lane < HD, grad, e)).astype(BF)
            total = total + jnp.sum(turned * v, axis=0, keepdims=True)
        sums = sq_ref if query else sk_ref
        sums[...] += jnp.broadcast_to(total, sums.shape)

    count = columns // LANES

    parts = tokens // chunk
    left = list(range(n - 4, 0, -2))
    for i in range(parts):
        back(i, range(QW // LANES), True)
        if i == 0:
            for k in left:
                keys.even(k, dkv_term(k))

    wide_ref[...] = down_ref[...].astype(F32)
    keys.own(dkv_term(0), dkv_own)

    @pl.loop(0, tokens // chunk)
    def _(i):
        back(i, range(QW // LANES, count), False)

    keys.drain(dkv_term(0))


def unproject(n, dq, dkv, raw, cos, sin, gq, gk, ones, down):
    tokens, columns = raw.shape
    rows = dkv.shape[0]
    span = tokens // rows
    kvw = columns - QW
    vmem = pl.BlockSpec(memory_space=pltpu.VMEM)
    return pl.pallas_call(
        functools.partial(unproject_kernel, n),
        in_specs=[vmem] * 9,
        out_specs=[vmem] * 4,
        out_shape=[
            jax.ShapeDtypeStruct((tokens, columns), BF),
            jax.ShapeDtypeStruct((8, LANES), F32),
            jax.ShapeDtypeStruct((8, LANES), F32),
            jax.ShapeDtypeStruct(down.shape, F32),
        ],
        scratch_shapes=[pltpu.VMEM((rows, span, kvw), F32)]
        + scatter_scratch(n, (rows, span, kvw), (span, kvw)),
        compiler_params=params(mib=60, axes=0, key=2),
        cost_estimate=TINY,
        name="unproject",
    )(dq, dkv, raw, cos, sin, gq, gk, ones, down)


GAIN_ROWS = 40


def finish_kernel(
    n, m, normed_ref, gj_ref, w_any, x_ref, mid_any, gain_ref, gout_any, sums_ref,
    grad_ref, attend_ref, out_ref, gains_ref,
    w_ref, term, error, mid_ref, gout_ref, own_w, up_w, across_w, own_o, up_o, across_o, landed,
    sem_w, sem_o, sem_g, load, *scratch,
):
    me, line = lax.axis_index("mp"), lax.axis_index("dp")
    depth = w_ref.shape[1]
    tokens, width = x_ref.shape
    pieces, piece = own_w.shape[0], own_w.shape[1]
    o_pieces, o_piece = own_o.shape[0], own_o.shape[1]
    chunk = error.shape[0]
    fetch = [pltpu.make_async_copy(w_any, w_ref, load.at[0])]
    fetch += [
        pltpu.make_async_copy(gout_any.at[flip(me, k)], gout_ref.at[k // 2], load.at[2 + k // 2])
        for k in range(0, n, 2)
    ]
    for c in fetch:
        c.start()

    def bring(i):
        here = pl.ds(pl.multiple_of(i * chunk, chunk), chunk)
        return pltpu.make_async_copy(mid_any.at[here], mid_ref, load.at[1])

    bring(0).start()
    greet_all(n, me, m, line)
    half, half_w = depth // 2, width // 2
    sums = make_scatter(n, me, lambda ref, h: ref.at[pl.ds(h * half, half)], scratch[:6])
    outs = make_scatter(n, me, lambda ref, h: ref.at[:, pl.ds(h * half_w, half_w)], scratch[6:])
    at = lambda ref: lambda c: ref.at[c]
    weights = Line(m, line, at(own_w), at(up_w), at(across_w), at(up_w), sem_w)
    out_line = Line(m, line, at(own_o), at(up_o), at(across_o), at(up_o), sem_o)
    gains_ref[...] = sums_ref[...]

    def tokens_part(i):
        here = pl.ds(pl.multiple_of(i * chunk, chunk), chunk)
        for b in range(n):
            error[:, b * depth : (b + 1) * depth] = dg(gj_ref[here, :], w_ref[b], NT)
        small = min(32, chunk)
        bring(i).wait()

        @pl.loop(0, chunk // small)
        def _(s):
            part = pl.ds(pl.multiple_of(s * small, small), small)
            rows = pl.ds(pl.multiple_of(i * chunk + s * small, small), small)
            e = error[part, :]
            x = x_ref[rows, :].astype(F32)
            scale = lax.rsqrt(jnp.mean(x * x, axis=-1, keepdims=True) + EPSILON)
            u = e * gain_ref[...]
            v = x * scale
            inner = jnp.mean(u * v, axis=-1, keepdims=True)
            grad_ref[rows, :] = mid_ref[part, :] + scale * (u - v * inner)
            total = jnp.sum(e * v, axis=0, keepdims=True)
            for b in range(width // LANES):
                gains_ref[b : b + 1, :] += total[:, b * LANES : (b + 1) * LANES]

        if i + 1 < tokens // chunk:
            bring(i + 1).start()

    def mine(k):
        return term.at[k // 2 if k % 2 else n // 2]

    def weight_part(k):
        columns = pl.ds(pl.multiple_of(flip(me, k) * depth, depth), depth)
        mine(k)[...] = dg(normed_ref[:, columns], gj_ref[...], TN).astype(BF)

    steps = [("mp", flip(me, 1 << i)) for i in range(n.bit_length() - 1)]
    steps += [("dp", flip(line, 1 << i)) for i in range(m.bit_length() - 1)]

    def exchange(i):
        axis, to = steps[i]
        return pltpu.make_async_remote_copy(
            src_ref=landed.at[2 * i],
            dst_ref=landed.at[2 * i + 1],
            send_sem=sem_g.at[0, i],
            recv_sem=sem_g.at[1, i],
            device_id={axis: to},
            device_id_type=MESH,
        )

    for k in range(n - 1, 0, -2):
        weight_part(k)
        sums.odd(k, mine(k))
        if k == n - 1:
            weight_part(n - 2)
            sums.even(n - 2, mine(n - 2))
    for c in fetch:
        c.wait()
    tokens_part(0)
    for k in range(n - 4, 0, -2):
        weight_part(k)
        sums.even(k, mine(k))
    weight_part(0)
    for i in range(1, tokens // chunk):
        tokens_part(i)
    for i in range(len(steps)):
        landed[2 * i] = gains_ref[...]
        exchange(i).start()
        exchange(i).wait_recv()
        gains_ref[...] = landed[2 * i] + landed[2 * i + 1]
    sums.own(mine(0), attend_ref)
    for c in range(pieces):
        own_w[c] = attend_ref[c * piece : (c + 1) * piece, :].astype(BF)
        weights.launch(c)

    def out_term(k):
        return gout_any.at[flip(me, k)] if k % 2 else gout_ref.at[k // 2]

    for k in range(n - 1, 0, -2):
        outs.odd(k, out_term(k))
    todo = list(range(n - 2, 0, -2))
    ahead = 2
    for c in range(pieces + ahead):
        if c < pieces:
            weights.inward(c)
        if c >= ahead:
            weights.outward(c - ahead)
        if todo:
            k = todo.pop(0)
            outs.even(k, out_term(k))
    for k in todo:
        outs.even(k, out_term(k))
    outs.own(out_term(0), out_ref)
    for c in range(o_pieces):
        own_o[c] = out_ref[c * o_piece : (c + 1) * o_piece, :].astype(BF)
        out_line.launch(c)
    kw = KVH * HD

    def widen(c):
        rows = slice(c * piece, (c + 1) * piece)
        attend_ref[rows, :QW] = up_w[c, :, :QW].astype(F32)
        for h in range(KVH):
            both = up_w[c, :, QW + 2 * h * HD : QW + 2 * (h + 1) * HD].astype(F32)
            attend_ref[rows, QW + h * HD : QW + (h + 1) * HD] = both[:, :HD]
            attend_ref[rows, QW + kw + h * HD : QW + kw + (h + 1) * HD] = both[:, HD:]

    for c in range(max(o_pieces + ahead, pieces)):
        if c < o_pieces:
            out_line.inward(c)
        if c < pieces:
            widen(c)
        if ahead <= c < o_pieces + ahead:
            out_line.outward(c - ahead)
    for c in range(o_pieces):
        out_ref[c * o_piece : (c + 1) * o_piece, :] = up_o[c].astype(F32)
        out_line.drain(c)
    for c in range(pieces):
        weights.drain(c)
    for i in range(len(steps)):
        exchange(i).wait_send()
    sums.drain(mine(0))
    outs.drain(out_term(0))


def finish(n, m, normed, gj, w, x, middle, gain, gout, sums):
    tokens, width = x.shape
    columns = gj.shape[1]
    depth = width // n
    share = gout.shape[1]
    pieces, o_pieces = 8, 5
    chunk = min(256, tokens)
    vmem = pl.BlockSpec(memory_space=pltpu.VMEM)
    hbm = pl.BlockSpec(memory_space=pl.ANY)
    steps = n.bit_length() + m.bit_length() - 2
    return pl.pallas_call(
        functools.partial(finish_kernel, n, m),
        in_specs=[vmem, vmem, hbm, vmem, hbm, vmem, hbm, vmem],
        out_specs=[vmem] * 4,
        out_shape=[
            jax.ShapeDtypeStruct((tokens, width), F32),
            jax.ShapeDtypeStruct((depth, columns), F32),
            jax.ShapeDtypeStruct((share, width), F32),
            jax.ShapeDtypeStruct((GAIN_ROWS, LANES), F32),
        ],
        scratch_shapes=[
            pltpu.VMEM(w.shape, BF),
            pltpu.VMEM((n // 2 + 1, depth, columns), BF),
            pltpu.VMEM((chunk, width), F32),
            pltpu.VMEM((chunk, width), F32),
            pltpu.VMEM((n // 2, share, width), BF),
        ]
        + [pltpu.VMEM((pieces, depth // pieces, columns), BF)] * 3
        + [pltpu.VMEM((o_pieces, share // o_pieces, width), BF)] * 3
        + [
            pltpu.VMEM((2 * steps, GAIN_ROWS, LANES), F32),
            pltpu.SemaphoreType.DMA((6, pieces)),
            pltpu.SemaphoreType.DMA((6, o_pieces)),
            pltpu.SemaphoreType.DMA((2, steps)),
            pltpu.SemaphoreType.DMA((2 + n // 2,)),
        ]
        + scatter_scratch(n, (depth, columns), (depth // 2, columns))
        + scatter_scratch(n, (share, width), (share, width // 2)),
        compiler_params=params(mib=60, axes=0, key=5),
        cost_estimate=TINY,
        name="finish",
    )(normed, gj, w, x, middle, gain, gout, sums)


def key_positions(shape, axis, group, per, span):
    return group * per * span + lax.broadcasted_iota(jnp.int32, shape, axis)


def attend_kernel(keys, info, q_ref, kv_ref, start_ref, ctx_ref, rl_ref, acc):
    span = q_ref.shape[1]
    per = keys // span
    row = pl.program_id(0)
    me, first, last_start = info[row, 0], info[row, 1], info[row, 2]
    low_q = lax.broadcasted_iota(jnp.int32, (span, LANES), 1) < HD
    low_k = lax.broadcasted_iota(jnp.int32, (keys, LANES), 1) < HD
    one = jnp.ones((keys, LANES), BF)
    none = jnp.zeros((span, LANES), BF)
    queries = []
    for h in range(GW // HD):
        pair = q_ref[0, :, (h // 2) * LANES : (h // 2 + 1) * LANES]
        queries.append(jnp.where(low_q, pair, none) if h % 2 == 0 else jnp.where(low_q, none, pair))
    acc[...] = jnp.zeros_like(acc)

    def block(g, masked):
        group = g
        kv = kv_ref[0, pl.ds(pl.multiple_of(group * keys, keys), keys), :]
        vk = jnp.concatenate([kv[:, HD:], kv[:, :HD]], axis=1)
        key_sides = (kv, vk)
        value_sides = (jnp.where(low_k, vk, one), jnp.where(low_k, one, kv))
        if masked:
            position = key_positions((span, keys), 1, group, per, span)
            own = me * span + lax.broadcasted_iota(jnp.int32, (span, keys), 0)
            seen = (position <= own) & (position >= start_ref[0][:, :1])
        for h in range(GW // HD):
            p = jnp.exp2(dg(queries[h], key_sides[h % 2], NT))
            if masked:
                p = jnp.where(seen, p, 0.0)
            acc[h] += mm(p.astype(BF), value_sides[h % 2])

    def step(g, carry):
        edge = (g == me // per) | (g * keys < last_start)
        pl.when(edge)(lambda: block(g, True))
        pl.when(jnp.logical_not(edge))(lambda: block(g, False))
        return carry

    lax.fori_loop(first, me // per + 1, step, 0)
    for pair in range(GW // LANES):
        even, odd = acc[2 * pair], acc[2 * pair + 1]
        total = jnp.where(low_q, pltpu.roll(even, HD, 1), pltpu.roll(odd, HD, 1))
        inverse = 1.0 / total
        lanes = slice(pair * LANES, (pair + 1) * LANES)
        ctx_ref[0, :, lanes] = (jnp.where(low_q, even, odd) * inverse).astype(BF)
        rl_ref[0, :, lanes] = inverse


def attend(info, q, kv, start):
    rows, span, _ = q.shape
    length = kv.shape[1]
    keys = min(512, length)
    own = lambda r, h, info: (r, 0, h)
    spec = pltpu.PrefetchScalarGridSpec(
        num_scalar_prefetch=1,
        grid=(rows, KVH),
        in_specs=[
            pl.BlockSpec((1, span, GW), own),
            pl.BlockSpec((1, length, LANES), own),
            pl.BlockSpec((1, span, LANES), lambda r, h, info: (r, 0, 0)),
        ],
        out_specs=[pl.BlockSpec((1, span, GW), own), pl.BlockSpec((1, span, GW), own)],
        scratch_shapes=[pltpu.VMEM((GW // HD, span, LANES), F32)],
    )
    return pl.pallas_call(
        functools.partial(attend_kernel, keys),
        grid_spec=spec,
        out_shape=[jax.ShapeDtypeStruct(q.shape, BF), jax.ShapeDtypeStruct(q.shape, F32)],
        compiler_params=params(axes=2),
        cost_estimate=pl.CostEstimate(
            flops=16 * rows * H * span * length * HD,
            bytes_accessed=rows * (length * 1280 + span * QW * 8),
            transcendentals=rows * H * span * length,
        ),
        name="attend",
    )(info, q, kv, start)


def attend_back_kernel(
    keys, n, q_ref, kv_ref, qa_ref, ka_ref, do_ref, ctx_ref, rl_ref, a_ref, w_any, base_any,
    dq_ref, dkv_ref, o_ref, acc, sides, *scratch,
):
    span = q_ref.shape[1]
    per = keys // span
    length = kv_ref.shape[1]
    me = lax.axis_index("mp")
    rows = o_ref.shape[0]
    now = pl.program_id(0) * KVH + pl.program_id(1)
    sums = TileSum(n, me, o_ref, w_any, scratch, base_any)
    batch = a_ref.shape[1]
    steps = rows * n // batch

    @pl.when(now == 0)
    def _():
        sums.start()

    @pl.when(now < steps)
    def _():
        @pl.loop(0, batch)
        def _(i):
            tile = now * batch + i
            _, slot = tile_at(tile, n)
            sums.step(tile, a_ref.at[0, lax.rem(xor_of(me, slot, n), batch)])

    lane = lax.broadcasted_iota(jnp.int32, (span, LANES), 1)
    low_q = lane < HD
    low_k = lax.broadcasted_iota(jnp.int32, (keys, LANES), 1) < HD
    one = jnp.ones((keys, LANES), BF)
    for h in range(GW // HD):
        lanes = slice((h // 2) * LANES, (h // 2 + 1) * LANES)
        mine = low_q if h % 2 == 0 else jnp.logical_not(low_q)
        scaled = do_ref[0, :, lanes].astype(F32) * rl_ref[0, :, lanes]
        own = jnp.where(mine, scaled, 0.0)
        delta = -jnp.sum(own * ctx_ref[0, :, lanes].astype(F32), axis=1, keepdims=True)
        one_part = delta.astype(BF).astype(F32)
        two_part = (delta - one_part).astype(BF).astype(F32)
        three_part = delta - one_part - two_part
        base = HD if h % 2 == 0 else 0
        extra = jnp.where(
            lane == base,
            one_part,
            jnp.where(lane == base + 1, two_part, jnp.where(lane == base + 2, three_part, 0.0)),
        )
        query = q_ref[0, :, lanes].astype(F32)
        sides[0, h] = jnp.where(mine, query, 0.0).astype(BF)
        sides[1, h] = own.astype(BF)
        sides[2, h] = jnp.where(mine, scaled, extra).astype(BF)
        sides[3, h] = jnp.where(mine, query, qa_ref[0].astype(F32)).astype(BF)
    acc[...] = jnp.zeros_like(acc)

    def block(g, masked):
        here = pl.ds(pl.multiple_of(g * keys, keys), keys)
        kv = kv_ref[0, here, :]
        ka = ka_ref[0, here, :]
        vk = jnp.concatenate([kv[:, HD:], kv[:, :HD]], axis=1)
        key_sides = (jnp.where(low_k, kv, ka), jnp.where(low_k, ka, vk))
        value_sides = (jnp.where(low_k, vk, one), jnp.where(low_k, one, kv))
        if masked:
            position = g * keys + lax.broadcasted_iota(jnp.int32, (keys, span), 0)
            seen = position <= me * span + lax.broadcasted_iota(jnp.int32, (keys, span), 1)
        grad_key = grad_value = 0.0
        for h in range(GW // HD):
            e = jnp.exp2(dg(key_sides[h % 2], sides[3, h], NT))
            if masked:
                e = jnp.where(seen, e, 0.0)
            ds = (e * dg(value_sides[h % 2], sides[2, h], NT)).astype(BF)
            grad_value = grad_value + mm(e.astype(BF), sides[1, h])
            grad_key = grad_key + mm(ds, sides[0, h])
            acc[h] += dg(ds, key_sides[h % 2], TN)
        grad_key = (grad_key + pltpu.roll(grad_key, HD, 1)) * LN2
        grad_value = grad_value + pltpu.roll(grad_value, HD, 1)
        dkv_ref[0, here, :] = jnp.where(low_k, grad_key, grad_value).astype(BF)

    last = lax.div(me, per)

    @pl.loop(0, last)
    def _(g):
        block(g, False)

    block(last, True)

    @pl.loop(last + 1, length // keys)
    def _(g):
        dkv_ref[0, pl.ds(pl.multiple_of(g * keys, keys), keys), :] = jnp.zeros((keys, LANES), BF)

    for pair in range(GW // LANES):
        lanes = slice(pair * LANES, (pair + 1) * LANES)
        dq_ref[0, :, lanes] = jnp.where(low_q, acc[2 * pair], acc[2 * pair + 1]) * (HD**-0.5)

    @pl.when(now == rows * KVH - 1)
    def _():
        sums.end()


def attend_back(n, q, kv, qa, ka, do, ctx, rl, a, w, base):
    rows, span, _ = q.shape
    length = kv.shape[1]
    keys = min(512, length)
    depth, width = w.shape
    batch = n // 4
    own = lambda r, h: (r, 0, h)

    def place(r, h):
        row, slot = tile_at(jnp.minimum(r * KVH + h, rows * n // batch - 1) * batch, n)
        return (row, lax.div(xor_of(lax.axis_index("mp"), slot, n), batch), 0, 0)

    return pl.pallas_call(
        functools.partial(attend_back_kernel, keys, n),
        grid=(rows, KVH),
        in_specs=[
            pl.BlockSpec((1, span, GW), own),
            pl.BlockSpec((1, length, LANES), own),
            pl.BlockSpec((1, span, LANES), lambda r, h: (r, 0, 0)),
            pl.BlockSpec((1, length, LANES), lambda r, h: (r, 0, 0)),
            pl.BlockSpec((1, span, GW), own),
            pl.BlockSpec((1, span, GW), own),
            pl.BlockSpec((1, span, GW), own),
            pl.BlockSpec((1, batch, span, depth), place),
            pl.BlockSpec(memory_space=pl.ANY),
            pl.BlockSpec(memory_space=pl.ANY),
        ],
        out_specs=[
            pl.BlockSpec((1, span, GW), own),
            pl.BlockSpec((1, length, LANES), own),
            pl.BlockSpec(memory_space=pltpu.VMEM),
        ],
        out_shape=[
            jax.ShapeDtypeStruct(q.shape, F32),
            jax.ShapeDtypeStruct(kv.shape, BF),
            jax.ShapeDtypeStruct((rows, span, width), F32),
        ],
        scratch_shapes=[
            pltpu.VMEM((GW // HD, span, LANES), F32),
            pltpu.VMEM((4, GW // HD, span, LANES), BF),
        ]
        + tile_scratch(n, rows, span, w),
        compiler_params=params(mib=60, axes=2, key=4),
        cost_estimate=TINY,
        name="attend_back",
    )(q, kv, qa, ka, do, ctx, rl, a, w, base)


def xor_of(a, b, n):
    total, bit = 0, 1
    while bit < n:
        total = total + bit * lax.rem(lax.div(a, bit) + lax.div(b, bit), 2)
        bit *= 2
    return total


def feed_kernel(
    n, live_ref, x_own, g_ref, gu_any, dt_any,
    x_all, hid_ref, dgu_ref, gd_any,
    x_vm, gu_ref, dt_ref, d_sum, out_d, x_send, x_recv, loads, stores, keep,
):
    me = lax.axis_index("mp")
    rows, span, width = x_own.shape
    slots = gu_ref.shape[0]
    r, p = pl.program_id(0), pl.program_id(1)
    pairs = n // 2
    now = r * pairs + p
    half = span // 2

    def gather(row):
        def slot(i, h, k):
            at = lax.rem(flip(me, k), 2) * span + h * half
            return x_vm.at[row, i // 2, pl.ds(pl.multiple_of(at, half), half)]

        return Gather(
            n,
            me,
            lambda h: x_own.at[row, pl.ds(h * half, half)],
            slot,
            x_send.at[row],
            x_recv.at[row],
            True,
        )

    def own_copy(row):
        at = pl.ds(pl.multiple_of(lax.rem(me, 2) * span, span), span)
        return pltpu.make_async_copy(x_own.at[row], x_vm.at[row, 0, at], loads.at[2 + row])

    fetch = [
        pltpu.make_async_copy(gu_any, gu_ref, loads.at[0]),
        pltpu.make_async_copy(dt_any, dt_ref, loads.at[1]),
    ]

    def events(row, upto):
        todo = gather(row).even
        ends = [0] * pairs
        for i in range(1, pairs):
            ends[i] = max(ends[i - 1], 1 + max(j for j, e in enumerate(todo) if e[0] == 2 * i))
        return todo[ends[upto - 1] if upto else 0 : ends[upto]]

    @pl.when(now == 0)
    def _():
        for row in range(rows):
            own_copy(row).start()
        for c in fetch:
            c.start()
        greet(n, me)
        gather(0).start()
        d_sum[...] = jnp.zeros_like(d_sum)
        own_copy(0).wait()
        for c in fetch:
            c.wait()

    for row in range(rows):
        for i in range(pairs):

            @pl.when(now == row * pairs + i)
            def _(row=row, i=i):
                if i == 0 and row:
                    own_copy(row).wait()
                for j, e in enumerate(events(row, i)):
                    gather(row).forward(*e)
                    if row + 1 < rows and i == 1 and j == 1:
                        gather(row + 1).start()
                for h in (0, 1):
                    gather(row).arrive(2 * i + 1, h)

    def save(row, i):
        block = lax.div(xor_of(me, 2 * i, n), 2)
        return pltpu.make_async_copy(x_vm.at[row, i], x_all.at[row, block], keep.at[row, i])

    save(r, p).start()
    x = x_vm.at[r, p]
    grad = mm(g_ref[0, 0], dt_ref[...])
    for t in range(slots):
        both = mm(x[...], gu_ref[t])
        gate, upper = both[:, :TILE], both[:, TILE:]
        live = live_ref[t]
        sig = jax.nn.sigmoid(gate)
        silu = gate * sig
        gh = grad[:, t * TILE : (t + 1) * TILE] * live
        hid_ref[0, 0, :, t * TILE : (t + 1) * TILE] = (silu * upper * live).astype(BF)
        dgu_ref[0, 0, :, 2 * t * TILE : (2 * t + 1) * TILE] = (
            gh * upper * (sig * (1.0 + gate * (1.0 - sig)))
        ).astype(BF)
        dgu_ref[0, 0, :, (2 * t + 1) * TILE : (2 * t + 2) * TILE] = (gh * silu).astype(BF)

    cut = LANES

    @pl.loop(0, slots * TILE // cut)
    def _(i):
        at = pl.ds(pl.multiple_of(i * cut, cut), cut)
        d_sum[at, :] += dg(hid_ref[0, 0, :, at], g_ref[0, 0], TN)

    @pl.when(now == rows * pairs - 1)
    def _():
        def store(t):
            return pltpu.make_async_copy(out_d.at[t % 2], gd_any.at[t], stores.at[t % 2])

        for t in range(slots):
            if t > 1:
                store(t - 2).wait()
            out_d[t % 2] = d_sum[t * TILE : (t + 1) * TILE, :].astype(BF)
            store(t).start()
        for t in range(max(slots - 2, 0), slots):
            store(t).wait()
        for row in range(rows):
            for i in range(pairs):
                save(row, i).wait()
        for row in range(rows):
            gather(row).drain()


def feed(n, live, x, g, gu, dt):
    rows, span, width = x.shape
    slots = gu.shape[0]
    hbm = pl.BlockSpec(memory_space=pl.ANY)
    pairs = n // 2

    def place(r, p):
        return (r, lax.div(xor_of(lax.axis_index("mp"), 2 * p, n), 2), 0, 0)

    return pl.pallas_call(
        functools.partial(feed_kernel, n),
        grid=(rows, pairs),
        in_specs=[
            pl.BlockSpec(memory_space=pltpu.SMEM),
            hbm,
            pl.BlockSpec((1, 1, 2 * span, width), place),
            hbm,
            hbm,
        ],
        out_specs=[
            hbm,
            pl.BlockSpec((1, 1, 2 * span, slots * TILE), place),
            pl.BlockSpec((1, 1, 2 * span, 2 * slots * TILE), place),
            hbm,
        ],
        out_shape=[
            jax.ShapeDtypeStruct((rows, pairs, 2 * span, width), BF),
            jax.ShapeDtypeStruct((rows, pairs, 2 * span, slots * TILE), BF),
            jax.ShapeDtypeStruct((rows, pairs, 2 * span, 2 * slots * TILE), BF),
            jax.ShapeDtypeStruct((slots, TILE, width), BF),
        ],
        scratch_shapes=[
            pltpu.VMEM((rows, pairs, 2 * span, width), BF),
            pltpu.VMEM(gu.shape, BF),
            pltpu.VMEM(dt.shape, BF),
            pltpu.VMEM((slots * TILE, width), F32),
            pltpu.VMEM((2, TILE, width), BF),
            pltpu.SemaphoreType.DMA((rows, n, 2)),
            pltpu.SemaphoreType.DMA((rows, n, 2)),
            pltpu.SemaphoreType.DMA((2 + rows,)),
            pltpu.SemaphoreType.DMA((2,)),
            pltpu.SemaphoreType.DMA((rows, pairs)),
        ],
        compiler_params=params(mib=62, axes=2, key=1),
        cost_estimate=pl.CostEstimate(
            flops=2 * 6 * rows * n * span * slots * TILE * width,
            bytes_accessed=6 * rows * n * span * width + 6 * slots * TILE * width,
            transcendentals=rows * n * span * slots * TILE,
        ),
        name="feed",
    )(live, x, g.reshape(rows, pairs, 2 * span, width), gu, dt)


def pick(index, table):
    total = 0
    for i, v in enumerate(table):
        total = total + v * jnp.where(index == i, 1, 0)
    return total


def tile_at(now, n):
    unit = n // 4
    at = lax.div(now, unit)
    row = pick(at, (0, 1, 0, 0, 1, 1, 0, 1))
    return row, pick(at, (3, 3, 2, 1, 2, 1, 0, 0)) * unit + unit - 1 - lax.rem(now, unit)


class TileSum:
    def __init__(self, n, me, o_ref, w_any, scratch, base=None):
        self.n, self.me, self.o_ref, self.w_any, self.base = n, me, o_ref, w_any, base
        self.w_ref, self.terms, self.core, self.link = scratch[:4]
        self.sems, self.load = scratch[4:8], scratch[8]
        self.rows, self.span, _ = o_ref.shape

    def scatter(self, row):
        half = self.span // 2
        return Scatter(
            self.n,
            self.me,
            lambda ref, h: ref.at[pl.ds(h * half, half)],
            lambda i: self.core.at[row, i],
            lambda h, i: self.link.at[row, h, i],
            tuple(s.at[row] for s in self.sems),
        )

    def start(self, meet=greet):
        fetch = [pltpu.make_async_copy(self.w_any, self.w_ref, self.load.at[0])]
        if self.base is not None:
            fetch.append(pltpu.make_async_copy(self.base, self.o_ref, self.load.at[1]))
        for c in fetch:
            c.start()
        meet(self.n, self.me)
        for c in fetch:
            c.wait()

    def close(self, row):
        last = self.scatter(row)
        for h in (0, 1):
            here = last.part(self.o_ref.at[row], h)
            joined = [here]
            for i in last.addends(0, h):
                last.link_copy(i, h).wait_recv()
                joined.append(last.link(h, i // 2 - 1))
            add_up(here, joined)

    def step(self, now, a_ref):
        n, terms = self.n, self.terms
        r, k = tile_at(now, n)

        @pl.when(now == 2 * n - n // 4)
        def _():
            self.close(0)

        for i in range(1, n, 2):

            @pl.when((r > 0) & (k == i))
            def _(i=i):
                self.scatter(r - 1).core_copy(i, terms.at[i // 2]).wait_send()

        at = lax.rem(k, 2) * lax.div(k, 2) + (1 - lax.rem(k, 2)) * (n // 2)
        terms[at] = mm(a_ref[...], self.w_ref[...]).astype(BF)
        mine = terms.at[n // 2]
        sums = self.scatter(r)
        for i in range(1, n):

            @pl.when(k == i)
            def _(i=i):
                if i % 2:
                    sums.odd(i, terms.at[i // 2])
                else:
                    sums.even(i, mine)

        @pl.when(k == 0)
        def _():
            sums.core_copy(1, self.core.at[r, 0]).wait_recv()
            here = self.o_ref.at[r]
            add_up(here, [mine, self.core.at[r, 0]] + ([] if self.base is None else [here]))

    def end(self):
        self.close(self.rows - 1)
        self.scatter(self.rows - 1).drain(self.terms.at[self.n // 2])
        for row in range(self.rows - 1):
            for i in range(2, self.n, 2):
                for h in (0, 1):
                    self.scatter(row).link_copy(i, h).wait_send()


def tile_scratch(n, rows, span, w):
    width = w.shape[1]
    return [
        pltpu.VMEM(w.shape, BF),
        pltpu.VMEM((n // 2 + 1, span, width), BF),
        pltpu.VMEM((rows, n // 2, span, width), BF),
        pltpu.VMEM((rows, 2, n // 2 - 1, span // 2, width), BF),
        pltpu.SemaphoreType.DMA((rows, n // 2)),
        pltpu.SemaphoreType.DMA((rows, n // 2)),
        pltpu.SemaphoreType.DMA((rows, 2, n // 2 - 1)),
        pltpu.SemaphoreType.DMA((rows, 2, n // 2 - 1)),
        pltpu.SemaphoreType.DMA((2,)),
    ]


def spread_kernel(
    n, m, a_ref, w_any, x_ref, b_ref, d_any,
    o_ref, grad_ref, total_any,
    acc, own, up, across, line_sems, moves, *scratch,
):
    me, line = lax.axis_index("mp"), lax.axis_index("dp")
    rows = o_ref.shape[0]
    now = pl.program_id(0) * n + pl.program_id(1)
    per = rows * n // BLOCKS
    sums = TileSum(n, me, o_ref, w_any, scratch)
    chunks = own.shape[0]
    at = lambda ref: lambda c: ref.at[c]
    down = Line(m, line, at(own), at(up), at(across), at(up), line_sems)
    bring = pltpu.make_async_copy(d_any, own, moves.at[0])
    send = pltpu.make_async_copy(up, total_any, moves.at[1])

    @pl.when(now == 0)
    def _():
        bring.start()
        sums.start(lambda n, me: greet_all(n, me, m, line))
        bring.wait()
        for c in range(chunks):
            down.launch(c)

    sums.step(now, a_ref.at[0, 0])
    for c in range(chunks):

        @pl.when(now == 1 + c)
        def _(c=c):
            down.inward(c)

        @pl.when(now == 3 + c)
        def _(c=c):
            down.outward(c)

    k = lax.rem(now, per)
    term = dg(x_ref[...], b_ref[...], TN)

    @pl.when(k == 0)
    def _():
        acc[...] = term

    @pl.when((k > 0) & (k < per - 1))
    def _():
        acc[...] += term

    @pl.when(k == per - 1)
    def _():
        done = acc[...] + term
        for t in range(grad_ref.shape[0]):
            grad_ref[t] = done[:, 2 * t * TILE : 2 * (t + 1) * TILE].astype(BF)

    @pl.when(now == rows * n - 1)
    def _():
        for c in range(chunks):
            down.drain(c)
        send.start()
        sums.end()
        send.wait()


BLOCKS = 4
CHUNKS = 12


def spread(n, m, a, w, x, down):
    rows, _, span, depth = a.shape
    width = w.shape[1]
    slots = depth // (2 * TILE)
    everything = rows * n * span
    per = rows * n // BLOCKS
    part, block = everything // per, width // BLOCKS
    flat = (slots * TILE // CHUNKS, width)

    def place(r, j):
        row, slot = tile_at(r * n + j, n)
        return (row, xor_of(lax.axis_index("mp"), slot, n), 0, 0)

    def token(r, j):
        return lax.rem(r * n + j, per)

    def column(r, j):
        return lax.div(r * n + j, per)

    hbm = pl.BlockSpec(memory_space=pl.ANY)
    out, grad, total = pl.pallas_call(
        functools.partial(spread_kernel, n, m),
        grid=(rows, n),
        in_specs=[
            pl.BlockSpec((1, 1, span, depth), place),
            hbm,
            pl.BlockSpec((part, block), lambda r, j: (token(r, j), column(r, j))),
            pl.BlockSpec((part, depth), lambda r, j: (token(r, j), 0)),
            hbm,
        ],
        out_specs=[
            pl.BlockSpec(memory_space=pltpu.VMEM),
            pl.BlockSpec((slots, block, 2 * TILE), lambda r, j: (0, column(r, j), 0)),
            hbm,
        ],
        out_shape=[
            jax.ShapeDtypeStruct((rows, span, width), F32),
            jax.ShapeDtypeStruct((slots, width, 2 * TILE), BF),
            jax.ShapeDtypeStruct((CHUNKS,) + flat, BF),
        ],
        scratch_shapes=[
            pltpu.VMEM((block, depth), F32),
            pltpu.VMEM((CHUNKS,) + flat, BF),
            pltpu.VMEM((CHUNKS,) + flat, BF),
            pltpu.VMEM((CHUNKS,) + flat, BF),
            pltpu.SemaphoreType.DMA((6, CHUNKS)),
            pltpu.SemaphoreType.DMA((2,)),
        ]
        + tile_scratch(n, rows, span, w),
        compiler_params=params(mib=63, axes=2, key=3),
        cost_estimate=TINY,
        name="spread",
    )(
        a,
        w,
        x.reshape(everything, width),
        a.reshape(everything, depth),
        down.reshape((CHUNKS,) + flat),
    )
    return out, grad, total.reshape(down.shape)


def shards(
    n,
    m,
    hidden_in,
    doc_ids,
    tile_slot,
    attention_gain,
    query_gain,
    key_gain,
    attend_weight,
    output_weight,
    feed_gain,
    gate_up_slots,
    down_slots,
    out_grad,
):
    rows, span, width = hidden_in.shape
    length = doc_ids.shape[1]
    slots = gate_up_slots.shape[0]
    tokens = rows * span
    me = lax.axis_index("mp")
    offset = me * span

    kw = KVH * HD
    keys_w = attend_weight[:, QW : QW + kw].reshape(-1, KVH, HD)
    values_w = attend_weight[:, QW + kw :].reshape(-1, KVH, HD)
    attend_w = jnp.concatenate(
        [attend_weight[:, :QW], jnp.concatenate([keys_w, values_w], 2).reshape(-1, 2 * kw)], 1
    )
    starts = doc_starts(doc_ids)
    local_start = lax.dynamic_slice_in_dim(starts, offset, span, 1)
    local_pos = offset + jnp.arange(span, dtype=jnp.int32)[None] - local_start
    cos, sin = rotary_tables(local_pos.reshape(tokens))
    gq = jnp.tile(query_gain, 2)[None]
    gk = jnp.concatenate([key_gain, jnp.ones_like(key_gain)])[None]
    lane = jnp.arange(LANES) // HD
    ones = (lane[:, None] == lane[None, :]).astype(BF)
    key_block = min(512, length)
    info = jnp.stack(
        [
            jnp.full((rows,), me, jnp.int32),
            local_start[:, 0] // key_block,
            local_start[:, -1],
        ],
        1,
    ).astype(jnp.int32)
    start_col = jnp.broadcast_to(local_start[:, :, None], (rows, span, LANES))
    document = jnp.arange(LANES) % HD
    member = (doc_ids[:, :, None] == document).astype(F32)
    ka = jnp.where(document == DOCS, 1.0, member).astype(BF)
    own_member = lax.dynamic_slice_in_dim(member, offset, span, 1)
    qa = jnp.where(document == DOCS, -AWAY, own_member * AWAY).astype(BF)

    x_own = hidden_in.reshape(tokens, width)
    x_value = x_own.astype(F32)
    normed_ab, raw, q, grad_branch, attend_all, kv_all, output_all = project(
        n,
        rows,
        x_own,
        attention_gain[None],
        attend_w,
        output_weight,
        cos,
        sin,
        gq,
        gk,
        ones,
        out_grad.reshape(tokens, width),
    )
    q = q.reshape(rows, span, QW)
    kv_all = kv_all.reshape(rows, length, -1)
    output_full = output_all.reshape(QW, width)
    grads_all = lax.all_gather(
        grad_branch.reshape(rows, span, width), "mp", axis=1, tiled=True
    )
    ctx, rl = attend(info, q, kv_all, start_col)
    context_b = ctx.reshape(tokens, QW)
    middle = x_value + mm(context_b, output_full)
    scale_f = rms_scale(middle)
    normed_fb = (middle * scale_f * feed_gain).astype(BF).reshape(rows, span, width)

    slot_index = me * slots + jnp.arange(slots, dtype=jnp.int32)
    live = jnp.any(tile_slot[None, :] == slot_index[:, None], axis=1).astype(F32)
    gate_up_slots, down_slots, middle = lax.optimization_barrier(
        (gate_up_slots, down_slots, middle)
    )
    gu_t = jnp.swapaxes(gate_up_slots, 1, 2).reshape(slots * 2 * TILE, width)
    d_flat = down_slots.reshape(slots * TILE, width)
    d_t = d_flat.T
    normed_all, hidden, grad_both, grad_down = feed(
        n, live, normed_fb, grads_all, gate_up_slots, d_t
    )
    hidden = hidden.reshape(rows, n, span, -1)
    grad_normed_f, grad_gate_up, down_total = spread(
        n, m, grad_both.reshape(rows, n, span, -1), gu_t, normed_all, grad_down
    )
    gate_up_total = lax.psum(grad_gate_up, "dp")
    grad_normed_f = grad_normed_f.reshape(tokens, width)

    weighted = grad_normed_f * feed_gain
    inner = jnp.mean(weighted * middle, axis=-1, keepdims=True)
    gain_feed = jnp.sum(grad_normed_f * middle * scale_f, axis=0)
    grad_middle = out_grad.reshape(tokens, width) + scale_f * (
        weighted - middle * scale_f * scale_f * inner
    )
    grad_attn_b = grad_middle.astype(BF)
    grad_context = dg(grad_attn_b, output_full, NT).astype(BF).reshape(rows, span, QW)
    grad_output = dg(context_b, grad_attn_b, TN).astype(BF)

    dq, dkv, layer_out = attend_back(
        n,
        q,
        kv_all,
        qa,
        ka,
        grad_context,
        ctx,
        rl,
        hidden,
        d_flat,
        middle.reshape(rows, span, width),
    )
    grad_joined_b, sum_q, sum_k, down_total = unproject(
        n,
        dq.reshape(tokens, QW),
        dkv.reshape(rows, n, span, -1),
        raw,
        cos,
        sin,
        gq,
        gk,
        ones,
        down_total.reshape(slots * TILE, width),
    )
    sums = jnp.concatenate(
        [
            jnp.zeros((width // LANES, LANES), F32),
            gain_feed.reshape(-1, LANES),
            sum_q[:1],
            sum_k[:1],
            jnp.zeros((GAIN_ROWS - 2 * (width // LANES) - 2, LANES), F32),
        ]
    )
    input_grad, attend_total, output_total, gains = finish(
        n,
        m,
        normed_ab,
        grad_joined_b,
        attend_all,
        x_own,
        grad_middle,
        attention_gain[None],
        grad_output.reshape(n, -1, width),
        sums,
    )
    gains = gains.reshape(-1)
    gain_query = gains[2 * width : 2 * width + HD] + gains[2 * width + HD : 2 * width + 2 * HD]
    gain_key = gains[2 * width + LANES : 2 * width + LANES + HD]
    shape = (rows, span, width)
    return (
        layer_out,
        input_grad.reshape(shape),
        attend_total,
        output_total,
        gate_up_total.astype(F32),
        down_total.reshape(slots, TILE, width),
        gains[:width],
        gain_query,
        gain_key,
        gains[width : 2 * width],
    )


def solution(mesh):
    placed = (
        P("dp", "mp", None),
        P("dp", None),
        P(),
        P(),
        P(),
        P(),
        P("mp", None),
        P("mp", None),
        P(),
        P("mp", None, None),
        P("mp", None, None),
        P("dp", "mp", None),
    )
    return jax.shard_map(
        functools.partial(shards, mesh.shape["mp"], mesh.shape["dp"]),
        mesh=mesh,
        in_specs=placed,
        out_specs=(
            P("dp", "mp", None),
            P("dp", "mp", None),
            P("mp", None),
            P("mp", None),
            P("mp", None, None),
            P("mp", None, None),
            P(),
            P(),
            P(),
            P(),
        ),
        check_vma=False,
    )
```

```python
import functools

import jax
import jax.numpy as jnp
from jax import lax
from jax.experimental import pallas as pl
from jax.experimental.pallas import tpu as pltpu
from jax.sharding import PartitionSpec as P

H = 20
KVH = 5
HD = 64
TILE = 128
EPSILON = 1e-06
QW = H * HD
LANES = 128
GW = (H // KVH) * HD
DOCS = 3
AWAY = 256.0
LOG2E = 1.4426950408889634
LN2 = 0.6931471805599453
BF = jnp.bfloat16
F32 = jnp.float32
MIB = 1 << 20
NT = (((1,), (1,)), ((), ()))
TN = (((0,), (0,)), ((), ()))


def params(mib=56, axes=1, key=None):
    if key is None:
        return pltpu.CompilerParams(
            vmem_limit_bytes=mib * MIB, dimension_semantics=("arbitrary",) * axes
        )
    return pltpu.CompilerParams(
        vmem_limit_bytes=mib * MIB,
        dimension_semantics=("arbitrary",) * axes if axes else None,
        collective_id=key,
        has_side_effects=True,
    )


TINY = pl.CostEstimate(flops=1, bytes_accessed=1, transcendentals=0)


def mm(a, b):
    return jnp.dot(a, b, preferred_element_type=F32)


def dg(a, b, dims):
    return lax.dot_general(a, b, dims, preferred_element_type=F32)


def doc_starts(docs):
    index = jnp.arange(docs.shape[-1], dtype=jnp.int32)
    change = jnp.concatenate(
        [jnp.ones(docs.shape[:-1] + (1,), dtype=jnp.bool_), docs[..., 1:] != docs[..., :-1]],
        axis=-1,
    )
    return lax.cummax(jnp.where(change, index, 0), axis=docs.ndim - 1)


def rotary_tables(positions):
    half_dim = HD // 2
    freqs = 1.0 / 10000.0 ** (jnp.arange(half_dim, dtype=jnp.float32) * 2.0 / HD)
    angles = positions.astype(jnp.float32)[..., None] * freqs
    return jnp.tile(jnp.cos(angles), 4), jnp.tile(jnp.sin(angles), 4)


def rms_scale(values):
    return lax.rsqrt(jnp.mean(values * values, axis=-1, keepdims=True) + EPSILON)


MESH = pl.DeviceIdType.MESH


def flip(me, k):
    bit = 1
    while bit <= k:
        if k & bit:
            me = me + bit - 2 * bit * lax.rem(lax.div(me, bit), 2)
        bit *= 2
    return me


def link_bits(n):
    return [1 << i for i in range(1, n.bit_length() - 1)]


def greet(n, me):
    barrier = pltpu.get_barrier_semaphore()
    bits = [1] + link_bits(n)
    for bit in bits:
        pl.semaphore_signal(barrier, inc=1, device_id={"mp": flip(me, bit)}, device_id_type=MESH)
    pl.semaphore_wait(barrier, len(bits))


def greet_all(n, me, m, line):
    barrier = pltpu.get_barrier_semaphore()
    bits = [1] + link_bits(n)
    for bit in bits:
        pl.semaphore_signal(barrier, inc=1, device_id={"mp": flip(me, bit)}, device_id_type=MESH)
    for step in range(1, m):
        other = lax.rem(line + step, m)
        pl.semaphore_signal(barrier, inc=1, device_id={"dp": other}, device_id_type=MESH)
    pl.semaphore_wait(barrier, len(bits) + m - 1)


class Line:
    def __init__(self, m, line, own, up, across, total, sems):
        self.own, self.up, self.across, self.total, self.sems = own, up, across, total, sems
        low = line < m // 2
        self.inner = jnp.where(low, line + 1, line - 1)
        self.outer = jnp.where(low, line - 1, line + 1)
        self.has_outer = (line > 0) & (line < m - 1)
        self.middle = (line == m // 2 - 1) | (line == m // 2)

    def copy(self, kind, c):
        src, dst, to = (
            (self.own, self.up, self.inner),
            (self.own, self.across, self.inner),
            (self.total, self.total, self.outer),
        )[kind]
        return pltpu.make_async_remote_copy(
            src_ref=src(c),
            dst_ref=dst(c),
            send_sem=self.sems.at[2 * kind, c],
            recv_sem=self.sems.at[2 * kind + 1, c],
            device_id={"dp": to},
            device_id_type=MESH,
        )

    def launch(self, c):
        @pl.when(jnp.logical_not(self.has_outer))
        def _():
            self.copy(0, c).start()

    def inward(self, c):
        @pl.when(self.has_outer)
        def _():
            self.copy(0, c).wait_recv()
            add_up(self.own(c), [self.own(c), self.up(c)])

            @pl.when(self.middle)
            def _():
                self.copy(1, c).start()

            @pl.when(jnp.logical_not(self.middle))
            def _():
                self.copy(0, c).start()

    def outward(self, c):
        @pl.when(self.middle)
        def _():
            self.copy(1, c).wait_recv()
            add_up(self.total(c), [self.own(c), self.across(c)])

        @pl.when(jnp.logical_not(self.middle))
        def _():
            self.copy(2, c).wait_recv()

        @pl.when(self.has_outer)
        def _():
            self.copy(2, c).start()

    def drain(self, c):
        @pl.when(self.middle)
        def _():
            self.copy(1, c).wait_send()

        @pl.when(jnp.logical_not(self.middle))
        def _():
            self.copy(0, c).wait_send()

        @pl.when(self.has_outer)
        def _():
            self.copy(2, c).wait_send()


class Gather:
    def __init__(self, n, me, own, slot, send, recv, relative=False):
        self.n, self.me, self.own, self.slot, self.send, self.recv = n, me, own, slot, send, recv
        self.relative = relative
        bits = link_bits(n)
        self.order = (bits + [1], bits[::-1] + [1])
        even = [(k, h) for k in range(2, n, 2) for h in (0, 1)]
        even.sort(key=lambda kh: (bin(kh[0]).count("1"), max(self.place(*kh)), kh[1]))
        self.even = even

    def place(self, k, half):
        return [i for i, bit in enumerate(self.order[half]) if k & bit]

    def copy(self, k, half, bit):
        return pltpu.make_async_remote_copy(
            src_ref=self.own(half) if k == 0 else self.here(k, half),
            dst_ref=self.slot(k ^ bit, half, k) if self.relative else self.slot(k, half),
            send_sem=self.send.at[k ^ bit, half],
            recv_sem=self.recv.at[k ^ bit, half],
            device_id={"mp": flip(self.me, bit)},
            device_id_type=MESH,
        )

    def here(self, k, half):
        return self.slot(k, half, k) if self.relative else self.slot(k, half)

    def onward(self, k, half):
        return self.order[half][(max(self.place(k, half)) + 1) if k else 0 :]

    def start(self):
        for i in range(len(self.order[0])):
            for half in (0, 1):
                self.copy(0, half, self.order[half][i]).start()

    def arrive(self, k, half):
        here = self.here(k, half)
        pltpu.make_async_remote_copy(
            src_ref=here,
            dst_ref=here,
            send_sem=self.send.at[k, half],
            recv_sem=self.recv.at[k, half],
            device_id={"mp": flip(self.me, 1)},
            device_id_type=MESH,
        ).wait_recv()

    def forward(self, k, half):
        self.arrive(k, half)
        for bit in self.onward(k, half):
            self.copy(k, half, bit).start()

    def rest(self):
        for k, half in [(1, 0), (1, 1)] + [(k + 1, h) for k, h in self.even]:
            self.arrive(k, half)

    def drain(self):
        for k in range(0, self.n, 2):
            for half in (0, 1):
                for bit in self.onward(k, half):
                    self.copy(k, half, bit).wait_send()


class Scatter:
    def __init__(self, n, me, part, core, link, sems):
        self.n, self.me, self.part = n, me, part
        self.core, self.link = core, link
        self.core_send, self.core_recv, self.link_send, self.link_recv = sems
        bits = link_bits(n)
        self.order = (bits[::-1], bits)

    def first(self, k, half):
        return next(i for i, bit in enumerate(self.order[half]) if k & bit)

    def core_copy(self, k, ref):
        return pltpu.make_async_remote_copy(
            src_ref=ref,
            dst_ref=self.core(k // 2),
            send_sem=self.core_send.at[k // 2],
            recv_sem=self.core_recv.at[k // 2],
            device_id={"mp": flip(self.me, 1)},
            device_id_type=MESH,
        )

    def link_copy(self, k, half):
        bit = self.order[half][self.first(k, half)]
        return pltpu.make_async_remote_copy(
            src_ref=self.part(self.core(k // 2), half),
            dst_ref=self.link(half, k // 2 - 1),
            send_sem=self.link_send.at[half, k // 2 - 1],
            recv_sem=self.link_recv.at[half, k // 2 - 1],
            device_id={"mp": flip(self.me, bit)},
            device_id_type=MESH,
        )

    def addends(self, k, half):
        upto = self.first(k, half) if k else len(self.order[half])
        return [k | bit for bit in self.order[half][:upto]]

    def odd(self, k, ref):
        self.core_copy(k, ref).start()

    def even(self, k, ref):
        self.core_copy(k + 1, self.core(k // 2)).wait_recv()
        for half in sorted((0, 1), key=lambda h: -len(self.addends(k, h))):
            joined = [self.part(ref, half), self.part(self.core(k // 2), half)]
            for j in self.addends(k, half):
                self.link_copy(j, half).wait_recv()
                joined.append(self.link(half, j // 2 - 1))
            add_up(joined[1], joined)
            self.link_copy(k, half).start()

    def own(self, ref, out):
        self.core_copy(1, self.core(0)).wait_recv()
        for half in (0, 1):
            joined = [self.part(ref, half), self.part(self.core(0), half)]
            for j in self.addends(0, half):
                self.link_copy(j, half).wait_recv()
                joined.append(self.link(half, j // 2 - 1))
            add_up(self.part(out, half), joined)

    def drain(self, ref):
        for k in range(1, self.n, 2):
            self.core_copy(k, ref).wait_send()
        for k in range(2, self.n, 2):
            for half in (0, 1):
                self.link_copy(k, half).wait_send()


def add_up(out, terms):
    rows = out.shape[-2]
    step = 16
    lead = (slice(None),) * (len(out.shape) - 2)

    @pl.loop(0, rows // step)
    def _(i):
        at = lead + (pl.ds(pl.multiple_of(i * step, step), step), slice(None))
        total = terms[0][at].astype(F32)
        for t in terms[1:]:
            total = total + t[at].astype(F32)
        out[at] = total.astype(out.dtype)


def scatter_scratch(n, shape, half):
    return [
        pltpu.VMEM((n // 2,) + shape, BF),
        pltpu.VMEM((2, n // 2 - 1) + half, BF),
        pltpu.SemaphoreType.DMA((n // 2,)),
        pltpu.SemaphoreType.DMA((n // 2,)),
        pltpu.SemaphoreType.DMA((2, n // 2 - 1)),
        pltpu.SemaphoreType.DMA((2, n // 2 - 1)),
    ]


def make_scatter(n, me, part, refs):
    core, link = refs[:2]
    return Scatter(
        n,
        me,
        part,
        lambda i: core.at[i],
        lambda h, i: link.at[h, i],
        refs[2:6],
    )


def half_turn(x, lane):
    first = (lane % HD) < HD // 2
    return jnp.where(first, -pltpu.roll(x, LANES - HD // 2, 1), pltpu.roll(x, HD // 2, 1))


def half_turn_back(x, lane):
    first = (lane % HD) < HD // 2
    return jnp.where(first, pltpu.roll(x, LANES - HD // 2, 1), -pltpu.roll(x, HD // 2, 1))


def group_mean(x, ones):
    high = x.astype(BF)
    low = (x - high.astype(F32)).astype(BF)
    return (mm(high, ones) + mm(low, ones)) * (1.0 / HD)


def project_kernel(
    n, x_any, gain_ref, w_ref, o_ref, cos_ref, sin_ref, gq_ref, gk_ref, ones_ref, grad_any,
    normed_any, raw_any, q_ref, branch_any, w_out, kv_out, o_out,
    x_ref, grad_ref, normed_ref, raw_ref, branch_ref, moves, w_all, kv_own, w_send, w_recv, kv_send, kv_recv, o_send, o_recv, local,
):
    me = lax.axis_index("mp")
    depth = w_ref.shape[0]
    tokens, width = x_ref.shape
    rows = kv_out.shape[0]
    span = tokens // rows
    half = depth // 2
    own_w = pltpu.make_async_copy(w_ref, w_all.at[me], local.at[0])
    own_w.start()
    early = [
        pltpu.make_async_copy(x_any, x_ref, moves.at[0]),
        pltpu.make_async_copy(grad_any, grad_ref, moves.at[1]),
    ]
    late = [
        pltpu.make_async_copy(normed_ref, normed_any, moves.at[2]),
        pltpu.make_async_copy(branch_ref, branch_any, moves.at[3]),
        pltpu.make_async_copy(raw_ref, raw_any, moves.at[4]),
    ]
    for c in early:
        c.start()
    own_o = pltpu.make_async_copy(o_ref, o_out.at[me], local.at[1 + rows])
    own_o.start()
    greet(n, me)
    wide = o_ref.shape[1] // 2
    outs = Gather(
        n,
        me,
        lambda h: o_ref.at[:, pl.ds(h * wide, wide)],
        lambda k, h: o_out.at[flip(me, k), :, pl.ds(h * wide, wide)],
        o_send,
        o_recv,
    )
    weights = Gather(
        n,
        me,
        lambda h: w_ref.at[pl.ds(h * half, half)],
        lambda k, h: w_all.at[flip(me, k), pl.ds(h * half, half)],
        w_send,
        w_recv,
    )
    weights.start()
    for c in early:
        c.wait()
    step = min(64, tokens)

    @pl.loop(0, tokens // step)
    def _(i):
        at = pl.ds(pl.multiple_of(i * step, step), step)
        x = x_ref[at, :].astype(F32)
        scale = lax.rsqrt(jnp.mean(x * x, axis=-1, keepdims=True) + EPSILON)
        normed_ref[at, :] = (x * scale * gain_ref[...]).astype(BF)
        branch_ref[at, :] = grad_ref[at, :].astype(BF)

    chunk = min(256, tokens)

    def accumulate(k, fresh):
        block = flip(me, k)
        columns = pl.ds(pl.multiple_of(block * depth, depth), depth)

        @pl.loop(0, tokens // chunk)
        def _(i):
            at = pl.ds(pl.multiple_of(i * chunk, chunk), chunk)
            term = mm(normed_ref[at, columns], w_all[block])
            raw_ref[at, :] = term if fresh else raw_ref[at, :] + term

    own_w.wait()
    accumulate(0, True)
    for h in (0, 1):
        weights.arrive(1, h)
    accumulate(1, False)
    for i, (k, h) in enumerate(weights.even):
        weights.forward(k, h)
        if any(k == other for other, _ in weights.even[:i]):
            accumulate(k, False)
    outs.start()
    for k in range(3, n, 2):
        for h in (0, 1):
            weights.arrive(k, h)
        accumulate(k, False)
    out_w = pltpu.make_async_copy(w_all, w_out, local.at[0])
    out_w.start()
    for c in late:
        c.start()

    chunk = min(128, tokens)
    lane = lax.broadcasted_iota(jnp.int32, (chunk, LANES), 1)

    def finish(i, tiles):
        at = pl.ds(pl.multiple_of(i * chunk, chunk), chunk)
        cos, sin = cos_ref[at, :], sin_ref[at, :]
        for tile in tiles:
            lanes = slice(tile * LANES, (tile + 1) * LANES)
            x = raw_ref[at, lanes]
            query = tile < QW // LANES
            scale = lax.rsqrt(group_mean(x * x, ones_ref[...]) + EPSILON)
            v = x * scale * (gq_ref[...] if query else gk_ref[...])
            y = v * cos + half_turn(v, lane) * sin
            if query:
                q_ref[at, lanes] = (y * (HD**-0.5 * LOG2E)).astype(BF)
            else:
                mine = slice(tile * LANES - QW, (tile + 1) * LANES - QW)
                kv_own[at, mine] = jnp.where(lane < HD, y, x).astype(BF)

    count = raw_ref.shape[1] // LANES

    @pl.loop(0, tokens // chunk)
    def _(i):
        finish(i, range(QW // LANES, count))

    both = rows // 2
    keep = [
        pltpu.make_async_copy(
            kv_own.at[pl.ds(r * span, span)], kv_out.at[r, me], local.at[1 + r]
        )
        for r in range(rows)
    ]
    for c in keep:
        c.start()
    kvs = Gather(
        n,
        me,
        lambda h: kv_own.at[pl.ds(h * span, span)],
        lambda k, h: kv_out.at[h, flip(me, k)],
        kv_send,
        kv_recv,
    )
    kvs.start()

    @pl.loop(0, tokens // chunk)
    def _(i):
        finish(i, range(QW // LANES))

    for k, h in kvs.even:
        outs.forward(k, h)
        kvs.forward(k, h)
    outs.rest()
    kvs.rest()
    for c in keep:
        c.wait()
    out_w.wait()
    own_o.wait()
    for c in late:
        c.wait()
    weights.drain()
    outs.drain()
    kvs.drain()


def project(n, rows, x, gain, w, o, cos, sin, gq, gk, ones, grad):
    tokens, width = x.shape
    depth, columns = w.shape
    vmem = pl.BlockSpec(memory_space=pltpu.VMEM)
    hbm = pl.BlockSpec(memory_space=pl.ANY)
    kvw = columns - QW
    return pl.pallas_call(
        functools.partial(project_kernel, n),
        in_specs=[hbm, vmem, hbm, hbm, vmem, vmem, vmem, vmem, vmem, hbm],
        out_specs=[hbm, hbm, vmem, hbm, hbm, hbm, hbm],
        out_shape=[
            jax.ShapeDtypeStruct((tokens, width), BF),
            jax.ShapeDtypeStruct((tokens, columns), F32),
            jax.ShapeDtypeStruct((tokens, QW), BF),
            jax.ShapeDtypeStruct((tokens, width), BF),
            jax.ShapeDtypeStruct((n, depth, columns), BF),
            jax.ShapeDtypeStruct((rows, n, tokens // rows, kvw), BF),
            jax.ShapeDtypeStruct((n,) + o.shape, BF),
        ],
        scratch_shapes=[
            pltpu.VMEM((tokens, width), BF),
            pltpu.VMEM((tokens, width), F32),
            pltpu.VMEM((tokens, width), BF),
            pltpu.VMEM((tokens, columns), F32),
            pltpu.VMEM((tokens, width), BF),
            pltpu.SemaphoreType.DMA((5,)),
            pltpu.VMEM((n, depth, columns), BF),
            pltpu.VMEM((tokens, kvw), BF),
            pltpu.SemaphoreType.DMA((n, 2)),
            pltpu.SemaphoreType.DMA((n, 2)),
            pltpu.SemaphoreType.DMA((n, 2)),
            pltpu.SemaphoreType.DMA((n, 2)),
            pltpu.SemaphoreType.DMA((n, 2)),
            pltpu.SemaphoreType.DMA((n, 2)),
            pltpu.SemaphoreType.DMA((2 + rows,)),
        ],
        compiler_params=params(axes=0, key=0),
        name="project",
    )(x, gain, w, o, cos, sin, gq, gk, ones, grad)


def unproject_kernel(
    n, dq_any, dkv_any, raw_any, cos_ref, sin_ref, gq_ref, gk_ref, ones_ref, down_any,
    gj_ref, sq_ref, sk_ref, wide_any,
    dkv_own, dkv_ref, dq_ref, raw_ref, down_ref, wide_ref, load, *scratch,
):
    me = lax.axis_index("mp")
    early = [
        pltpu.make_async_copy(dkv_any.at[:, flip(me, k)], dkv_ref.at[k // 2], load.at[4 + k // 2])
        for k in range(n - 2, -1, -2)
    ]
    late = [
        pltpu.make_async_copy(dq_any, dq_ref, load.at[0]),
        pltpu.make_async_copy(raw_any, raw_ref, load.at[1]),
        pltpu.make_async_copy(down_any, down_ref, load.at[2]),
    ]
    for c in early + late:
        c.start()
    greet(n, me)
    tokens = dq_ref.shape[0]
    rows = dkv_any.shape[0]
    span = tokens // rows
    columns = raw_ref.shape[1]
    keys = make_scatter(n, me, lambda ref, h: ref.at[h], scratch[:6])

    def dkv_term(k):
        return dkv_any.at[:, flip(me, k)] if k % 2 else dkv_ref.at[k // 2]

    for k in range(n - 1, 0, -2):
        keys.odd(k, dkv_term(k))
    for c in early:
        c.wait()
    keys.even(n - 2, dkv_term(n - 2))
    for c in late:
        c.wait()

    chunk = min(128, tokens)
    lane = lax.broadcasted_iota(jnp.int32, (chunk, LANES), 1)
    sq_ref[...] = jnp.zeros_like(sq_ref)
    sk_ref[...] = jnp.zeros_like(sk_ref)

    def back(i, tiles, query):
        at = pl.ds(pl.multiple_of(i * chunk, chunk), chunk)
        cos, sin = cos_ref[at, :], sin_ref[at, :]
        total = 0.0
        for tile in tiles:
            lanes = slice(tile * LANES, (tile + 1) * LANES)
            x = raw_ref[at, lanes]
            if query:
                e = dq_ref[at, lanes]
            else:
                per = span // chunk
                here = pl.ds(pl.multiple_of(lax.rem(i, per) * chunk, chunk), chunk)
                e = dkv_own[lax.div(i, per), here, slice(tile * LANES - QW, (tile + 1) * LANES - QW)]
            scale = lax.rsqrt(group_mean(x * x, ones_ref[...]) + EPSILON)
            v = x * scale
            turned = e * cos + half_turn_back(e * sin, lane)
            u = turned * (gq_ref[...] if query else gk_ref[...])
            grad = scale * (u - v * group_mean(u * v, ones_ref[...]))
            gj_ref[at, lanes] = (grad if query else jnp.where(lane < HD, grad, e)).astype(BF)
            total = total + jnp.sum(turned * v, axis=0, keepdims=True)
        sums = sq_ref if query else sk_ref
        sums[...] += jnp.broadcast_to(total, sums.shape)

    count = columns // LANES

    parts = tokens // chunk
    left = list(range(n - 4, 0, -2))
    for i in range(parts):
        back(i, range(QW // LANES), True)
        if i == 0:
            for k in left:
                keys.even(k, dkv_term(k))

    wide_ref[...] = down_ref[...].astype(F32)
    keep = pltpu.make_async_copy(wide_ref, wide_any, load.at[3])
    keep.start()
    keys.own(dkv_term(0), dkv_own)

    @pl.loop(0, tokens // chunk)
    def _(i):
        back(i, range(QW // LANES, count), False)

    keys.drain(dkv_term(0))
    keep.wait()


def unproject(n, dq, dkv, raw, cos, sin, gq, gk, ones, down):
    tokens, columns = raw.shape
    rows = dkv.shape[0]
    span = tokens // rows
    kvw = columns - QW
    vmem = pl.BlockSpec(memory_space=pltpu.VMEM)
    hbm = pl.BlockSpec(memory_space=pl.ANY)
    return pl.pallas_call(
        functools.partial(unproject_kernel, n),
        in_specs=[hbm] * 3 + [vmem] * 5 + [hbm],
        out_specs=[vmem] * 3 + [hbm],
        out_shape=[
            jax.ShapeDtypeStruct((tokens, columns), BF),
            jax.ShapeDtypeStruct((8, LANES), F32),
            jax.ShapeDtypeStruct((8, LANES), F32),
            jax.ShapeDtypeStruct(down.shape, F32),
        ],
        scratch_shapes=[
            pltpu.VMEM((rows, span, kvw), F32),
            pltpu.VMEM((n // 2, rows, span, kvw), BF),
            pltpu.VMEM(dq.shape, F32),
            pltpu.VMEM(raw.shape, F32),
            pltpu.VMEM(down.shape, BF),
            pltpu.VMEM(down.shape, F32),
            pltpu.SemaphoreType.DMA((4 + n // 2,)),
        ]
        + scatter_scratch(n, (rows, span, kvw), (span, kvw)),
        compiler_params=params(mib=60, axes=0, key=2),
        cost_estimate=TINY,
        name="unproject",
    )(dq, dkv, raw, cos, sin, gq, gk, ones, down)


GAIN_ROWS = 40


def finish_kernel(
    n, m, normed_any, gj_any, w_any, x_any, mid_any, gain_ref, share_any, sums_ref,
    grad_any, attend_ref, out_ref, gains_ref,
    normed_ref, gj_ref, x_ref, grad_ref,
    w_ref, term, error, mid_ref, own_w, up_w, across_w, own_o, up_o, across_o, landed,
    sem_w, sem_o, sem_g, load, *scratch,
):
    me, line = lax.axis_index("mp"), lax.axis_index("dp")
    depth = w_ref.shape[1]
    tokens, width = x_ref.shape
    pieces, piece = own_w.shape[0], own_w.shape[1]
    o_pieces, o_piece = own_o.shape[0], own_o.shape[1]
    chunk = error.shape[0]
    early = [
        pltpu.make_async_copy(normed_any, normed_ref, load.at[2]),
        pltpu.make_async_copy(gj_any, gj_ref, load.at[3]),
        pltpu.make_async_copy(share_any, own_o, load.at[4]),
    ]
    fetch = [
        pltpu.make_async_copy(w_any, w_ref, load.at[0]),
        pltpu.make_async_copy(x_any, x_ref, load.at[5]),
    ]
    keep = pltpu.make_async_copy(grad_ref, grad_any, load.at[6])
    for c in early + fetch:
        c.start()

    def bring(i):
        here = pl.ds(pl.multiple_of(i * chunk, chunk), chunk)
        return pltpu.make_async_copy(mid_any.at[here], mid_ref, load.at[1])

    bring(0).start()
    greet_all(n, me, m, line)
    half = depth // 2
    sums = make_scatter(n, me, lambda ref, h: ref.at[pl.ds(h * half, half)], scratch)
    at = lambda ref: lambda c: ref.at[c]
    weights = Line(m, line, at(own_w), at(up_w), at(across_w), at(up_w), sem_w)
    out_line = Line(m, line, at(own_o), at(up_o), at(across_o), at(up_o), sem_o)
    gains_ref[...] = sums_ref[...]

    def tokens_part(i):
        here = pl.ds(pl.multiple_of(i * chunk, chunk), chunk)
        for b in range(n):
            error[:, b * depth : (b + 1) * depth] = dg(gj_ref[here, :], w_ref[b], NT)
        small = min(32, chunk)
        bring(i).wait()

        @pl.loop(0, chunk // small)
        def _(s):
            part = pl.ds(pl.multiple_of(s * small, small), small)
            rows = pl.ds(pl.multiple_of(i * chunk + s * small, small), small)
            e = error[part, :]
            x = x_ref[rows, :].astype(F32)
            scale = lax.rsqrt(jnp.mean(x * x, axis=-1, keepdims=True) + EPSILON)
            u = e * gain_ref[...]
            v = x * scale
            inner = jnp.mean(u * v, axis=-1, keepdims=True)
            grad_ref[rows, :] = mid_ref[part, :] + scale * (u - v * inner)
            total = jnp.sum(e * v, axis=0, keepdims=True)
            for b in range(width // LANES):
                gains_ref[b : b + 1, :] += total[:, b * LANES : (b + 1) * LANES]

        if i + 1 < tokens // chunk:
            bring(i + 1).start()

    def mine(k):
        return term.at[k // 2 if k % 2 else n // 2]

    def weight_part(k):
        columns = pl.ds(pl.multiple_of(flip(me, k) * depth, depth), depth)
        mine(k)[...] = dg(normed_ref[:, columns], gj_ref[...], TN).astype(BF)

    steps = [("mp", flip(me, 1 << i)) for i in range(n.bit_length() - 1)]
    steps += [("dp", flip(line, 1 << i)) for i in range(m.bit_length() - 1)]

    def exchange(i):
        axis, to = steps[i]
        return pltpu.make_async_remote_copy(
            src_ref=landed.at[2 * i],
            dst_ref=landed.at[2 * i + 1],
            send_sem=sem_g.at[0, i],
            recv_sem=sem_g.at[1, i],
            device_id={axis: to},
            device_id_type=MESH,
        )

    for c in early:
        c.wait()
    for c in range(o_pieces):
        out_line.launch(c)
    for k in range(n - 1, 0, -2):
        weight_part(k)
        sums.odd(k, mine(k))
        if k == n - 1:
            weight_part(n - 2)
            sums.even(n - 2, mine(n - 2))
    for c in fetch:
        c.wait()
    tokens_part(0)
    for k in range(n - 4, 0, -2):
        weight_part(k)
        sums.even(k, mine(k))
    weight_part(0)
    for i in range(1, tokens // chunk):
        tokens_part(i)
    keep.start()
    for i in range(len(steps)):
        landed[2 * i] = gains_ref[...]
        exchange(i).start()
        exchange(i).wait_recv()
        gains_ref[...] = landed[2 * i] + landed[2 * i + 1]
    for c in range(o_pieces):
        out_line.inward(c)
    sums.own(mine(0), attend_ref)
    for c in range(pieces):
        own_w[c] = attend_ref[c * piece : (c + 1) * piece, :].astype(BF)
        weights.launch(c)
    kw = KVH * HD

    def widen(c):
        rows = slice(c * piece, (c + 1) * piece)
        attend_ref[rows, :QW] = up_w[c, :, :QW].astype(F32)
        for h in range(KVH):
            both = up_w[c, :, QW + 2 * h * HD : QW + 2 * (h + 1) * HD].astype(F32)
            attend_ref[rows, QW + h * HD : QW + (h + 1) * HD] = both[:, :HD]
            attend_ref[rows, QW + kw + h * HD : QW + kw + (h + 1) * HD] = both[:, HD:]

    ahead = 2
    for c in range(pieces + ahead):
        if c < pieces:
            weights.inward(c)
        if c < o_pieces:
            out_line.outward(c)
            out_ref[c * o_piece : (c + 1) * o_piece, :] = up_o[c].astype(F32)
        if c >= ahead:
            weights.outward(c - ahead)
            widen(c - ahead)
    keep.wait()
    for c in range(o_pieces):
        out_line.drain(c)
    for c in range(pieces):
        weights.drain(c)
    for i in range(len(steps)):
        exchange(i).wait_send()
    sums.drain(mine(0))


def finish(n, m, normed, gj, w, x, middle, gain, share, sums):
    tokens, width = x.shape
    columns = gj.shape[1]
    depth = width // n
    pieces, o_pieces = 8, 5
    split = (o_pieces, share.shape[0] // o_pieces, width)
    chunk = min(256, tokens)
    vmem = pl.BlockSpec(memory_space=pltpu.VMEM)
    hbm = pl.BlockSpec(memory_space=pl.ANY)
    steps = n.bit_length() + m.bit_length() - 2
    return pl.pallas_call(
        functools.partial(finish_kernel, n, m),
        in_specs=[hbm, hbm, hbm, hbm, hbm, vmem, hbm, vmem],
        out_specs=[hbm, vmem, vmem, vmem],
        out_shape=[
            jax.ShapeDtypeStruct((tokens, width), F32),
            jax.ShapeDtypeStruct((depth, columns), F32),
            jax.ShapeDtypeStruct(share.shape, F32),
            jax.ShapeDtypeStruct((GAIN_ROWS, LANES), F32),
        ],
        scratch_shapes=[
            pltpu.VMEM((tokens, width), BF),
            pltpu.VMEM((tokens, columns), BF),
            pltpu.VMEM((tokens, width), BF),
            pltpu.VMEM((tokens, width), F32),
            pltpu.VMEM(w.shape, BF),
            pltpu.VMEM((n // 2 + 1, depth, columns), BF),
            pltpu.VMEM((chunk, width), F32),
            pltpu.VMEM((chunk, width), F32),
        ]
        + [pltpu.VMEM((pieces, depth // pieces, columns), BF)] * 3
        + [pltpu.VMEM(split, BF)] * 3
        + [
            pltpu.VMEM((2 * steps, GAIN_ROWS, LANES), F32),
            pltpu.SemaphoreType.DMA((6, pieces)),
            pltpu.SemaphoreType.DMA((6, o_pieces)),
            pltpu.SemaphoreType.DMA((2, steps)),
            pltpu.SemaphoreType.DMA((7,)),
        ]
        + scatter_scratch(n, (depth, columns), (depth // 2, columns)),
        compiler_params=params(mib=60, axes=0, key=5),
        cost_estimate=TINY,
        name="finish",
    )(normed, gj, w, x, middle, gain, share.reshape(split), sums)


def key_positions(shape, axis, group, per, span):
    return group * per * span + lax.broadcasted_iota(jnp.int32, shape, axis)


def attend_kernel(keys, info, q_ref, kv_ref, start_ref, ctx_ref, rl_ref, acc):
    span = q_ref.shape[1]
    per = keys // span
    row = pl.program_id(0)
    me, first, last_start = info[row, 0], info[row, 1], info[row, 2]
    low_q = lax.broadcasted_iota(jnp.int32, (span, LANES), 1) < HD
    low_k = lax.broadcasted_iota(jnp.int32, (keys, LANES), 1) < HD
    one = jnp.ones((keys, LANES), BF)
    none = jnp.zeros((span, LANES), BF)
    queries = []
    for h in range(GW // HD):
        pair = q_ref[0, :, (h // 2) * LANES : (h // 2 + 1) * LANES]
        queries.append(jnp.where(low_q, pair, none) if h % 2 == 0 else jnp.where(low_q, none, pair))
    acc[...] = jnp.zeros_like(acc)

    def block(g, masked):
        group = g
        kv = kv_ref[0, pl.ds(pl.multiple_of(group * keys, keys), keys), :]
        vk = jnp.concatenate([kv[:, HD:], kv[:, :HD]], axis=1)
        key_sides = (kv, vk)
        value_sides = (jnp.where(low_k, vk, one), jnp.where(low_k, one, kv))
        if masked:
            position = key_positions((span, keys), 1, group, per, span)
            own = me * span + lax.broadcasted_iota(jnp.int32, (span, keys), 0)
            seen = (position <= own) & (position >= start_ref[0][:, :1])
        for h in range(GW // HD):
            p = jnp.exp2(dg(queries[h], key_sides[h % 2], NT))
            if masked:
                p = jnp.where(seen, p, 0.0)
            acc[h] += mm(p.astype(BF), value_sides[h % 2])

    def step(g, carry):
        edge = (g == me // per) | (g * keys < last_start)
        pl.when(edge)(lambda: block(g, True))
        pl.when(jnp.logical_not(edge))(lambda: block(g, False))
        return carry

    lax.fori_loop(first, me // per + 1, step, 0)
    for pair in range(GW // LANES):
        even, odd = acc[2 * pair], acc[2 * pair + 1]
        total = jnp.where(low_q, pltpu.roll(even, HD, 1), pltpu.roll(odd, HD, 1))
        inverse = 1.0 / total
        lanes = slice(pair * LANES, (pair + 1) * LANES)
        ctx_ref[0, :, lanes] = (jnp.where(low_q, even, odd) * inverse).astype(BF)
        rl_ref[0, :, lanes] = inverse


def attend(info, q, kv, start):
    rows, span, _ = q.shape
    length = kv.shape[1]
    keys = min(512, length)
    own = lambda r, h, info: (r, 0, h)
    spec = pltpu.PrefetchScalarGridSpec(
        num_scalar_prefetch=1,
        grid=(rows, KVH),
        in_specs=[
            pl.BlockSpec((1, span, GW), own),
            pl.BlockSpec((1, length, LANES), own),
            pl.BlockSpec((1, span, LANES), lambda r, h, info: (r, 0, 0)),
        ],
        out_specs=[pl.BlockSpec((1, span, GW), own), pl.BlockSpec((1, span, GW), own)],
        scratch_shapes=[pltpu.VMEM((GW // HD, span, LANES), F32)],
    )
    return pl.pallas_call(
        functools.partial(attend_kernel, keys),
        grid_spec=spec,
        out_shape=[jax.ShapeDtypeStruct(q.shape, BF), jax.ShapeDtypeStruct(q.shape, F32)],
        compiler_params=params(axes=2),
        cost_estimate=pl.CostEstimate(
            flops=16 * rows * H * span * length * HD,
            bytes_accessed=rows * (length * 1280 + span * QW * 8),
            transcendentals=rows * H * span * length,
        ),
        name="attend",
    )(info, q, kv, start)


def attend_back_kernel(
    keys, n, q_ref, kv_ref, qa_ref, ka_ref, do_ref, ctx_ref, rl_ref, a_ref, w_any, base_any,
    gout_any, dq_ref, dkv_ref, o_ref, share_ref, acc, sides, gout_ref, moves, *scratch,
):
    span = q_ref.shape[1]
    per = keys // span
    length = kv_ref.shape[1]
    me = lax.axis_index("mp")
    rows = o_ref.shape[0]
    now = pl.program_id(0) * KVH + pl.program_id(1)
    sums = TileSum(n, me, o_ref, w_any, scratch, base_any)
    half_w = share_ref.shape[1] // 2
    outs = make_scatter(
        n, me, lambda ref, h: ref.at[:, pl.ds(h * half_w, half_w)], scratch[-6:]
    )

    def out_term(k):
        return gout_any.at[flip(me, k)] if k % 2 else gout_ref.at[k // 2]

    def bring(k):
        return pltpu.make_async_copy(gout_any.at[flip(me, k)], out_term(k), moves.at[k // 2])

    def out_event(i):
        if i == 0:
            for k in range(0, n, 2):
                bring(k).start()
            for k in range(n - 1, 0, -2):
                outs.odd(k, out_term(k))
        elif i < n // 2:
            k = n - 2 * i
            bring(k).wait()
            outs.even(k, out_term(k))
        else:
            bring(0).wait()
            outs.own(out_term(0), share_ref)

    batch = a_ref.shape[1]
    steps = rows * n // batch

    @pl.when(now == 0)
    def _():
        sums.start()

    @pl.when(now < steps)
    def _():
        @pl.loop(0, batch)
        def _(i):
            tile = now * batch + i
            _, slot = tile_at(tile, n)
            sums.step(tile, a_ref.at[0, lax.rem(xor_of(me, slot, n), batch)])

    count = n // 2 + 1
    for i in range(count):
        when = 1 + i if i < 2 else 5 + (i - 2) * 4 // (count - 2)

        @pl.when(now == (when if i < count - 1 else rows * KVH - 1))
        def _(i=i):
            out_event(i)

    lane = lax.broadcasted_iota(jnp.int32, (span, LANES), 1)
    low_q = lane < HD
    low_k = lax.broadcasted_iota(jnp.int32, (keys, LANES), 1) < HD
    one = jnp.ones((keys, LANES), BF)
    for h in range(GW // HD):
        lanes = slice((h // 2) * LANES, (h // 2 + 1) * LANES)
        mine = low_q if h % 2 == 0 else jnp.logical_not(low_q)
        scaled = do_ref[0, :, lanes].astype(F32) * rl_ref[0, :, lanes]
        own = jnp.where(mine, scaled, 0.0)
        delta = -jnp.sum(own * ctx_ref[0, :, lanes].astype(F32), axis=1, keepdims=True)
        one_part = delta.astype(BF).astype(F32)
        two_part = (delta - one_part).astype(BF).astype(F32)
        three_part = delta - one_part - two_part
        base = HD if h % 2 == 0 else 0
        extra = jnp.where(
            lane == base,
            one_part,
            jnp.where(lane == base + 1, two_part, jnp.where(lane == base + 2, three_part, 0.0)),
        )
        query = q_ref[0, :, lanes].astype(F32)
        sides[0, h] = jnp.where(mine, query, 0.0).astype(BF)
        sides[1, h] = own.astype(BF)
        sides[2, h] = jnp.where(mine, scaled, extra).astype(BF)
        sides[3, h] = jnp.where(mine, query, qa_ref[0].astype(F32)).astype(BF)
    acc[...] = jnp.zeros_like(acc)

    def block(g, masked):
        here = pl.ds(pl.multiple_of(g * keys, keys), keys)
        kv = kv_ref[0, here, :]
        ka = ka_ref[0, here, :]
        vk = jnp.concatenate([kv[:, HD:], kv[:, :HD]], axis=1)
        key_sides = (jnp.where(low_k, kv, ka), jnp.where(low_k, ka, vk))
        value_sides = (jnp.where(low_k, vk, one), jnp.where(low_k, one, kv))
        if masked:
            position = g * keys + lax.broadcasted_iota(jnp.int32, (keys, span), 0)
            seen = position <= me * span + lax.broadcasted_iota(jnp.int32, (keys, span), 1)
        turned = [s.T for s in key_sides]
        grad_key = grad_value = 0.0
        for h in range(GW // HD):
            e = jnp.exp2(dg(key_sides[h % 2], sides[3, h], NT))
            if masked:
                e = jnp.where(seen, e, 0.0)
            ds = (e * dg(value_sides[h % 2], sides[2, h], NT)).astype(BF)
            grad_value = grad_value + mm(e.astype(BF), sides[1, h])
            grad_key = grad_key + mm(ds, sides[0, h])
            acc[h] += mm(turned[h % 2], ds)
        grad_key = (grad_key + pltpu.roll(grad_key, HD, 1)) * LN2
        grad_value = grad_value + pltpu.roll(grad_value, HD, 1)
        dkv_ref[0, here, :] = jnp.where(low_k, grad_key, grad_value).astype(BF)

    last = lax.div(me, per)

    @pl.loop(0, last)
    def _(g):
        block(g, False)

    block(last, True)

    @pl.loop(last + 1, length // keys)
    def _(g):
        dkv_ref[0, pl.ds(pl.multiple_of(g * keys, keys), keys), :] = jnp.zeros((keys, LANES), BF)

    for pair in range(GW // LANES):
        lanes = slice(pair * LANES, (pair + 1) * LANES)
        dq_ref[0, :, lanes] = jnp.where(low_q, acc[2 * pair].T, acc[2 * pair + 1].T) * (HD**-0.5)

    @pl.when(now == rows * KVH - 1)
    def _():
        sums.end()
        outs.drain(out_term(0))


def attend_back(n, q, kv, qa, ka, do, ctx, rl, a, w, base, gout):
    rows, span, _ = q.shape
    length = kv.shape[1]
    keys = min(512, length)
    depth, width = w.shape
    batch = n // 4
    own = lambda r, h: (r, 0, h)

    def place(r, h):
        row, slot = tile_at(jnp.minimum(r * KVH + h, rows * n // batch - 1) * batch, n)
        return (row, lax.div(xor_of(lax.axis_index("mp"), slot, n), batch), 0, 0)

    return pl.pallas_call(
        functools.partial(attend_back_kernel, keys, n),
        grid=(rows, KVH),
        in_specs=[
            pl.BlockSpec((1, span, GW), own),
            pl.BlockSpec((1, length, LANES), own),
            pl.BlockSpec((1, span, LANES), lambda r, h: (r, 0, 0)),
            pl.BlockSpec((1, length, LANES), lambda r, h: (r, 0, 0)),
            pl.BlockSpec((1, span, GW), own),
            pl.BlockSpec((1, span, GW), own),
            pl.BlockSpec((1, span, GW), own),
            pl.BlockSpec((1, batch, span, depth), place),
            pl.BlockSpec(memory_space=pl.ANY),
            pl.BlockSpec(memory_space=pl.ANY),
            pl.BlockSpec(memory_space=pl.ANY),
        ],
        out_specs=[
            pl.BlockSpec((1, span, GW), own),
            pl.BlockSpec((1, length, LANES), own),
            pl.BlockSpec(memory_space=pltpu.VMEM),
            pl.BlockSpec(memory_space=pltpu.VMEM),
        ],
        out_shape=[
            jax.ShapeDtypeStruct(q.shape, F32),
            jax.ShapeDtypeStruct(kv.shape, BF),
            jax.ShapeDtypeStruct((rows, span, width), F32),
            jax.ShapeDtypeStruct(gout.shape[1:], BF),
        ],
        scratch_shapes=[
            pltpu.VMEM((GW // HD, LANES, span), F32),
            pltpu.VMEM((4, GW // HD, span, LANES), BF),
            pltpu.VMEM((n // 2,) + gout.shape[1:], BF),
            pltpu.SemaphoreType.DMA((n // 2,)),
        ]
        + tile_scratch(n, rows, span, w)
        + scatter_scratch(n, gout.shape[1:], (gout.shape[1], width // 2)),
        compiler_params=params(mib=60, axes=2, key=4),
        cost_estimate=TINY,
        name="attend_back",
    )(q, kv, qa, ka, do, ctx, rl, a, w, base, gout)


def xor_of(a, b, n):
    total, bit = 0, 1
    while bit < n:
        total = total + bit * lax.rem(lax.div(a, bit) + lax.div(b, bit), 2)
        bit *= 2
    return total


def feed_kernel(
    n, live_ref, x_own, g_ref, g_any, gu_any, dt_any,
    x_all, hid_ref, dgu_ref, gd_any,
    x_vm, gu_ref, dt_ref, d_sum, out_d, g_two, back, x_send, x_recv, loads, stores, keep,
):
    me = lax.axis_index("mp")
    rows, span, width = x_own.shape
    slots = gu_ref.shape[0]
    r, p = pl.program_id(0), pl.program_id(1)
    pairs = n // 2
    now = r * pairs + p
    half = span // 2

    def gather(row):
        def slot(i, h, k):
            at = lax.rem(flip(me, k), 2) * span + h * half
            return x_vm.at[row, i // 2, pl.ds(pl.multiple_of(at, half), half)]

        return Gather(
            n,
            me,
            lambda h: x_own.at[row, pl.ds(h * half, half)],
            slot,
            x_send.at[row],
            x_recv.at[row],
            True,
        )

    def own_copy(row):
        at = pl.ds(pl.multiple_of(lax.rem(me, 2) * span, span), span)
        return pltpu.make_async_copy(x_own.at[row], x_vm.at[row, 0, at], loads.at[2 + row])

    fetch = [
        pltpu.make_async_copy(gu_any, gu_ref, loads.at[0]),
        pltpu.make_async_copy(dt_any, dt_ref, loads.at[1]),
    ]

    def events(row, upto):
        todo = gather(row).even
        ends = [0] * pairs
        for i in range(1, pairs):
            ends[i] = max(ends[i - 1], 1 + max(j for j, e in enumerate(todo) if e[0] == 2 * i))
        return todo[ends[upto - 1] if upto else 0 : ends[upto]]

    def ahead(i):
        block = lax.div(xor_of(me, 2 * lax.rem(i, pairs), n), 2)
        to = lax.rem(i, 2)
        return pltpu.make_async_copy(
            g_any.at[lax.div(i, pairs), block], g_two.at[to], loads.at[2 + rows + to]
        )

    @pl.when(now == 0)
    def _():
        for row in range(rows):
            own_copy(row).start()
        for c in fetch:
            c.start()
        greet(n, me)
        gather(0).start()
        ahead(0).start()
        d_sum[...] = jnp.zeros_like(d_sum)
        own_copy(0).wait()
        for c in fetch:
            c.wait()

        @pl.loop(0, rows * pairs)
        def _(i):
            @pl.when(i + 1 < rows * pairs)
            def _():
                ahead(i + 1).start()

            ahead(i).wait()
            back[i] = mm(g_two[lax.rem(i, 2)], dt_ref[...]).astype(BF)

            @pl.when(i == rows * pairs - 2)
            def _():
                for e in gather(0).even[:2]:
                    gather(0).forward(*e)
                for row in range(1, rows):
                    gather(row).start()

    for row in range(rows):
        for i in range(pairs):

            @pl.when(now == row * pairs + i)
            def _(row=row, i=i):
                if i == 0 and row:
                    own_copy(row).wait()
                for e in events(row, i):
                    if row or e not in gather(0).even[:2]:
                        gather(row).forward(*e)
                for h in (0, 1):
                    gather(row).arrive(2 * i + 1, h)

    def save(row, i):
        block = lax.div(xor_of(me, 2 * i, n), 2)
        return pltpu.make_async_copy(x_vm.at[row, i], x_all.at[row, block], keep.at[row, i])

    save(r, p).start()
    x = x_vm.at[r, p]
    for t in range(slots):
        both = mm(x[...], gu_ref[t])
        gate, upper = both[:, :TILE], both[:, TILE:]
        live = live_ref[t]
        sig = jax.nn.sigmoid(gate)
        silu = gate * sig
        gh = back[now, :, t * TILE : (t + 1) * TILE].astype(F32) * live
        hid_ref[0, 0, :, t * TILE : (t + 1) * TILE] = (silu * upper * live).astype(BF)
        dgu_ref[0, 0, :, 2 * t * TILE : (2 * t + 1) * TILE] = (
            gh * upper * (sig * (1.0 + gate * (1.0 - sig)))
        ).astype(BF)
        dgu_ref[0, 0, :, (2 * t + 1) * TILE : (2 * t + 2) * TILE] = (gh * silu).astype(BF)

    cut = LANES

    @pl.loop(0, slots * TILE // cut)
    def _(i):
        at = pl.ds(pl.multiple_of(i * cut, cut), cut)
        d_sum[at, :] += dg(hid_ref[0, 0, :, at], g_ref[0, 0], TN)

    @pl.when(now == rows * pairs - 1)
    def _():
        def store(t):
            return pltpu.make_async_copy(out_d.at[t % 2], gd_any.at[t], stores.at[t % 2])

        for t in range(slots):
            if t > 1:
                store(t - 2).wait()
            out_d[t % 2] = d_sum[t * TILE : (t + 1) * TILE, :].astype(BF)
            store(t).start()
        for t in range(max(slots - 2, 0), slots):
            store(t).wait()
        for row in range(rows):
            for i in range(pairs):
                save(row, i).wait()
        for row in range(rows):
            gather(row).drain()


def feed(n, live, x, g, gu, dt):
    rows, span, width = x.shape
    slots = gu.shape[0]
    hbm = pl.BlockSpec(memory_space=pl.ANY)
    pairs = n // 2

    g = g.reshape(rows, pairs, 2 * span, width)

    def place(r, p):
        return (r, lax.div(xor_of(lax.axis_index("mp"), 2 * p, n), 2), 0, 0)

    return pl.pallas_call(
        functools.partial(feed_kernel, n),
        grid=(rows, pairs),
        in_specs=[
            pl.BlockSpec(memory_space=pltpu.SMEM),
            hbm,
            pl.BlockSpec((1, 1, 2 * span, width), place),
            hbm,
            hbm,
            hbm,
        ],
        out_specs=[
            hbm,
            pl.BlockSpec((1, 1, 2 * span, slots * TILE), place),
            pl.BlockSpec((1, 1, 2 * span, 2 * slots * TILE), place),
            hbm,
        ],
        out_shape=[
            jax.ShapeDtypeStruct((rows, pairs, 2 * span, width), BF),
            jax.ShapeDtypeStruct((rows, pairs, 2 * span, slots * TILE), BF),
            jax.ShapeDtypeStruct((rows, pairs, 2 * span, 2 * slots * TILE), BF),
            jax.ShapeDtypeStruct((slots, TILE, width), BF),
        ],
        scratch_shapes=[
            pltpu.VMEM((rows, pairs, 2 * span, width), BF),
            pltpu.VMEM(gu.shape, BF),
            pltpu.VMEM(dt.shape, BF),
            pltpu.VMEM((slots * TILE, width), F32),
            pltpu.VMEM((2, TILE, width), BF),
            pltpu.VMEM((2, 2 * span, width), BF),
            pltpu.VMEM((rows * pairs, 2 * span, slots * TILE), BF),
            pltpu.SemaphoreType.DMA((rows, n, 2)),
            pltpu.SemaphoreType.DMA((rows, n, 2)),
            pltpu.SemaphoreType.DMA((4 + rows,)),
            pltpu.SemaphoreType.DMA((2,)),
            pltpu.SemaphoreType.DMA((rows, pairs)),
        ],
        compiler_params=params(mib=62, axes=2, key=1),
        cost_estimate=pl.CostEstimate(
            flops=2 * 6 * rows * n * span * slots * TILE * width,
            bytes_accessed=6 * rows * n * span * width + 6 * slots * TILE * width,
            transcendentals=rows * n * span * slots * TILE,
        ),
        name="feed",
    )(live, x, g, g, gu, dt)


def pick(index, table):
    total = 0
    for i, v in enumerate(table):
        total = total + v * jnp.where(index == i, 1, 0)
    return total


def tile_at(now, n):
    unit = n // 4
    at = lax.div(now, unit)
    row = pick(at, (0, 1, 0, 0, 1, 1, 0, 1))
    return row, pick(at, (3, 3, 2, 1, 2, 1, 0, 0)) * unit + unit - 1 - lax.rem(now, unit)


class TileSum:
    def __init__(self, n, me, o_ref, w_any, scratch, base=None):
        self.n, self.me, self.o_ref, self.w_any, self.base = n, me, o_ref, w_any, base
        self.w_ref, self.terms, self.core, self.link = scratch[:4]
        self.sems, self.load = scratch[4:8], scratch[8]
        self.rows, self.span, _ = o_ref.shape

    def scatter(self, row):
        half = self.span // 2
        return Scatter(
            self.n,
            self.me,
            lambda ref, h: ref.at[pl.ds(h * half, half)],
            lambda i: self.core.at[row, i],
            lambda h, i: self.link.at[row, h, i],
            tuple(s.at[row] for s in self.sems),
        )

    def start(self, meet=greet):
        fetch = [pltpu.make_async_copy(self.w_any, self.w_ref, self.load.at[0])]
        if self.base is not None:
            fetch.append(pltpu.make_async_copy(self.base, self.o_ref, self.load.at[1]))
        for c in fetch:
            c.start()
        meet(self.n, self.me)
        for c in fetch:
            c.wait()

    def close(self, row):
        last = self.scatter(row)
        for h in (0, 1):
            here = last.part(self.o_ref.at[row], h)
            joined = [here]
            for i in last.addends(0, h):
                last.link_copy(i, h).wait_recv()
                joined.append(last.link(h, i // 2 - 1))
            add_up(here, joined)

    def step(self, now, a_ref):
        n, terms = self.n, self.terms
        r, k = tile_at(now, n)

        @pl.when(now == 2 * n - n // 4)
        def _():
            self.close(0)

        for i in range(1, n, 2):

            @pl.when((r > 0) & (k == i))
            def _(i=i):
                self.scatter(r - 1).core_copy(i, terms.at[i // 2]).wait_send()

        at = lax.rem(k, 2) * lax.div(k, 2) + (1 - lax.rem(k, 2)) * (n // 2)
        terms[at] = mm(a_ref[...], self.w_ref[...]).astype(BF)
        mine = terms.at[n // 2]
        sums = self.scatter(r)
        for i in range(1, n):

            @pl.when(k == i)
            def _(i=i):
                if i % 2:
                    sums.odd(i, terms.at[i // 2])
                else:
                    sums.even(i, mine)

        @pl.when(k == 0)
        def _():
            sums.core_copy(1, self.core.at[r, 0]).wait_recv()
            here = self.o_ref.at[r]
            add_up(here, [mine, self.core.at[r, 0]] + ([] if self.base is None else [here]))

    def end(self):
        self.close(self.rows - 1)
        self.scatter(self.rows - 1).drain(self.terms.at[self.n // 2])
        for row in range(self.rows - 1):
            for i in range(2, self.n, 2):
                for h in (0, 1):
                    self.scatter(row).link_copy(i, h).wait_send()


def tile_scratch(n, rows, span, w):
    width = w.shape[1]
    return [
        pltpu.VMEM(w.shape, BF),
        pltpu.VMEM((n // 2 + 1, span, width), BF),
        pltpu.VMEM((rows, n // 2, span, width), BF),
        pltpu.VMEM((rows, 2, n // 2 - 1, span // 2, width), BF),
        pltpu.SemaphoreType.DMA((rows, n // 2)),
        pltpu.SemaphoreType.DMA((rows, n // 2)),
        pltpu.SemaphoreType.DMA((rows, 2, n // 2 - 1)),
        pltpu.SemaphoreType.DMA((rows, 2, n // 2 - 1)),
        pltpu.SemaphoreType.DMA((2,)),
    ]


def spread_kernel(
    n, m, a_ref, w_any, x_ref, b_ref, d_any,
    o_ref, grad_ref, total_any,
    acc, own, up, across, line_sems, moves, *scratch,
):
    me, line = lax.axis_index("mp"), lax.axis_index("dp")
    rows = o_ref.shape[0]
    now = pl.program_id(0) * n + pl.program_id(1)
    per = rows * n // BLOCKS
    sums = TileSum(n, me, o_ref, w_any, scratch)
    chunks = own.shape[0]
    at = lambda ref: lambda c: ref.at[c]
    down = Line(m, line, at(own), at(up), at(across), at(up), line_sems)
    bring = pltpu.make_async_copy(d_any, own, moves.at[0])
    send = pltpu.make_async_copy(up, total_any, moves.at[1])

    @pl.when(now == 0)
    def _():
        bring.start()
        sums.start(lambda n, me: greet_all(n, me, m, line))
        bring.wait()
        for c in range(chunks):
            down.launch(c)

    sums.step(now, a_ref.at[0, 0])
    for c in range(chunks):

        @pl.when(now == 1 + c)
        def _(c=c):
            down.inward(c)

        @pl.when(now == 3 + c)
        def _(c=c):
            down.outward(c)

    k = lax.rem(now, per)
    term = dg(x_ref[...], b_ref[...], TN)

    @pl.when(k == 0)
    def _():
        acc[...] = term

    @pl.when((k > 0) & (k < per - 1))
    def _():
        acc[...] += term

    @pl.when(k == per - 1)
    def _():
        done = acc[...] + term
        for t in range(grad_ref.shape[0]):
            grad_ref[t] = done[:, 2 * t * TILE : 2 * (t + 1) * TILE].astype(BF)

    @pl.when(now == rows * n - 1)
    def _():
        for c in range(chunks):
            down.drain(c)
        send.start()
        sums.end()
        send.wait()


BLOCKS = 4
CHUNKS = 12


def spread(n, m, a, w, x, down):
    rows, _, span, depth = a.shape
    width = w.shape[1]
    slots = depth // (2 * TILE)
    everything = rows * n * span
    per = rows * n // BLOCKS
    part, block = everything // per, width // BLOCKS
    flat = (slots * TILE // CHUNKS, width)

    def place(r, j):
        row, slot = tile_at(r * n + j, n)
        return (row, xor_of(lax.axis_index("mp"), slot, n), 0, 0)

    def token(r, j):
        return lax.rem(r * n + j, per)

    def column(r, j):
        return lax.div(r * n + j, per)

    hbm = pl.BlockSpec(memory_space=pl.ANY)
    out, grad, total = pl.pallas_call(
        functools.partial(spread_kernel, n, m),
        grid=(rows, n),
        in_specs=[
            pl.BlockSpec((1, 1, span, depth), place),
            hbm,
            pl.BlockSpec((part, block), lambda r, j: (token(r, j), column(r, j))),
            pl.BlockSpec((part, depth), lambda r, j: (token(r, j), 0)),
            hbm,
        ],
        out_specs=[
            pl.BlockSpec(memory_space=pltpu.VMEM),
            pl.BlockSpec((slots, block, 2 * TILE), lambda r, j: (0, column(r, j), 0)),
            hbm,
        ],
        out_shape=[
            jax.ShapeDtypeStruct((rows, span, width), F32),
            jax.ShapeDtypeStruct((slots, width, 2 * TILE), BF),
            jax.ShapeDtypeStruct((CHUNKS,) + flat, BF),
        ],
        scratch_shapes=[
            pltpu.VMEM((block, depth), F32),
            pltpu.VMEM((CHUNKS,) + flat, BF),
            pltpu.VMEM((CHUNKS,) + flat, BF),
            pltpu.VMEM((CHUNKS,) + flat, BF),
            pltpu.SemaphoreType.DMA((6, CHUNKS)),
            pltpu.SemaphoreType.DMA((2,)),
        ]
        + tile_scratch(n, rows, span, w),
        compiler_params=params(mib=63, axes=2, key=3),
        cost_estimate=TINY,
        name="spread",
    )(
        a,
        w,
        x.reshape(everything, width),
        a.reshape(everything, depth),
        down.reshape((CHUNKS,) + flat),
    )
    return out, grad, total.reshape(down.shape)


def shards(
    n,
    m,
    hidden_in,
    doc_ids,
    tile_slot,
    attention_gain,
    query_gain,
    key_gain,
    attend_weight,
    output_weight,
    feed_gain,
    gate_up_slots,
    down_slots,
    out_grad,
):
    rows, span, width = hidden_in.shape
    length = doc_ids.shape[1]
    slots = gate_up_slots.shape[0]
    tokens = rows * span
    me = lax.axis_index("mp")
    offset = me * span

    kw = KVH * HD
    keys_w = attend_weight[:, QW : QW + kw].reshape(-1, KVH, HD)
    values_w = attend_weight[:, QW + kw :].reshape(-1, KVH, HD)
    attend_w = jnp.concatenate(
        [attend_weight[:, :QW], jnp.concatenate([keys_w, values_w], 2).reshape(-1, 2 * kw)], 1
    )
    starts = doc_starts(doc_ids)
    local_start = lax.dynamic_slice_in_dim(starts, offset, span, 1)
    local_pos = offset + jnp.arange(span, dtype=jnp.int32)[None] - local_start
    cos, sin = rotary_tables(local_pos.reshape(tokens))
    gq = jnp.tile(query_gain, 2)[None]
    gk = jnp.concatenate([key_gain, jnp.ones_like(key_gain)])[None]
    lane = jnp.arange(LANES) // HD
    ones = (lane[:, None] == lane[None, :]).astype(BF)
    key_block = min(512, length)
    info = jnp.stack(
        [
            jnp.full((rows,), me, jnp.int32),
            local_start[:, 0] // key_block,
            local_start[:, -1],
        ],
        1,
    ).astype(jnp.int32)
    start_col = jnp.broadcast_to(local_start[:, :, None], (rows, span, LANES))
    document = jnp.arange(LANES) % HD
    member = (doc_ids[:, :, None] == document).astype(F32)
    ka = jnp.where(document == DOCS, 1.0, member).astype(BF)
    own_member = lax.dynamic_slice_in_dim(member, offset, span, 1)
    qa = jnp.where(document == DOCS, -AWAY, own_member * AWAY).astype(BF)

    x_own = hidden_in.reshape(tokens, width)
    x_value = x_own.astype(F32)
    normed_ab, raw, q, grad_branch, attend_all, kv_all, output_all = project(
        n,
        rows,
        x_own,
        attention_gain[None],
        attend_w,
        output_weight,
        cos,
        sin,
        gq,
        gk,
        ones,
        out_grad.reshape(tokens, width),
    )
    q = q.reshape(rows, span, QW)
    kv_all = kv_all.reshape(rows, length, -1)
    output_full = output_all.reshape(QW, width)
    grads_all = lax.all_gather(
        grad_branch.reshape(rows, span, width), "mp", axis=1, tiled=True
    )
    ctx, rl = attend(info, q, kv_all, start_col)
    context_b = ctx.reshape(tokens, QW)
    middle = x_value + mm(context_b, output_full)
    scale_f = rms_scale(middle)
    normed_fb = (middle * scale_f * feed_gain).astype(BF).reshape(rows, span, width)

    slot_index = me * slots + jnp.arange(slots, dtype=jnp.int32)
    live = jnp.any(tile_slot[None, :] == slot_index[:, None], axis=1).astype(F32)
    gate_up_slots, down_slots, middle = lax.optimization_barrier(
        (gate_up_slots, down_slots, middle)
    )
    middle, qa, ka = lax.optimization_barrier((middle, qa, ka))
    gu_t = jnp.swapaxes(gate_up_slots, 1, 2).reshape(slots * 2 * TILE, width)
    d_flat = down_slots.reshape(slots * TILE, width)
    d_t = d_flat.T
    normed_all, hidden, grad_both, grad_down = feed(
        n, live, normed_fb, grads_all, gate_up_slots, d_t
    )
    hidden = hidden.reshape(rows, n, span, -1)
    grad_normed_f, grad_gate_up, down_total = spread(
        n, m, grad_both.reshape(rows, n, span, -1), gu_t, normed_all, grad_down
    )
    gate_up_total = lax.psum(grad_gate_up, "dp")
    grad_normed_f = grad_normed_f.reshape(tokens, width)

    weighted = grad_normed_f * feed_gain
    inner = jnp.mean(weighted * middle, axis=-1, keepdims=True)
    gain_feed = jnp.sum(grad_normed_f * middle * scale_f, axis=0)
    grad_middle = out_grad.reshape(tokens, width) + scale_f * (
        weighted - middle * scale_f * scale_f * inner
    )
    grad_attn_b = grad_middle.astype(BF)
    grad_context = dg(grad_attn_b, output_full, NT).astype(BF).reshape(rows, span, QW)
    grad_output = dg(context_b, grad_attn_b, TN).astype(BF)

    dq, dkv, layer_out, output_share = attend_back(
        n,
        q,
        kv_all,
        qa,
        ka,
        grad_context,
        ctx,
        rl,
        hidden,
        d_flat,
        middle.reshape(rows, span, width),
        grad_output.reshape(n, -1, width),
    )
    grad_joined_b, sum_q, sum_k, down_total = unproject(
        n,
        dq.reshape(tokens, QW),
        dkv.reshape(rows, n, span, -1),
        raw,
        cos,
        sin,
        gq,
        gk,
        ones,
        down_total.reshape(slots * TILE, width),
    )
    sums = jnp.concatenate(
        [
            jnp.zeros((width // LANES, LANES), F32),
            gain_feed.reshape(-1, LANES),
            sum_q[:1],
            sum_k[:1],
            jnp.zeros((GAIN_ROWS - 2 * (width // LANES) - 2, LANES), F32),
        ]
    )
    input_grad, attend_total, output_total, gains = finish(
        n,
        m,
        normed_ab,
        grad_joined_b,
        attend_all,
        x_own,
        grad_middle,
        attention_gain[None],
        output_share,
        sums,
    )
    gains = gains.reshape(-1)
    gain_query = gains[2 * width : 2 * width + HD] + gains[2 * width + HD : 2 * width + 2 * HD]
    gain_key = gains[2 * width + LANES : 2 * width + LANES + HD]
    shape = (rows, span, width)
    return (
        layer_out,
        input_grad.reshape(shape),
        attend_total,
        output_total,
        gate_up_total.astype(F32),
        down_total.reshape(slots, TILE, width),
        gains[:width],
        gain_query,
        gain_key,
        gains[width : 2 * width],
    )


def solution(mesh):
    placed = (
        P("dp", "mp", None),
        P("dp", None),
        P(),
        P(),
        P(),
        P(),
        P("mp", None),
        P("mp", None),
        P(),
        P("mp", None, None),
        P("mp", None, None),
        P("dp", "mp", None),
    )
    return jax.shard_map(
        functools.partial(shards, mesh.shape["mp"], mesh.shape["dp"]),
        mesh=mesh,
        in_specs=placed,
        out_specs=(
            P("dp", "mp", None),
            P("dp", "mp", None),
            P("mp", None),
            P("mp", None),
            P("mp", None, None),
            P("mp", None, None),
            P(),
            P(),
            P(),
            P(),
        ),
        check_vma=False,
    )
```

```python
import functools

import jax
import jax.numpy as jnp
import numpy as np
from jax import lax
from jax.experimental import pallas as pl
from jax.experimental.pallas import tpu as pltpu
from jax.sharding import PartitionSpec as P

H = 20
KVH = 5
HD = 64
TILE = 128
EPSILON = 1e-06
QW = H * HD
LANES = 128
GW = (H // KVH) * HD
DOCS = 3
AWAY = 256.0
LOG2E = 1.4426950408889634
LN2 = 0.6931471805599453
BF = jnp.bfloat16
F32 = jnp.float32
MIB = 1 << 20
NT = (((1,), (1,)), ((), ()))
TN = (((0,), (0,)), ((), ()))


def params(mib=56, axes=1, key=None):
    if key is None:
        return pltpu.CompilerParams(
            vmem_limit_bytes=mib * MIB, dimension_semantics=("arbitrary",) * axes
        )
    return pltpu.CompilerParams(
        vmem_limit_bytes=mib * MIB,
        dimension_semantics=("arbitrary",) * axes if axes else None,
        collective_id=key,
        has_side_effects=True,
    )


TINY = pl.CostEstimate(flops=1, bytes_accessed=1, transcendentals=0)


def mm(a, b):
    return jnp.dot(a, b, preferred_element_type=F32)


def dg(a, b, dims):
    return lax.dot_general(a, b, dims, preferred_element_type=F32)


def rotary_tables(positions):
    half_dim = HD // 2
    freqs = 1.0 / 10000.0 ** (jnp.arange(half_dim, dtype=jnp.float32) * 2.0 / HD)
    angles = positions.astype(jnp.float32)[..., None] * jnp.tile(freqs, 4)
    return jnp.cos(angles), jnp.sin(angles)


def rms_scale(values):
    return lax.rsqrt(jnp.mean(values * values, axis=-1, keepdims=True) + EPSILON)


MESH = pl.DeviceIdType.MESH


def flip(me, k):
    bit = 1
    while bit <= k:
        if k & bit:
            me = me + bit - 2 * bit * lax.rem(lax.div(me, bit), 2)
        bit *= 2
    return me


def link_bits(n):
    return [1 << i for i in range(1, n.bit_length() - 1)]


def greet(n, me):
    barrier = pltpu.get_barrier_semaphore()
    bits = [1] + link_bits(n)
    for bit in bits:
        pl.semaphore_signal(barrier, inc=1, device_id={"mp": flip(me, bit)}, device_id_type=MESH)
    pl.semaphore_wait(barrier, len(bits))


def greet_all(n, me, m, line):
    barrier = pltpu.get_barrier_semaphore()
    bits = [1] + link_bits(n)
    for bit in bits:
        pl.semaphore_signal(barrier, inc=1, device_id={"mp": flip(me, bit)}, device_id_type=MESH)
    for step in range(1, m):
        other = lax.rem(line + step, m)
        pl.semaphore_signal(barrier, inc=1, device_id={"dp": other}, device_id_type=MESH)
    pl.semaphore_wait(barrier, len(bits) + m - 1)


class Line:
    def __init__(self, m, line, own, up, across, total, sems):
        self.own, self.up, self.across, self.total, self.sems = own, up, across, total, sems
        low = line < m // 2
        self.inner = jnp.where(low, line + 1, line - 1)
        self.outer = jnp.where(low, line - 1, line + 1)
        self.has_outer = (line > 0) & (line < m - 1)
        self.middle = (line == m // 2 - 1) | (line == m // 2)

    def copy(self, kind, c):
        src, dst, to = (
            (self.own, self.up, self.inner),
            (self.own, self.across, self.inner),
            (self.total, self.total, self.outer),
        )[kind]
        return pltpu.make_async_remote_copy(
            src_ref=src(c),
            dst_ref=dst(c),
            send_sem=self.sems.at[2 * kind, c],
            recv_sem=self.sems.at[2 * kind + 1, c],
            device_id={"dp": to},
            device_id_type=MESH,
        )

    def launch(self, c):
        @pl.when(jnp.logical_not(self.has_outer))
        def _():
            self.copy(0, c).start()

    def inward(self, c):
        @pl.when(self.has_outer)
        def _():
            self.copy(0, c).wait_recv()
            add_up(self.own(c), [self.own(c), self.up(c)])

            @pl.when(self.middle)
            def _():
                self.copy(1, c).start()

            @pl.when(jnp.logical_not(self.middle))
            def _():
                self.copy(0, c).start()

    def outward(self, c):
        @pl.when(self.middle)
        def _():
            self.copy(1, c).wait_recv()
            add_up(self.total(c), [self.own(c), self.across(c)])

        @pl.when(jnp.logical_not(self.middle))
        def _():
            self.copy(2, c).wait_recv()

        @pl.when(self.has_outer)
        def _():
            self.copy(2, c).start()

    def drain(self, c):
        @pl.when(self.middle)
        def _():
            self.copy(1, c).wait_send()

        @pl.when(jnp.logical_not(self.middle))
        def _():
            self.copy(0, c).wait_send()

        @pl.when(self.has_outer)
        def _():
            self.copy(2, c).wait_send()


class Gather:
    def __init__(self, n, me, own, slot, send, recv, relative=False):
        self.n, self.me, self.own, self.slot, self.send, self.recv = n, me, own, slot, send, recv
        self.relative = relative
        bits = link_bits(n)
        self.order = (bits + [1], bits[::-1] + [1])
        even = [(k, h) for k in range(2, n, 2) for h in (0, 1)]
        even.sort(key=lambda kh: (bin(kh[0]).count("1"), max(self.place(*kh)), kh[1]))
        self.even = even

    def place(self, k, half):
        return [i for i, bit in enumerate(self.order[half]) if k & bit]

    def copy(self, k, half, bit):
        return pltpu.make_async_remote_copy(
            src_ref=self.own(half) if k == 0 else self.here(k, half),
            dst_ref=self.slot(k ^ bit, half, k) if self.relative else self.slot(k, half),
            send_sem=self.send.at[k ^ bit, half],
            recv_sem=self.recv.at[k ^ bit, half],
            device_id={"mp": flip(self.me, bit)},
            device_id_type=MESH,
        )

    def here(self, k, half):
        return self.slot(k, half, k) if self.relative else self.slot(k, half)

    def onward(self, k, half):
        return self.order[half][(max(self.place(k, half)) + 1) if k else 0 :]

    def start(self):
        for i in range(len(self.order[0])):
            for half in (0, 1):
                self.copy(0, half, self.order[half][i]).start()

    def arrive(self, k, half):
        here = self.here(k, half)
        pltpu.make_async_remote_copy(
            src_ref=here,
            dst_ref=here,
            send_sem=self.send.at[k, half],
            recv_sem=self.recv.at[k, half],
            device_id={"mp": flip(self.me, 1)},
            device_id_type=MESH,
        ).wait_recv()

    def forward(self, k, half):
        self.arrive(k, half)
        for bit in self.onward(k, half):
            self.copy(k, half, bit).start()

    def rest(self):
        for k, half in [(1, 0), (1, 1)] + [(k + 1, h) for k, h in self.even]:
            self.arrive(k, half)

    def drain(self):
        for k in range(0, self.n, 2):
            for half in (0, 1):
                for bit in self.onward(k, half):
                    self.copy(k, half, bit).wait_send()


class Scatter:
    def __init__(self, n, me, part, core, link, sems):
        self.n, self.me, self.part = n, me, part
        self.core, self.link = core, link
        self.core_send, self.core_recv, self.link_send, self.link_recv = sems
        bits = link_bits(n)
        self.order = (bits[::-1], bits)

    def first(self, k, half):
        return next(i for i, bit in enumerate(self.order[half]) if k & bit)

    def core_copy(self, k, ref):
        return pltpu.make_async_remote_copy(
            src_ref=ref,
            dst_ref=self.core(k // 2),
            send_sem=self.core_send.at[k // 2],
            recv_sem=self.core_recv.at[k // 2],
            device_id={"mp": flip(self.me, 1)},
            device_id_type=MESH,
        )

    def link_copy(self, k, half):
        bit = self.order[half][self.first(k, half)]
        return pltpu.make_async_remote_copy(
            src_ref=self.part(self.core(k // 2), half),
            dst_ref=self.link(half, k // 2 - 1),
            send_sem=self.link_send.at[half, k // 2 - 1],
            recv_sem=self.link_recv.at[half, k // 2 - 1],
            device_id={"mp": flip(self.me, bit)},
            device_id_type=MESH,
        )

    def addends(self, k, half):
        upto = self.first(k, half) if k else len(self.order[half])
        return [k | bit for bit in self.order[half][:upto]]

    def odd(self, k, ref):
        self.core_copy(k, ref).start()

    def even(self, k, ref):
        self.core_copy(k + 1, self.core(k // 2)).wait_recv()
        for half in sorted((0, 1), key=lambda h: -len(self.addends(k, h))):
            joined = [self.part(ref, half), self.part(self.core(k // 2), half)]
            for j in self.addends(k, half):
                self.link_copy(j, half).wait_recv()
                joined.append(self.link(half, j // 2 - 1))
            add_up(joined[1], joined)
            self.link_copy(k, half).start()

    def own(self, ref, out):
        self.core_copy(1, self.core(0)).wait_recv()
        for half in (0, 1):
            joined = [self.part(ref, half), self.part(self.core(0), half)]
            for j in self.addends(0, half):
                self.link_copy(j, half).wait_recv()
                joined.append(self.link(half, j // 2 - 1))
            add_up(self.part(out, half), joined)

    def drain(self, ref):
        for k in range(1, self.n, 2):
            self.core_copy(k, ref).wait_send()
        for k in range(2, self.n, 2):
            for half in (0, 1):
                self.link_copy(k, half).wait_send()


def add_up(out, terms):
    rows, width = out.shape[-2:]
    step = 16
    while 2 * step * width <= 32768 and rows % (2 * step) == 0:
        step *= 2
    lead = (slice(None),) * (len(out.shape) - 2)

    @pl.loop(0, rows // step)
    def _(i):
        at = lead + (pl.ds(pl.multiple_of(i * step, step), step), slice(None))
        if len(terms) == 2 and all(t.dtype == BF for t in (out, *terms)):
            out[at] = terms[0][at] + terms[1][at]
        else:
            total = terms[0][at].astype(F32)
            for t in terms[1:]:
                total = total + t[at].astype(F32)
            out[at] = total.astype(out.dtype)


def scatter_scratch(n, shape, half):
    return [
        pltpu.VMEM((n // 2,) + shape, BF),
        pltpu.VMEM((2, n // 2 - 1) + half, BF),
        pltpu.SemaphoreType.DMA((n // 2,)),
        pltpu.SemaphoreType.DMA((n // 2,)),
        pltpu.SemaphoreType.DMA((2, n // 2 - 1)),
        pltpu.SemaphoreType.DMA((2, n // 2 - 1)),
    ]


def make_scatter(n, me, part, refs):
    core, link = refs[:2]
    return Scatter(
        n,
        me,
        part,
        lambda i: core.at[i],
        lambda h, i: link.at[h, i],
        refs[2:6],
    )


def half_turn(x, lane):
    first = (lane % HD) < HD // 2
    return jnp.where(first, -pltpu.roll(x, LANES - HD // 2, 1), pltpu.roll(x, HD // 2, 1))


def half_turn_back(x, lane):
    first = (lane % HD) < HD // 2
    return jnp.where(first, pltpu.roll(x, LANES - HD // 2, 1), -pltpu.roll(x, HD // 2, 1))


def group_mean(x, ones):
    high = x.astype(BF)
    low = (x - high.astype(F32)).astype(BF)
    return (mm(high, ones) + mm(low, ones)) * (1.0 / HD)


def project_kernel(
    n, x_any, gain_ref, w_ref, o_ref, cos_ref, sin_ref, gq_ref, gk_ref, ones_ref, grad_any,
    normed_any, raw_any, q_ref, branch_any, w_out, kv_out, o_out,
    x_ref, grad_ref, normed_ref, raw_ref, branch_ref, moves, w_all, kv_own, w_send, w_recv, kv_send, kv_recv, o_send, o_recv, local,
):
    me = lax.axis_index("mp")
    depth = w_ref.shape[0]
    tokens, width = x_ref.shape
    rows = kv_out.shape[0]
    span = tokens // rows
    half = depth // 2
    own_w = pltpu.make_async_copy(w_ref, w_all.at[me], local.at[0])
    own_w.start()
    early = [
        pltpu.make_async_copy(x_any, x_ref, moves.at[0]),
        pltpu.make_async_copy(grad_any, grad_ref, moves.at[1]),
    ]
    late = [
        pltpu.make_async_copy(normed_ref, normed_any, moves.at[2]),
        pltpu.make_async_copy(branch_ref, branch_any, moves.at[3]),
        pltpu.make_async_copy(raw_ref, raw_any, moves.at[4]),
    ]
    for c in early:
        c.start()
    own_o = pltpu.make_async_copy(o_ref, o_out.at[me], local.at[1 + rows])
    own_o.start()
    greet(n, me)
    wide = o_ref.shape[1] // 2
    outs = Gather(
        n,
        me,
        lambda h: o_ref.at[:, pl.ds(h * wide, wide)],
        lambda k, h: o_out.at[flip(me, k), :, pl.ds(h * wide, wide)],
        o_send,
        o_recv,
    )
    weights = Gather(
        n,
        me,
        lambda h: w_ref.at[pl.ds(h * half, half)],
        lambda k, h: w_all.at[flip(me, k), pl.ds(h * half, half)],
        w_send,
        w_recv,
    )
    weights.start()
    for c in early:
        c.wait()
    step = min(64, tokens)

    @pl.loop(0, tokens // step)
    def _(i):
        at = pl.ds(pl.multiple_of(i * step, step), step)
        x = x_ref[at, :].astype(F32)
        scale = lax.rsqrt(jnp.mean(x * x, axis=-1, keepdims=True) + EPSILON)
        normed_ref[at, :] = (x * scale * gain_ref[...]).astype(BF)
        branch_ref[at, :] = grad_ref[at, :].astype(BF)

    chunk = min(256, tokens)

    def accumulate(k, fresh):
        block = flip(me, k)
        columns = pl.ds(pl.multiple_of(block * depth, depth), depth)

        @pl.loop(0, tokens // chunk)
        def _(i):
            at = pl.ds(pl.multiple_of(i * chunk, chunk), chunk)
            term = mm(normed_ref[at, columns], w_all[block])
            raw_ref[at, :] = term if fresh else raw_ref[at, :] + term

    own_w.wait()
    accumulate(0, True)
    for h in (0, 1):
        weights.arrive(1, h)
    accumulate(1, False)
    for i, (k, h) in enumerate(weights.even):
        weights.forward(k, h)
        if any(k == other for other, _ in weights.even[:i]):
            accumulate(k, False)
    outs.start()
    for k in range(3, n, 2):
        for h in (0, 1):
            weights.arrive(k, h)
        accumulate(k, False)
    out_w = pltpu.make_async_copy(w_all, w_out, local.at[0])
    out_w.start()
    for c in late:
        c.start()

    chunk = min(128, tokens)
    lane = lax.broadcasted_iota(jnp.int32, (chunk, LANES), 1)

    def finish(i, tiles):
        at = pl.ds(pl.multiple_of(i * chunk, chunk), chunk)
        cos, sin = cos_ref[at, :], sin_ref[at, :]
        for tile in tiles:
            lanes = slice(tile * LANES, (tile + 1) * LANES)
            x = raw_ref[at, lanes]
            query = tile < QW // LANES
            scale = lax.rsqrt(group_mean(x * x, ones_ref[...]) + EPSILON)
            v = x * scale * (gq_ref[...] if query else gk_ref[...])
            y = v * cos + half_turn(v, lane) * sin
            if query:
                q_ref[at, lanes] = (y * (HD**-0.5 * LOG2E)).astype(BF)
            else:
                mine = slice(tile * LANES - QW, (tile + 1) * LANES - QW)
                kv_own[at, mine] = jnp.where(lane < HD, y, x).astype(BF)

    count = raw_ref.shape[1] // LANES

    @pl.loop(0, tokens // chunk)
    def _(i):
        finish(i, range(QW // LANES, count))

    both = rows // 2
    keep = [
        pltpu.make_async_copy(
            kv_own.at[pl.ds(r * span, span)], kv_out.at[r, me], local.at[1 + r]
        )
        for r in range(rows)
    ]
    for c in keep:
        c.start()
    kvs = Gather(
        n,
        me,
        lambda h: kv_own.at[pl.ds(h * span, span)],
        lambda k, h: kv_out.at[h, flip(me, k)],
        kv_send,
        kv_recv,
    )
    kvs.start()

    @pl.loop(0, tokens // chunk)
    def _(i):
        finish(i, range(QW // LANES))

    for k, h in kvs.even:
        outs.forward(k, h)
        kvs.forward(k, h)
    outs.rest()
    kvs.rest()
    for c in keep:
        c.wait()
    out_w.wait()
    own_o.wait()
    for c in late:
        c.wait()
    weights.drain()
    outs.drain()
    kvs.drain()


def project(n, rows, x, gain, w, o, cos, sin, gq, gk, ones, grad):
    tokens, width = x.shape
    depth, columns = w.shape
    vmem = pl.BlockSpec(memory_space=pltpu.VMEM)
    hbm = pl.BlockSpec(memory_space=pl.ANY)
    kvw = columns - QW
    return pl.pallas_call(
        functools.partial(project_kernel, n),
        in_specs=[hbm, vmem, hbm, hbm, vmem, vmem, vmem, vmem, vmem, hbm],
        out_specs=[hbm, hbm, vmem, hbm, hbm, hbm, hbm],
        out_shape=[
            jax.ShapeDtypeStruct((tokens, width), BF),
            jax.ShapeDtypeStruct((tokens, columns), F32),
            jax.ShapeDtypeStruct((tokens, QW), BF),
            jax.ShapeDtypeStruct((tokens, width), BF),
            jax.ShapeDtypeStruct((n, depth, columns), BF),
            jax.ShapeDtypeStruct((rows, n, tokens // rows, kvw), BF),
            jax.ShapeDtypeStruct((n,) + o.shape, BF),
        ],
        scratch_shapes=[
            pltpu.VMEM((tokens, width), BF),
            pltpu.VMEM((tokens, width), F32),
            pltpu.VMEM((tokens, width), BF),
            pltpu.VMEM((tokens, columns), F32),
            pltpu.VMEM((tokens, width), BF),
            pltpu.SemaphoreType.DMA((5,)),
            pltpu.VMEM((n, depth, columns), BF),
            pltpu.VMEM((tokens, kvw), BF),
            pltpu.SemaphoreType.DMA((n, 2)),
            pltpu.SemaphoreType.DMA((n, 2)),
            pltpu.SemaphoreType.DMA((n, 2)),
            pltpu.SemaphoreType.DMA((n, 2)),
            pltpu.SemaphoreType.DMA((n, 2)),
            pltpu.SemaphoreType.DMA((n, 2)),
            pltpu.SemaphoreType.DMA((2 + rows,)),
        ],
        compiler_params=params(axes=0, key=0),
        name="project",
    )(x, gain, w, o, cos, sin, gq, gk, ones, grad)


def unproject_kernel(
    n, dq_any, dkv_any, raw_any, cos_ref, sin_ref, gq_ref, gk_ref, ones_ref,
    gj_ref, sq_ref, sk_ref,
    dkv_own, dkv_ref, dq_ref, raw_ref, load, *scratch,
):
    me = lax.axis_index("mp")
    early = [
        pltpu.make_async_copy(dkv_any.at[:, flip(me, k)], dkv_ref.at[k // 2], load.at[2 + k // 2])
        for k in range(n - 2, -1, -2)
    ]
    late = [
        pltpu.make_async_copy(dq_any, dq_ref, load.at[0]),
        pltpu.make_async_copy(raw_any, raw_ref, load.at[1]),
    ]
    for c in early + late:
        c.start()
    greet(n, me)
    tokens = dq_ref.shape[0]
    rows = dkv_any.shape[0]
    span = tokens // rows
    columns = raw_ref.shape[1]
    keys = make_scatter(n, me, lambda ref, h: ref.at[h], scratch[:6])

    def dkv_term(k):
        return dkv_any.at[:, flip(me, k)] if k % 2 else dkv_ref.at[k // 2]

    for k in range(n - 1, 0, -2):
        keys.odd(k, dkv_term(k))
    for c in early:
        c.wait()
    keys.even(n - 2, dkv_term(n - 2))
    for c in late:
        c.wait()

    chunk = min(128, tokens)
    lane = lax.broadcasted_iota(jnp.int32, (chunk, LANES), 1)
    sq_ref[...] = jnp.zeros_like(sq_ref)
    sk_ref[...] = jnp.zeros_like(sk_ref)

    def back(i, tiles, query):
        at = pl.ds(pl.multiple_of(i * chunk, chunk), chunk)
        cos, sin = cos_ref[at, :], sin_ref[at, :]
        total = 0.0
        for tile in tiles:
            lanes = slice(tile * LANES, (tile + 1) * LANES)
            x = raw_ref[at, lanes]
            if query:
                e = dq_ref[at, lanes]
            else:
                per = span // chunk
                here = pl.ds(pl.multiple_of(lax.rem(i, per) * chunk, chunk), chunk)
                e = dkv_own[lax.div(i, per), here, slice(tile * LANES - QW, (tile + 1) * LANES - QW)]
            scale = lax.rsqrt(group_mean(x * x, ones_ref[...]) + EPSILON)
            v = x * scale
            turned = e * cos + half_turn_back(e * sin, lane)
            u = turned * (gq_ref[...] if query else gk_ref[...])
            grad = scale * (u - v * group_mean(u * v, ones_ref[...]))
            gj_ref[at, lanes] = (grad if query else jnp.where(lane < HD, grad, e)).astype(BF)
            total = total + jnp.sum(turned * v, axis=0, keepdims=True)
        sums = sq_ref if query else sk_ref
        sums[...] += jnp.broadcast_to(total, sums.shape)

    count = columns // LANES

    parts = tokens // chunk
    left = list(range(n - 4, 0, -2))
    for i in range(parts):
        back(i, range(QW // LANES), True)
        if i == 0:
            for k in left:
                keys.even(k, dkv_term(k))

    keys.own(dkv_term(0), dkv_own)

    @pl.loop(0, tokens // chunk)
    def _(i):
        back(i, range(QW // LANES, count), False)

    keys.drain(dkv_term(0))


def unproject(n, dq, dkv, raw, cos, sin, gq, gk, ones):
    tokens, columns = raw.shape
    rows = dkv.shape[0]
    span = tokens // rows
    kvw = columns - QW
    vmem = pl.BlockSpec(memory_space=pltpu.VMEM)
    hbm = pl.BlockSpec(memory_space=pl.ANY)
    return pl.pallas_call(
        functools.partial(unproject_kernel, n),
        in_specs=[hbm] * 3 + [vmem] * 5,
        out_specs=[vmem] * 3,
        out_shape=[
            jax.ShapeDtypeStruct((tokens, columns), BF),
            jax.ShapeDtypeStruct((8, LANES), F32),
            jax.ShapeDtypeStruct((8, LANES), F32),
        ],
        scratch_shapes=[
            pltpu.VMEM((rows, span, kvw), F32),
            pltpu.VMEM((n // 2, rows, span, kvw), BF),
            pltpu.VMEM(dq.shape, F32),
            pltpu.VMEM(raw.shape, F32),
            pltpu.SemaphoreType.DMA((2 + n // 2,)),
        ]
        + scatter_scratch(n, (rows, span, kvw), (span, kvw)),
        compiler_params=params(mib=60, axes=0, key=2),
        cost_estimate=TINY,
        name="unproject",
    )(dq, dkv, raw, cos, sin, gq, gk, ones)


GAIN_ROWS = 40


def finish_kernel(
    n, m, normed_any, gj_any, w_any, x_any, mid_any, gain_ref, share_any, sums_ref,
    grad_any, attend_ref, out_ref, gains_ref,
    normed_ref, gj_ref, x_ref, grad_ref,
    w_ref, term, error, mid_ref, own_w, up_w, across_w, own_o, up_o, across_o, landed,
    sem_w, sem_o, sem_g, load, *scratch,
):
    me, line = lax.axis_index("mp"), lax.axis_index("dp")
    depth = w_ref.shape[1]
    tokens, width = x_ref.shape
    pieces, piece = own_w.shape[0], own_w.shape[1]
    o_pieces, o_piece = own_o.shape[0], own_o.shape[1]
    chunk = error.shape[0]
    early = [
        pltpu.make_async_copy(normed_any, normed_ref, load.at[2]),
        pltpu.make_async_copy(gj_any, gj_ref, load.at[3]),
        pltpu.make_async_copy(share_any, own_o, load.at[4]),
    ]
    fetch = [
        pltpu.make_async_copy(w_any, w_ref, load.at[0]),
        pltpu.make_async_copy(x_any, x_ref, load.at[5]),
    ]
    keep = pltpu.make_async_copy(grad_ref, grad_any, load.at[6])
    for c in early + fetch:
        c.start()

    def bring(i):
        here = pl.ds(pl.multiple_of(i * chunk, chunk), chunk)
        return pltpu.make_async_copy(mid_any.at[here], mid_ref, load.at[1])

    bring(0).start()
    greet_all(n, me, m, line)
    half = depth // 2
    sums = make_scatter(n, me, lambda ref, h: ref.at[pl.ds(h * half, half)], scratch)
    at = lambda ref: lambda c: ref.at[c]
    weights = Line(m, line, at(own_w), at(up_w), at(across_w), at(up_w), sem_w)
    out_line = Line(m, line, at(own_o), at(up_o), at(across_o), at(up_o), sem_o)
    gains_ref[...] = sums_ref[...]

    def tokens_part(i):
        here = pl.ds(pl.multiple_of(i * chunk, chunk), chunk)
        for b in range(n):
            error[:, b * depth : (b + 1) * depth] = dg(gj_ref[here, :], w_ref[b], NT)
        small = min(32, chunk)
        bring(i).wait()

        @pl.loop(0, chunk // small)
        def _(s):
            part = pl.ds(pl.multiple_of(s * small, small), small)
            rows = pl.ds(pl.multiple_of(i * chunk + s * small, small), small)
            e = error[part, :]
            x = x_ref[rows, :].astype(F32)
            scale = lax.rsqrt(jnp.mean(x * x, axis=-1, keepdims=True) + EPSILON)
            u = e * gain_ref[...]
            v = x * scale
            inner = jnp.mean(u * v, axis=-1, keepdims=True)
            grad_ref[rows, :] = mid_ref[part, :] + scale * (u - v * inner)
            total = jnp.sum(e * v, axis=0, keepdims=True)
            for b in range(width // LANES):
                gains_ref[b : b + 1, :] += total[:, b * LANES : (b + 1) * LANES]

        if i + 1 < tokens // chunk:
            bring(i + 1).start()

    def mine(k):
        return term.at[k // 2 if k % 2 else n // 2]

    def weight_part(k):
        columns = pl.ds(pl.multiple_of(flip(me, k) * depth, depth), depth)
        mine(k)[...] = dg(normed_ref[:, columns], gj_ref[...], TN).astype(BF)

    steps = [("mp", flip(me, 1 << i)) for i in range(n.bit_length() - 1)]
    steps += [("dp", flip(line, 1 << i)) for i in range(m.bit_length() - 1)]

    def exchange(i):
        axis, to = steps[i]
        return pltpu.make_async_remote_copy(
            src_ref=landed.at[2 * i],
            dst_ref=landed.at[2 * i + 1],
            send_sem=sem_g.at[0, i],
            recv_sem=sem_g.at[1, i],
            device_id={axis: to},
            device_id_type=MESH,
        )

    for c in early:
        c.wait()
    for c in range(o_pieces):
        out_line.launch(c)
    for k in range(n - 1, 0, -2):
        weight_part(k)
        sums.odd(k, mine(k))
        if k == n - 1:
            weight_part(n - 2)
            sums.even(n - 2, mine(n - 2))
    for c in fetch:
        c.wait()
    tokens_part(0)
    for k in range(n - 4, 0, -2):
        weight_part(k)
        sums.even(k, mine(k))
    weight_part(0)
    for i in range(1, tokens // chunk):
        tokens_part(i)
    keep.start()
    for i in range(len(steps)):
        landed[2 * i] = gains_ref[...]
        exchange(i).start()
        exchange(i).wait_recv()
        gains_ref[...] = landed[2 * i] + landed[2 * i + 1]
    for c in range(o_pieces):
        out_line.inward(c)
    sums.own(mine(0), attend_ref)
    for c in range(pieces):
        own_w[c] = attend_ref[c * piece : (c + 1) * piece, :].astype(BF)
        weights.launch(c)
    kw = KVH * HD

    def widen(c):
        rows = slice(c * piece, (c + 1) * piece)
        attend_ref[rows, :QW] = up_w[c, :, :QW].astype(F32)
        for h in range(KVH):
            both = up_w[c, :, QW + 2 * h * HD : QW + 2 * (h + 1) * HD].astype(F32)
            attend_ref[rows, QW + h * HD : QW + (h + 1) * HD] = both[:, :HD]
            attend_ref[rows, QW + kw + h * HD : QW + kw + (h + 1) * HD] = both[:, HD:]

    ahead = 2
    for c in range(pieces + ahead):
        if c < pieces:
            weights.inward(c)
        if c < o_pieces:
            out_line.outward(c)
            out_ref[c * o_piece : (c + 1) * o_piece, :] = up_o[c].astype(F32)
        if c >= ahead:
            weights.outward(c - ahead)
            widen(c - ahead)
    keep.wait()
    for c in range(o_pieces):
        out_line.drain(c)
    for c in range(pieces):
        weights.drain(c)
    for i in range(len(steps)):
        exchange(i).wait_send()
    sums.drain(mine(0))


def finish(n, m, normed, gj, w, x, middle, gain, share, sums):
    tokens, width = x.shape
    columns = gj.shape[1]
    depth = width // n
    pieces, o_pieces = 8, 5
    split = (o_pieces, share.shape[0] // o_pieces, width)
    chunk = min(256, tokens)
    vmem = pl.BlockSpec(memory_space=pltpu.VMEM)
    hbm = pl.BlockSpec(memory_space=pl.ANY)
    steps = n.bit_length() + m.bit_length() - 2
    return pl.pallas_call(
        functools.partial(finish_kernel, n, m),
        in_specs=[hbm, hbm, hbm, hbm, hbm, vmem, hbm, vmem],
        out_specs=[hbm, vmem, vmem, vmem],
        out_shape=[
            jax.ShapeDtypeStruct((tokens, width), F32),
            jax.ShapeDtypeStruct((depth, columns), F32),
            jax.ShapeDtypeStruct(share.shape, F32),
            jax.ShapeDtypeStruct((GAIN_ROWS, LANES), F32),
        ],
        scratch_shapes=[
            pltpu.VMEM((tokens, width), BF),
            pltpu.VMEM((tokens, columns), BF),
            pltpu.VMEM((tokens, width), BF),
            pltpu.VMEM((tokens, width), F32),
            pltpu.VMEM(w.shape, BF),
            pltpu.VMEM((n // 2 + 1, depth, columns), BF),
            pltpu.VMEM((chunk, width), F32),
            pltpu.VMEM((chunk, width), F32),
        ]
        + [pltpu.VMEM((pieces, depth // pieces, columns), BF)] * 3
        + [pltpu.VMEM(split, BF)] * 3
        + [
            pltpu.VMEM((2 * steps, GAIN_ROWS, LANES), F32),
            pltpu.SemaphoreType.DMA((6, pieces)),
            pltpu.SemaphoreType.DMA((6, o_pieces)),
            pltpu.SemaphoreType.DMA((2, steps)),
            pltpu.SemaphoreType.DMA((7,)),
        ]
        + scatter_scratch(n, (depth, columns), (depth // 2, columns)),
        compiler_params=params(mib=60, axes=0, key=5),
        cost_estimate=TINY,
        name="finish",
    )(normed, gj, w, x, middle, gain, share.reshape(split), sums)


def key_positions(shape, axis, group, per, span):
    return group * per * span + lax.broadcasted_iota(jnp.int32, shape, axis)


def attend_kernel(keys, info, q_ref, kv_ref, start_ref, ctx_ref, rl_ref, acc):
    span = q_ref.shape[1]
    per = keys // span
    row = pl.program_id(0)
    me, first, last_start = info[row, 0], info[row, 1], info[row, 2]
    low_q = lax.broadcasted_iota(jnp.int32, (span, LANES), 1) < HD
    low_k = lax.broadcasted_iota(jnp.int32, (keys, LANES), 1) < HD
    one = jnp.ones((keys, LANES), BF)
    none = jnp.zeros((span, LANES), BF)
    queries = []
    for h in range(GW // HD):
        pair = q_ref[0, :, (h // 2) * LANES : (h // 2 + 1) * LANES]
        queries.append(jnp.where(low_q, pair, none) if h % 2 == 0 else jnp.where(low_q, none, pair))
    acc[...] = jnp.zeros_like(acc)

    def block(g, masked):
        group = g
        kv = kv_ref[0, pl.ds(pl.multiple_of(group * keys, keys), keys), :]
        vk = jnp.concatenate([kv[:, HD:], kv[:, :HD]], axis=1)
        key_sides = (kv, vk)
        value_sides = (jnp.where(low_k, vk, one), jnp.where(low_k, one, kv))
        if masked:
            position = key_positions((span, keys), 1, group, per, span)
            own = me * span + lax.broadcasted_iota(jnp.int32, (span, keys), 0)
            seen = (position <= own) & (position >= start_ref[0][:, :1])
        for h in range(GW // HD):
            p = jnp.exp2(dg(queries[h], key_sides[h % 2], NT))
            if masked:
                p = jnp.where(seen, p, 0.0)
            acc[h] += mm(p.astype(BF), value_sides[h % 2])

    def step(g, carry):
        edge = (g == me // per) | (g * keys < last_start)
        pl.when(edge)(lambda: block(g, True))
        pl.when(jnp.logical_not(edge))(lambda: block(g, False))
        return carry

    lax.fori_loop(first, me // per + 1, step, 0)
    for pair in range(GW // LANES):
        even, odd = acc[2 * pair], acc[2 * pair + 1]
        total = jnp.where(low_q, pltpu.roll(even, HD, 1), pltpu.roll(odd, HD, 1))
        inverse = 1.0 / total
        lanes = slice(pair * LANES, (pair + 1) * LANES)
        ctx_ref[0, :, lanes] = (jnp.where(low_q, even, odd) * inverse).astype(BF)
        rl_ref[0, :, lanes] = inverse


def attend(info, q, kv, start):
    rows, span, _ = q.shape
    length = kv.shape[1]
    keys = min(512, length)
    own = lambda r, h, info: (r, 0, h)
    spec = pltpu.PrefetchScalarGridSpec(
        num_scalar_prefetch=1,
        grid=(rows, KVH),
        in_specs=[
            pl.BlockSpec((1, span, GW), own),
            pl.BlockSpec((1, length, LANES), own),
            pl.BlockSpec((1, span, LANES), lambda r, h, info: (r, 0, 0)),
        ],
        out_specs=[pl.BlockSpec((1, span, GW), own), pl.BlockSpec((1, span, GW), own)],
        scratch_shapes=[pltpu.VMEM((GW // HD, span, LANES), F32)],
    )
    return pl.pallas_call(
        functools.partial(attend_kernel, keys),
        grid_spec=spec,
        out_shape=[jax.ShapeDtypeStruct(q.shape, BF), jax.ShapeDtypeStruct(q.shape, F32)],
        compiler_params=params(axes=2),
        cost_estimate=pl.CostEstimate(
            flops=16 * rows * H * span * length * HD,
            bytes_accessed=rows * (length * 1280 + span * QW * 8),
            transcendentals=rows * H * span * length,
        ),
        name="attend",
    )(info, q, kv, start)


def attend_back_kernel(
    keys, n, q_ref, kv_ref, qa_ref, ka_ref, do_ref, ctx_ref, rl_ref, a_ref, w_any,
    gout_any, dq_ref, dkv_ref, o_ref, share_ref, acc, sides, gout_ref, moves, *scratch,
):
    span = q_ref.shape[1]
    per = keys // span
    length = kv_ref.shape[1]
    me = lax.axis_index("mp")
    rows = o_ref.shape[0]
    now = pl.program_id(0) * KVH + pl.program_id(1)
    sums = TileSum(n, me, o_ref, w_any, scratch)
    half_w = share_ref.shape[1] // 2
    outs = make_scatter(
        n, me, lambda ref, h: ref.at[:, pl.ds(h * half_w, half_w)], scratch[-6:]
    )

    def out_term(k):
        return gout_any.at[flip(me, k)] if k % 2 else gout_ref.at[k // 2]

    def bring(k):
        return pltpu.make_async_copy(gout_any.at[flip(me, k)], out_term(k), moves.at[k // 2])

    def out_event(i):
        if i == 0:
            for k in range(0, n, 2):
                bring(k).start()
            for k in range(n - 1, 0, -2):
                outs.odd(k, out_term(k))
        elif i < n // 2:
            k = n - 2 * i
            bring(k).wait()
            outs.even(k, out_term(k))
        else:
            bring(0).wait()
            outs.own(out_term(0), share_ref)

    batch = a_ref.shape[1]
    steps = rows * n // batch

    @pl.when(now == 0)
    def _():
        sums.start()

    @pl.when(now < steps)
    def _():
        @pl.loop(0, batch)
        def _(i):
            tile = now * batch + i
            _, slot = tile_at(tile, n)
            sums.step(tile, a_ref.at[0, lax.rem(xor_of(me, slot, n), batch)])

    count = n // 2 + 1
    for i in range(count):
        when = 1 + i if i < 2 else 5 + (i - 2) * 4 // (count - 2)

        @pl.when(now == (when if i < count - 1 else rows * KVH - 1))
        def _(i=i):
            out_event(i)

    lane = lax.broadcasted_iota(jnp.int32, (span, LANES), 1)
    low_q = lane < HD
    low_k = lax.broadcasted_iota(jnp.int32, (keys, LANES), 1) < HD
    one = jnp.ones((keys, LANES), BF)
    for h in range(GW // HD):
        lanes = slice((h // 2) * LANES, (h // 2 + 1) * LANES)
        mine = low_q if h % 2 == 0 else jnp.logical_not(low_q)
        scaled = do_ref[0, :, lanes].astype(F32) * rl_ref[0, :, lanes]
        own = jnp.where(mine, scaled, 0.0)
        delta = -jnp.sum(own * ctx_ref[0, :, lanes].astype(F32), axis=1, keepdims=True)
        one_part = delta.astype(BF).astype(F32)
        two_part = (delta - one_part).astype(BF).astype(F32)
        three_part = delta - one_part - two_part
        base = HD if h % 2 == 0 else 0
        extra = jnp.where(
            lane == base,
            one_part,
            jnp.where(lane == base + 1, two_part, jnp.where(lane == base + 2, three_part, 0.0)),
        )
        query = q_ref[0, :, lanes].astype(F32)
        sides[0, h] = jnp.where(mine, query, 0.0).astype(BF)
        sides[1, h] = own.astype(BF)
        sides[2, h] = jnp.where(mine, scaled, extra).astype(BF)
        sides[3, h] = jnp.where(mine, query, qa_ref[0].astype(F32)).astype(BF)
    acc[...] = jnp.zeros_like(acc)

    def block(g, masked):
        here = pl.ds(pl.multiple_of(g * keys, keys), keys)
        kv = kv_ref[0, here, :]
        ka = ka_ref[0, here, :]
        vk = jnp.concatenate([kv[:, HD:], kv[:, :HD]], axis=1)
        key_sides = (jnp.where(low_k, kv, ka), jnp.where(low_k, ka, vk))
        value_sides = (jnp.where(low_k, vk, one), jnp.where(low_k, one, kv))
        if masked:
            position = g * keys + lax.broadcasted_iota(jnp.int32, (keys, span), 0)
            seen = position <= me * span + lax.broadcasted_iota(jnp.int32, (keys, span), 1)
        turned = [s.T for s in key_sides]
        grad_key = grad_value = 0.0
        for h in range(GW // HD):
            e = jnp.exp2(dg(key_sides[h % 2], sides[3, h], NT))
            if masked:
                e = jnp.where(seen, e, 0.0)
            ds = (e * dg(value_sides[h % 2], sides[2, h], NT)).astype(BF)
            grad_value = grad_value + mm(e.astype(BF), sides[1, h])
            grad_key = grad_key + mm(ds, sides[0, h])
            acc[h] += mm(turned[h % 2], ds)
        grad_key = (grad_key + pltpu.roll(grad_key, HD, 1)) * LN2
        grad_value = grad_value + pltpu.roll(grad_value, HD, 1)
        dkv_ref[0, here, :] = jnp.where(low_k, grad_key, grad_value).astype(BF)

    last = lax.div(me, per)

    @pl.loop(0, last)
    def _(g):
        block(g, False)

    block(last, True)

    @pl.loop(last + 1, length // keys)
    def _(g):
        dkv_ref[0, pl.ds(pl.multiple_of(g * keys, keys), keys), :] = jnp.zeros((keys, LANES), BF)

    for pair in range(GW // LANES):
        lanes = slice(pair * LANES, (pair + 1) * LANES)
        dq_ref[0, :, lanes] = jnp.where(low_q, acc[2 * pair].T, acc[2 * pair + 1].T) * (HD**-0.5)

    @pl.when(now == rows * KVH - 1)
    def _():
        sums.end()
        outs.drain(out_term(0))


def attend_back(n, q, kv, qa, ka, do, ctx, rl, a, w, gout):
    rows, span, _ = q.shape
    length = kv.shape[1]
    keys = min(512, length)
    depth, width = w.shape
    batch = n // 4
    own = lambda r, h: (r, 0, h)

    def place(r, h):
        row, slot = tile_at(jnp.minimum(r * KVH + h, rows * n // batch - 1) * batch, n)
        return (row, lax.div(xor_of(lax.axis_index("mp"), slot, n), batch), 0, 0)

    return pl.pallas_call(
        functools.partial(attend_back_kernel, keys, n),
        grid=(rows, KVH),
        in_specs=[
            pl.BlockSpec((1, span, GW), own),
            pl.BlockSpec((1, length, LANES), own),
            pl.BlockSpec((1, span, LANES), lambda r, h: (r, 0, 0)),
            pl.BlockSpec((1, length, LANES), lambda r, h: (r, 0, 0)),
            pl.BlockSpec((1, span, GW), own),
            pl.BlockSpec((1, span, GW), own),
            pl.BlockSpec((1, span, GW), own),
            pl.BlockSpec((1, batch, span, depth), place),
            pl.BlockSpec(memory_space=pl.ANY),
            pl.BlockSpec(memory_space=pl.ANY),
        ],
        out_specs=[
            pl.BlockSpec((1, span, GW), own),
            pl.BlockSpec((1, length, LANES), own),
            pl.BlockSpec(memory_space=pltpu.VMEM),
            pl.BlockSpec(memory_space=pltpu.VMEM),
        ],
        out_shape=[
            jax.ShapeDtypeStruct(q.shape, F32),
            jax.ShapeDtypeStruct(kv.shape, BF),
            jax.ShapeDtypeStruct((rows, span, width), F32),
            jax.ShapeDtypeStruct(gout.shape[1:], BF),
        ],
        scratch_shapes=[
            pltpu.VMEM((GW // HD, LANES, span), F32),
            pltpu.VMEM((4, GW // HD, span, LANES), BF),
            pltpu.VMEM((n // 2,) + gout.shape[1:], BF),
            pltpu.SemaphoreType.DMA((n // 2,)),
        ]
        + tile_scratch(n, rows, span, w)
        + scatter_scratch(n, gout.shape[1:], (gout.shape[1], width // 2)),
        compiler_params=params(mib=60, axes=2, key=4),
        cost_estimate=TINY,
        name="attend_back",
    )(q, kv, qa, ka, do, ctx, rl, a, w, gout)


def xor_of(a, b, n):
    total, bit = 0, 1
    while bit < n:
        total = total + bit * lax.rem(lax.div(a, bit) + lax.div(b, bit), 2)
        bit *= 2
    return total


def feed_kernel(
    n, live_ref, x_own, g_ref, g_any, gu_any, dt_any,
    x_all, hid_ref, dgu_ref, gd_any,
    x_vm, gu_ref, dt_ref, d_sum, out_d, g_two, back, x_send, x_recv, loads, stores, keep,
):
    me = lax.axis_index("mp")
    rows, span, width = x_own.shape
    slots = gu_any.shape[0]
    r, p = pl.program_id(0), pl.program_id(1)
    pairs = n // 2
    now = r * pairs + p
    half = span // 2

    def gather(row):
        def slot(i, h, k):
            at = lax.rem(flip(me, k), 2) * span + h * half
            return x_vm.at[row, i // 2, pl.ds(pl.multiple_of(at, half), half)]

        return Gather(
            n,
            me,
            lambda h: x_own.at[row, pl.ds(h * half, half)],
            slot,
            x_send.at[row],
            x_recv.at[row],
            True,
        )

    def own_copy(row):
        at = pl.ds(pl.multiple_of(lax.rem(me, 2) * span, span), span)
        return pltpu.make_async_copy(x_own.at[row], x_vm.at[row, 0, at], loads.at[1 + row])

    fetch = [
        pltpu.make_async_copy(
            gu_any.at[t], gu_ref.at[:, pl.ds(2 * t * TILE, 2 * TILE)], loads.at[3 + rows + t]
        )
        for t in range(slots)
    ]
    fetch.append(pltpu.make_async_copy(dt_any, dt_ref, loads.at[0]))

    def events(row, upto):
        todo = gather(row).even
        ends = [0] * pairs
        for i in range(1, pairs):
            ends[i] = max(ends[i - 1], 1 + max(j for j, e in enumerate(todo) if e[0] == 2 * i))
        return todo[ends[upto - 1] if upto else 0 : ends[upto]]

    def ahead(i):
        block = lax.div(xor_of(me, 2 * lax.rem(i, pairs), n), 2)
        to = lax.rem(i, 2)
        return pltpu.make_async_copy(
            g_any.at[lax.div(i, pairs), block], g_two.at[to], loads.at[1 + rows + to]
        )

    @pl.when(now == 0)
    def _():
        for row in range(rows):
            own_copy(row).start()
        for c in fetch:
            c.start()
        greet(n, me)
        gather(0).start()
        ahead(0).start()
        d_sum[...] = jnp.zeros_like(d_sum)
        own_copy(0).wait()
        for c in fetch:
            c.wait()

        @pl.loop(0, rows * pairs)
        def _(i):
            @pl.when(i + 1 < rows * pairs)
            def _():
                ahead(i + 1).start()

            ahead(i).wait()
            back[i] = mm(g_two[lax.rem(i, 2)], dt_ref[...]).astype(BF)

            @pl.when(i == rows * pairs - 2)
            def _():
                for e in gather(0).even[:2]:
                    gather(0).forward(*e)
                for row in range(1, rows):
                    gather(row).start()

    for row in range(rows):
        for i in range(pairs):

            @pl.when(now == row * pairs + i)
            def _(row=row, i=i):
                if i == 0 and row:
                    own_copy(row).wait()
                for e in events(row, i):
                    if row or e not in gather(0).even[:2]:
                        gather(row).forward(*e)
                for h in (0, 1):
                    gather(row).arrive(2 * i + 1, h)

    def save(row, i):
        block = lax.div(xor_of(me, 2 * i, n), 2)
        return pltpu.make_async_copy(x_vm.at[row, i], x_all.at[row, block], keep.at[row, i])

    save(r, p).start()
    x = x_vm.at[r, p]
    full = mm(x[...], gu_ref[...])
    for t in range(slots):
        both = full[:, 2 * t * TILE : 2 * (t + 1) * TILE]
        gate, upper = both[:, :TILE], both[:, TILE:]
        live = live_ref[t]
        sig = jax.nn.sigmoid(gate)
        silu = gate * sig
        gh = back[now, :, t * TILE : (t + 1) * TILE].astype(F32) * live
        hid_ref[0, 0, :, t * TILE : (t + 1) * TILE] = (silu * upper * live).astype(BF)
        dgu_ref[0, 0, :, 2 * t * TILE : (2 * t + 1) * TILE] = (
            gh * upper * (sig * (1.0 + gate * (1.0 - sig)))
        ).astype(BF)
        dgu_ref[0, 0, :, (2 * t + 1) * TILE : (2 * t + 2) * TILE] = (gh * silu).astype(BF)

    d_sum[...] += dg(hid_ref[0, 0], g_ref[0, 0], TN)

    @pl.when(now == rows * pairs - 1)
    def _():
        def store(t):
            return pltpu.make_async_copy(out_d.at[t % 2], gd_any.at[t], stores.at[t % 2])

        for t in range(slots):
            if t > 1:
                store(t - 2).wait()
            out_d[t % 2] = d_sum[t * TILE : (t + 1) * TILE, :].astype(BF)
            store(t).start()
        for t in range(max(slots - 2, 0), slots):
            store(t).wait()
        for row in range(rows):
            for i in range(pairs):
                save(row, i).wait()
        for row in range(rows):
            gather(row).drain()


def feed(n, live, x, g, gu, dt):
    rows, span, width = x.shape
    slots = gu.shape[0]
    hbm = pl.BlockSpec(memory_space=pl.ANY)
    pairs = n // 2

    g = g.reshape(rows, pairs, 2 * span, width)

    def place(r, p):
        return (r, lax.div(xor_of(lax.axis_index("mp"), 2 * p, n), 2), 0, 0)

    return pl.pallas_call(
        functools.partial(feed_kernel, n),
        grid=(rows, pairs),
        in_specs=[
            pl.BlockSpec(memory_space=pltpu.SMEM),
            hbm,
            pl.BlockSpec((1, 1, 2 * span, width), place),
            hbm,
            hbm,
            hbm,
        ],
        out_specs=[
            hbm,
            pl.BlockSpec((1, 1, 2 * span, slots * TILE), place),
            pl.BlockSpec((1, 1, 2 * span, 2 * slots * TILE), place),
            hbm,
        ],
        out_shape=[
            jax.ShapeDtypeStruct((rows, pairs, 2 * span, width), BF),
            jax.ShapeDtypeStruct((rows, pairs, 2 * span, slots * TILE), BF),
            jax.ShapeDtypeStruct((rows, pairs, 2 * span, 2 * slots * TILE), BF),
            jax.ShapeDtypeStruct((slots, TILE, width), BF),
        ],
        scratch_shapes=[
            pltpu.VMEM((rows, pairs, 2 * span, width), BF),
            pltpu.VMEM((width, slots * 2 * TILE), BF),
            pltpu.VMEM(dt.shape, BF),
            pltpu.VMEM((slots * TILE, width), F32),
            pltpu.VMEM((2, TILE, width), BF),
            pltpu.VMEM((2, 2 * span, width), BF),
            pltpu.VMEM((rows * pairs, 2 * span, slots * TILE), BF),
            pltpu.SemaphoreType.DMA((rows, n, 2)),
            pltpu.SemaphoreType.DMA((rows, n, 2)),
            pltpu.SemaphoreType.DMA((3 + rows + slots,)),
            pltpu.SemaphoreType.DMA((2,)),
            pltpu.SemaphoreType.DMA((rows, pairs)),
        ],
        compiler_params=params(mib=62, axes=2, key=1),
        cost_estimate=pl.CostEstimate(
            flops=2 * 6 * rows * n * span * slots * TILE * width,
            bytes_accessed=6 * rows * n * span * width + 6 * slots * TILE * width,
            transcendentals=rows * n * span * slots * TILE,
        ),
        name="feed",
    )(live, x, g, g, gu, dt)


def pick(index, table):
    total = 0
    for i, v in enumerate(table):
        total = total + v * jnp.where(index == i, 1, 0)
    return total


def tile_at(now, n):
    unit = n // 4
    at = lax.div(now, unit)
    row = pick(at, (0, 1, 0, 0, 1, 1, 0, 1))
    return row, pick(at, (3, 3, 2, 1, 2, 1, 0, 0)) * unit + unit - 1 - lax.rem(now, unit)


class TileSum:
    def __init__(self, n, me, o_ref, w_any, scratch):
        self.n, self.me, self.o_ref, self.w_any = n, me, o_ref, w_any
        self.w_ref, self.terms, self.core, self.link = scratch[:4]
        self.sems, self.load = scratch[4:8], scratch[8]
        self.rows, self.span, _ = o_ref.shape

    def scatter(self, row):
        half = self.span // 2
        return Scatter(
            self.n,
            self.me,
            lambda ref, h: ref.at[pl.ds(h * half, half)],
            lambda i: self.core.at[row, i],
            lambda h, i: self.link.at[row, h, i],
            tuple(s.at[row] for s in self.sems),
        )

    def start(self, meet=greet):
        fetch = pltpu.make_async_copy(self.w_any, self.w_ref, self.load.at[0])
        fetch.start()
        meet(self.n, self.me)
        fetch.wait()

    def close(self, row):
        last = self.scatter(row)
        for h in (0, 1):
            here = last.part(self.o_ref.at[row], h)
            joined = [here]
            for i in last.addends(0, h):
                last.link_copy(i, h).wait_recv()
                joined.append(last.link(h, i // 2 - 1))
            add_up(here, joined)

    def step(self, now, a_ref):
        n, terms = self.n, self.terms
        r, k = tile_at(now, n)

        @pl.when(now == 2 * n - n // 4)
        def _():
            self.close(0)

        for i in range(1, n, 2):

            @pl.when((r > 0) & (k == i))
            def _(i=i):
                self.scatter(r - 1).core_copy(i, terms.at[i // 2]).wait_send()

        at = lax.rem(k, 2) * lax.div(k, 2) + (1 - lax.rem(k, 2)) * (n // 2)
        terms[at] = mm(a_ref[...], self.w_ref[...]).astype(BF)
        mine = terms.at[n // 2]
        sums = self.scatter(r)
        for i in range(1, n):

            @pl.when(k == i)
            def _(i=i):
                if i % 2:
                    sums.odd(i, terms.at[i // 2])
                else:
                    sums.even(i, mine)

        @pl.when(k == 0)
        def _():
            sums.core_copy(1, self.core.at[r, 0]).wait_recv()
            add_up(self.o_ref.at[r], [mine, self.core.at[r, 0]])

    def end(self):
        self.close(self.rows - 1)
        self.scatter(self.rows - 1).drain(self.terms.at[self.n // 2])
        for row in range(self.rows - 1):
            for i in range(2, self.n, 2):
                for h in (0, 1):
                    self.scatter(row).link_copy(i, h).wait_send()


def tile_scratch(n, rows, span, w):
    width = w.shape[1]
    return [
        pltpu.VMEM(w.shape, BF),
        pltpu.VMEM((n // 2 + 1, span, width), BF),
        pltpu.VMEM((rows, n // 2, span, width), BF),
        pltpu.VMEM((rows, 2, n // 2 - 1, span // 2, width), BF),
        pltpu.SemaphoreType.DMA((rows, n // 2)),
        pltpu.SemaphoreType.DMA((rows, n // 2)),
        pltpu.SemaphoreType.DMA((rows, 2, n // 2 - 1)),
        pltpu.SemaphoreType.DMA((rows, 2, n // 2 - 1)),
        pltpu.SemaphoreType.DMA((1,)),
    ]


def spread_kernel(
    n, m, a_ref, w_any, x_ref, b_ref, d_any,
    o_ref, grad_ref, total_any,
    acc, own, up, across, line_sems, moves, *scratch,
):
    me, line = lax.axis_index("mp"), lax.axis_index("dp")
    rows = o_ref.shape[0]
    now = pl.program_id(0) * n + pl.program_id(1)
    per = rows * n // BLOCKS
    sums = TileSum(n, me, o_ref, w_any, scratch)
    chunks = own.shape[0]
    at = lambda ref: lambda c: ref.at[c]
    down = Line(m, line, at(own), at(up), at(across), at(up), line_sems)
    bring = pltpu.make_async_copy(d_any, own, moves.at[0])
    send = pltpu.make_async_copy(up, total_any, moves.at[1])

    @pl.when(now == 0)
    def _():
        bring.start()
        sums.start(lambda n, me: greet_all(n, me, m, line))
        bring.wait()
        for c in range(chunks):
            down.launch(c)

    sums.step(now, a_ref.at[0, 0])
    for c in range(chunks):

        @pl.when(now == 1 + c)
        def _(c=c):
            down.inward(c)

        @pl.when(now == 3 + c)
        def _(c=c):
            down.outward(c)

    k = lax.rem(now, per)
    term = dg(x_ref[...], b_ref[...], TN)

    @pl.when(k == 0)
    def _():
        acc[...] = term

    @pl.when((k > 0) & (k < per - 1))
    def _():
        acc[...] += term

    @pl.when(k == per - 1)
    def _():
        done = acc[...] + term
        for t in range(grad_ref.shape[0]):
            grad_ref[t] = done[:, 2 * t * TILE : 2 * (t + 1) * TILE].astype(BF)

    @pl.when(now == rows * n - 1)
    def _():
        for c in range(chunks):
            down.drain(c)
        send.start()
        sums.end()
        send.wait()


BLOCKS = 4
CHUNKS = 12


def spread(n, m, a, w, x, down):
    rows, _, span, depth = a.shape
    width = w.shape[1]
    slots = depth // (2 * TILE)
    everything = rows * n * span
    per = rows * n // BLOCKS
    part, block = everything // per, width // BLOCKS
    flat = (slots * TILE // CHUNKS, width)

    def place(r, j):
        row, slot = tile_at(r * n + j, n)
        return (row, xor_of(lax.axis_index("mp"), slot, n), 0, 0)

    def token(r, j):
        return lax.rem(r * n + j, per)

    def column(r, j):
        return lax.div(r * n + j, per)

    hbm = pl.BlockSpec(memory_space=pl.ANY)
    out, grad, total = pl.pallas_call(
        functools.partial(spread_kernel, n, m),
        grid=(rows, n),
        in_specs=[
            pl.BlockSpec((1, 1, span, depth), place),
            hbm,
            pl.BlockSpec((part, block), lambda r, j: (token(r, j), column(r, j))),
            pl.BlockSpec((part, depth), lambda r, j: (token(r, j), 0)),
            hbm,
        ],
        out_specs=[
            pl.BlockSpec(memory_space=pltpu.VMEM),
            pl.BlockSpec((slots, block, 2 * TILE), lambda r, j: (0, column(r, j), 0)),
            hbm,
        ],
        out_shape=[
            jax.ShapeDtypeStruct((rows, span, width), F32),
            jax.ShapeDtypeStruct((slots, width, 2 * TILE), BF),
            jax.ShapeDtypeStruct((CHUNKS,) + flat, BF),
        ],
        scratch_shapes=[
            pltpu.VMEM((block, depth), F32),
            pltpu.VMEM((CHUNKS,) + flat, BF),
            pltpu.VMEM((CHUNKS,) + flat, BF),
            pltpu.VMEM((CHUNKS,) + flat, BF),
            pltpu.SemaphoreType.DMA((6, CHUNKS)),
            pltpu.SemaphoreType.DMA((2,)),
        ]
        + tile_scratch(n, rows, span, w),
        compiler_params=params(mib=63, axes=2, key=3),
        cost_estimate=TINY,
        name="spread",
    )(
        a,
        w,
        x.reshape(everything, width),
        a.reshape(everything, depth),
        down.reshape((CHUNKS,) + flat),
    )
    return out, grad, total.reshape(down.shape)


def shards(
    n,
    m,
    hidden_in,
    doc_ids,
    tile_slot,
    attention_gain,
    query_gain,
    key_gain,
    attend_weight,
    output_weight,
    feed_gain,
    gate_up_slots,
    down_slots,
    out_grad,
):
    rows, span, width = hidden_in.shape
    length = doc_ids.shape[1]
    slots = gate_up_slots.shape[0]
    tokens = rows * span
    me = lax.axis_index("mp")
    offset = me * span

    kw = KVH * HD
    keys_w = attend_weight[:, QW : QW + kw].reshape(-1, KVH, HD)
    values_w = attend_weight[:, QW + kw :].reshape(-1, KVH, HD)
    attend_w = jnp.concatenate(
        [attend_weight[:, :QW], jnp.concatenate([keys_w, values_w], 2).reshape(-1, 2 * kw)], 1
    )
    below = [jnp.sum((doc_ids < d).astype(jnp.int32), axis=1, keepdims=True) for d in (1, 2)]
    local_docs = lax.dynamic_slice_in_dim(doc_ids, offset, span, 1)
    local_start = jnp.where(local_docs == 2, below[1], jnp.where(local_docs == 1, below[0], 0))
    local_pos = offset + jnp.arange(span, dtype=jnp.int32)[None] - local_start
    cos, sin = rotary_tables(local_pos.reshape(tokens))
    gq = jnp.tile(query_gain, 2)[None]
    gk = jnp.concatenate([key_gain, jnp.ones_like(key_gain)])[None]
    ones = jnp.asarray(np.kron(np.eye(LANES // HD), np.ones((HD, HD))), BF)
    key_block = min(512, length)
    info = jnp.stack(
        [
            jnp.full((rows,), me, jnp.int32),
            local_start[:, 0] // key_block,
            local_start[:, -1],
        ],
        1,
    ).astype(jnp.int32)
    start_col = jnp.broadcast_to(local_start[:, :, None], (rows, span, LANES))
    document = jnp.arange(LANES) % HD
    member = (doc_ids[:, :, None] == document).astype(F32)
    ka = jnp.where(document == DOCS, 1.0, member).astype(BF)
    own_member = lax.dynamic_slice_in_dim(member, offset, span, 1)
    qa = jnp.where(document == DOCS, -AWAY, own_member * AWAY).astype(BF)

    x_own = hidden_in.reshape(tokens, width)
    x_value = x_own.astype(F32)
    normed_ab, raw, q, grad_branch, attend_all, kv_all, output_all = project(
        n,
        rows,
        x_own,
        attention_gain[None],
        attend_w,
        output_weight,
        cos,
        sin,
        gq,
        gk,
        ones,
        out_grad.reshape(tokens, width),
    )
    q = q.reshape(rows, span, QW)
    kv_all = kv_all.reshape(rows, length, -1)
    output_full = output_all.reshape(QW, width)
    grads_all = lax.all_gather(
        grad_branch.reshape(rows, span, width), "mp", axis=1, tiled=True
    )
    ctx, rl = attend(info, q, kv_all, start_col)
    context_b = ctx.reshape(tokens, QW)
    middle = x_value + mm(context_b, output_full)
    scale_f = rms_scale(middle)
    normed_fb = (middle * scale_f * feed_gain).astype(BF).reshape(rows, span, width)

    slot_index = me * slots + jnp.arange(slots, dtype=jnp.int32)
    live = jnp.any(tile_slot[None, :] == slot_index[:, None], axis=1).astype(F32)
    gate_up_slots, down_slots, middle = lax.optimization_barrier(
        (gate_up_slots, down_slots, middle)
    )
    normed_fb, qa, ka = lax.optimization_barrier((normed_fb, qa, ka))
    gu_t = jnp.swapaxes(gate_up_slots, 1, 2).reshape(slots * 2 * TILE, width)
    d_flat = down_slots.reshape(slots * TILE, width)
    d_t = d_flat.T
    normed_all, hidden, grad_both, grad_down = feed(
        n, live, normed_fb, grads_all, gate_up_slots, d_t
    )
    hidden = hidden.reshape(rows, n, span, -1)
    grad_normed_f, grad_gate_up, down_total = spread(
        n, m, grad_both.reshape(rows, n, span, -1), gu_t, normed_all, grad_down
    )
    gate_up_total = lax.psum(grad_gate_up, "dp")
    grad_normed_f = grad_normed_f.reshape(tokens, width)

    weighted = grad_normed_f * feed_gain
    inner = jnp.mean(weighted * middle, axis=-1, keepdims=True)
    gain_feed = jnp.sum(grad_normed_f * middle * scale_f, axis=0)
    grad_middle = out_grad.reshape(tokens, width) + scale_f * (
        weighted - middle * scale_f * scale_f * inner
    )
    grad_attn_b = grad_middle.astype(BF)
    grad_context = dg(grad_attn_b, output_full, NT).astype(BF).reshape(rows, span, QW)
    grad_output = dg(context_b, grad_attn_b, TN).astype(BF)

    dq, dkv, ffn_out, output_share = attend_back(
        n,
        q,
        kv_all,
        qa,
        ka,
        grad_context,
        ctx,
        rl,
        hidden,
        d_flat,
        grad_output.reshape(n, -1, width),
    )
    layer_out = middle.reshape(rows, span, width) + ffn_out
    grad_joined_b, sum_q, sum_k = unproject(
        n,
        dq.reshape(tokens, QW),
        dkv.reshape(rows, n, span, -1),
        raw,
        cos,
        sin,
        gq,
        gk,
        ones,
    )
    down_total = down_total.astype(F32)
    grad_joined_b, layer_out, down_total = lax.optimization_barrier(
        (grad_joined_b, layer_out, down_total)
    )
    sums = jnp.concatenate(
        [
            jnp.zeros((width // LANES, LANES), F32),
            gain_feed.reshape(-1, LANES),
            sum_q[:1],
            sum_k[:1],
            jnp.zeros((GAIN_ROWS - 2 * (width // LANES) - 2, LANES), F32),
        ]
    )
    input_grad, attend_total, output_total, gains = finish(
        n,
        m,
        normed_ab,
        grad_joined_b,
        attend_all,
        x_own,
        grad_middle,
        attention_gain[None],
        output_share,
        sums,
    )
    gains = gains.reshape(-1)
    gain_query = gains[2 * width : 2 * width + HD] + gains[2 * width + HD : 2 * width + 2 * HD]
    gain_key = gains[2 * width + LANES : 2 * width + LANES + HD]
    shape = (rows, span, width)
    return (
        layer_out,
        input_grad.reshape(shape),
        attend_total,
        output_total,
        gate_up_total.astype(F32),
        down_total,
        gains[:width],
        gain_query,
        gain_key,
        gains[width : 2 * width],
    )


def solution(mesh):
    placed = (
        P("dp", "mp", None),
        P("dp", None),
        P(),
        P(),
        P(),
        P(),
        P("mp", None),
        P("mp", None),
        P(),
        P("mp", None, None),
        P("mp", None, None),
        P("dp", "mp", None),
    )
    return jax.shard_map(
        functools.partial(shards, mesh.shape["mp"], mesh.shape["dp"]),
        mesh=mesh,
        in_specs=placed,
        out_specs=(
            P("dp", "mp", None),
            P("dp", "mp", None),
            P("mp", None),
            P("mp", None),
            P("mp", None, None),
            P("mp", None, None),
            P(),
            P(),
            P(),
            P(),
        ),
        check_vma=False,
    )
```

```python
import functools

import jax
import jax.numpy as jnp
import numpy as np
from jax import lax
from jax.experimental import pallas as pl
from jax.experimental.pallas import tpu as pltpu
from jax.sharding import PartitionSpec as P

H = 20
KVH = 5
HD = 64
TILE = 128
EPSILON = 1e-06
QW = H * HD
LANES = 128
GW = (H // KVH) * HD
DOCS = 3
AWAY = 256.0
LOG2E = 1.4426950408889634
LN2 = 0.6931471805599453
BF = jnp.bfloat16
F32 = jnp.float32
MIB = 1 << 20
NT = (((1,), (1,)), ((), ()))
TN = (((0,), (0,)), ((), ()))


def params(mib=56, axes=1, key=None):
    if key is None:
        return pltpu.CompilerParams(
            vmem_limit_bytes=mib * MIB, dimension_semantics=("arbitrary",) * axes
        )
    return pltpu.CompilerParams(
        vmem_limit_bytes=mib * MIB,
        dimension_semantics=("arbitrary",) * axes if axes else None,
        collective_id=key,
        has_side_effects=True,
    )


TINY = pl.CostEstimate(flops=1, bytes_accessed=1, transcendentals=0)


def mm(a, b):
    return jnp.dot(a, b, preferred_element_type=F32)


def dg(a, b, dims):
    return lax.dot_general(a, b, dims, preferred_element_type=F32)


def rotary_tables(positions):
    half_dim = HD // 2
    freqs = 1.0 / 10000.0 ** (jnp.arange(half_dim, dtype=jnp.float32) * 2.0 / HD)
    angles = positions.astype(jnp.float32)[..., None] * jnp.tile(freqs, 4)
    return jnp.cos(angles), jnp.sin(angles)


def rms_scale(values):
    return lax.rsqrt(jnp.mean(values * values, axis=-1, keepdims=True) + EPSILON)


MESH = pl.DeviceIdType.MESH


def flip(me, k):
    bit = 1
    while bit <= k:
        if k & bit:
            me = me + bit - 2 * bit * lax.rem(lax.div(me, bit), 2)
        bit *= 2
    return me


def link_bits(n):
    return [1 << i for i in range(1, n.bit_length() - 1)]


def greet(n, me):
    barrier = pltpu.get_barrier_semaphore()
    bits = [1] + link_bits(n)
    for bit in bits:
        pl.semaphore_signal(barrier, inc=1, device_id={"mp": flip(me, bit)}, device_id_type=MESH)
    pl.semaphore_wait(barrier, len(bits))


def greet_all(n, me, m, line):
    barrier = pltpu.get_barrier_semaphore()
    bits = [1] + link_bits(n)
    for bit in bits:
        pl.semaphore_signal(barrier, inc=1, device_id={"mp": flip(me, bit)}, device_id_type=MESH)
    for step in range(1, m):
        other = lax.rem(line + step, m)
        pl.semaphore_signal(barrier, inc=1, device_id={"dp": other}, device_id_type=MESH)
    pl.semaphore_wait(barrier, len(bits) + m - 1)


class Line:
    def __init__(self, m, line, own, up, across, total, sems):
        self.own, self.up, self.across, self.total, self.sems = own, up, across, total, sems
        low = line < m // 2
        self.inner = jnp.where(low, line + 1, line - 1)
        self.outer = jnp.where(low, line - 1, line + 1)
        self.has_outer = (line > 0) & (line < m - 1)
        self.middle = (line == m // 2 - 1) | (line == m // 2)

    def copy(self, kind, c):
        src, dst, to = (
            (self.own, self.up, self.inner),
            (self.own, self.across, self.inner),
            (self.total, self.total, self.outer),
        )[kind]
        return pltpu.make_async_remote_copy(
            src_ref=src(c),
            dst_ref=dst(c),
            send_sem=self.sems.at[2 * kind, c],
            recv_sem=self.sems.at[2 * kind + 1, c],
            device_id={"dp": to},
            device_id_type=MESH,
        )

    def launch(self, c):
        @pl.when(jnp.logical_not(self.has_outer))
        def _():
            self.copy(0, c).start()

    def inward(self, c):
        @pl.when(self.has_outer)
        def _():
            self.copy(0, c).wait_recv()
            add_up(self.own(c), [self.own(c), self.up(c)])

            @pl.when(self.middle)
            def _():
                self.copy(1, c).start()

            @pl.when(jnp.logical_not(self.middle))
            def _():
                self.copy(0, c).start()

    def outward(self, c):
        @pl.when(self.middle)
        def _():
            self.copy(1, c).wait_recv()
            add_up(self.total(c), [self.own(c), self.across(c)])

        @pl.when(jnp.logical_not(self.middle))
        def _():
            self.copy(2, c).wait_recv()

        @pl.when(self.has_outer)
        def _():
            self.copy(2, c).start()

    def drain(self, c):
        @pl.when(self.middle)
        def _():
            self.copy(1, c).wait_send()

        @pl.when(jnp.logical_not(self.middle))
        def _():
            self.copy(0, c).wait_send()

        @pl.when(self.has_outer)
        def _():
            self.copy(2, c).wait_send()


class Gather:
    def __init__(self, n, me, own, slot, send, recv, relative=False):
        self.n, self.me, self.own, self.slot, self.send, self.recv = n, me, own, slot, send, recv
        self.relative = relative
        bits = link_bits(n)
        self.order = (bits + [1], bits[::-1] + [1])
        even = [(k, h) for k in range(2, n, 2) for h in (0, 1)]
        even.sort(key=lambda kh: (bin(kh[0]).count("1"), max(self.place(*kh)), kh[1]))
        self.even = even

    def place(self, k, half):
        return [i for i, bit in enumerate(self.order[half]) if k & bit]

    def copy(self, k, half, bit):
        return pltpu.make_async_remote_copy(
            src_ref=self.own(half) if k == 0 else self.here(k, half),
            dst_ref=self.slot(k ^ bit, half, k) if self.relative else self.slot(k, half),
            send_sem=self.send.at[k ^ bit, half],
            recv_sem=self.recv.at[k ^ bit, half],
            device_id={"mp": flip(self.me, bit)},
            device_id_type=MESH,
        )

    def here(self, k, half):
        return self.slot(k, half, k) if self.relative else self.slot(k, half)

    def onward(self, k, half):
        return self.order[half][(max(self.place(k, half)) + 1) if k else 0 :]

    def start(self):
        for i in range(len(self.order[0])):
            for half in (0, 1):
                self.copy(0, half, self.order[half][i]).start()

    def arrive(self, k, half):
        here = self.here(k, half)
        pltpu.make_async_remote_copy(
            src_ref=here,
            dst_ref=here,
            send_sem=self.send.at[k, half],
            recv_sem=self.recv.at[k, half],
            device_id={"mp": flip(self.me, 1)},
            device_id_type=MESH,
        ).wait_recv()

    def forward(self, k, half):
        self.arrive(k, half)
        for bit in self.onward(k, half):
            self.copy(k, half, bit).start()

    def rest(self):
        for k, half in [(1, 0), (1, 1)] + [(k + 1, h) for k, h in self.even]:
            self.arrive(k, half)

    def drain(self):
        for k in range(0, self.n, 2):
            for half in (0, 1):
                for bit in self.onward(k, half):
                    self.copy(k, half, bit).wait_send()


class Scatter:
    def __init__(self, n, me, part, core, link, sems):
        self.n, self.me, self.part = n, me, part
        self.core, self.link = core, link
        self.core_send, self.core_recv, self.link_send, self.link_recv = sems
        bits = link_bits(n)
        self.order = (bits[::-1], bits)

    def first(self, k, half):
        return next(i for i, bit in enumerate(self.order[half]) if k & bit)

    def core_copy(self, k, ref):
        return pltpu.make_async_remote_copy(
            src_ref=ref,
            dst_ref=self.core(k // 2),
            send_sem=self.core_send.at[k // 2],
            recv_sem=self.core_recv.at[k // 2],
            device_id={"mp": flip(self.me, 1)},
            device_id_type=MESH,
        )

    def link_copy(self, k, half):
        bit = self.order[half][self.first(k, half)]
        return pltpu.make_async_remote_copy(
            src_ref=self.part(self.core(k // 2), half),
            dst_ref=self.link(half, k // 2 - 1),
            send_sem=self.link_send.at[half, k // 2 - 1],
            recv_sem=self.link_recv.at[half, k // 2 - 1],
            device_id={"mp": flip(self.me, bit)},
            device_id_type=MESH,
        )

    def addends(self, k, half):
        upto = self.first(k, half) if k else len(self.order[half])
        return [k | bit for bit in self.order[half][:upto]]

    def odd(self, k, ref):
        self.core_copy(k, ref).start()

    def even(self, k, ref):
        self.core_copy(k + 1, self.core(k // 2)).wait_recv()
        for half in sorted((0, 1), key=lambda h: -len(self.addends(k, h))):
            joined = [self.part(ref, half), self.part(self.core(k // 2), half)]
            for j in self.addends(k, half):
                self.link_copy(j, half).wait_recv()
                joined.append(self.link(half, j // 2 - 1))
            add_up(joined[1], joined)
            self.link_copy(k, half).start()

    def own(self, ref, out):
        self.core_copy(1, self.core(0)).wait_recv()
        for half in (0, 1):
            joined = [self.part(ref, half), self.part(self.core(0), half)]
            for j in self.addends(0, half):
                self.link_copy(j, half).wait_recv()
                joined.append(self.link(half, j // 2 - 1))
            add_up(self.part(out, half), joined)

    def drain(self, ref):
        for k in range(1, self.n, 2):
            self.core_copy(k, ref).wait_send()
        for k in range(2, self.n, 2):
            for half in (0, 1):
                self.link_copy(k, half).wait_send()


def add_up(out, terms):
    rows, width = out.shape[-2:]
    step = 16
    while 2 * step * width <= 32768 and rows % (2 * step) == 0:
        step *= 2
    lead = (slice(None),) * (len(out.shape) - 2)

    @pl.loop(0, rows // step)
    def _(i):
        at = lead + (pl.ds(pl.multiple_of(i * step, step), step), slice(None))
        if len(terms) == 2 and all(t.dtype == BF for t in (out, *terms)):
            out[at] = terms[0][at] + terms[1][at]
        else:
            total = terms[0][at].astype(F32)
            for t in terms[1:]:
                total = total + t[at].astype(F32)
            out[at] = total.astype(out.dtype)


def scatter_scratch(n, shape, half):
    return [
        pltpu.VMEM((n // 2,) + shape, BF),
        pltpu.VMEM((2, n // 2 - 1) + half, BF),
        pltpu.SemaphoreType.DMA((n // 2,)),
        pltpu.SemaphoreType.DMA((n // 2,)),
        pltpu.SemaphoreType.DMA((2, n // 2 - 1)),
        pltpu.SemaphoreType.DMA((2, n // 2 - 1)),
    ]


def make_scatter(n, me, part, refs):
    core, link = refs[:2]
    return Scatter(
        n,
        me,
        part,
        lambda i: core.at[i],
        lambda h, i: link.at[h, i],
        refs[2:6],
    )


def half_turn(x, lane):
    first = (lane % HD) < HD // 2
    return jnp.where(first, -pltpu.roll(x, LANES - HD // 2, 1), pltpu.roll(x, HD // 2, 1))


def half_turn_back(x, lane):
    first = (lane % HD) < HD // 2
    return jnp.where(first, pltpu.roll(x, LANES - HD // 2, 1), -pltpu.roll(x, HD // 2, 1))


def group_mean(x, ones):
    high = x.astype(BF)
    low = (x - high.astype(F32)).astype(BF)
    return (mm(high, ones) + mm(low, ones)) * (1.0 / HD)


def project_kernel(
    n, x_any, gain_ref, w_ref, o_ref, cos_ref, sin_ref, gq_ref, gk_ref, ones_ref, grad_any,
    normed_any, raw_any, q_ref, branch_any, w_out, kv_out, o_out,
    x_ref, grad_ref, normed_ref, raw_ref, branch_ref, moves, w_all, kv_own, w_send, w_recv, kv_send, kv_recv, o_send, o_recv, local,
):
    me = lax.axis_index("mp")
    depth = w_ref.shape[0]
    tokens, width = x_ref.shape
    rows = kv_out.shape[0]
    span = tokens // rows
    half = depth // 2
    own_w = pltpu.make_async_copy(w_ref, w_all.at[me], local.at[0])
    own_w.start()
    early = [
        pltpu.make_async_copy(x_any, x_ref, moves.at[0]),
        pltpu.make_async_copy(grad_any, grad_ref, moves.at[1]),
    ]
    late = [
        pltpu.make_async_copy(normed_ref, normed_any, moves.at[2]),
        pltpu.make_async_copy(branch_ref, branch_any, moves.at[3]),
        pltpu.make_async_copy(raw_ref, raw_any, moves.at[4]),
    ]
    for c in early:
        c.start()
    own_o = pltpu.make_async_copy(o_ref, o_out.at[me], local.at[1 + rows])
    own_o.start()
    greet(n, me)
    wide = o_ref.shape[1] // 2
    outs = Gather(
        n,
        me,
        lambda h: o_ref.at[:, pl.ds(h * wide, wide)],
        lambda k, h: o_out.at[flip(me, k), :, pl.ds(h * wide, wide)],
        o_send,
        o_recv,
    )
    weights = Gather(
        n,
        me,
        lambda h: w_ref.at[pl.ds(h * half, half)],
        lambda k, h: w_all.at[flip(me, k), pl.ds(h * half, half)],
        w_send,
        w_recv,
    )
    weights.start()
    for c in early:
        c.wait()
    step = min(64, tokens)

    @pl.loop(0, tokens // step)
    def _(i):
        at = pl.ds(pl.multiple_of(i * step, step), step)
        x = x_ref[at, :].astype(F32)
        scale = lax.rsqrt(jnp.mean(x * x, axis=-1, keepdims=True) + EPSILON)
        normed_ref[at, :] = (x * scale * gain_ref[...]).astype(BF)
        branch_ref[at, :] = grad_ref[at, :].astype(BF)

    chunk = min(256, tokens)

    def accumulate(k, fresh):
        block = flip(me, k)
        columns = pl.ds(pl.multiple_of(block * depth, depth), depth)

        @pl.loop(0, tokens // chunk)
        def _(i):
            at = pl.ds(pl.multiple_of(i * chunk, chunk), chunk)
            term = mm(normed_ref[at, columns], w_all[block])
            raw_ref[at, :] = term if fresh else raw_ref[at, :] + term

    own_w.wait()
    accumulate(0, True)
    for h in (0, 1):
        weights.arrive(1, h)
    accumulate(1, False)
    for i, (k, h) in enumerate(weights.even):
        weights.forward(k, h)
        if any(k == other for other, _ in weights.even[:i]):
            accumulate(k, False)
    outs.start()
    for k in range(3, n, 2):
        for h in (0, 1):
            weights.arrive(k, h)
        accumulate(k, False)
    out_w = pltpu.make_async_copy(w_all, w_out, local.at[0])
    out_w.start()
    for c in late:
        c.start()

    chunk = min(128, tokens)
    lane = lax.broadcasted_iota(jnp.int32, (chunk, LANES), 1)

    gain_q = jnp.concatenate([gq_ref[...], gq_ref[...]], axis=1)
    gain_k = jnp.concatenate([gk_ref[...], jnp.ones_like(gk_ref[...])], axis=1)

    def finish(i, tiles):
        at = pl.ds(pl.multiple_of(i * chunk, chunk), chunk)
        cos, sin = cos_ref[at, :], sin_ref[at, :]
        for tile in tiles:
            lanes = slice(tile * LANES, (tile + 1) * LANES)
            x = raw_ref[at, lanes]
            query = tile < QW // LANES
            scale = lax.rsqrt(group_mean(x * x, ones_ref[...]) + EPSILON)
            v = x * scale * (gain_q if query else gain_k)
            y = v * cos + half_turn(v, lane) * sin
            if query:
                q_ref[at, lanes] = (y * (HD**-0.5 * LOG2E)).astype(BF)
            else:
                mine = slice(tile * LANES - QW, (tile + 1) * LANES - QW)
                kv_own[at, mine] = jnp.where(lane < HD, y, x).astype(BF)

    count = raw_ref.shape[1] // LANES

    @pl.loop(0, tokens // chunk)
    def _(i):
        finish(i, range(QW // LANES, count))

    both = rows // 2
    keep = [
        pltpu.make_async_copy(
            kv_own.at[pl.ds(r * span, span)], kv_out.at[r, me], local.at[1 + r]
        )
        for r in range(rows)
    ]
    for c in keep:
        c.start()
    kvs = Gather(
        n,
        me,
        lambda h: kv_own.at[pl.ds(h * span, span)],
        lambda k, h: kv_out.at[h, flip(me, k)],
        kv_send,
        kv_recv,
    )
    kvs.start()

    @pl.loop(0, tokens // chunk)
    def _(i):
        finish(i, range(QW // LANES))

    for k, h in kvs.even:
        outs.forward(k, h)
        kvs.forward(k, h)
    outs.rest()
    kvs.rest()
    for c in keep:
        c.wait()
    out_w.wait()
    own_o.wait()
    for c in late:
        c.wait()
    weights.drain()
    outs.drain()
    kvs.drain()


def project(n, rows, x, gain, w, o, cos, sin, gq, gk, ones, grad):
    tokens, width = x.shape
    depth, columns = w.shape
    vmem = pl.BlockSpec(memory_space=pltpu.VMEM)
    hbm = pl.BlockSpec(memory_space=pl.ANY)
    kvw = columns - QW
    return pl.pallas_call(
        functools.partial(project_kernel, n),
        in_specs=[hbm, vmem, hbm, hbm, vmem, vmem, vmem, vmem, vmem, hbm],
        out_specs=[hbm, hbm, vmem, hbm, hbm, hbm, hbm],
        out_shape=[
            jax.ShapeDtypeStruct((tokens, width), BF),
            jax.ShapeDtypeStruct((tokens, columns), F32),
            jax.ShapeDtypeStruct((tokens, QW), BF),
            jax.ShapeDtypeStruct((tokens, width), BF),
            jax.ShapeDtypeStruct((n, depth, columns), BF),
            jax.ShapeDtypeStruct((rows, n, tokens // rows, kvw), BF),
            jax.ShapeDtypeStruct((n,) + o.shape, BF),
        ],
        scratch_shapes=[
            pltpu.VMEM((tokens, width), BF),
            pltpu.VMEM((tokens, width), F32),
            pltpu.VMEM((tokens, width), BF),
            pltpu.VMEM((tokens, columns), F32),
            pltpu.VMEM((tokens, width), BF),
            pltpu.SemaphoreType.DMA((5,)),
            pltpu.VMEM((n, depth, columns), BF),
            pltpu.VMEM((tokens, kvw), BF),
            pltpu.SemaphoreType.DMA((n, 2)),
            pltpu.SemaphoreType.DMA((n, 2)),
            pltpu.SemaphoreType.DMA((n, 2)),
            pltpu.SemaphoreType.DMA((n, 2)),
            pltpu.SemaphoreType.DMA((n, 2)),
            pltpu.SemaphoreType.DMA((n, 2)),
            pltpu.SemaphoreType.DMA((2 + rows,)),
        ],
        compiler_params=params(axes=0, key=0),
        name="project",
    )(x, gain, w, o, cos, sin, gq, gk, ones, grad)


def unproject_kernel(
    n, dq_any, dkv_any, raw_any, cos_ref, sin_ref, gq_ref, gk_ref, ones_ref,
    gj_ref, sq_ref, sk_ref,
    dkv_own, dkv_ref, dq_ref, raw_ref, load, *scratch,
):
    me = lax.axis_index("mp")
    early = [
        pltpu.make_async_copy(dkv_any.at[:, flip(me, k)], dkv_ref.at[k // 2], load.at[2 + k // 2])
        for k in range(n - 2, -1, -2)
    ]
    late = [
        pltpu.make_async_copy(dq_any, dq_ref, load.at[0]),
        pltpu.make_async_copy(raw_any, raw_ref, load.at[1]),
    ]
    for c in early + late:
        c.start()
    greet(n, me)
    tokens = dq_ref.shape[0]
    rows = dkv_any.shape[0]
    span = tokens // rows
    columns = raw_ref.shape[1]
    keys = make_scatter(n, me, lambda ref, h: ref.at[h], scratch[:6])

    def dkv_term(k):
        return dkv_any.at[:, flip(me, k)] if k % 2 else dkv_ref.at[k // 2]

    for k in range(n - 1, 0, -2):
        keys.odd(k, dkv_term(k))
    for c in early:
        c.wait()
    keys.even(n - 2, dkv_term(n - 2))
    for c in late:
        c.wait()

    chunk = min(128, tokens)
    lane = lax.broadcasted_iota(jnp.int32, (chunk, LANES), 1)
    sq_ref[...] = jnp.zeros_like(sq_ref)
    sk_ref[...] = jnp.zeros_like(sk_ref)

    def back(i, tiles, query):
        at = pl.ds(pl.multiple_of(i * chunk, chunk), chunk)
        cos, sin = cos_ref[at, :], sin_ref[at, :]
        total = 0.0
        for tile in tiles:
            lanes = slice(tile * LANES, (tile + 1) * LANES)
            x = raw_ref[at, lanes]
            if query:
                e = dq_ref[at, lanes]
            else:
                per = span // chunk
                here = pl.ds(pl.multiple_of(lax.rem(i, per) * chunk, chunk), chunk)
                e = dkv_own[lax.div(i, per), here, slice(tile * LANES - QW, (tile + 1) * LANES - QW)]
            scale = lax.rsqrt(group_mean(x * x, ones_ref[...]) + EPSILON)
            v = x * scale
            turned = e * cos + half_turn_back(e * sin, lane)
            u = turned * (gq_ref[...] if query else gk_ref[...])
            grad = scale * (u - v * group_mean(u * v, ones_ref[...]))
            gj_ref[at, lanes] = (grad if query else jnp.where(lane < HD, grad, e)).astype(BF)
            total = total + jnp.sum(turned * v, axis=0, keepdims=True)
        sums = sq_ref if query else sk_ref
        sums[...] += jnp.broadcast_to(total, sums.shape)

    count = columns // LANES

    parts = tokens // chunk
    left = list(range(n - 4, 0, -2))
    for i in range(parts):
        back(i, range(QW // LANES), True)
        if i == 0:
            for k in left:
                keys.even(k, dkv_term(k))

    keys.own(dkv_term(0), dkv_own)

    @pl.loop(0, tokens // chunk)
    def _(i):
        back(i, range(QW // LANES, count), False)

    keys.drain(dkv_term(0))


def unproject(n, dq, dkv, raw, cos, sin, gq, gk, ones):
    tokens, columns = raw.shape
    rows = dkv.shape[0]
    span = tokens // rows
    kvw = columns - QW
    vmem = pl.BlockSpec(memory_space=pltpu.VMEM)
    hbm = pl.BlockSpec(memory_space=pl.ANY)
    return pl.pallas_call(
        functools.partial(unproject_kernel, n),
        in_specs=[hbm] * 3 + [vmem] * 5,
        out_specs=[vmem] * 3,
        out_shape=[
            jax.ShapeDtypeStruct((tokens, columns), BF),
            jax.ShapeDtypeStruct((8, LANES), F32),
            jax.ShapeDtypeStruct((8, LANES), F32),
        ],
        scratch_shapes=[
            pltpu.VMEM((rows, span, kvw), F32),
            pltpu.VMEM((n // 2, rows, span, kvw), BF),
            pltpu.VMEM(dq.shape, F32),
            pltpu.VMEM(raw.shape, F32),
            pltpu.SemaphoreType.DMA((2 + n // 2,)),
        ]
        + scatter_scratch(n, (rows, span, kvw), (span, kvw)),
        compiler_params=params(mib=60, axes=0, key=2),
        cost_estimate=TINY,
        name="unproject",
    )(dq, dkv, raw, cos, sin, gq, gk, ones)


GAIN_ROWS = 40


def finish_kernel(
    n, m, normed_any, gj_any, w_any, x_any, mid_any, gain_ref, share_any, sums_ref,
    grad_any, attend_ref, out_ref, gains_ref,
    normed_ref, gj_ref, x_ref, grad_ref,
    w_ref, term, error, mid_ref, own_w, up_w, across_w, own_o, up_o, across_o, landed,
    sem_w, sem_o, sem_g, load, *scratch,
):
    me, line = lax.axis_index("mp"), lax.axis_index("dp")
    depth = w_ref.shape[1]
    tokens, width = x_ref.shape
    pieces, piece = own_w.shape[0], own_w.shape[1]
    o_pieces, o_piece = own_o.shape[0], own_o.shape[1]
    chunk = error.shape[0]
    early = [
        pltpu.make_async_copy(normed_any, normed_ref, load.at[2]),
        pltpu.make_async_copy(gj_any, gj_ref, load.at[3]),
        pltpu.make_async_copy(share_any, own_o, load.at[4]),
    ]
    fetch = [
        pltpu.make_async_copy(w_any, w_ref, load.at[0]),
        pltpu.make_async_copy(x_any, x_ref, load.at[5]),
    ]
    keep = pltpu.make_async_copy(grad_ref, grad_any, load.at[6])
    for c in early + fetch:
        c.start()

    def bring(i):
        here = pl.ds(pl.multiple_of(i * chunk, chunk), chunk)
        return pltpu.make_async_copy(mid_any.at[here], mid_ref, load.at[1])

    bring(0).start()
    greet_all(n, me, m, line)
    half = depth // 2
    sums = make_scatter(n, me, lambda ref, h: ref.at[pl.ds(h * half, half)], scratch)
    at = lambda ref: lambda c: ref.at[c]
    weights = Line(m, line, at(own_w), at(up_w), at(across_w), at(up_w), sem_w)
    out_line = Line(m, line, at(own_o), at(up_o), at(across_o), at(up_o), sem_o)
    gains_ref[...] = sums_ref[...]

    def tokens_part(i):
        here = pl.ds(pl.multiple_of(i * chunk, chunk), chunk)
        for b in range(n):
            error[:, b * depth : (b + 1) * depth] = dg(gj_ref[here, :], w_ref[b], NT)
        small = min(32, chunk)
        bring(i).wait()

        @pl.loop(0, chunk // small)
        def _(s):
            part = pl.ds(pl.multiple_of(s * small, small), small)
            rows = pl.ds(pl.multiple_of(i * chunk + s * small, small), small)
            e = error[part, :]
            x = x_ref[rows, :].astype(F32)
            scale = lax.rsqrt(jnp.mean(x * x, axis=-1, keepdims=True) + EPSILON)
            u = e * gain_ref[...]
            v = x * scale
            inner = jnp.mean(u * v, axis=-1, keepdims=True)
            grad_ref[rows, :] = mid_ref[part, :] + scale * (u - v * inner)
            total = jnp.sum(e * v, axis=0, keepdims=True)
            for b in range(width // LANES):
                gains_ref[b : b + 1, :] += total[:, b * LANES : (b + 1) * LANES]

        if i + 1 < tokens // chunk:
            bring(i + 1).start()

    def mine(k):
        return term.at[k // 2 if k % 2 else n // 2]

    def weight_part(k):
        columns = pl.ds(pl.multiple_of(flip(me, k) * depth, depth), depth)
        mine(k)[...] = dg(normed_ref[:, columns], gj_ref[...], TN).astype(BF)

    steps = [("mp", flip(me, 1 << i)) for i in range(n.bit_length() - 1)]
    steps += [("dp", flip(line, 1 << i)) for i in range(m.bit_length() - 1)]

    def exchange(i):
        axis, to = steps[i]
        return pltpu.make_async_remote_copy(
            src_ref=landed.at[2 * i],
            dst_ref=landed.at[2 * i + 1],
            send_sem=sem_g.at[0, i],
            recv_sem=sem_g.at[1, i],
            device_id={axis: to},
            device_id_type=MESH,
        )

    for c in early:
        c.wait()
    for c in range(o_pieces):
        out_line.launch(c)
    for k in range(n - 1, 0, -2):
        weight_part(k)
        sums.odd(k, mine(k))
        if k == n - 1:
            weight_part(n - 2)
            sums.even(n - 2, mine(n - 2))
    for c in fetch:
        c.wait()
    tokens_part(0)
    for k in range(n - 4, 0, -2):
        weight_part(k)
        sums.even(k, mine(k))
    weight_part(0)
    for i in range(1, tokens // chunk):
        tokens_part(i)
    keep.start()
    for i in range(len(steps)):
        landed[2 * i] = gains_ref[...]
        exchange(i).start()
        exchange(i).wait_recv()
        gains_ref[...] = landed[2 * i] + landed[2 * i + 1]
    sums.own(mine(0), attend_ref)
    for c in range(pieces):
        own_w[c] = attend_ref[c * piece : (c + 1) * piece, :].astype(BF)
        weights.launch(c)
    for c in range(o_pieces):
        out_line.inward(c)
    kw = KVH * HD

    def widen(c):
        rows = slice(c * piece, (c + 1) * piece)
        attend_ref[rows, :QW] = up_w[c, :, :QW].astype(F32)
        for h in range(KVH):
            both = up_w[c, :, QW + 2 * h * HD : QW + 2 * (h + 1) * HD].astype(F32)
            attend_ref[rows, QW + h * HD : QW + (h + 1) * HD] = both[:, :HD]
            attend_ref[rows, QW + kw + h * HD : QW + kw + (h + 1) * HD] = both[:, HD:]

    ahead = 2
    for c in range(pieces + ahead):
        if c < pieces:
            weights.inward(c)
        if c < o_pieces:
            out_line.outward(c)
            out_ref[c * o_piece : (c + 1) * o_piece, :] = up_o[c].astype(F32)
        if c >= ahead:
            weights.outward(c - ahead)
            widen(c - ahead)
    keep.wait()
    for c in range(o_pieces):
        out_line.drain(c)
    for c in range(pieces):
        weights.drain(c)
    for i in range(len(steps)):
        exchange(i).wait_send()
    sums.drain(mine(0))


def finish(n, m, normed, gj, w, x, middle, gain, share, sums):
    tokens, width = x.shape
    columns = gj.shape[1]
    depth = width // n
    pieces, o_pieces = 8, 5
    split = (o_pieces, share.shape[0] // o_pieces, width)
    chunk = min(256, tokens)
    vmem = pl.BlockSpec(memory_space=pltpu.VMEM)
    hbm = pl.BlockSpec(memory_space=pl.ANY)
    steps = n.bit_length() + m.bit_length() - 2
    return pl.pallas_call(
        functools.partial(finish_kernel, n, m),
        in_specs=[hbm, hbm, hbm, hbm, hbm, vmem, hbm, vmem],
        out_specs=[hbm, vmem, vmem, vmem],
        out_shape=[
            jax.ShapeDtypeStruct((tokens, width), F32),
            jax.ShapeDtypeStruct((depth, columns), F32),
            jax.ShapeDtypeStruct(share.shape, F32),
            jax.ShapeDtypeStruct((GAIN_ROWS, LANES), F32),
        ],
        scratch_shapes=[
            pltpu.VMEM((tokens, width), BF),
            pltpu.VMEM((tokens, columns), BF),
            pltpu.VMEM((tokens, width), BF),
            pltpu.VMEM((tokens, width), F32),
            pltpu.VMEM(w.shape, BF),
            pltpu.VMEM((n // 2 + 1, depth, columns), BF),
            pltpu.VMEM((chunk, width), F32),
            pltpu.VMEM((chunk, width), F32),
        ]
        + [pltpu.VMEM((pieces, depth // pieces, columns), BF)] * 3
        + [pltpu.VMEM(split, BF)] * 3
        + [
            pltpu.VMEM((2 * steps, GAIN_ROWS, LANES), F32),
            pltpu.SemaphoreType.DMA((6, pieces)),
            pltpu.SemaphoreType.DMA((6, o_pieces)),
            pltpu.SemaphoreType.DMA((2, steps)),
            pltpu.SemaphoreType.DMA((7,)),
        ]
        + scatter_scratch(n, (depth, columns), (depth // 2, columns)),
        compiler_params=params(mib=60, axes=0, key=5),
        cost_estimate=TINY,
        name="finish",
    )(normed, gj, w, x, middle, gain, share.reshape(split), sums)


def key_positions(shape, axis, group, per, span):
    return group * per * span + lax.broadcasted_iota(jnp.int32, shape, axis)


def attend_kernel(keys, info, q_ref, kv_ref, start_ref, ctx_ref, rl_ref, acc):
    span = q_ref.shape[1]
    per = keys // span
    row = pl.program_id(0)
    me, first, last_start = info[row, 0], info[row, 1], info[row, 2]
    low_q = lax.broadcasted_iota(jnp.int32, (span, LANES), 1) < HD
    low_k = lax.broadcasted_iota(jnp.int32, (keys, LANES), 1) < HD
    one = jnp.ones((keys, LANES), BF)
    none = jnp.zeros((span, LANES), BF)
    queries = []
    for h in range(GW // HD):
        pair = q_ref[0, :, (h // 2) * LANES : (h // 2 + 1) * LANES]
        queries.append(jnp.where(low_q, pair, none) if h % 2 == 0 else jnp.where(low_q, none, pair))
    acc[...] = jnp.zeros_like(acc)

    def block(g, masked):
        group = g
        kv = kv_ref[0, pl.ds(pl.multiple_of(group * keys, keys), keys), :]
        vk = jnp.concatenate([kv[:, HD:], kv[:, :HD]], axis=1)
        key_sides = (kv, vk)
        value_sides = (jnp.where(low_k, vk, one), jnp.where(low_k, one, kv))
        if masked:
            position = key_positions((span, keys), 1, group, per, span)
            own = me * span + lax.broadcasted_iota(jnp.int32, (span, keys), 0)
            seen = (position <= own) & (position >= start_ref[0][:, :1])
        for h in range(GW // HD):
            p = jnp.exp2(dg(queries[h], key_sides[h % 2], NT))
            if masked:
                p = jnp.where(seen, p, 0.0)
            acc[h] += mm(p.astype(BF), value_sides[h % 2])

    def step(g, carry):
        edge = (g == me // per) | (g * keys < last_start)
        pl.when(edge)(lambda: block(g, True))
        pl.when(jnp.logical_not(edge))(lambda: block(g, False))
        return carry

    lax.fori_loop(first, me // per + 1, step, 0)
    for pair in range(GW // LANES):
        even, odd = acc[2 * pair], acc[2 * pair + 1]
        total = jnp.where(low_q, pltpu.roll(even, HD, 1), pltpu.roll(odd, HD, 1))
        inverse = 1.0 / total
        lanes = slice(pair * LANES, (pair + 1) * LANES)
        ctx_ref[0, :, lanes] = (jnp.where(low_q, even, odd) * inverse).astype(BF)
        rl_ref[0, :, lanes] = inverse


def attend(info, q, kv, start):
    rows, span, _ = q.shape
    length = kv.shape[1]
    keys = min(512, length)
    own = lambda r, h, info: (r, 0, h)
    spec = pltpu.PrefetchScalarGridSpec(
        num_scalar_prefetch=1,
        grid=(rows, KVH),
        in_specs=[
            pl.BlockSpec((1, span, GW), own),
            pl.BlockSpec((1, length, LANES), own),
            pl.BlockSpec((1, span, LANES), lambda r, h, info: (r, 0, 0)),
        ],
        out_specs=[pl.BlockSpec((1, span, GW), own), pl.BlockSpec((1, span, GW), own)],
        scratch_shapes=[pltpu.VMEM((GW // HD, span, LANES), F32)],
    )
    return pl.pallas_call(
        functools.partial(attend_kernel, keys),
        grid_spec=spec,
        out_shape=[jax.ShapeDtypeStruct(q.shape, BF), jax.ShapeDtypeStruct(q.shape, F32)],
        compiler_params=params(axes=2),
        cost_estimate=pl.CostEstimate(
            flops=16 * rows * H * span * length * HD,
            bytes_accessed=rows * (length * 1280 + span * QW * 8),
            transcendentals=rows * H * span * length,
        ),
        name="attend",
    )(info, q, kv, start)


def attend_back_kernel(
    keys, n, q_ref, kv_ref, qa_ref, ka_ref, do_ref, ctx_ref, rl_ref, a_ref, w_any,
    gout_any, dq_ref, dkv_ref, o_ref, share_ref, acc, sides, gout_ref, moves, *scratch,
):
    span = q_ref.shape[1]
    per = keys // span
    length = kv_ref.shape[1]
    me = lax.axis_index("mp")
    rows = o_ref.shape[0]
    now = pl.program_id(0) * KVH + pl.program_id(1)
    sums = TileSum(n, me, o_ref, w_any, scratch)
    half_w = share_ref.shape[1] // 2
    outs = make_scatter(
        n, me, lambda ref, h: ref.at[:, pl.ds(h * half_w, half_w)], scratch[-6:]
    )

    def out_term(k):
        return gout_any.at[flip(me, k)] if k % 2 else gout_ref.at[k // 2]

    def bring(k):
        return pltpu.make_async_copy(gout_any.at[flip(me, k)], out_term(k), moves.at[k // 2])

    def out_event(i):
        if i == 0:
            for k in range(0, n, 2):
                bring(k).start()
            for k in range(n - 1, 0, -2):
                outs.odd(k, out_term(k))
        elif i < n // 2:
            k = n - 2 * i
            bring(k).wait()
            outs.even(k, out_term(k))
        else:
            bring(0).wait()
            outs.own(out_term(0), share_ref)

    batch = a_ref.shape[1]
    steps = rows * n // batch

    @pl.when(now == 0)
    def _():
        sums.start()

    @pl.when(now < steps)
    def _():
        @pl.loop(0, batch)
        def _(i):
            tile = now * batch + i
            _, slot = tile_at(tile, n)
            sums.step(tile, a_ref.at[0, lax.rem(xor_of(me, slot, n), batch)])

    count = n // 2 + 1
    for i in range(count):
        when = 1 + i if i < 2 else 5 + (i - 2) * 4 // (count - 2)

        @pl.when(now == (when if i < count - 1 else rows * KVH - 1))
        def _(i=i):
            out_event(i)

    lane = lax.broadcasted_iota(jnp.int32, (span, LANES), 1)
    low_q = lane < HD
    low_k = lax.broadcasted_iota(jnp.int32, (keys, LANES), 1) < HD
    one = jnp.ones((keys, LANES), BF)
    for h in range(GW // HD):
        lanes = slice((h // 2) * LANES, (h // 2 + 1) * LANES)
        mine = low_q if h % 2 == 0 else jnp.logical_not(low_q)
        scaled = do_ref[0, :, lanes].astype(F32) * rl_ref[0, :, lanes]
        own = jnp.where(mine, scaled, 0.0)
        delta = -jnp.sum(own * ctx_ref[0, :, lanes].astype(F32), axis=1, keepdims=True)
        one_part = delta.astype(BF).astype(F32)
        two_part = (delta - one_part).astype(BF).astype(F32)
        three_part = delta - one_part - two_part
        base = HD if h % 2 == 0 else 0
        extra = jnp.where(
            lane == base,
            one_part,
            jnp.where(lane == base + 1, two_part, jnp.where(lane == base + 2, three_part, 0.0)),
        )
        query = q_ref[0, :, lanes].astype(F32)
        sides[0, h] = jnp.where(mine, query, 0.0).astype(BF)
        sides[1, h] = own.astype(BF)
        sides[2, h] = jnp.where(mine, scaled, extra).astype(BF)
        sides[3, h] = jnp.where(mine, query, qa_ref[0].astype(F32)).astype(BF)
    acc[...] = jnp.zeros_like(acc)

    def block(g, masked):
        here = pl.ds(pl.multiple_of(g * keys, keys), keys)
        kv = kv_ref[0, here, :]
        ka = ka_ref[0, here, :]
        vk = jnp.concatenate([kv[:, HD:], kv[:, :HD]], axis=1)
        key_sides = (jnp.where(low_k, kv, ka), jnp.where(low_k, ka, vk))
        value_sides = (jnp.where(low_k, vk, one), jnp.where(low_k, one, kv))
        if masked:
            position = g * keys + lax.broadcasted_iota(jnp.int32, (keys, span), 0)
            seen = position <= me * span + lax.broadcasted_iota(jnp.int32, (keys, span), 1)
        turned = [s.T for s in key_sides]
        grad_key = grad_value = 0.0
        for h in range(GW // HD):
            e = jnp.exp2(dg(key_sides[h % 2], sides[3, h], NT))
            if masked:
                e = jnp.where(seen, e, 0.0)
            ds = (e * dg(value_sides[h % 2], sides[2, h], NT)).astype(BF)
            grad_value = grad_value + mm(e.astype(BF), sides[1, h])
            grad_key = grad_key + mm(ds, sides[0, h])
            acc[h] += mm(turned[h % 2], ds)
        grad_key = (grad_key + pltpu.roll(grad_key, HD, 1)) * LN2
        grad_value = grad_value + pltpu.roll(grad_value, HD, 1)
        dkv_ref[0, here, :] = jnp.where(low_k, grad_key, grad_value).astype(BF)

    last = lax.div(me, per)

    @pl.loop(0, last)
    def _(g):
        block(g, False)

    block(last, True)

    @pl.loop(last + 1, length // keys)
    def _(g):
        dkv_ref[0, pl.ds(pl.multiple_of(g * keys, keys), keys), :] = jnp.zeros((keys, LANES), BF)

    for pair in range(GW // LANES):
        lanes = slice(pair * LANES, (pair + 1) * LANES)
        dq_ref[0, :, lanes] = jnp.where(low_q, acc[2 * pair].T, acc[2 * pair + 1].T) * (HD**-0.5)

    @pl.when(now == rows * KVH - 1)
    def _():
        sums.end()
        outs.drain(out_term(0))


def attend_back(n, q, kv, qa, ka, do, ctx, rl, a, w, gout):
    rows, span, _ = q.shape
    length = kv.shape[1]
    keys = min(512, length)
    depth, width = w.shape
    batch = n // 4
    own = lambda r, h: (r, 0, h)

    def place(r, h):
        row, slot = tile_at(jnp.minimum(r * KVH + h, rows * n // batch - 1) * batch, n)
        return (row, lax.div(xor_of(lax.axis_index("mp"), slot, n), batch), 0, 0)

    return pl.pallas_call(
        functools.partial(attend_back_kernel, keys, n),
        grid=(rows, KVH),
        in_specs=[
            pl.BlockSpec((1, span, GW), own),
            pl.BlockSpec((1, length, LANES), own),
            pl.BlockSpec((1, span, LANES), lambda r, h: (r, 0, 0)),
            pl.BlockSpec((1, length, LANES), lambda r, h: (r, 0, 0)),
            pl.BlockSpec((1, span, GW), own),
            pl.BlockSpec((1, span, GW), own),
            pl.BlockSpec((1, span, GW), own),
            pl.BlockSpec((1, batch, span, depth), place),
            pl.BlockSpec(memory_space=pl.ANY),
            pl.BlockSpec(memory_space=pl.ANY),
        ],
        out_specs=[
            pl.BlockSpec((1, span, GW), own),
            pl.BlockSpec((1, length, LANES), own),
            pl.BlockSpec(memory_space=pltpu.VMEM),
            pl.BlockSpec(memory_space=pltpu.VMEM),
        ],
        out_shape=[
            jax.ShapeDtypeStruct(q.shape, F32),
            jax.ShapeDtypeStruct(kv.shape, BF),
            jax.ShapeDtypeStruct((rows, span, width), F32),
            jax.ShapeDtypeStruct(gout.shape[1:], BF),
        ],
        scratch_shapes=[
            pltpu.VMEM((GW // HD, LANES, span), F32),
            pltpu.VMEM((4, GW // HD, span, LANES), BF),
            pltpu.VMEM((n // 2,) + gout.shape[1:], BF),
            pltpu.SemaphoreType.DMA((n // 2,)),
        ]
        + tile_scratch(n, rows, span, w)
        + scatter_scratch(n, gout.shape[1:], (gout.shape[1], width // 2)),
        compiler_params=params(mib=60, axes=2, key=4),
        cost_estimate=TINY,
        name="attend_back",
    )(q, kv, qa, ka, do, ctx, rl, a, w, gout)


def xor_of(a, b, n):
    total, bit = 0, 1
    while bit < n:
        total = total + bit * lax.rem(lax.div(a, bit) + lax.div(b, bit), 2)
        bit *= 2
    return total


def feed_kernel(
    n, live_ref, x_own, g_ref, g_any, gu_any, dt_any,
    x_all, hid_ref, dgu_ref, gd_any,
    x_vm, gu_ref, dt_ref, d_sum, out_d, g_two, back, x_send, x_recv, loads, stores, keep,
):
    me = lax.axis_index("mp")
    rows, span, width = x_own.shape
    slots = gu_any.shape[0]
    r, p = pl.program_id(0), pl.program_id(1)
    pairs = n // 2
    now = r * pairs + p
    half = span // 2

    def gather(row):
        def slot(i, h, k):
            at = lax.rem(flip(me, k), 2) * span + h * half
            return x_vm.at[row, i // 2, pl.ds(pl.multiple_of(at, half), half)]

        return Gather(
            n,
            me,
            lambda h: x_own.at[row, pl.ds(h * half, half)],
            slot,
            x_send.at[row],
            x_recv.at[row],
            True,
        )

    def own_copy(row):
        at = pl.ds(pl.multiple_of(lax.rem(me, 2) * span, span), span)
        return pltpu.make_async_copy(x_own.at[row], x_vm.at[row, 0, at], loads.at[1 + row])

    fetch = [
        pltpu.make_async_copy(
            gu_any.at[t], gu_ref.at[:, pl.ds(2 * t * TILE, 2 * TILE)], loads.at[3 + rows + t]
        )
        for t in range(slots)
    ]
    fetch.append(pltpu.make_async_copy(dt_any, dt_ref, loads.at[0]))

    def events(row, upto):
        todo = gather(row).even
        ends = [0] * pairs
        for i in range(1, pairs):
            ends[i] = max(ends[i - 1], 1 + max(j for j, e in enumerate(todo) if e[0] == 2 * i))
        return todo[ends[upto - 1] if upto else 0 : ends[upto]]

    def ahead(i):
        block = lax.div(xor_of(me, 2 * lax.rem(i, pairs), n), 2)
        to = lax.rem(i, 2)
        return pltpu.make_async_copy(
            g_any.at[lax.div(i, pairs), block], g_two.at[to], loads.at[1 + rows + to]
        )

    @pl.when(now == 0)
    def _():
        for row in range(rows):
            own_copy(row).start()
        for c in fetch:
            c.start()
        greet(n, me)
        gather(0).start()
        ahead(0).start()
        d_sum[...] = jnp.zeros_like(d_sum)
        own_copy(0).wait()
        for c in fetch:
            c.wait()

        @pl.loop(0, rows * pairs)
        def _(i):
            @pl.when(i + 1 < rows * pairs)
            def _():
                ahead(i + 1).start()

            ahead(i).wait()
            back[i] = mm(g_two[lax.rem(i, 2)], dt_ref[...]).astype(BF)

            @pl.when(i == rows * pairs - 2)
            def _():
                for e in gather(0).even[:2]:
                    gather(0).forward(*e)
                for row in range(1, rows):
                    gather(row).start()

    for row in range(rows):
        for i in range(pairs):

            @pl.when(now == row * pairs + i)
            def _(row=row, i=i):
                if i == 0 and row:
                    own_copy(row).wait()
                for e in events(row, i):
                    if row or e not in gather(0).even[:2]:
                        gather(row).forward(*e)
                for h in (0, 1):
                    gather(row).arrive(2 * i + 1, h)

    def save(row, i):
        block = lax.div(xor_of(me, 2 * i, n), 2)
        return pltpu.make_async_copy(x_vm.at[row, i], x_all.at[row, block], keep.at[row, i])

    save(r, p).start()
    x = x_vm.at[r, p]
    full = mm(x[...], gu_ref[...])
    for t in range(slots):
        both = full[:, 2 * t * TILE : 2 * (t + 1) * TILE]
        gate, upper = both[:, :TILE], both[:, TILE:]
        live = live_ref[t]
        sig = jax.nn.sigmoid(gate)
        silu = gate * sig
        gh = back[now, :, t * TILE : (t + 1) * TILE].astype(F32) * live
        hid_ref[0, 0, :, t * TILE : (t + 1) * TILE] = (silu * upper * live).astype(BF)
        dgu_ref[0, 0, :, 2 * t * TILE : (2 * t + 1) * TILE] = (
            gh * upper * (sig * (1.0 + gate * (1.0 - sig)))
        ).astype(BF)
        dgu_ref[0, 0, :, (2 * t + 1) * TILE : (2 * t + 2) * TILE] = (gh * silu).astype(BF)

    d_sum[...] += dg(hid_ref[0, 0], g_ref[0, 0], TN)

    @pl.when(now == rows * pairs - 1)
    def _():
        def store(t):
            return pltpu.make_async_copy(out_d.at[t % 2], gd_any.at[t], stores.at[t % 2])

        for t in range(slots):
            if t > 1:
                store(t - 2).wait()
            out_d[t % 2] = d_sum[t * TILE : (t + 1) * TILE, :].astype(BF)
            store(t).start()
        for t in range(max(slots - 2, 0), slots):
            store(t).wait()
        for row in range(rows):
            for i in range(pairs):
                save(row, i).wait()
        for row in range(rows):
            gather(row).drain()


def feed(n, live, x, g, gu, dt):
    rows, span, width = x.shape
    slots = gu.shape[0]
    hbm = pl.BlockSpec(memory_space=pl.ANY)
    pairs = n // 2

    g = g.reshape(rows, pairs, 2 * span, width)

    def place(r, p):
        return (r, lax.div(xor_of(lax.axis_index("mp"), 2 * p, n), 2), 0, 0)

    return pl.pallas_call(
        functools.partial(feed_kernel, n),
        grid=(rows, pairs),
        in_specs=[
            pl.BlockSpec(memory_space=pltpu.SMEM),
            hbm,
            pl.BlockSpec((1, 1, 2 * span, width), place),
            hbm,
            hbm,
            hbm,
        ],
        out_specs=[
            hbm,
            pl.BlockSpec((1, 1, 2 * span, slots * TILE), place),
            pl.BlockSpec((1, 1, 2 * span, 2 * slots * TILE), place),
            hbm,
        ],
        out_shape=[
            jax.ShapeDtypeStruct((rows, pairs, 2 * span, width), BF),
            jax.ShapeDtypeStruct((rows, pairs, 2 * span, slots * TILE), BF),
            jax.ShapeDtypeStruct((rows, pairs, 2 * span, 2 * slots * TILE), BF),
            jax.ShapeDtypeStruct((slots, TILE, width), BF),
        ],
        scratch_shapes=[
            pltpu.VMEM((rows, pairs, 2 * span, width), BF),
            pltpu.VMEM((width, slots * 2 * TILE), BF),
            pltpu.VMEM(dt.shape, BF),
            pltpu.VMEM((slots * TILE, width), F32),
            pltpu.VMEM((2, TILE, width), BF),
            pltpu.VMEM((2, 2 * span, width), BF),
            pltpu.VMEM((rows * pairs, 2 * span, slots * TILE), BF),
            pltpu.SemaphoreType.DMA((rows, n, 2)),
            pltpu.SemaphoreType.DMA((rows, n, 2)),
            pltpu.SemaphoreType.DMA((3 + rows + slots,)),
            pltpu.SemaphoreType.DMA((2,)),
            pltpu.SemaphoreType.DMA((rows, pairs)),
        ],
        compiler_params=params(mib=62, axes=2, key=1),
        cost_estimate=pl.CostEstimate(
            flops=2 * 6 * rows * n * span * slots * TILE * width,
            bytes_accessed=6 * rows * n * span * width + 6 * slots * TILE * width,
            transcendentals=rows * n * span * slots * TILE,
        ),
        name="feed",
    )(live, x, g, g, gu, dt)


def pick(index, table):
    total = 0
    for i, v in enumerate(table):
        total = total + v * jnp.where(index == i, 1, 0)
    return total


def tile_at(now, n):
    unit = n // 4
    at = lax.div(now, unit)
    row = pick(at, (0, 1, 0, 0, 1, 1, 0, 1))
    return row, pick(at, (3, 3, 2, 1, 2, 1, 0, 0)) * unit + unit - 1 - lax.rem(now, unit)


class TileSum:
    def __init__(self, n, me, o_ref, w_any, scratch):
        self.n, self.me, self.o_ref, self.w_any = n, me, o_ref, w_any
        self.w_ref, self.terms, self.core, self.link = scratch[:4]
        self.sems, self.load = scratch[4:8], scratch[8]
        self.rows, self.span, _ = o_ref.shape

    def scatter(self, row):
        half = self.span // 2
        return Scatter(
            self.n,
            self.me,
            lambda ref, h: ref.at[pl.ds(h * half, half)],
            lambda i: self.core.at[row, i],
            lambda h, i: self.link.at[row, h, i],
            tuple(s.at[row] for s in self.sems),
        )

    def start(self, meet=greet):
        fetch = pltpu.make_async_copy(self.w_any, self.w_ref, self.load.at[0])
        fetch.start()
        meet(self.n, self.me)
        fetch.wait()

    def close(self, row):
        last = self.scatter(row)
        for h in (0, 1):
            here = last.part(self.o_ref.at[row], h)
            joined = [here]
            for i in last.addends(0, h):
                last.link_copy(i, h).wait_recv()
                joined.append(last.link(h, i // 2 - 1))
            add_up(here, joined)

    def step(self, now, a_ref):
        n, terms = self.n, self.terms
        r, k = tile_at(now, n)

        @pl.when(now == 2 * n - n // 4)
        def _():
            self.close(0)

        for i in range(1, n, 2):

            @pl.when((r > 0) & (k == i))
            def _(i=i):
                self.scatter(r - 1).core_copy(i, terms.at[i // 2]).wait_send()

        at = lax.rem(k, 2) * lax.div(k, 2) + (1 - lax.rem(k, 2)) * (n // 2)
        terms[at] = mm(a_ref[...], self.w_ref[...]).astype(BF)
        mine = terms.at[n // 2]
        sums = self.scatter(r)
        for i in range(1, n):

            @pl.when(k == i)
            def _(i=i):
                if i % 2:
                    sums.odd(i, terms.at[i // 2])
                else:
                    sums.even(i, mine)

        @pl.when(k == 0)
        def _():
            sums.core_copy(1, self.core.at[r, 0]).wait_recv()
            add_up(self.o_ref.at[r], [mine, self.core.at[r, 0]])

    def end(self):
        self.close(self.rows - 1)
        self.scatter(self.rows - 1).drain(self.terms.at[self.n // 2])
        for row in range(self.rows - 1):
            for i in range(2, self.n, 2):
                for h in (0, 1):
                    self.scatter(row).link_copy(i, h).wait_send()


def tile_scratch(n, rows, span, w):
    width = w.shape[1]
    return [
        pltpu.VMEM(w.shape, BF),
        pltpu.VMEM((n // 2 + 1, span, width), BF),
        pltpu.VMEM((rows, n // 2, span, width), BF),
        pltpu.VMEM((rows, 2, n // 2 - 1, span // 2, width), BF),
        pltpu.SemaphoreType.DMA((rows, n // 2)),
        pltpu.SemaphoreType.DMA((rows, n // 2)),
        pltpu.SemaphoreType.DMA((rows, 2, n // 2 - 1)),
        pltpu.SemaphoreType.DMA((rows, 2, n // 2 - 1)),
        pltpu.SemaphoreType.DMA((1,)),
    ]


def spread_kernel(
    n, m, a_ref, w_any, x_ref, b_ref, d_any,
    o_ref, grad_ref, total_any,
    acc, own, up, across, line_sems, moves, *scratch,
):
    me, line = lax.axis_index("mp"), lax.axis_index("dp")
    rows = o_ref.shape[0]
    now = pl.program_id(0) * n + pl.program_id(1)
    per = rows * n // BLOCKS
    sums = TileSum(n, me, o_ref, w_any, scratch)
    chunks = own.shape[0]
    at = lambda ref: lambda c: ref.at[c]
    down = Line(m, line, at(own), at(up), at(across), at(up), line_sems)
    bring = pltpu.make_async_copy(d_any, own, moves.at[0])
    send = pltpu.make_async_copy(up, total_any, moves.at[1])

    @pl.when(now == 0)
    def _():
        bring.start()
        sums.start(lambda n, me: greet_all(n, me, m, line))
        bring.wait()
        for c in range(chunks):
            down.launch(c)

    sums.step(now, a_ref.at[0, 0])
    for c in range(chunks):

        @pl.when(now == 1 + c)
        def _(c=c):
            down.inward(c)

        @pl.when(now == 3 + c)
        def _(c=c):
            down.outward(c)

    k = lax.rem(now, per)
    term = dg(x_ref[...], b_ref[...], TN)

    @pl.when(k == 0)
    def _():
        acc[...] = term

    @pl.when((k > 0) & (k < per - 1))
    def _():
        acc[...] += term

    @pl.when(k == per - 1)
    def _():
        done = acc[...] + term
        for t in range(grad_ref.shape[0]):
            grad_ref[t] = done[:, 2 * t * TILE : 2 * (t + 1) * TILE].astype(BF)

    @pl.when(now == rows * n - 1)
    def _():
        for c in range(chunks):
            down.drain(c)
        send.start()
        sums.end()
        send.wait()


BLOCKS = 4
CHUNKS = 12


def spread(n, m, a, w, x, down):
    rows, _, span, depth = a.shape
    width = w.shape[1]
    slots = depth // (2 * TILE)
    everything = rows * n * span
    per = rows * n // BLOCKS
    part, block = everything // per, width // BLOCKS
    flat = (slots * TILE // CHUNKS, width)

    def place(r, j):
        row, slot = tile_at(r * n + j, n)
        return (row, xor_of(lax.axis_index("mp"), slot, n), 0, 0)

    def token(r, j):
        return lax.rem(r * n + j, per)

    def column(r, j):
        return lax.div(r * n + j, per)

    hbm = pl.BlockSpec(memory_space=pl.ANY)
    out, grad, total = pl.pallas_call(
        functools.partial(spread_kernel, n, m),
        grid=(rows, n),
        in_specs=[
            pl.BlockSpec((1, 1, span, depth), place),
            hbm,
            pl.BlockSpec((part, block), lambda r, j: (token(r, j), column(r, j))),
            pl.BlockSpec((part, depth), lambda r, j: (token(r, j), 0)),
            hbm,
        ],
        out_specs=[
            pl.BlockSpec(memory_space=pltpu.VMEM),
            pl.BlockSpec((slots, block, 2 * TILE), lambda r, j: (0, column(r, j), 0)),
            hbm,
        ],
        out_shape=[
            jax.ShapeDtypeStruct((rows, span, width), F32),
            jax.ShapeDtypeStruct((slots, width, 2 * TILE), BF),
            jax.ShapeDtypeStruct((CHUNKS,) + flat, BF),
        ],
        scratch_shapes=[
            pltpu.VMEM((block, depth), F32),
            pltpu.VMEM((CHUNKS,) + flat, BF),
            pltpu.VMEM((CHUNKS,) + flat, BF),
            pltpu.VMEM((CHUNKS,) + flat, BF),
            pltpu.SemaphoreType.DMA((6, CHUNKS)),
            pltpu.SemaphoreType.DMA((2,)),
        ]
        + tile_scratch(n, rows, span, w),
        compiler_params=params(mib=63, axes=2, key=3),
        cost_estimate=TINY,
        name="spread",
    )(
        a,
        w,
        x.reshape(everything, width),
        a.reshape(everything, depth),
        down.reshape((CHUNKS,) + flat),
    )
    return out, grad, total.reshape(down.shape)


def shards(
    n,
    m,
    hidden_in,
    doc_ids,
    tile_slot,
    attention_gain,
    query_gain,
    key_gain,
    attend_weight,
    output_weight,
    feed_gain,
    gate_up_slots,
    down_slots,
    out_grad,
):
    rows, span, width = hidden_in.shape
    length = doc_ids.shape[1]
    slots = gate_up_slots.shape[0]
    tokens = rows * span
    me = lax.axis_index("mp")
    offset = me * span

    kw = KVH * HD
    keys_w = attend_weight[:, QW : QW + kw].reshape(-1, KVH, HD)
    values_w = attend_weight[:, QW + kw :].reshape(-1, KVH, HD)
    attend_w = jnp.concatenate(
        [attend_weight[:, :QW], jnp.concatenate([keys_w, values_w], 2).reshape(-1, 2 * kw)], 1
    )
    below = [jnp.sum((doc_ids < d).astype(jnp.int32), axis=1, keepdims=True) for d in (1, 2)]
    local_docs = lax.dynamic_slice_in_dim(doc_ids, offset, span, 1)
    local_start = jnp.where(local_docs == 2, below[1], jnp.where(local_docs == 1, below[0], 0))
    local_pos = offset + jnp.arange(span, dtype=jnp.int32)[None] - local_start
    cos, sin = rotary_tables(local_pos.reshape(tokens))
    gq = jnp.tile(query_gain, 2)[None]
    gk = jnp.concatenate([key_gain, jnp.ones_like(key_gain)])[None]
    ones = jnp.asarray(np.kron(np.eye(LANES // HD), np.ones((HD, HD))), BF)
    key_block = min(512, length)
    info = jnp.stack(
        [
            jnp.full((rows,), me, jnp.int32),
            local_start[:, 0] // key_block,
            local_start[:, -1],
        ],
        1,
    ).astype(jnp.int32)
    start_col = jnp.broadcast_to(local_start[:, :, None], (rows, span, LANES))
    document = jnp.arange(LANES) % HD
    member = (doc_ids[:, :, None] == document).astype(F32)
    ka = jnp.where(document == DOCS, 1.0, member).astype(BF)
    own_member = lax.dynamic_slice_in_dim(member, offset, span, 1)
    qa = jnp.where(document == DOCS, -AWAY, own_member * AWAY).astype(BF)

    x_own = hidden_in.reshape(tokens, width)
    x_value = x_own.astype(F32)
    normed_ab, raw, q, grad_branch, attend_all, kv_all, output_all = project(
        n,
        rows,
        x_own,
        attention_gain[None],
        attend_w,
        output_weight,
        cos,
        sin,
        query_gain[None],
        key_gain[None],
        ones,
        out_grad.reshape(tokens, width),
    )
    q = q.reshape(rows, span, QW)
    kv_all = kv_all.reshape(rows, length, -1)
    output_full = output_all.reshape(QW, width)
    grads_all = lax.all_gather(
        grad_branch.reshape(rows, span, width), "mp", axis=1, tiled=True
    )
    ctx, rl = attend(info, q, kv_all, start_col)
    context_b = ctx.reshape(tokens, QW)
    middle = x_value + mm(context_b, output_full)
    scale_f = rms_scale(middle)
    normed_fb = (middle * scale_f * feed_gain).astype(BF).reshape(rows, span, width)

    slot_index = me * slots + jnp.arange(slots, dtype=jnp.int32)
    live = jnp.any(tile_slot[None, :] == slot_index[:, None], axis=1).astype(F32)
    gate_up_slots, down_slots, middle = lax.optimization_barrier(
        (gate_up_slots, down_slots, middle)
    )
    normed_fb, qa, ka = lax.optimization_barrier((normed_fb, qa, ka))
    gu_t = jnp.swapaxes(gate_up_slots, 1, 2).reshape(slots * 2 * TILE, width)
    d_flat = down_slots.reshape(slots * TILE, width)
    d_t = d_flat.T
    normed_all, hidden, grad_both, grad_down = feed(
        n, live, normed_fb, grads_all, gate_up_slots, d_t
    )
    hidden = hidden.reshape(rows, n, span, -1)
    grad_normed_f, grad_gate_up, down_total = spread(
        n, m, grad_both.reshape(rows, n, span, -1), gu_t, normed_all, grad_down
    )
    gate_up_total = lax.psum(grad_gate_up, "dp")
    grad_normed_f = grad_normed_f.reshape(tokens, width)

    weighted = grad_normed_f * feed_gain
    inner = jnp.mean(weighted * middle, axis=-1, keepdims=True)
    gain_feed = jnp.sum(grad_normed_f * middle * scale_f, axis=0)
    grad_middle = out_grad.reshape(tokens, width) + scale_f * (
        weighted - middle * scale_f * scale_f * inner
    )
    grad_attn_b = grad_middle.astype(BF)
    grad_context = dg(grad_attn_b, output_full, NT).astype(BF).reshape(rows, span, QW)
    grad_output = dg(context_b, grad_attn_b, TN).astype(BF)

    dq, dkv, ffn_out, output_share = attend_back(
        n,
        q,
        kv_all,
        qa,
        ka,
        grad_context,
        ctx,
        rl,
        hidden,
        d_flat,
        grad_output.reshape(n, -1, width),
    )
    layer_out = middle + ffn_out.reshape(tokens, width)
    grad_joined_b, sum_q, sum_k = unproject(
        n,
        dq.reshape(tokens, QW),
        dkv.reshape(rows, n, span, -1),
        raw,
        cos,
        sin,
        gq,
        gk,
        ones,
    )
    down_total = down_total.astype(F32)
    grad_joined_b, layer_out, down_total = lax.optimization_barrier(
        (grad_joined_b, layer_out, down_total)
    )
    sums = jnp.concatenate(
        [
            jnp.zeros((width // LANES, LANES), F32),
            gain_feed.reshape(-1, LANES),
            sum_q[:1],
            sum_k[:1],
            jnp.zeros((GAIN_ROWS - 2 * (width // LANES) - 2, LANES), F32),
        ]
    )
    input_grad, attend_total, output_total, gains = finish(
        n,
        m,
        normed_ab,
        grad_joined_b,
        attend_all,
        x_own,
        grad_middle,
        attention_gain[None],
        output_share,
        sums,
    )
    gains = gains.reshape(-1)
    gain_query = gains[2 * width : 2 * width + HD] + gains[2 * width + HD : 2 * width + 2 * HD]
    gain_key = gains[2 * width + LANES : 2 * width + LANES + HD]
    shape = (rows, span, width)
    return (
        layer_out.reshape(shape),
        input_grad.reshape(shape),
        attend_total,
        output_total,
        gate_up_total.astype(F32),
        down_total,
        gains[:width],
        gain_query,
        gain_key,
        gains[width : 2 * width],
    )


def solution(mesh):
    placed = (
        P("dp", "mp", None),
        P("dp", None),
        P(),
        P(),
        P(),
        P(),
        P("mp", None),
        P("mp", None),
        P(),
        P("mp", None, None),
        P("mp", None, None),
        P("dp", "mp", None),
    )
    return jax.shard_map(
        functools.partial(shards, mesh.shape["mp"], mesh.shape["dp"]),
        mesh=mesh,
        in_specs=placed,
        out_specs=(
            P("dp", "mp", None),
            P("dp", "mp", None),
            P("mp", None),
            P("mp", None),
            P("mp", None, None),
            P("mp", None, None),
            P(),
            P(),
            P(),
            P(),
        ),
        check_vma=False,
    )
```

```python
import functools

import jax
import jax.numpy as jnp
import numpy as np
from jax import lax
from jax.experimental import pallas as pl
from jax.experimental.pallas import tpu as pltpu
from jax.sharding import PartitionSpec as P

H = 20
KVH = 5
HD = 64
TILE = 128
EPSILON = 1e-06
QW = H * HD
LANES = 128
GW = (H // KVH) * HD
DOCS = 3
AWAY = 256.0
LOG2E = 1.4426950408889634
LN2 = 0.6931471805599453
BF = jnp.bfloat16
F32 = jnp.float32
MIB = 1 << 20
NT = (((1,), (1,)), ((), ()))
TN = (((0,), (0,)), ((), ()))


def params(mib=56, axes=1, key=None):
    if key is None:
        return pltpu.CompilerParams(
            vmem_limit_bytes=mib * MIB, dimension_semantics=("arbitrary",) * axes
        )
    return pltpu.CompilerParams(
        vmem_limit_bytes=mib * MIB,
        dimension_semantics=("arbitrary",) * axes if axes else None,
        collective_id=key,
        has_side_effects=True,
    )


TINY = pl.CostEstimate(flops=1, bytes_accessed=1, transcendentals=0)


def mm(a, b):
    return jnp.dot(a, b, preferred_element_type=F32)


def dg(a, b, dims):
    return lax.dot_general(a, b, dims, preferred_element_type=F32)


def rotary_tables(positions):
    half_dim = HD // 2
    freqs = 1.0 / 10000.0 ** (jnp.arange(half_dim, dtype=jnp.float32) * 2.0 / HD)
    angles = positions.astype(jnp.float32)[..., None] * jnp.tile(freqs, 4)
    return jnp.cos(angles), jnp.sin(angles)


def rms_scale(values):
    return lax.rsqrt(jnp.mean(values * values, axis=-1, keepdims=True) + EPSILON)


MESH = pl.DeviceIdType.MESH


def flip(me, k):
    bit = 1
    while bit <= k:
        if k & bit:
            me = me + bit - 2 * bit * lax.rem(lax.div(me, bit), 2)
        bit *= 2
    return me


def link_bits(n):
    return [1 << i for i in range(1, n.bit_length() - 1)]


def greet(n, me):
    barrier = pltpu.get_barrier_semaphore()
    bits = [1] + link_bits(n)
    for bit in bits:
        pl.semaphore_signal(barrier, inc=1, device_id={"mp": flip(me, bit)}, device_id_type=MESH)
    pl.semaphore_wait(barrier, len(bits))


def greet_all(n, me, m, line):
    barrier = pltpu.get_barrier_semaphore()
    bits = [1] + link_bits(n)
    for bit in bits:
        pl.semaphore_signal(barrier, inc=1, device_id={"mp": flip(me, bit)}, device_id_type=MESH)
    for step in range(1, m):
        other = lax.rem(line + step, m)
        pl.semaphore_signal(barrier, inc=1, device_id={"dp": other}, device_id_type=MESH)
    pl.semaphore_wait(barrier, len(bits) + m - 1)


class Line:
    def __init__(self, m, line, own, up, across, total, sems):
        self.own, self.up, self.across, self.total, self.sems = own, up, across, total, sems
        low = line < m // 2
        self.inner = jnp.where(low, line + 1, line - 1)
        self.outer = jnp.where(low, line - 1, line + 1)
        self.has_outer = (line > 0) & (line < m - 1)
        self.middle = (line == m // 2 - 1) | (line == m // 2)

    def copy(self, kind, c):
        src, dst, to = (
            (self.own, self.up, self.inner),
            (self.own, self.across, self.inner),
            (self.total, self.total, self.outer),
        )[kind]
        return pltpu.make_async_remote_copy(
            src_ref=src(c),
            dst_ref=dst(c),
            send_sem=self.sems.at[2 * kind, c],
            recv_sem=self.sems.at[2 * kind + 1, c],
            device_id={"dp": to},
            device_id_type=MESH,
        )

    def launch(self, c):
        @pl.when(jnp.logical_not(self.has_outer))
        def _():
            self.copy(0, c).start()

    def inward(self, c):
        @pl.when(self.has_outer)
        def _():
            self.copy(0, c).wait_recv()
            add_up(self.own(c), [self.own(c), self.up(c)])

            @pl.when(self.middle)
            def _():
                self.copy(1, c).start()

            @pl.when(jnp.logical_not(self.middle))
            def _():
                self.copy(0, c).start()

    def outward(self, c):
        @pl.when(self.middle)
        def _():
            self.copy(1, c).wait_recv()
            add_up(self.total(c), [self.own(c), self.across(c)])

        @pl.when(jnp.logical_not(self.middle))
        def _():
            self.copy(2, c).wait_recv()

        @pl.when(self.has_outer)
        def _():
            self.copy(2, c).start()

    def drain(self, c):
        @pl.when(self.middle)
        def _():
            self.copy(1, c).wait_send()

        @pl.when(jnp.logical_not(self.middle))
        def _():
            self.copy(0, c).wait_send()

        @pl.when(self.has_outer)
        def _():
            self.copy(2, c).wait_send()


class Gather:
    def __init__(self, n, me, own, slot, send, recv, relative=False):
        self.n, self.me, self.own, self.slot, self.send, self.recv = n, me, own, slot, send, recv
        self.relative = relative
        bits = link_bits(n)
        self.order = (bits + [1], bits[::-1] + [1])
        even = [(k, h) for k in range(2, n, 2) for h in (0, 1)]
        even.sort(key=lambda kh: (bin(kh[0]).count("1"), max(self.place(*kh)), kh[1]))
        self.even = even

    def place(self, k, half):
        return [i for i, bit in enumerate(self.order[half]) if k & bit]

    def copy(self, k, half, bit):
        return pltpu.make_async_remote_copy(
            src_ref=self.own(half) if k == 0 else self.here(k, half),
            dst_ref=self.slot(k ^ bit, half, k) if self.relative else self.slot(k, half),
            send_sem=self.send.at[k ^ bit, half],
            recv_sem=self.recv.at[k ^ bit, half],
            device_id={"mp": flip(self.me, bit)},
            device_id_type=MESH,
        )

    def here(self, k, half):
        return self.slot(k, half, k) if self.relative else self.slot(k, half)

    def onward(self, k, half):
        return self.order[half][(max(self.place(k, half)) + 1) if k else 0 :]

    def start(self):
        for i in range(len(self.order[0])):
            for half in (0, 1):
                self.copy(0, half, self.order[half][i]).start()

    def arrive(self, k, half):
        here = self.here(k, half)
        pltpu.make_async_remote_copy(
            src_ref=here,
            dst_ref=here,
            send_sem=self.send.at[k, half],
            recv_sem=self.recv.at[k, half],
            device_id={"mp": flip(self.me, 1)},
            device_id_type=MESH,
        ).wait_recv()

    def forward(self, k, half):
        self.arrive(k, half)
        for bit in self.onward(k, half):
            self.copy(k, half, bit).start()

    def rest(self):
        for k, half in [(1, 0), (1, 1)] + [(k + 1, h) for k, h in self.even]:
            self.arrive(k, half)

    def drain(self):
        for k in range(0, self.n, 2):
            for half in (0, 1):
                for bit in self.onward(k, half):
                    self.copy(k, half, bit).wait_send()


class Scatter:
    def __init__(self, n, me, part, core, link, sems):
        self.n, self.me, self.part = n, me, part
        self.core, self.link = core, link
        self.core_send, self.core_recv, self.link_send, self.link_recv = sems
        bits = link_bits(n)
        self.order = (bits[::-1], bits)

    def first(self, k, half):
        return next(i for i, bit in enumerate(self.order[half]) if k & bit)

    def core_copy(self, k, ref):
        return pltpu.make_async_remote_copy(
            src_ref=ref,
            dst_ref=self.core(k // 2),
            send_sem=self.core_send.at[k // 2],
            recv_sem=self.core_recv.at[k // 2],
            device_id={"mp": flip(self.me, 1)},
            device_id_type=MESH,
        )

    def link_copy(self, k, half):
        bit = self.order[half][self.first(k, half)]
        return pltpu.make_async_remote_copy(
            src_ref=self.part(self.core(k // 2), half),
            dst_ref=self.link(half, k // 2 - 1),
            send_sem=self.link_send.at[half, k // 2 - 1],
            recv_sem=self.link_recv.at[half, k // 2 - 1],
            device_id={"mp": flip(self.me, bit)},
            device_id_type=MESH,
        )

    def addends(self, k, half):
        upto = self.first(k, half) if k else len(self.order[half])
        return [k | bit for bit in self.order[half][:upto]]

    def odd(self, k, ref):
        self.core_copy(k, ref).start()

    def even(self, k, ref):
        self.core_copy(k + 1, self.core(k // 2)).wait_recv()
        for half in sorted((0, 1), key=lambda h: -len(self.addends(k, h))):
            joined = [self.part(ref, half), self.part(self.core(k // 2), half)]
            for j in self.addends(k, half):
                self.link_copy(j, half).wait_recv()
                joined.append(self.link(half, j // 2 - 1))
            add_up(joined[1], joined)
            self.link_copy(k, half).start()

    def own(self, ref, out):
        self.core_copy(1, self.core(0)).wait_recv()
        for half in (0, 1):
            joined = [self.part(ref, half), self.part(self.core(0), half)]
            for j in self.addends(0, half):
                self.link_copy(j, half).wait_recv()
                joined.append(self.link(half, j // 2 - 1))
            add_up(self.part(out, half), joined)

    def drain(self, ref):
        for k in range(1, self.n, 2):
            self.core_copy(k, ref).wait_send()
        for k in range(2, self.n, 2):
            for half in (0, 1):
                self.link_copy(k, half).wait_send()


def add_up(out, terms):
    rows, width = out.shape[-2:]
    step = 16
    while 2 * step * width <= 32768 and rows % (2 * step) == 0:
        step *= 2
    lead = (slice(None),) * (len(out.shape) - 2)

    @pl.loop(0, rows // step)
    def _(i):
        at = lead + (pl.ds(pl.multiple_of(i * step, step), step), slice(None))
        if len(terms) == 2 and all(t.dtype == BF for t in (out, *terms)):
            out[at] = terms[0][at] + terms[1][at]
        else:
            total = terms[0][at].astype(F32)
            for t in terms[1:]:
                total = total + t[at].astype(F32)
            out[at] = total.astype(out.dtype)


def scatter_scratch(n, shape, half):
    return [
        pltpu.VMEM((n // 2,) + shape, BF),
        pltpu.VMEM((2, n // 2 - 1) + half, BF),
        pltpu.SemaphoreType.DMA((n // 2,)),
        pltpu.SemaphoreType.DMA((n // 2,)),
        pltpu.SemaphoreType.DMA((2, n // 2 - 1)),
        pltpu.SemaphoreType.DMA((2, n // 2 - 1)),
    ]


def make_scatter(n, me, part, refs):
    core, link = refs[:2]
    return Scatter(
        n,
        me,
        part,
        lambda i: core.at[i],
        lambda h, i: link.at[h, i],
        refs[2:6],
    )


def half_turn(x, lane):
    first = (lane % HD) < HD // 2
    return jnp.where(first, -pltpu.roll(x, LANES - HD // 2, 1), pltpu.roll(x, HD // 2, 1))


def half_turn_back(x, lane):
    first = (lane % HD) < HD // 2
    return jnp.where(first, pltpu.roll(x, LANES - HD // 2, 1), -pltpu.roll(x, HD // 2, 1))


def group_mean(x, ones):
    high = x.astype(BF)
    low = (x - high.astype(F32)).astype(BF)
    return (mm(high, ones) + mm(low, ones)) * (1.0 / HD)


def project_kernel(
    n, x_any, gain_ref, w_ref, o_ref, cos_ref, sin_ref, gq_ref, gk_ref, ones_ref, grad_any,
    normed_any, raw_any, q_ref, branch_any, w_out, kv_out, o_out,
    x_ref, grad_ref, normed_ref, raw_ref, branch_ref, moves, w_all, kv_own, w_send, w_recv, kv_send, kv_recv, o_send, o_recv, local,
):
    me = lax.axis_index("mp")
    depth = w_ref.shape[0]
    tokens, width = x_ref.shape
    rows = kv_out.shape[0]
    span = tokens // rows
    half = depth // 2
    own_w = pltpu.make_async_copy(w_ref, w_all.at[me], local.at[0])
    own_w.start()
    early = [
        pltpu.make_async_copy(x_any, x_ref, moves.at[0]),
        pltpu.make_async_copy(grad_any, grad_ref, moves.at[1]),
    ]
    late = [
        pltpu.make_async_copy(normed_ref, normed_any, moves.at[2]),
        pltpu.make_async_copy(branch_ref, branch_any, moves.at[3]),
        pltpu.make_async_copy(raw_ref, raw_any, moves.at[4]),
    ]
    for c in early:
        c.start()
    own_o = pltpu.make_async_copy(o_ref, o_out.at[me], local.at[1 + rows])
    own_o.start()
    greet(n, me)
    wide = o_ref.shape[1] // 2
    outs = Gather(
        n,
        me,
        lambda h: o_ref.at[:, pl.ds(h * wide, wide)],
        lambda k, h: o_out.at[flip(me, k), :, pl.ds(h * wide, wide)],
        o_send,
        o_recv,
    )
    weights = Gather(
        n,
        me,
        lambda h: w_ref.at[pl.ds(h * half, half)],
        lambda k, h: w_all.at[flip(me, k), pl.ds(h * half, half)],
        w_send,
        w_recv,
    )
    weights.start()
    for c in early:
        c.wait()
    step = min(64, tokens)

    @pl.loop(0, tokens // step)
    def _(i):
        at = pl.ds(pl.multiple_of(i * step, step), step)
        x = x_ref[at, :].astype(F32)
        scale = lax.rsqrt(jnp.mean(x * x, axis=-1, keepdims=True) + EPSILON)
        normed_ref[at, :] = (x * scale * gain_ref[...]).astype(BF)
        branch_ref[at, :] = grad_ref[at, :].astype(BF)

    chunk = min(256, tokens)

    def accumulate(k, fresh):
        block = flip(me, k)
        columns = pl.ds(pl.multiple_of(block * depth, depth), depth)

        @pl.loop(0, tokens // chunk)
        def _(i):
            at = pl.ds(pl.multiple_of(i * chunk, chunk), chunk)
            term = mm(normed_ref[at, columns], w_all[block])
            raw_ref[at, :] = term if fresh else raw_ref[at, :] + term

    own_w.wait()
    accumulate(0, True)
    for h in (0, 1):
        weights.arrive(1, h)
    accumulate(1, False)
    for i, (k, h) in enumerate(weights.even):
        weights.forward(k, h)
        if any(k == other for other, _ in weights.even[:i]):
            accumulate(k, False)
    outs.start()
    for k in range(3, n, 2):
        for h in (0, 1):
            weights.arrive(k, h)
        accumulate(k, False)
    out_w = pltpu.make_async_copy(w_all, w_out, local.at[0])
    out_w.start()
    for c in late:
        c.start()

    chunk = min(128, tokens)
    lane = lax.broadcasted_iota(jnp.int32, (chunk, LANES), 1)

    gain_q = jnp.concatenate([gq_ref[...], gq_ref[...]], axis=1)
    gain_k = jnp.concatenate([gk_ref[...], jnp.ones_like(gk_ref[...])], axis=1)

    def finish(i, tiles):
        at = pl.ds(pl.multiple_of(i * chunk, chunk), chunk)
        cos, sin = cos_ref[at, :], sin_ref[at, :]
        for tile in tiles:
            lanes = slice(tile * LANES, (tile + 1) * LANES)
            x = raw_ref[at, lanes]
            query = tile < QW // LANES
            scale = lax.rsqrt(group_mean(x * x, ones_ref[...]) + EPSILON)
            v = x * scale * (gain_q if query else gain_k)
            y = v * cos + half_turn(v, lane) * sin
            if query:
                q_ref[at, lanes] = (y * (HD**-0.5 * LOG2E)).astype(BF)
            else:
                mine = slice(tile * LANES - QW, (tile + 1) * LANES - QW)
                kv_own[at, mine] = jnp.where(lane < HD, y, x).astype(BF)

    count = raw_ref.shape[1] // LANES

    @pl.loop(0, tokens // chunk)
    def _(i):
        finish(i, range(QW // LANES, count))

    both = rows // 2
    keep = [
        pltpu.make_async_copy(
            kv_own.at[pl.ds(r * span, span)], kv_out.at[r, me], local.at[1 + r]
        )
        for r in range(rows)
    ]
    for c in keep:
        c.start()
    kvs = Gather(
        n,
        me,
        lambda h: kv_own.at[pl.ds(h * span, span)],
        lambda k, h: kv_out.at[h, flip(me, k)],
        kv_send,
        kv_recv,
    )
    kvs.start()

    @pl.loop(0, tokens // chunk)
    def _(i):
        finish(i, range(QW // LANES))

    for k, h in kvs.even:
        outs.forward(k, h)
        kvs.forward(k, h)
    outs.rest()
    kvs.rest()
    for c in keep:
        c.wait()
    out_w.wait()
    own_o.wait()
    for c in late:
        c.wait()
    weights.drain()
    outs.drain()
    kvs.drain()


def project(n, rows, x, gain, w, o, cos, sin, gq, gk, ones, grad):
    tokens, width = x.shape
    depth, columns = w.shape
    vmem = pl.BlockSpec(memory_space=pltpu.VMEM)
    hbm = pl.BlockSpec(memory_space=pl.ANY)
    kvw = columns - QW
    return pl.pallas_call(
        functools.partial(project_kernel, n),
        in_specs=[hbm, vmem, hbm, hbm, vmem, vmem, vmem, vmem, vmem, hbm],
        out_specs=[hbm, hbm, vmem, hbm, hbm, hbm, hbm],
        out_shape=[
            jax.ShapeDtypeStruct((tokens, width), BF),
            jax.ShapeDtypeStruct((tokens, columns), F32),
            jax.ShapeDtypeStruct((tokens, QW), BF),
            jax.ShapeDtypeStruct((tokens, width), BF),
            jax.ShapeDtypeStruct((n, depth, columns), BF),
            jax.ShapeDtypeStruct((rows, n, tokens // rows, kvw), BF),
            jax.ShapeDtypeStruct((n,) + o.shape, BF),
        ],
        scratch_shapes=[
            pltpu.VMEM((tokens, width), BF),
            pltpu.VMEM((tokens, width), F32),
            pltpu.VMEM((tokens, width), BF),
            pltpu.VMEM((tokens, columns), F32),
            pltpu.VMEM((tokens, width), BF),
            pltpu.SemaphoreType.DMA((5,)),
            pltpu.VMEM((n, depth, columns), BF),
            pltpu.VMEM((tokens, kvw), BF),
            pltpu.SemaphoreType.DMA((n, 2)),
            pltpu.SemaphoreType.DMA((n, 2)),
            pltpu.SemaphoreType.DMA((n, 2)),
            pltpu.SemaphoreType.DMA((n, 2)),
            pltpu.SemaphoreType.DMA((n, 2)),
            pltpu.SemaphoreType.DMA((n, 2)),
            pltpu.SemaphoreType.DMA((2 + rows,)),
        ],
        compiler_params=params(axes=0, key=0),
        name="project",
    )(x, gain, w, o, cos, sin, gq, gk, ones, grad)


def unproject_kernel(
    n, dq_any, dkv_any, raw_any, cos_ref, sin_ref, gq_ref, gk_ref, ones_ref,
    gj_ref, sq_ref, sk_ref,
    dkv_own, dkv_ref, dq_ref, raw_ref, load, *scratch,
):
    me = lax.axis_index("mp")
    early = [
        pltpu.make_async_copy(dkv_any.at[:, flip(me, k)], dkv_ref.at[k // 2], load.at[2 + k // 2])
        for k in range(n - 2, -1, -2)
    ]
    late = [
        pltpu.make_async_copy(dq_any, dq_ref, load.at[0]),
        pltpu.make_async_copy(raw_any, raw_ref, load.at[1]),
    ]
    for c in early + late:
        c.start()
    greet(n, me)
    tokens = dq_ref.shape[0]
    rows = dkv_any.shape[0]
    span = tokens // rows
    columns = raw_ref.shape[1]
    keys = make_scatter(n, me, lambda ref, h: ref.at[h], scratch[:6])

    def dkv_term(k):
        return dkv_any.at[:, flip(me, k)] if k % 2 else dkv_ref.at[k // 2]

    for k in range(n - 1, 0, -2):
        keys.odd(k, dkv_term(k))
    for c in early:
        c.wait()
    keys.even(n - 2, dkv_term(n - 2))
    for c in late:
        c.wait()

    chunk = min(128, tokens)
    lane = lax.broadcasted_iota(jnp.int32, (chunk, LANES), 1)
    sq_ref[...] = jnp.zeros_like(sq_ref)
    sk_ref[...] = jnp.zeros_like(sk_ref)

    def back(i, tiles, query):
        at = pl.ds(pl.multiple_of(i * chunk, chunk), chunk)
        cos, sin = cos_ref[at, :], sin_ref[at, :]
        total = 0.0
        for tile in tiles:
            lanes = slice(tile * LANES, (tile + 1) * LANES)
            x = raw_ref[at, lanes]
            if query:
                e = dq_ref[at, lanes]
            else:
                per = span // chunk
                here = pl.ds(pl.multiple_of(lax.rem(i, per) * chunk, chunk), chunk)
                e = dkv_own[lax.div(i, per), here, slice(tile * LANES - QW, (tile + 1) * LANES - QW)]
            scale = lax.rsqrt(group_mean(x * x, ones_ref[...]) + EPSILON)
            v = x * scale
            turned = e * cos + half_turn_back(e * sin, lane)
            u = turned * (gq_ref[...] if query else gk_ref[...])
            grad = scale * (u - v * group_mean(u * v, ones_ref[...]))
            gj_ref[at, lanes] = (grad if query else jnp.where(lane < HD, grad, e)).astype(BF)
            total = total + jnp.sum(turned * v, axis=0, keepdims=True)
        sums = sq_ref if query else sk_ref
        sums[...] += jnp.broadcast_to(total, sums.shape)

    count = columns // LANES

    parts = tokens // chunk
    left = list(range(n - 4, 0, -2))
    for i in range(parts):
        back(i, range(QW // LANES), True)
        if i == 0:
            for k in left:
                keys.even(k, dkv_term(k))

    keys.own(dkv_term(0), dkv_own)

    @pl.loop(0, tokens // chunk)
    def _(i):
        back(i, range(QW // LANES, count), False)

    keys.drain(dkv_term(0))


def unproject(n, dq, dkv, raw, cos, sin, gq, gk, ones):
    tokens, columns = raw.shape
    rows = dkv.shape[0]
    span = tokens // rows
    kvw = columns - QW
    vmem = pl.BlockSpec(memory_space=pltpu.VMEM)
    hbm = pl.BlockSpec(memory_space=pl.ANY)
    return pl.pallas_call(
        functools.partial(unproject_kernel, n),
        in_specs=[hbm] * 3 + [vmem] * 5,
        out_specs=[vmem] * 3,
        out_shape=[
            jax.ShapeDtypeStruct((tokens, columns), BF),
            jax.ShapeDtypeStruct((8, LANES), F32),
            jax.ShapeDtypeStruct((8, LANES), F32),
        ],
        scratch_shapes=[
            pltpu.VMEM((rows, span, kvw), F32),
            pltpu.VMEM((n // 2, rows, span, kvw), BF),
            pltpu.VMEM(dq.shape, F32),
            pltpu.VMEM(raw.shape, F32),
            pltpu.SemaphoreType.DMA((2 + n // 2,)),
        ]
        + scatter_scratch(n, (rows, span, kvw), (span, kvw)),
        compiler_params=params(mib=60, axes=0, key=2),
        cost_estimate=TINY,
        name="unproject",
    )(dq, dkv, raw, cos, sin, gq, gk, ones)


GAIN_ROWS = 40


def finish_kernel(
    n, m, normed_any, gj_any, w_any, x_any, mid_any, gain_ref, share_any, feed_ref, sq_ref, sk_ref,
    grad_any, attend_ref, out_ref, gains_ref,
    normed_ref, gj_ref, x_ref, grad_ref,
    w_ref, term, error, mid_ref, own_w, up_w, across_w, own_o, up_o, across_o, landed,
    sem_w, sem_o, sem_g, load, *scratch,
):
    me, line = lax.axis_index("mp"), lax.axis_index("dp")
    depth = w_ref.shape[1]
    tokens, width = x_ref.shape
    pieces, piece = own_w.shape[0], own_w.shape[1]
    o_pieces, o_piece = own_o.shape[0], own_o.shape[1]
    chunk = error.shape[0]
    early = [
        pltpu.make_async_copy(normed_any, normed_ref, load.at[2]),
        pltpu.make_async_copy(gj_any, gj_ref, load.at[3]),
        pltpu.make_async_copy(share_any, own_o, load.at[4]),
    ]
    fetch = [
        pltpu.make_async_copy(w_any, w_ref, load.at[0]),
        pltpu.make_async_copy(x_any, x_ref, load.at[5]),
    ]
    keep = pltpu.make_async_copy(grad_ref, grad_any, load.at[6])
    for c in early + fetch:
        c.start()

    def bring(i):
        here = pl.ds(pl.multiple_of(i * chunk, chunk), chunk)
        return pltpu.make_async_copy(mid_any.at[here], mid_ref, load.at[1])

    bring(0).start()
    greet_all(n, me, m, line)
    half = depth // 2
    sums = make_scatter(n, me, lambda ref, h: ref.at[pl.ds(h * half, half)], scratch)
    at = lambda ref: lambda c: ref.at[c]
    weights = Line(m, line, at(own_w), at(up_w), at(across_w), at(up_w), sem_w)
    out_line = Line(m, line, at(own_o), at(up_o), at(across_o), at(up_o), sem_o)
    tiles = width // LANES
    gains_ref[...] = jnp.zeros_like(gains_ref)
    gains_ref[tiles : 2 * tiles, :] = feed_ref[...]
    gains_ref[2 * tiles : 2 * tiles + 1, :] = sq_ref[:1, :]
    gains_ref[2 * tiles + 1 : 2 * tiles + 2, :] = sk_ref[:1, :]

    def tokens_part(i):
        here = pl.ds(pl.multiple_of(i * chunk, chunk), chunk)
        for b in range(n):
            error[:, b * depth : (b + 1) * depth] = dg(gj_ref[here, :], w_ref[b], NT)
        small = min(32, chunk)
        bring(i).wait()

        @pl.loop(0, chunk // small)
        def _(s):
            part = pl.ds(pl.multiple_of(s * small, small), small)
            rows = pl.ds(pl.multiple_of(i * chunk + s * small, small), small)
            e = error[part, :]
            x = x_ref[rows, :].astype(F32)
            scale = lax.rsqrt(jnp.mean(x * x, axis=-1, keepdims=True) + EPSILON)
            u = e * gain_ref[...]
            v = x * scale
            inner = jnp.mean(u * v, axis=-1, keepdims=True)
            grad_ref[rows, :] = mid_ref[part, :] + scale * (u - v * inner)
            total = jnp.sum(e * v, axis=0, keepdims=True)
            for b in range(width // LANES):
                gains_ref[b : b + 1, :] += total[:, b * LANES : (b + 1) * LANES]

        if i + 1 < tokens // chunk:
            bring(i + 1).start()

    def mine(k):
        return term.at[k // 2 if k % 2 else n // 2]

    def weight_part(k):
        columns = pl.ds(pl.multiple_of(flip(me, k) * depth, depth), depth)
        mine(k)[...] = dg(normed_ref[:, columns], gj_ref[...], TN).astype(BF)

    steps = [("mp", flip(me, 1 << i)) for i in range(n.bit_length() - 1)]
    steps += [("dp", flip(line, 1 << i)) for i in range(m.bit_length() - 1)]

    def exchange(i):
        axis, to = steps[i]
        return pltpu.make_async_remote_copy(
            src_ref=landed.at[2 * i],
            dst_ref=landed.at[2 * i + 1],
            send_sem=sem_g.at[0, i],
            recv_sem=sem_g.at[1, i],
            device_id={axis: to},
            device_id_type=MESH,
        )

    for c in early:
        c.wait()
    for c in range(o_pieces):
        out_line.launch(c)
    for k in range(n - 1, 0, -2):
        weight_part(k)
        sums.odd(k, mine(k))
        if k == n - 1:
            weight_part(n - 2)
            sums.even(n - 2, mine(n - 2))
    for c in fetch:
        c.wait()
    tokens_part(0)
    for k in range(n - 4, 0, -2):
        weight_part(k)
        sums.even(k, mine(k))
    weight_part(0)
    for i in range(1, tokens // chunk):
        tokens_part(i)
    keep.start()
    for i in range(len(steps)):
        landed[2 * i] = gains_ref[...]
        exchange(i).start()
        exchange(i).wait_recv()
        gains_ref[...] = landed[2 * i] + landed[2 * i + 1]
    sums.own(mine(0), attend_ref)
    for c in range(pieces):
        own_w[c] = attend_ref[c * piece : (c + 1) * piece, :].astype(BF)
        weights.launch(c)
    for c in range(o_pieces):
        out_line.inward(c)
    kw = KVH * HD

    def widen(c):
        rows = slice(c * piece, (c + 1) * piece)
        attend_ref[rows, :QW] = up_w[c, :, :QW].astype(F32)
        for h in range(KVH):
            both = up_w[c, :, QW + 2 * h * HD : QW + 2 * (h + 1) * HD].astype(F32)
            attend_ref[rows, QW + h * HD : QW + (h + 1) * HD] = both[:, :HD]
            attend_ref[rows, QW + kw + h * HD : QW + kw + (h + 1) * HD] = both[:, HD:]

    ahead = 2
    for c in range(pieces + ahead):
        if c < pieces:
            weights.inward(c)
        if c < o_pieces:
            out_line.outward(c)
            out_ref[c * o_piece : (c + 1) * o_piece, :] = up_o[c].astype(F32)
        if c >= ahead:
            weights.outward(c - ahead)
            widen(c - ahead)
    keep.wait()
    for c in range(o_pieces):
        out_line.drain(c)
    for c in range(pieces):
        weights.drain(c)
    for i in range(len(steps)):
        exchange(i).wait_send()
    sums.drain(mine(0))


def finish(n, m, normed, gj, w, x, middle, gain, share, gain_feed, sum_q, sum_k):
    tokens, width = x.shape
    columns = gj.shape[1]
    depth = width // n
    pieces, o_pieces = 8, 5
    split = (o_pieces, share.shape[0] // o_pieces, width)
    chunk = min(256, tokens)
    vmem = pl.BlockSpec(memory_space=pltpu.VMEM)
    hbm = pl.BlockSpec(memory_space=pl.ANY)
    steps = n.bit_length() + m.bit_length() - 2
    return pl.pallas_call(
        functools.partial(finish_kernel, n, m),
        in_specs=[hbm, hbm, hbm, hbm, hbm, vmem, hbm, vmem, vmem, vmem],
        out_specs=[hbm, vmem, vmem, vmem],
        out_shape=[
            jax.ShapeDtypeStruct((tokens, width), F32),
            jax.ShapeDtypeStruct((depth, columns), F32),
            jax.ShapeDtypeStruct(share.shape, F32),
            jax.ShapeDtypeStruct((GAIN_ROWS, LANES), F32),
        ],
        scratch_shapes=[
            pltpu.VMEM((tokens, width), BF),
            pltpu.VMEM((tokens, columns), BF),
            pltpu.VMEM((tokens, width), BF),
            pltpu.VMEM((tokens, width), F32),
            pltpu.VMEM(w.shape, BF),
            pltpu.VMEM((n // 2 + 1, depth, columns), BF),
            pltpu.VMEM((chunk, width), F32),
            pltpu.VMEM((chunk, width), F32),
        ]
        + [pltpu.VMEM((pieces, depth // pieces, columns), BF)] * 3
        + [pltpu.VMEM(split, BF)] * 3
        + [
            pltpu.VMEM((2 * steps, GAIN_ROWS, LANES), F32),
            pltpu.SemaphoreType.DMA((6, pieces)),
            pltpu.SemaphoreType.DMA((6, o_pieces)),
            pltpu.SemaphoreType.DMA((2, steps)),
            pltpu.SemaphoreType.DMA((7,)),
        ]
        + scatter_scratch(n, (depth, columns), (depth // 2, columns)),
        compiler_params=params(mib=60, axes=0, key=5),
        cost_estimate=TINY,
        name="finish",
    )(normed, gj, w, x, middle, gain, share.reshape(split), gain_feed, sum_q, sum_k)


def key_positions(shape, axis, group, per, span):
    return group * per * span + lax.broadcasted_iota(jnp.int32, shape, axis)


def attend_kernel(keys, info, q_ref, kv_ref, start_ref, ctx_ref, rl_ref, acc):
    span = q_ref.shape[1]
    per = keys // span
    row = pl.program_id(0)
    me, first, last_start = info[row, 0], info[row, 1], info[row, 2]
    low_q = lax.broadcasted_iota(jnp.int32, (span, LANES), 1) < HD
    low_k = lax.broadcasted_iota(jnp.int32, (keys, LANES), 1) < HD
    one = jnp.ones((keys, LANES), BF)
    none = jnp.zeros((span, LANES), BF)
    queries = []
    for h in range(GW // HD):
        pair = q_ref[0, :, (h // 2) * LANES : (h // 2 + 1) * LANES]
        queries.append(jnp.where(low_q, pair, none) if h % 2 == 0 else jnp.where(low_q, none, pair))
    acc[...] = jnp.zeros_like(acc)

    def block(g, masked):
        group = g
        kv = kv_ref[0, pl.ds(pl.multiple_of(group * keys, keys), keys), :]
        vk = jnp.concatenate([kv[:, HD:], kv[:, :HD]], axis=1)
        key_sides = (kv, vk)
        value_sides = (jnp.where(low_k, vk, one), jnp.where(low_k, one, kv))
        if masked:
            position = key_positions((span, keys), 1, group, per, span)
            own = me * span + lax.broadcasted_iota(jnp.int32, (span, keys), 0)
            seen = (position <= own) & (position >= start_ref[0][:, :1])
        for h in range(GW // HD):
            p = jnp.exp2(dg(queries[h], key_sides[h % 2], NT))
            if masked:
                p = jnp.where(seen, p, 0.0)
            acc[h] += mm(p.astype(BF), value_sides[h % 2])

    def step(g, carry):
        edge = (g == me // per) | (g * keys < last_start)
        pl.when(edge)(lambda: block(g, True))
        pl.when(jnp.logical_not(edge))(lambda: block(g, False))
        return carry

    lax.fori_loop(first, me // per + 1, step, 0)
    for pair in range(GW // LANES):
        even, odd = acc[2 * pair], acc[2 * pair + 1]
        total = jnp.where(low_q, pltpu.roll(even, HD, 1), pltpu.roll(odd, HD, 1))
        inverse = 1.0 / total
        lanes = slice(pair * LANES, (pair + 1) * LANES)
        ctx_ref[0, :, lanes] = (jnp.where(low_q, even, odd) * inverse).astype(BF)
        rl_ref[0, :, lanes] = inverse


def attend(info, q, kv, start):
    rows, span, _ = q.shape
    length = kv.shape[1]
    keys = min(512, length)
    own = lambda r, h, info: (r, 0, h)
    spec = pltpu.PrefetchScalarGridSpec(
        num_scalar_prefetch=1,
        grid=(rows, KVH),
        in_specs=[
            pl.BlockSpec((1, span, GW), own),
            pl.BlockSpec((1, length, LANES), own),
            pl.BlockSpec((1, span, LANES), lambda r, h, info: (r, 0, 0)),
        ],
        out_specs=[pl.BlockSpec((1, span, GW), own), pl.BlockSpec((1, span, GW), own)],
        scratch_shapes=[pltpu.VMEM((GW // HD, span, LANES), F32)],
    )
    return pl.pallas_call(
        functools.partial(attend_kernel, keys),
        grid_spec=spec,
        out_shape=[jax.ShapeDtypeStruct(q.shape, BF), jax.ShapeDtypeStruct(q.shape, F32)],
        compiler_params=params(axes=2),
        cost_estimate=pl.CostEstimate(
            flops=16 * rows * H * span * length * HD,
            bytes_accessed=rows * (length * 1280 + span * QW * 8),
            transcendentals=rows * H * span * length,
        ),
        name="attend",
    )(info, q, kv, start)


def attend_back_kernel(
    keys, n, q_ref, kv_ref, qa_ref, ka_ref, do_ref, ctx_ref, rl_ref, a_ref, w_any,
    gout_any, dq_ref, dkv_ref, o_ref, share_ref, acc, sides, gout_ref, moves, *scratch,
):
    span = q_ref.shape[1]
    per = keys // span
    length = kv_ref.shape[1]
    me = lax.axis_index("mp")
    rows = o_ref.shape[0]
    now = pl.program_id(0) * KVH + pl.program_id(1)
    sums = TileSum(n, me, o_ref, w_any, scratch)
    half_w = share_ref.shape[1] // 2
    outs = make_scatter(
        n, me, lambda ref, h: ref.at[:, pl.ds(h * half_w, half_w)], scratch[-6:]
    )

    def out_term(k):
        return gout_any.at[flip(me, k)] if k % 2 else gout_ref.at[k // 2]

    def bring(k):
        return pltpu.make_async_copy(gout_any.at[flip(me, k)], out_term(k), moves.at[k // 2])

    def out_event(i):
        if i == 0:
            for k in range(0, n, 2):
                bring(k).start()
            for k in range(n - 1, 0, -2):
                outs.odd(k, out_term(k))
        elif i < n // 2:
            k = n - 2 * i
            bring(k).wait()
            outs.even(k, out_term(k))
        else:
            bring(0).wait()
            outs.own(out_term(0), share_ref)

    batch = a_ref.shape[1]
    steps = rows * n // batch

    @pl.when(now == 0)
    def _():
        sums.start()

    @pl.when(now < steps)
    def _():
        @pl.loop(0, batch)
        def _(i):
            tile = now * batch + i
            _, slot = tile_at(tile, n)
            sums.step(tile, a_ref.at[0, lax.rem(xor_of(me, slot, n), batch)])

    count = n // 2 + 1
    for i in range(count):
        when = 1 + i if i < 2 else 5 + (i - 2) * 4 // (count - 2)

        @pl.when(now == (when if i < count - 1 else rows * KVH - 1))
        def _(i=i):
            out_event(i)

    lane = lax.broadcasted_iota(jnp.int32, (span, LANES), 1)
    low_q = lane < HD
    low_k = lax.broadcasted_iota(jnp.int32, (keys, LANES), 1) < HD
    one = jnp.ones((keys, LANES), BF)
    for h in range(GW // HD):
        lanes = slice((h // 2) * LANES, (h // 2 + 1) * LANES)
        mine = low_q if h % 2 == 0 else jnp.logical_not(low_q)
        scaled = do_ref[0, :, lanes].astype(F32) * rl_ref[0, :, lanes]
        own = jnp.where(mine, scaled, 0.0)
        delta = -jnp.sum(own * ctx_ref[0, :, lanes].astype(F32), axis=1, keepdims=True)
        one_part = delta.astype(BF).astype(F32)
        two_part = (delta - one_part).astype(BF).astype(F32)
        three_part = delta - one_part - two_part
        base = HD if h % 2 == 0 else 0
        extra = jnp.where(
            lane == base,
            one_part,
            jnp.where(lane == base + 1, two_part, jnp.where(lane == base + 2, three_part, 0.0)),
        )
        query = q_ref[0, :, lanes].astype(F32)
        sides[0, h] = jnp.where(mine, query, 0.0).astype(BF)
        sides[1, h] = own.astype(BF)
        sides[2, h] = jnp.where(mine, scaled, extra).astype(BF)
        sides[3, h] = jnp.where(mine, query, qa_ref[0].astype(F32)).astype(BF)
    acc[...] = jnp.zeros_like(acc)

    def block(g, masked):
        here = pl.ds(pl.multiple_of(g * keys, keys), keys)
        kv = kv_ref[0, here, :]
        ka = ka_ref[0, here, :]
        vk = jnp.concatenate([kv[:, HD:], kv[:, :HD]], axis=1)
        key_sides = (jnp.where(low_k, kv, ka), jnp.where(low_k, ka, vk))
        value_sides = (jnp.where(low_k, vk, one), jnp.where(low_k, one, kv))
        if masked:
            position = g * keys + lax.broadcasted_iota(jnp.int32, (keys, span), 0)
            seen = position <= me * span + lax.broadcasted_iota(jnp.int32, (keys, span), 1)
        turned = [s.T for s in key_sides]
        grad_key = grad_value = 0.0
        for h in range(GW // HD):
            e = jnp.exp2(dg(key_sides[h % 2], sides[3, h], NT))
            if masked:
                e = jnp.where(seen, e, 0.0)
            ds = (e * dg(value_sides[h % 2], sides[2, h], NT)).astype(BF)
            grad_value = grad_value + mm(e.astype(BF), sides[1, h])
            grad_key = grad_key + mm(ds, sides[0, h])
            acc[h] += mm(turned[h % 2], ds)
        grad_key = (grad_key + pltpu.roll(grad_key, HD, 1)) * LN2
        grad_value = grad_value + pltpu.roll(grad_value, HD, 1)
        dkv_ref[0, here, :] = jnp.where(low_k, grad_key, grad_value).astype(BF)

    last = lax.div(me, per)

    @pl.loop(0, last)
    def _(g):
        block(g, False)

    block(last, True)

    @pl.loop(last + 1, length // keys)
    def _(g):
        dkv_ref[0, pl.ds(pl.multiple_of(g * keys, keys), keys), :] = jnp.zeros((keys, LANES), BF)

    for pair in range(GW // LANES):
        lanes = slice(pair * LANES, (pair + 1) * LANES)
        dq_ref[0, :, lanes] = jnp.where(low_q, acc[2 * pair].T, acc[2 * pair + 1].T) * (HD**-0.5)

    @pl.when(now == rows * KVH - 1)
    def _():
        sums.end()
        outs.drain(out_term(0))


def attend_back(n, q, kv, qa, ka, do, ctx, rl, a, w, gout):
    rows, span, _ = q.shape
    length = kv.shape[1]
    keys = min(512, length)
    depth, width = w.shape
    batch = n // 4
    own = lambda r, h: (r, 0, h)

    def place(r, h):
        row, slot = tile_at(jnp.minimum(r * KVH + h, rows * n // batch - 1) * batch, n)
        return (row, lax.div(xor_of(lax.axis_index("mp"), slot, n), batch), 0, 0)

    return pl.pallas_call(
        functools.partial(attend_back_kernel, keys, n),
        grid=(rows, KVH),
        in_specs=[
            pl.BlockSpec((1, span, GW), own),
            pl.BlockSpec((1, length, LANES), own),
            pl.BlockSpec((1, span, LANES), lambda r, h: (r, 0, 0)),
            pl.BlockSpec((1, length, LANES), lambda r, h: (r, 0, 0)),
            pl.BlockSpec((1, span, GW), own),
            pl.BlockSpec((1, span, GW), own),
            pl.BlockSpec((1, span, GW), own),
            pl.BlockSpec((1, batch, span, depth), place),
            pl.BlockSpec(memory_space=pl.ANY),
            pl.BlockSpec(memory_space=pl.ANY),
        ],
        out_specs=[
            pl.BlockSpec((1, span, GW), own),
            pl.BlockSpec((1, length, LANES), own),
            pl.BlockSpec(memory_space=pltpu.VMEM),
            pl.BlockSpec(memory_space=pltpu.VMEM),
        ],
        out_shape=[
            jax.ShapeDtypeStruct(q.shape, F32),
            jax.ShapeDtypeStruct(kv.shape, BF),
            jax.ShapeDtypeStruct((rows, span, width), F32),
            jax.ShapeDtypeStruct(gout.shape[1:], BF),
        ],
        scratch_shapes=[
            pltpu.VMEM((GW // HD, LANES, span), F32),
            pltpu.VMEM((4, GW // HD, span, LANES), BF),
            pltpu.VMEM((n // 2,) + gout.shape[1:], BF),
            pltpu.SemaphoreType.DMA((n // 2,)),
        ]
        + tile_scratch(n, rows, span, w)
        + scatter_scratch(n, gout.shape[1:], (gout.shape[1], width // 2)),
        compiler_params=params(mib=60, axes=2, key=4),
        cost_estimate=TINY,
        name="attend_back",
    )(q, kv, qa, ka, do, ctx, rl, a, w, gout)


def xor_of(a, b, n):
    total, bit = 0, 1
    while bit < n:
        total = total + bit * lax.rem(lax.div(a, bit) + lax.div(b, bit), 2)
        bit *= 2
    return total


def feed_kernel(
    n, live_ref, x_own, g_ref, g_any, gu_any, dt_any,
    x_all, hid_ref, dgu_ref, gd_any,
    x_vm, gu_ref, dt_ref, d_sum, out_d, g_two, back, x_send, x_recv, loads, stores, keep,
):
    me = lax.axis_index("mp")
    rows, span, width = x_own.shape
    slots = gu_any.shape[0]
    r, p = pl.program_id(0), pl.program_id(1)
    pairs = n // 2
    now = r * pairs + p
    half = span // 2

    def gather(row):
        def slot(i, h, k):
            at = lax.rem(flip(me, k), 2) * span + h * half
            return x_vm.at[row, i // 2, pl.ds(pl.multiple_of(at, half), half)]

        return Gather(
            n,
            me,
            lambda h: x_own.at[row, pl.ds(h * half, half)],
            slot,
            x_send.at[row],
            x_recv.at[row],
            True,
        )

    def own_copy(row):
        at = pl.ds(pl.multiple_of(lax.rem(me, 2) * span, span), span)
        return pltpu.make_async_copy(x_own.at[row], x_vm.at[row, 0, at], loads.at[1 + row])

    fetch = [
        pltpu.make_async_copy(
            gu_any.at[t], gu_ref.at[:, pl.ds(2 * t * TILE, 2 * TILE)], loads.at[3 + rows + t]
        )
        for t in range(slots)
    ]
    fetch.append(pltpu.make_async_copy(dt_any, dt_ref, loads.at[0]))

    def events(row, upto):
        todo = gather(row).even
        ends = [0] * pairs
        for i in range(1, pairs):
            ends[i] = max(ends[i - 1], 1 + max(j for j, e in enumerate(todo) if e[0] == 2 * i))
        return todo[ends[upto - 1] if upto else 0 : ends[upto]]

    def ahead(i):
        block = lax.div(xor_of(me, 2 * lax.rem(i, pairs), n), 2)
        to = lax.rem(i, 2)
        return pltpu.make_async_copy(
            g_any.at[lax.div(i, pairs), block], g_two.at[to], loads.at[1 + rows + to]
        )

    @pl.when(now == 0)
    def _():
        for row in range(rows):
            own_copy(row).start()
        for c in fetch:
            c.start()
        greet(n, me)
        gather(0).start()
        ahead(0).start()
        d_sum[...] = jnp.zeros_like(d_sum)
        own_copy(0).wait()
        for c in fetch:
            c.wait()

        @pl.loop(0, rows * pairs)
        def _(i):
            @pl.when(i + 1 < rows * pairs)
            def _():
                ahead(i + 1).start()

            ahead(i).wait()
            back[i] = mm(g_two[lax.rem(i, 2)], dt_ref[...]).astype(BF)

            @pl.when(i == rows * pairs - 2)
            def _():
                for e in gather(0).even[:2]:
                    gather(0).forward(*e)
                for row in range(1, rows):
                    gather(row).start()

    for row in range(rows):
        for i in range(pairs):

            @pl.when(now == row * pairs + i)
            def _(row=row, i=i):
                if i == 0 and row:
                    own_copy(row).wait()
                for e in events(row, i):
                    if row or e not in gather(0).even[:2]:
                        gather(row).forward(*e)
                for h in (0, 1):
                    gather(row).arrive(2 * i + 1, h)

    def save(row, i):
        block = lax.div(xor_of(me, 2 * i, n), 2)
        return pltpu.make_async_copy(x_vm.at[row, i], x_all.at[row, block], keep.at[row, i])

    save(r, p).start()
    x = x_vm.at[r, p]
    full = mm(x[...], gu_ref[...])
    for t in range(slots):
        both = full[:, 2 * t * TILE : 2 * (t + 1) * TILE]
        gate, upper = both[:, :TILE], both[:, TILE:]
        live = live_ref[t]
        sig = jax.nn.sigmoid(gate)
        silu = gate * sig
        gh = back[now, :, t * TILE : (t + 1) * TILE].astype(F32) * live
        hid_ref[0, 0, :, t * TILE : (t + 1) * TILE] = (silu * upper * live).astype(BF)
        dgu_ref[0, 0, :, 2 * t * TILE : (2 * t + 1) * TILE] = (
            gh * upper * (sig * (1.0 + gate * (1.0 - sig)))
        ).astype(BF)
        dgu_ref[0, 0, :, (2 * t + 1) * TILE : (2 * t + 2) * TILE] = (gh * silu).astype(BF)

    d_sum[...] += dg(hid_ref[0, 0], g_ref[0, 0], TN)

    @pl.when(now == rows * pairs - 1)
    def _():
        def store(t):
            return pltpu.make_async_copy(out_d.at[t % 2], gd_any.at[t], stores.at[t % 2])

        for t in range(slots):
            if t > 1:
                store(t - 2).wait()
            out_d[t % 2] = d_sum[t * TILE : (t + 1) * TILE, :].astype(BF)
            store(t).start()
        for t in range(max(slots - 2, 0), slots):
            store(t).wait()
        for row in range(rows):
            for i in range(pairs):
                save(row, i).wait()
        for row in range(rows):
            gather(row).drain()


def feed(n, live, x, g, gu, dt):
    rows, span, width = x.shape
    slots = gu.shape[0]
    hbm = pl.BlockSpec(memory_space=pl.ANY)
    pairs = n // 2

    g = g.reshape(rows, pairs, 2 * span, width)

    def place(r, p):
        return (r, lax.div(xor_of(lax.axis_index("mp"), 2 * p, n), 2), 0, 0)

    return pl.pallas_call(
        functools.partial(feed_kernel, n),
        grid=(rows, pairs),
        in_specs=[
            pl.BlockSpec(memory_space=pltpu.SMEM),
            hbm,
            pl.BlockSpec((1, 1, 2 * span, width), place),
            hbm,
            hbm,
            hbm,
        ],
        out_specs=[
            hbm,
            pl.BlockSpec((1, 1, 2 * span, slots * TILE), place),
            pl.BlockSpec((1, 1, 2 * span, 2 * slots * TILE), place),
            hbm,
        ],
        out_shape=[
            jax.ShapeDtypeStruct((rows, pairs, 2 * span, width), BF),
            jax.ShapeDtypeStruct((rows, pairs, 2 * span, slots * TILE), BF),
            jax.ShapeDtypeStruct((rows, pairs, 2 * span, 2 * slots * TILE), BF),
            jax.ShapeDtypeStruct((slots, TILE, width), BF),
        ],
        scratch_shapes=[
            pltpu.VMEM((rows, pairs, 2 * span, width), BF),
            pltpu.VMEM((width, slots * 2 * TILE), BF),
            pltpu.VMEM(dt.shape, BF),
            pltpu.VMEM((slots * TILE, width), F32),
            pltpu.VMEM((2, TILE, width), BF),
            pltpu.VMEM((2, 2 * span, width), BF),
            pltpu.VMEM((rows * pairs, 2 * span, slots * TILE), BF),
            pltpu.SemaphoreType.DMA((rows, n, 2)),
            pltpu.SemaphoreType.DMA((rows, n, 2)),
            pltpu.SemaphoreType.DMA((3 + rows + slots,)),
            pltpu.SemaphoreType.DMA((2,)),
            pltpu.SemaphoreType.DMA((rows, pairs)),
        ],
        compiler_params=params(mib=62, axes=2, key=1),
        cost_estimate=pl.CostEstimate(
            flops=2 * 6 * rows * n * span * slots * TILE * width,
            bytes_accessed=6 * rows * n * span * width + 6 * slots * TILE * width,
            transcendentals=rows * n * span * slots * TILE,
        ),
        name="feed",
    )(live, x, g, g, gu, dt)


def pick(index, table):
    total = 0
    for i, v in enumerate(table):
        total = total + v * jnp.where(index == i, 1, 0)
    return total


def tile_at(now, n):
    unit = n // 4
    at = lax.div(now, unit)
    row = pick(at, (0, 1, 0, 0, 1, 1, 0, 1))
    return row, pick(at, (3, 3, 2, 1, 2, 1, 0, 0)) * unit + unit - 1 - lax.rem(now, unit)


class TileSum:
    def __init__(self, n, me, o_ref, w_any, scratch):
        self.n, self.me, self.o_ref, self.w_any = n, me, o_ref, w_any
        self.w_ref, self.terms, self.core, self.link = scratch[:4]
        self.sems, self.load = scratch[4:8], scratch[8]
        self.rows, self.span, _ = o_ref.shape

    def scatter(self, row):
        half = self.span // 2
        return Scatter(
            self.n,
            self.me,
            lambda ref, h: ref.at[pl.ds(h * half, half)],
            lambda i: self.core.at[row, i],
            lambda h, i: self.link.at[row, h, i],
            tuple(s.at[row] for s in self.sems),
        )

    def start(self, meet=greet):
        fetch = pltpu.make_async_copy(self.w_any, self.w_ref, self.load.at[0])
        fetch.start()
        meet(self.n, self.me)
        fetch.wait()

    def close(self, row):
        last = self.scatter(row)
        for h in (0, 1):
            here = last.part(self.o_ref.at[row], h)
            joined = [here]
            for i in last.addends(0, h):
                last.link_copy(i, h).wait_recv()
                joined.append(last.link(h, i // 2 - 1))
            add_up(here, joined)

    def step(self, now, a_ref):
        n, terms = self.n, self.terms
        r, k = tile_at(now, n)

        @pl.when(now == 2 * n - n // 4)
        def _():
            self.close(0)

        for i in range(1, n, 2):

            @pl.when((r > 0) & (k == i))
            def _(i=i):
                self.scatter(r - 1).core_copy(i, terms.at[i // 2]).wait_send()

        at = lax.rem(k, 2) * lax.div(k, 2) + (1 - lax.rem(k, 2)) * (n // 2)
        terms[at] = mm(a_ref[...], self.w_ref[...]).astype(BF)
        mine = terms.at[n // 2]
        sums = self.scatter(r)
        for i in range(1, n):

            @pl.when(k == i)
            def _(i=i):
                if i % 2:
                    sums.odd(i, terms.at[i // 2])
                else:
                    sums.even(i, mine)

        @pl.when(k == 0)
        def _():
            sums.core_copy(1, self.core.at[r, 0]).wait_recv()
            add_up(self.o_ref.at[r], [mine, self.core.at[r, 0]])

    def end(self):
        self.close(self.rows - 1)
        self.scatter(self.rows - 1).drain(self.terms.at[self.n // 2])
        for row in range(self.rows - 1):
            for i in range(2, self.n, 2):
                for h in (0, 1):
                    self.scatter(row).link_copy(i, h).wait_send()


def tile_scratch(n, rows, span, w):
    width = w.shape[1]
    return [
        pltpu.VMEM(w.shape, BF),
        pltpu.VMEM((n // 2 + 1, span, width), BF),
        pltpu.VMEM((rows, n // 2, span, width), BF),
        pltpu.VMEM((rows, 2, n // 2 - 1, span // 2, width), BF),
        pltpu.SemaphoreType.DMA((rows, n // 2)),
        pltpu.SemaphoreType.DMA((rows, n // 2)),
        pltpu.SemaphoreType.DMA((rows, 2, n // 2 - 1)),
        pltpu.SemaphoreType.DMA((rows, 2, n // 2 - 1)),
        pltpu.SemaphoreType.DMA((1,)),
    ]


def spread_kernel(
    n, m, a_ref, w_any, x_ref, b_ref, d_any,
    o_ref, grad_ref, total_any,
    acc, own, up, across, line_sems, moves, *scratch,
):
    me, line = lax.axis_index("mp"), lax.axis_index("dp")
    rows = o_ref.shape[0]
    now = pl.program_id(0) * n + pl.program_id(1)
    per = rows * n // BLOCKS
    sums = TileSum(n, me, o_ref, w_any, scratch)
    chunks = own.shape[0]
    at = lambda ref: lambda c: ref.at[c]
    down = Line(m, line, at(own), at(up), at(across), at(up), line_sems)
    bring = pltpu.make_async_copy(d_any, own, moves.at[0])
    send = pltpu.make_async_copy(up, total_any, moves.at[1])

    @pl.when(now == 0)
    def _():
        bring.start()

        def meet(n, me):
            greet_all(n, me, m, line)
            bring.wait()
            for c in range(chunks):
                down.launch(c)

        sums.start(meet)

    sums.step(now, a_ref.at[0, 0])
    for c in range(chunks):

        @pl.when(now == 1 + c)
        def _(c=c):
            down.inward(c)

        @pl.when(now == 3 + c)
        def _(c=c):
            down.outward(c)

    k = lax.rem(now, per)
    term = dg(x_ref[...], b_ref[...], TN)

    @pl.when(k == 0)
    def _():
        acc[...] = term

    @pl.when((k > 0) & (k < per - 1))
    def _():
        acc[...] += term

    @pl.when(k == per - 1)
    def _():
        done = acc[...] + term
        for t in range(grad_ref.shape[0]):
            grad_ref[t] = done[:, 2 * t * TILE : 2 * (t + 1) * TILE].astype(BF)

    @pl.when(now == rows * n - 1)
    def _():
        for c in range(chunks):
            down.drain(c)
        send.start()
        sums.end()
        send.wait()


BLOCKS = 4
CHUNKS = 12


def spread(n, m, a, w, x, down):
    rows, _, span, depth = a.shape
    width = w.shape[1]
    slots = depth // (2 * TILE)
    everything = rows * n * span
    per = rows * n // BLOCKS
    part, block = everything // per, width // BLOCKS
    flat = (slots * TILE // CHUNKS, width)

    def place(r, j):
        row, slot = tile_at(r * n + j, n)
        return (row, xor_of(lax.axis_index("mp"), slot, n), 0, 0)

    def token(r, j):
        return lax.rem(r * n + j, per)

    def column(r, j):
        return lax.div(r * n + j, per)

    hbm = pl.BlockSpec(memory_space=pl.ANY)
    out, grad, total = pl.pallas_call(
        functools.partial(spread_kernel, n, m),
        grid=(rows, n),
        in_specs=[
            pl.BlockSpec((1, 1, span, depth), place),
            hbm,
            pl.BlockSpec((part, block), lambda r, j: (token(r, j), column(r, j))),
            pl.BlockSpec((part, depth), lambda r, j: (token(r, j), 0)),
            hbm,
        ],
        out_specs=[
            pl.BlockSpec(memory_space=pltpu.VMEM),
            pl.BlockSpec((slots, block, 2 * TILE), lambda r, j: (0, column(r, j), 0)),
            hbm,
        ],
        out_shape=[
            jax.ShapeDtypeStruct((rows, span, width), F32),
            jax.ShapeDtypeStruct((slots, width, 2 * TILE), BF),
            jax.ShapeDtypeStruct((CHUNKS,) + flat, BF),
        ],
        scratch_shapes=[
            pltpu.VMEM((block, depth), F32),
            pltpu.VMEM((CHUNKS,) + flat, BF),
            pltpu.VMEM((CHUNKS,) + flat, BF),
            pltpu.VMEM((CHUNKS,) + flat, BF),
            pltpu.SemaphoreType.DMA((6, CHUNKS)),
            pltpu.SemaphoreType.DMA((2,)),
        ]
        + tile_scratch(n, rows, span, w),
        compiler_params=params(mib=63, axes=2, key=3),
        cost_estimate=TINY,
        name="spread",
    )(
        a,
        w,
        x.reshape(everything, width),
        a.reshape(everything, depth),
        down.reshape((CHUNKS,) + flat),
    )
    return out, grad, total.reshape(down.shape)


def shards(
    n,
    m,
    hidden_in,
    doc_ids,
    tile_slot,
    attention_gain,
    query_gain,
    key_gain,
    attend_weight,
    output_weight,
    feed_gain,
    gate_up_slots,
    down_slots,
    out_grad,
):
    rows, span, width = hidden_in.shape
    length = doc_ids.shape[1]
    slots = gate_up_slots.shape[0]
    tokens = rows * span
    me = lax.axis_index("mp")
    offset = me * span

    kw = KVH * HD
    keys_w = attend_weight[:, QW : QW + kw].reshape(-1, KVH, HD)
    values_w = attend_weight[:, QW + kw :].reshape(-1, KVH, HD)
    attend_w = jnp.concatenate(
        [attend_weight[:, :QW], jnp.concatenate([keys_w, values_w], 2).reshape(-1, 2 * kw)], 1
    )
    below = [jnp.sum((doc_ids < d).astype(jnp.int32), axis=1, keepdims=True) for d in (1, 2)]
    local_docs = lax.dynamic_slice_in_dim(doc_ids, offset, span, 1)
    local_start = jnp.where(local_docs == 2, below[1], jnp.where(local_docs == 1, below[0], 0))
    local_pos = offset + jnp.arange(span, dtype=jnp.int32)[None] - local_start
    cos, sin = rotary_tables(local_pos.reshape(tokens))
    gq = jnp.tile(query_gain, 2)[None]
    gk = jnp.concatenate([key_gain, jnp.ones_like(key_gain)])[None]
    ones = jnp.asarray(np.kron(np.eye(LANES // HD), np.ones((HD, HD))), BF)
    key_block = min(512, length)
    info = jnp.stack(
        [
            jnp.full((rows,), me, jnp.int32),
            local_start[:, 0] // key_block,
            local_start[:, -1],
        ],
        1,
    ).astype(jnp.int32)
    start_col = jnp.broadcast_to(local_start[:, :, None], (rows, span, LANES))
    document = jnp.arange(LANES) % HD
    member = (doc_ids[:, :, None] == document).astype(F32)
    ka = jnp.where(document == DOCS, 1.0, member).astype(BF)
    own_member = lax.dynamic_slice_in_dim(member, offset, span, 1)
    qa = jnp.where(document == DOCS, -AWAY, own_member * AWAY).astype(BF)

    x_own = hidden_in.reshape(tokens, width)
    x_value = x_own.astype(F32)
    normed_ab, raw, q, grad_branch, attend_all, kv_all, output_all = project(
        n,
        rows,
        x_own,
        attention_gain[None],
        attend_w,
        output_weight,
        cos,
        sin,
        query_gain[None],
        key_gain[None],
        ones,
        out_grad.reshape(tokens, width),
    )
    q = q.reshape(rows, span, QW)
    kv_all = kv_all.reshape(rows, length, -1)
    output_full = output_all.reshape(QW, width)
    grads_all = lax.all_gather(
        grad_branch.reshape(rows, span, width), "mp", axis=1, tiled=True
    )
    ctx, rl = attend(info, q, kv_all, start_col)
    context_b = ctx.reshape(tokens, QW)
    middle = x_value + mm(context_b, output_full)
    scale_f = rms_scale(middle)
    normed_fb = (middle * scale_f * feed_gain).astype(BF).reshape(rows, span, width)

    slot_index = me * slots + jnp.arange(slots, dtype=jnp.int32)
    live = jnp.any(tile_slot[None, :] == slot_index[:, None], axis=1).astype(F32)
    gate_up_slots, down_slots, middle = lax.optimization_barrier(
        (gate_up_slots, down_slots, middle)
    )
    normed_fb, qa, ka = lax.optimization_barrier((normed_fb, qa, ka))
    gu_t = jnp.swapaxes(gate_up_slots, 1, 2).reshape(slots * 2 * TILE, width)
    d_flat = down_slots.reshape(slots * TILE, width)
    d_t = d_flat.T
    normed_all, hidden, grad_both, grad_down = feed(
        n, live, normed_fb, grads_all, gate_up_slots, d_t
    )
    hidden = hidden.reshape(rows, n, span, -1)
    grad_normed_f, grad_gate_up, down_total = spread(
        n, m, grad_both.reshape(rows, n, span, -1), gu_t, normed_all, grad_down
    )
    gate_up_total = lax.psum(grad_gate_up, "dp")
    grad_normed_f = grad_normed_f.reshape(tokens, width)

    weighted = grad_normed_f * feed_gain
    inner = jnp.mean(weighted * middle, axis=-1, keepdims=True)
    gain_feed = jnp.sum(grad_normed_f * middle * scale_f, axis=0)
    grad_middle = out_grad.reshape(tokens, width) + scale_f * (
        weighted - middle * scale_f * scale_f * inner
    )
    grad_attn_b = grad_middle.astype(BF)
    grad_context = dg(grad_attn_b, output_full, NT).astype(BF).reshape(rows, span, QW)
    grad_output = dg(context_b, grad_attn_b, TN).astype(BF)

    dq, dkv, ffn_out, output_share = attend_back(
        n,
        q,
        kv_all,
        qa,
        ka,
        grad_context,
        ctx,
        rl,
        hidden,
        d_flat,
        grad_output.reshape(n, -1, width),
    )
    layer_out = middle + ffn_out.reshape(tokens, width)
    grad_joined_b, sum_q, sum_k = unproject(
        n,
        dq.reshape(tokens, QW),
        dkv.reshape(rows, n, span, -1),
        raw,
        cos,
        sin,
        gq,
        gk,
        ones,
    )
    down_total = down_total.astype(F32)
    grad_joined_b, layer_out, down_total = lax.optimization_barrier(
        (grad_joined_b, layer_out, down_total)
    )
    input_grad, attend_total, output_total, gains = finish(
        n,
        m,
        normed_ab,
        grad_joined_b,
        attend_all,
        x_own,
        grad_middle,
        attention_gain[None],
        output_share,
        gain_feed.reshape(-1, LANES),
        sum_q,
        sum_k,
    )
    gains = gains.reshape(-1)
    gain_query = gains[2 * width : 2 * width + HD] + gains[2 * width + HD : 2 * width + 2 * HD]
    gain_key = gains[2 * width + LANES : 2 * width + LANES + HD]
    shape = (rows, span, width)
    return (
        layer_out.reshape(shape),
        input_grad.reshape(shape),
        attend_total,
        output_total,
        gate_up_total.astype(F32),
        down_total,
        gains[:width],
        gain_query,
        gain_key,
        gains[width : 2 * width],
    )


def solution(mesh):
    placed = (
        P("dp", "mp", None),
        P("dp", None),
        P(),
        P(),
        P(),
        P(),
        P("mp", None),
        P("mp", None),
        P(),
        P("mp", None, None),
        P("mp", None, None),
        P("dp", "mp", None),
    )
    return jax.shard_map(
        functools.partial(shards, mesh.shape["mp"], mesh.shape["dp"]),
        mesh=mesh,
        in_specs=placed,
        out_specs=(
            P("dp", "mp", None),
            P("dp", "mp", None),
            P("mp", None),
            P("mp", None),
            P("mp", None, None),
            P("mp", None, None),
            P(),
            P(),
            P(),
            P(),
        ),
        check_vma=False,
    )
```
